128 devices in a mesh: rows: 2 (over z_hi), seq: 64 (over x, z_lo, y, core).
Axes of the slice: x: 4, y: 4, z: 4 (z_hi: 2, z_lo: 2; z = z_hi * 2 + z_lo), core: 2. Of those that a mesh axis runs over, the one named last changes fastest.
Arguments:
- tokens: float32 [2, 8192, 576], P('rows', 'seq'), may hold values from -6 to 6
- cotangent: float32 [2, 8192, 576], P('rows', 'seq'), may hold values from -6 to 6
- segment_ids: int32 [2, 8192], P('rows', 'seq'), may hold values from 0 to 15, as said below
- gain_attn: float32 [576], replicated, may hold values from 0.5 to 1.5
- w_query: bfloat16 [576, 576], replicated, may hold values from -0.25 to 0.25
- w_key: bfloat16 [576, 192], replicated, may hold values from -0.25 to 0.25
- w_value: bfloat16 [576, 192], replicated, may hold values from -0.25 to 0.25
- w_out: bfloat16 [576, 576], replicated, may hold values from -4 to 4
- gain_mlp: float32 [576], replicated, may hold values from 0.5 to 1.5
- w_gate: bfloat16 [576, 1536], replicated, may hold values from -0.25 to 0.25
- w_up: bfloat16 [576, 1536], replicated, may hold values from -0.25 to 0.25
- w_down: bfloat16 [1536, 576], replicated, may hold values from -0.15625 to 0.15625
Outputs:
- output: float32 [2, 8192, 576], P('rows', 'seq')
- grad_tokens: float32 [2, 8192, 576], P('rows', 'seq')
- grad_gain_attn: float32 [576], replicated
- grad_query: float32 [576, 576], replicated
- grad_key: float32 [576, 192], replicated
- grad_value: float32 [576, 192], replicated
- grad_out: float32 [576, 576], replicated
- grad_gain_mlp: float32 [576], replicated
- grad_gate: float32 [576, 1536], replicated
- grad_up: float32 [576, 1536], replicated
- grad_down: float32 [1536, 576], replicated
The draws below stay inside these ranges and needn't reach their ends.
Inputs may be any that keep to these rules, and one draw needn't show every extreme that they name: `segment_ids`: along each row the document numbers never fall; some numbers may have no tokens. In one of the rows one document starts within the first 128 tokens and ends within the last 128; the other rows are cut into up to 16 documents at places anywhere in the row.
All inputs are finite; a program needn't handle non-finite values.
Results may differ from the reference program's by a relative error of at most 0.03.
Values may be sent and summed in bfloat16 or wider, within the bound.
A program may use at most 128 MiB of HBM per device.

```python
import math
import jax
import jax.numpy as jnp
from jax import lax

D = 576
HEADS = 9
KV_HEADS = 3
HD = 64
FF = 1536
TOK_DEV = 128
LAYERS = 2
DOCS = 16
SEQ = 8192
ROWS = 2


def draw_segment_ids(key, part):
    key = jax.random.fold_in(key, 7)
    token_index = jnp.arange(SEQ, dtype=jnp.int32)
    key_pick, key_rows = jax.random.split(key, 2)
    spanning_row = jax.random.randint(key_pick, (), 0, ROWS)

    def one_row(row_key, row_number):
        key_begin, key_early, key_end, key_late, key_cuts = jax.random.split(row_key, 5)
        doc_begin = jax.random.randint(key_begin, (), 1, TOK_DEV)
        cut_early = jax.random.randint(key_early, (), 1, doc_begin + 1)
        doc_end = jax.random.randint(key_end, (), SEQ - TOK_DEV + 1, SEQ)
        cut_late = jax.random.randint(key_late, (), doc_end, SEQ)
        spanning = (token_index >= cut_early).astype(jnp.int32) + (token_index >= doc_begin).astype(jnp.int32) + (token_index >= doc_end).astype(jnp.int32) + (token_index >= cut_late).astype(jnp.int32)
        cuts = jnp.sort(jax.random.randint(key_cuts, (DOCS - 1,), 1, SEQ))
        packed = jnp.sum((token_index[:, None] >= cuts[None, :]).astype(jnp.int32), axis=1)
        return jnp.where(row_number == spanning_row, spanning, packed).astype(jnp.int32)
    return jax.vmap(one_row)(jax.random.split(key_rows, ROWS), jnp.arange(ROWS, dtype=jnp.int32))


def block_levels(stream_key, dims, shards, low, high):
    factor_of = 1.0
    for axis_at, parts in shards:
        draws = jax.random.uniform(jax.random.fold_in(jax.random.fold_in(stream_key, 6), axis_at), (parts,), jnp.float32, low / len(shards), high / len(shards))
        factor_of = factor_of * jnp.repeat(jnp.exp(draws), dims[axis_at] // parts).reshape((-1,) + (1,) * (len(dims) - 1 - axis_at))
    return factor_of


def bell_draw(stream_key, dims, width, limit, cuts=(), kind=jnp.bfloat16):
    gain = block_levels(stream_key, dims, cuts, -0.22, 0.18) if cuts else 1.0
    values = jax.random.normal(stream_key, dims, jnp.float32) * width * gain
    return jnp.minimum(jnp.maximum(values, -limit), limit).astype(kind)


def setup_inputs(seed: int = 0) -> dict:
    seeds = jax.random.split(jax.random.key(seed), 13)
    tokens = bell_draw(seeds[0], (ROWS, SEQ, D), 1.0, 6.0, ((0, 2), (1, 64)), jnp.float32)
    cotangent = bell_draw(seeds[1], (ROWS, SEQ, D), 1.0, 6.0, ((0, 2), (1, 64)), jnp.float32)
    segment_ids = draw_segment_ids(jax.random.fold_in(seeds[12], 71), 0)
    gain_attn = jnp.clip(1.0 + 0.1 * jax.random.normal(seeds[3], (D,), jnp.float32), 0.5, 1.5)
    w_query = bell_draw(seeds[4], (D, HEADS * HD), D ** -0.5, 0.25)
    w_key = bell_draw(seeds[5], (D, KV_HEADS * HD), D ** -0.5, 0.25)
    w_value = bell_draw(seeds[6], (D, KV_HEADS * HD), D ** -0.5, 0.25)
    w_out = bell_draw(seeds[7], (HEADS * HD, D), (max(2, HEADS * HD * 16 // SEQ)) ** -0.5, 4.0)
    gain_mlp = jnp.clip(1.0 + 0.1 * jax.random.normal(seeds[8], (D,), jnp.float32), 0.5, 1.5)
    w_gate = bell_draw(seeds[9], (D, FF), D ** -0.5, 0.25)
    w_up = bell_draw(seeds[10], (D, FF), D ** -0.5, 0.25)
    w_down = bell_draw(seeds[11], (FF, D), FF ** -0.5, 0.15625)
    return dict(tokens=tokens, cotangent=cotangent, segment_ids=segment_ids, gain_attn=gain_attn, w_query=w_query, w_key=w_key, w_value=w_value, w_out=w_out, gain_mlp=gain_mlp, w_gate=w_gate, w_up=w_up, w_down=w_down)


highest = lax.Precision.HIGHEST
epsilon = 1e-05
score_scale = 0.125
masked_value = -1e+30

@jax.custom_vjp
def low(v):
    return lax.optimization_barrier(v.astype(jnp.bfloat16)).astype(jnp.float32)

@jax.custom_vjp
def low_back(v):
    return v

def low_keep(v):
    return (low(v), None)

def low_pass(kept, grad):
    return (grad,)

def back_keep(v):
    return (v, None)

def back_low(kept, grad):
    return (low(grad),)
low.defvjp(low_keep, low_pass)
low_back.defvjp(back_keep, back_low)

def matmul(left_side, right_side):
    return jnp.dot(left_side, right_side, precision=highest, preferred_element_type=jnp.float32)

def rms_scale(values, gain_vector):
    return values * lax.rsqrt(lax.optimization_barrier(jnp.mean(values * values, axis=-1, keepdims=True)) + epsilon) * gain_vector

def rotary_tables(positions):
    half_width = HD // 2
    frequencies = jnp.exp(jnp.arange(half_width, dtype=jnp.float32) * (-2.0 / HD) * math.log(10000.0))
    angles = positions.astype(jnp.float32)[:, None] * frequencies[None, :]
    return (jnp.cos(angles)[:, None, :], jnp.sin(angles)[:, None, :])

def rotate(values, cosine_table, sine_table):
    half_width = values.shape[-1] // 2
    front_half = values[..., :half_width]
    back_half = values[..., half_width:]
    return jnp.concatenate([front_half * cosine_table - back_half * sine_table, back_half * cosine_table + front_half * sine_table], axis=-1)

def doc_starts(segments):
    doc_numbers = jnp.arange(DOCS, dtype=jnp.int32)
    doc_sizes = lax.optimization_barrier(jnp.sum((segments[:, None] == doc_numbers[None, :]).astype(jnp.int32), axis=0))
    return lax.optimization_barrier(jnp.sum(jnp.where(segments[:, None] > doc_numbers[None, :], doc_sizes[None, :], 0), axis=1)).astype(jnp.int32)

def attend(queries, key_rows, value_rows, starts):
    length = queries.shape[0]
    block_rows = math.gcd(length, 512)
    key_index = jnp.arange(length, dtype=jnp.int32)

    def one_block(block_args):
        query_block, start_block, index_block = block_args
        scores = jnp.einsum('tgjd,ngd->tgjn', query_block, key_rows, precision=highest) * score_scale
        scores = low_back(scores)
        allowed = (key_index[None, :] >= start_block[:, None]) & (key_index[None, :] <= index_block[:, None])
        allowed = allowed[:, None, None, :]
        scores = jnp.where(allowed, scores, masked_value)
        top_score = lax.optimization_barrier(jnp.max(scores, axis=-1, keepdims=True))
        exponents = jnp.where(allowed, jnp.exp(scores - top_score), 0.0)
        probabilities = exponents / lax.optimization_barrier(jnp.sum(exponents, axis=-1, keepdims=True))
        return jnp.einsum('tgjn,ngd->tgjd', low(probabilities), value_rows, precision=highest)
    block_count = length // block_rows
    pieces = (queries.reshape((block_count, block_rows) + queries.shape[1:]), starts.reshape(block_count, block_rows), key_index.reshape(block_count, block_rows))
    result = lax.map(jax.checkpoint(one_block), pieces)
    return result.reshape(queries.shape)

def block_pass(inputs, params, starts, cosine_table, sine_table):
    gain_attn, w_query, w_key, w_value, w_out, gain_mlp, w_gate, w_up, w_down = params
    length = inputs.shape[0]
    group_size = HEADS // KV_HEADS
    normed = low(rms_scale(inputs, gain_attn))
    query_pre = low_back(matmul(normed, w_query))
    key_pre = low_back(matmul(normed, w_key))
    value_rows = low(low_back(matmul(normed, w_value)))
    query_rot = low(rotate(query_pre.reshape(length, HEADS, HD), cosine_table, sine_table))
    key_rot = low(rotate(key_pre.reshape(length, KV_HEADS, HD), cosine_table, sine_table))
    attended = attend(query_rot.reshape(length, KV_HEADS, group_size, HD), key_rot, value_rows.reshape(length, KV_HEADS, HD), starts)
    attended = low(low_back(attended.reshape(length, HEADS * HD)))
    middle = inputs + low_back(matmul(attended, w_out))
    normed_mlp = low(rms_scale(middle, gain_mlp))
    gate_rows = low_back(matmul(normed_mlp, w_gate))
    upward = low_back(matmul(normed_mlp, w_up))
    hidden = low(gate_rows * jax.nn.sigmoid(gate_rows) * upward)
    return middle + low_back(matmul(hidden, w_down))

def reference(tokens, cotangent, segment_ids, gain_attn, w_query, w_key, w_value, w_out, gain_mlp, w_gate, w_up, w_down):
    weights = tuple((weight_array.astype(jnp.float32) for weight_array in (gain_attn, w_query, w_key, w_value, w_out, gain_mlp, w_gate, w_up, w_down)))
    row_tables = []
    for row_number in range(ROWS):
        starts = doc_starts(segment_ids[row_number])
        positions = jnp.arange(SEQ, dtype=jnp.int32) - starts
        cosine_table, sine_table = rotary_tables(positions)
        row_tables.append((starts, cosine_table, sine_table))

    def forward(inputs, params):
        outputs = []
        for row_number in range(ROWS):
            row_state = inputs[row_number]
            starts, cosine_table, sine_table = row_tables[row_number]
            for repeat in range(LAYERS):
                row_state = block_pass(row_state, params, starts, cosine_table, sine_table)
            outputs.append(row_state)
        return jnp.stack(outputs)
    output, pullback = jax.vjp(forward, tokens.astype(jnp.float32), weights)
    grad_tokens, weight_grads = pullback(cotangent.astype(jnp.float32))
    return (output, grad_tokens, weight_grads[0], weight_grads[1], weight_grads[2], weight_grads[3], weight_grads[4], weight_grads[5], weight_grads[6], weight_grads[7], weight_grads[8])
```

```python
import functools
import math

import jax
import jax.numpy as jnp
from jax import lax
from jax.experimental import pallas as pl
from jax.experimental.pallas import tpu as pltpu
from jax.sharding import PartitionSpec as P

F32 = jnp.float32
BF16 = jnp.bfloat16
MESH = pl.DeviceIdType.MESH

D = 576
HEADS = 9
HD = 64
KV = 192
FF = 1536
TOK = 128
DOCS = 16
EPS = 1e-05
SCALE = 0.125
EXP_SCALE = SCALE * 1.4426950408889634
MASKED = -1e30
LOWEST = -1e20

VM = pl.BlockSpec(memory_space=pltpu.VMEM)


def dot(a, b, ca, cb):
    return lax.dot_general(a, b, (((ca,), (cb,)), ((), ())), preferred_element_type=F32)


def sds(shape, dtype):
    return jax.ShapeDtypeStruct(shape, dtype)


def params(collective=None, limit=50 << 20):
    if collective is None:
        return pltpu.CompilerParams(vmem_limit_bytes=limit)
    return pltpu.CompilerParams(
        vmem_limit_bytes=limit, collective_id=collective, has_side_effects=True
    )


def place():
    seq = lax.axis_index("seq")
    row = lax.axis_index("rows")
    return row, seq, seq // 8, lax.rem(seq, 8)


def slot_of(w):
    return lax.rem(w, 2) * 4 + w // 2


def octet_of(n, w):
    return jnp.where(lax.rem(w, 2) == 0, n, 7 - n)


def greet(row, n, w):
    bar = pltpu.get_barrier_semaphore()
    for k in range(1, 8):
        pl.semaphore_signal(
            bar, inc=1, device_id=(row, 8 * n + lax.rem(w + k, 8)), device_id_type=MESH
        )
        pl.semaphore_signal(
            bar, inc=1, device_id=(row, 8 * lax.rem(n + k, 8) + w), device_id_type=MESH
        )
    return bar


def remote(src, dst, send, recv, target):
    return pltpu.make_async_remote_copy(
        src_ref=src,
        dst_ref=dst,
        send_sem=send,
        recv_sem=recv,
        device_id=target,
        device_id_type=MESH,
    )


def entry_kernel(
    tok_ref, ids_ref, x_ref, starts_ref, pos_ref, ids_all, starts_all, ysend, yrecv, xsend, xrecv,
    tsend, trecv
):
    row, seq, n, w = place()
    core = lax.rem(w, 2)
    mirror = 8 * (7 - n) + w
    bar = greet(row, n, w)

    pl.semaphore_wait(bar, 14)
    move = remote(tok_ref, x_ref, tsend, trecv, (row, mirror))

    @pl.when(core == 1)
    def _():
        move.start()

    ids_all[seq] = ids_ref[...]
    sent = []
    for k in range(1, 8):
        cp = remote(
            ids_all.at[seq], ids_all.at[seq], ysend.at[k], yrecv.at[k],
            (row, 8 * n + lax.rem(w + k, 8)),
        )
        cp.start()
        sent.append(cp)
    for cp in sent:
        cp.wait()
    own = ids_all.at[pl.ds(8 * n, 8)]
    sent = []
    for k in range(1, 8):
        cp = remote(own, own, xsend.at[k], xrecv.at[k], (row, 8 * lax.rem(n + k, 8) + w))
        cp.start()
        sent.append(cp)
    for cp in sent:
        cp.wait()

    ids = jnp.concatenate([ids_all[i] for i in range(64)], axis=0)
    total = jnp.zeros((64, TOK), jnp.int32)
    for doc in range(DOCS - 1):
        count = jnp.where(ids == doc, 1.0, 0.0)
        count = jnp.sum(jnp.sum(count, axis=0, keepdims=True), axis=1, keepdims=True)
        total = total + jnp.where(ids > doc, count.astype(jnp.int32), 0)
    starts_all[...] = total[:, None, :]
    for half in range(2):
        octet = n if half == 0 else 7 - n
        for y in range(4):
            starts_ref[half, :, TOK * y : TOK * y + TOK] = starts_all[8 * octet + 2 * y + half]
    mine = 8 * octet_of(n, w) + w
    pos_ref[...] = (
        mine * TOK + lax.broadcasted_iota(jnp.int32, (1, TOK), 1) - starts_all[mine]
    )

    @pl.when(core == 1)
    def _():
        move.wait()

    @pl.when(core == 0)
    def _():
        x_ref[...] = tok_ref[...]


def entry(tokens, ids):
    return pl.pallas_call(
        entry_kernel,
        name="entry",
        out_shape=(
            sds((TOK, D), F32),
            sds((2, 1, 4 * TOK), jnp.int32),
            sds((1, TOK), jnp.int32),
        ),
        in_specs=[VM] * 2,
        out_specs=(VM,) * 3,
        scratch_shapes=[
            pltpu.VMEM((64, 1, TOK), jnp.int32),
            pltpu.VMEM((64, 1, TOK), jnp.int32),
        ]
        + [pltpu.SemaphoreType.DMA((8,))] * 4
        + [pltpu.SemaphoreType.DMA] * 2,
        compiler_params=params(1),
    )(tokens, ids)


def norm_in(x, gain):
    inverse = lax.rsqrt(jnp.mean(x * x, axis=-1, keepdims=True) + EPS)
    return (x * inverse * gain).astype(BF16), inverse


def norm_back(x, inverse, gain, grad):
    scaled = grad * gain
    grad_gain = jnp.sum(grad * (x * inverse), axis=0, keepdims=True)
    inner = jnp.mean(scaled * x, axis=-1, keepdims=True)
    return inverse * scaled - x * (inverse * inverse * inverse) * inner, grad_gain


def project(x, gain, wq, wk, wv, cos, sin, q_out, kv_out, h_out):
    h, _ = norm_in(x, gain)
    h_out[...] = h
    qt = dot(h, wq, 1, 0).T
    for i in range(HEADS):
        a = qt[HD * i : HD * i + 32]
        b = qt[HD * i + 32 : HD * i + 64]
        q_out[HD * i : HD * i + 32, :] = (a * cos - b * sin).astype(BF16)
        q_out[HD * i + 32 : HD * i + 64, :] = (b * cos + a * sin).astype(BF16)
    kt = dot(h, wk, 1, 0).T
    for i in range(3):
        a = kt[HD * i : HD * i + 32]
        b = kt[HD * i + 32 : HD * i + 64]
        kv_out[HD * i : HD * i + 32, :] = (a * cos - b * sin).astype(BF16)
        kv_out[HD * i + 32 : HD * i + 64, :] = (b * cos + a * sin).astype(BF16)
    kv_out[KV:, :] = dot(h, wv, 1, 0).T.astype(BF16)


def combine(part, stat, o_out, lse_out):
    tops = [stat[i, 0:HEADS, :] for i in range(8)]
    top = functools.reduce(jnp.maximum, tops)
    factors = [jnp.exp2((t - top) * EXP_SCALE) for t in tops]
    total = sum(f * stat[i, 16 : 16 + HEADS, :] for i, f in enumerate(factors))
    inverse = 1.0 / total
    factors = [f * inverse for f in factors]
    lse_out[0:HEADS, :] = top + jnp.log2(total) * (1.0 / EXP_SCALE)
    for h in range(HEADS):
        rows = slice(HD * h, HD * h + HD)
        o_out[rows, :] = sum(
            part[i, rows, :].astype(F32) * factors[i][h : h + 1, :] for i in range(8)
        )


def feed_forward(x, o_t, wo, gain, wg, wu, wd):
    x1 = x + dot(o_t, wo, 0, 0)
    h2, inverse = norm_in(x1, gain)
    gate = dot(h2, wg, 1, 0)
    up = dot(h2, wu, 1, 0)
    hid = (gate * jax.nn.sigmoid(gate) * up).astype(BF16)
    return x1, h2, inverse, gate, up, hid, x1 + dot(hid, wd, 1, 0)


def feed_back(g, x1, inverse, gate, up, wo, gain, wg, wu, wd, o_ref, lse,
              do_out, stat_out, gm_out, dgate_out, dup_out, da_out):
    gm = g.astype(BF16)
    gm_out[...] = gm
    dhid = dot(gm, wd, 1, 1)
    sg = jax.nn.sigmoid(gate)
    dgate = (dhid * up * sg * (1.0 + gate * (1.0 - sg))).astype(BF16)
    dup = (dhid * gate * sg).astype(BF16)
    dgate_out[...] = dgate
    dup_out[...] = dup
    dh2 = dot(dgate, wg, 1, 1) + dot(dup, wu, 1, 1)
    dy, grad_gain = norm_back(x1, inverse, gain, dh2)
    dx1 = g + dy
    da = dx1.astype(BF16)
    da_out[...] = da
    do_t = dot(wo, da, 1, 1).astype(BF16)
    do_out[...] = do_t
    stat_out[...] = jnp.zeros(stat_out.shape, F32)
    stat_out[0:HEADS, :] = lse
    for h in range(HEADS):
        rows = slice(HD * h, HD * h + HD)
        stat_out[16 + h : 17 + h, :] = jnp.sum(
            do_t[rows].astype(F32) * o_ref[rows, :], axis=0, keepdims=True
        )
    return dx1, grad_gain


def project_back(dq_part, dkv_part, x, dx1, gain, wq, wk, wv, cos, sin, dqkv_out):
    for h in range(HEADS + 3):
        part, base = (dq_part, HD * h) if h < HEADS else (dkv_part, HD * (h - HEADS))
        a = sum(part[i, base : base + 32, :].astype(F32) for i in range(8))
        b = sum(part[i, base + 32 : base + 64, :].astype(F32) for i in range(8))
        dqkv_out[HD * h : HD * h + 32, :] = (a * cos + b * sin).astype(BF16)
        dqkv_out[HD * h + 32 : HD * h + 64, :] = (b * cos - a * sin).astype(BF16)
    dqkv_out[D + KV :, :] = sum(dkv_part[i, KV:, :].astype(F32) for i in range(8)).astype(BF16)
    dh1 = (
        dot(dqkv_out[0:D, :], wq, 0, 1)
        + dot(dqkv_out[D : D + KV, :], wk, 0, 1)
        + dot(dqkv_out[D + KV :, :], wv, 0, 1)
    )
    inverse = lax.rsqrt(jnp.mean(x * x, axis=-1, keepdims=True) + EPS)
    dy, grad_gain = norm_back(x, inverse, gain, dh1)
    return dx1 + dy, grad_gain


Q_T = sds((D, TOK), BF16)
KV_T = sds((2 * KV, TOK), BF16)
H_S = sds((TOK, D), BF16)
X_S = sds((TOK, D), F32)
F_S = sds((TOK, FF), F32)
FB_S = sds((TOK, FF), BF16)
ST_S = sds((32, TOK), F32)
G_S = sds((1, D), F32)


def project_kernel(x, gain, wq, wk, wv, cos, sin, q_out, kv_out, h_out):
    project(x[...], gain[...], wq[...], wk[...], wv[...], cos[...], sin[...], q_out, kv_out, h_out)


def middle_kernel(
    part, stat, x, ga, wq, wk, wv, wo, gm, wg, wu, wd, cos, sin,
    q_out, kv_out, h_out, x_out, x1_out, h2_out, inv_out, gate_out, up_out, hid_out, o_out, lse_out
):
    combine(part, stat, o_out, lse_out)
    x1, h2, inverse, gate, up, hid, x2 = feed_forward(
        x[...], o_out[...].astype(BF16), wo[...], gm[...], wg[...], wu[...], wd[...]
    )
    x1_out[...] = x1
    h2_out[...] = h2
    inv_out[...] = jnp.broadcast_to(inverse, inv_out.shape)
    gate_out[...] = gate
    up_out[...] = up
    hid_out[...] = hid
    x_out[...] = x2
    project(x2, ga[...], wq[...], wk[...], wv[...], cos[...], sin[...], q_out, kv_out, h_out)


def turn_kernel(
    part, stat, x, g, wo, gm, wg, wu, wd,
    x_out, h2_out, hid_out, ob_out, do_out, stat_out, gmo, dgate, dup, da, dx1_out, gg_out, o_s, lse_s
):
    combine(part, stat, o_s, lse_s)
    ob = o_s[...].astype(BF16)
    ob_out[...] = ob
    x1, h2, inverse, gate, up, hid, x2 = feed_forward(
        x[...], ob, wo[...], gm[...], wg[...], wu[...], wd[...]
    )
    h2_out[...] = h2
    hid_out[...] = hid
    x_out[...] = x2
    dx1, gg = feed_back(
        g[...], x1, inverse, gate, up, wo[...], gm[...], wg[...], wu[...], wd[...], o_s,
        lse_s[0:HEADS, :], do_out, stat_out, gmo, dgate, dup, da
    )
    dx1_out[...] = dx1
    gg_out[...] = gg


def between_kernel(
    dq, dkv, x, dx1, ga, wq, wk, wv, cos, sin, x1, inv, gate, up, wo, gm, wg, wu, wd, o, lse,
    dqkv_out, gga_out, do_out, stat_out, gmo, dgate, dup, da, dx1_out, ggm_out
):
    g, gga = project_back(
        dq, dkv, x[...], dx1[...], ga[...], wq[...], wk[...], wv[...], cos[...], sin[...], dqkv_out
    )
    gga_out[...] = gga
    dx0, ggm = feed_back(
        g, x1[...], inv[:, 0:1], gate[...], up[...], wo[...], gm[...], wg[...], wu[...], wd[...], o,
        lse[0:HEADS, :], do_out, stat_out, gmo, dgate, dup, da
    )
    dx1_out[...] = dx0
    ggm_out[...] = ggm


def last_kernel(dq, dkv, x, dx1, ga, wq, wk, wv, cos, sin, dqkv_out, gga_out, g_out):
    g, gga = project_back(
        dq, dkv, x[...], dx1[...], ga[...], wq[...], wk[...], wv[...], cos[...], sin[...], dqkv_out
    )
    gga_out[...] = gga
    g_out[...] = g


def local(kernel, name, outs, args, scratch=()):
    return pl.pallas_call(
        kernel,
        name=name,
        out_shape=tuple(outs),
        in_specs=[VM] * len(args),
        out_specs=(VM,) * len(outs),
        scratch_shapes=list(scratch),
        compiler_params=params(),
    )(*args)


def gather_queries(row, n, w, blocks, send, recv):
    core = lax.rem(w, 2)
    y = w // 2
    partner = (row, 8 * n + 2 * y + 1 - core)
    own = core * 4 + y
    started = []
    for k in range(1, 4):
        peer = (row, 8 * n + 2 * lax.rem(y + k, 4) + core)
        for i, ref in enumerate(blocks):
            cp = remote(ref.at[own], ref.at[own], send.at[i, k], recv.at[i, k], peer)
            cp.start()
            started.append((i, k, cp))
    passed = []
    for i, ref in enumerate(blocks):
        cp = remote(ref.at[own], ref.at[own], send.at[i, 4], recv.at[i, 4], partner)
        cp.start()
        passed.append(cp)
    for k in range(1, 4):
        came = core * 4 + lax.rem(y + 4 - k, 4)
        for i, ref in enumerate(blocks):
            started[(k - 1) * len(blocks) + i][2].wait_recv()
            cp = remote(ref.at[came], ref.at[came], send.at[i, 4 + k], recv.at[i, 4 + k], partner)
            cp.start()
            passed.append(cp)
    return [s[2] for s in started], passed


def gather_keys(row, n, w, ref, send, recv):
    own = octet_of(n, w)
    started = []
    for k in range(1, 8):
        cp = remote(
            ref.at[own], ref.at[own], send.at[k], recv.at[k], (row, 8 * lax.rem(n + k, 8) + w)
        )
        cp.start()
        started.append(cp)
    return started


def steps_of(n):
    return (n + 2) // 2


def mask_of(w, kc, sel, starts_ref, n):
    line = lax.broadcasted_iota(jnp.int32, (256, 512), 0)
    key = (2 * kc + line // TOK) * 1024 + w * TOK + lax.rem(line, TOK)
    col = lax.broadcasted_iota(jnp.int32, (1, 512), 1)
    octet = jnp.where(sel == 0, n, 7 - n)
    query = octet * 1024 + (2 * (col // TOK) + sel) * TOK + lax.rem(col, TOK)
    return jnp.where((key >= starts_ref[sel]) & (key <= query), 0.0, MASKED)


def attend_kernel(
    q_ref, kv_ref, starts_ref, q_all, kv_all, part_ref, stat_ref,
    k_nat, bias, top, total, acc, o_low, o_stat, qs, qr, ks, kr, os, orr
):
    row, seq, n, w = place()
    bar = greet(row, n, w)
    own_q = slot_of(w)
    q_all[own_q] = q_ref[...]
    kv_all[octet_of(n, w)] = kv_ref[...]
    pl.semaphore_wait(bar, 14)
    keys = gather_keys(row, n, w, kv_all, ks, kr)
    first, passed = gather_queries(row, n, w, [q_all], qs, qr)
    top[...] = jnp.full(top.shape, LOWEST, F32)
    total[...] = jnp.zeros(total.shape, F32)
    acc[...] = jnp.zeros(acc.shape, F32)
    for cp in keys:
        cp.wait()
    for g in range(3):
        for j in range(8):
            k_nat[g, j // 2, (j % 2) * TOK : (j % 2) * TOK + TOK, :] = jnp.transpose(
                kv_all[j, HD * g : HD * g + HD, :]
            )
    for cp in first:
        cp.wait_send()
    for cp in passed:
        cp.wait()
    turn = steps_of(n)

    def step(t, carry):
        sel = jnp.where(t >= turn, 1, 0)
        kc = jnp.where(t >= turn, t - turn, t)
        bias[...] = mask_of(w, kc, sel, starts_ref, n)
        for h in range(HEADS):
            g = h // 3
            qt = jnp.concatenate(
                [q_all[4 * sel + y, HD * h : HD * h + HD, :] for y in range(4)], axis=1
            )
            s = dot(k_nat[g, kc], qt, 1, 0) + bias[...]
            old = top[sel, h : h + 1, :]
            new = jnp.maximum(old, jnp.max(s, axis=0, keepdims=True))
            p = jnp.exp2((s - new) * EXP_SCALE)
            shrink = jnp.exp2((old - new) * EXP_SCALE)
            top[sel, h : h + 1, :] = new
            total[sel, h : h + 1, :] = total[sel, h : h + 1, :] * shrink + jnp.sum(
                p, axis=0, keepdims=True
            )
            vt = jnp.concatenate(
                [kv_all[2 * kc + i, KV + HD * g : KV + HD * g + HD, :] for i in range(2)], axis=1
            )
            rows = slice(HD * h, HD * h + HD)
            acc[sel, rows, :] = acc[sel, rows, :] * shrink + dot(vt, p.astype(BF16), 1, 0)
        return carry

    lax.fori_loop(0, 5, step, 0)
    for half in range(2):
        for y in range(4):
            cols = slice(TOK * y, TOK * y + TOK)
            o_low[4 * half + y] = acc[half, :, cols].astype(BF16)
            o_stat[4 * half + y, 0:16, :] = top[half, :, cols]
            o_stat[4 * half + y, 16:32, :] = total[half, :, cols]
    sent = []
    for k in range(1, 8):
        to = lax.rem(w + k, 8)
        peer = (row, 8 * n + to)
        cp = remote(o_low.at[slot_of(to)], part_ref.at[own_q], os.at[0, k], orr.at[0, k], peer)
        cp.start()
        sent.append(cp)
        cp = remote(o_stat.at[slot_of(to)], stat_ref.at[own_q], os.at[1, k], orr.at[1, k], peer)
        cp.start()
        sent.append(cp)
    part_ref[own_q] = o_low[own_q]
    stat_ref[own_q] = o_stat[own_q]
    for cp in sent:
        cp.wait()


DMA = pltpu.SemaphoreType.DMA


def attend(q, kv, starts):
    return pl.pallas_call(
        attend_kernel,
        name="attend",
        out_shape=(
            sds((8, D, TOK), BF16),
            sds((8, 2 * KV, TOK), BF16),
            sds((8, D, TOK), BF16),
            sds((8, 32, TOK), F32),
        ),
        in_specs=[VM] * 3,
        out_specs=(VM,) * 4,
        scratch_shapes=[
            pltpu.VMEM((3, 4, 256, HD), BF16),
            pltpu.VMEM((256, 512), F32),
            pltpu.VMEM((2, 16, 512), F32),
            pltpu.VMEM((2, 16, 512), F32),
            pltpu.VMEM((2, D, 512), F32),
            pltpu.VMEM((8, D, TOK), BF16),
            pltpu.VMEM((8, 32, TOK), F32),
            DMA((1, 8)), DMA((1, 8)), DMA((8,)), DMA((8,)), DMA((2, 8)), DMA((2, 8)),
        ],
        compiler_params=params(2),
    )(q, kv, starts)


def attend_back_kernel(
    do_ref, st_ref, q_all, kv_all, starts_ref, dq_part, dkv_part,
    do_all, st_all, k_nat, v_nat, bias, dq, dkv, dq_low, dkv_low, qs, qr, os, orr, ks, kr
):
    row, seq, n, w = place()
    bar = greet(row, n, w)
    own_q = slot_of(w)
    do_all[own_q] = do_ref[...]
    st_all[own_q] = st_ref[...]
    pl.semaphore_wait(bar, 14)
    first, passed = gather_queries(row, n, w, [do_all, st_all], qs, qr)
    dq[...] = jnp.zeros(dq.shape, F32)
    dkv[...] = jnp.zeros(dkv.shape, F32)
    for g in range(3):
        for j in range(8):
            at = slice((j % 2) * TOK, (j % 2) * TOK + TOK)
            k_nat[g, j // 2, at, :] = jnp.transpose(kv_all[j, HD * g : HD * g + HD, :])
            v_nat[g, j // 2, at, :] = jnp.transpose(kv_all[j, KV + HD * g : KV + HD * g + HD, :])
    for cp in first:
        cp.wait_send()
    for cp in passed:
        cp.wait()
    turn = steps_of(n)

    def step(t, carry):
        sel = jnp.where(t >= turn, 1, 0)
        kc = jnp.where(t >= turn, t - turn, t)
        bias[...] = mask_of(w, kc, sel, starts_ref, n)
        for h in range(HEADS):
            g = h // 3
            rows = slice(HD * h, HD * h + HD)
            qt = jnp.concatenate([q_all[4 * sel + y, rows, :] for y in range(4)], axis=1)
            dt = jnp.concatenate([do_all[4 * sel + y, rows, :] for y in range(4)], axis=1)
            lse = jnp.concatenate([st_all[4 * sel + y, h : h + 1, :] for y in range(4)], axis=1)
            dsum = jnp.concatenate(
                [st_all[4 * sel + y, 16 + h : 17 + h, :] for y in range(4)], axis=1
            )
            s = dot(k_nat[g, kc], qt, 1, 0) + bias[...]
            p = jnp.exp2((s - lse) * EXP_SCALE)
            dp = dot(v_nat[g, kc], dt, 1, 0)
            ds = (p * (dp - dsum)).astype(BF16)
            keys = slice(HD * g, HD * g + HD)
            values = slice(KV + HD * g, KV + HD * g + HD)
            dkv[kc, keys, :] += dot(qt, ds, 1, 1)
            dkv[kc, values, :] += dot(dt, p.astype(BF16), 1, 1)
            kt = jnp.concatenate([kv_all[2 * kc + i, keys, :] for i in range(2)], axis=1)
            dq[sel, rows, :] += dot(kt, ds, 1, 0)
        return carry

    lax.fori_loop(0, 5, step, 0)
    for j in range(8):
        cols = slice((j % 2) * TOK, (j % 2) * TOK + TOK)
        dkv_low[j, 0:KV, :] = (dkv[j // 2, 0:KV, cols] * SCALE).astype(BF16)
        dkv_low[j, KV:, :] = dkv[j // 2, KV:, cols].astype(BF16)
    own_k = octet_of(n, w)
    sent = []
    for k in range(1, 8):
        to = lax.rem(n + k, 8)
        cp = remote(
            dkv_low.at[octet_of(to, w)], dkv_part.at[n], ks.at[k], kr.at[k], (row, 8 * to + w)
        )
        cp.start()
        sent.append(cp)
    for half in range(2):
        for y in range(4):
            cols = slice(TOK * y, TOK * y + TOK)
            dq_low[4 * half + y] = (dq[half, :, cols] * SCALE).astype(BF16)
    for k in range(1, 8):
        to = lax.rem(w + k, 8)
        cp = remote(
            dq_low.at[slot_of(to)], dq_part.at[own_q], os.at[k], orr.at[k], (row, 8 * n + to)
        )
        cp.start()
        sent.append(cp)
    dkv_part[n] = dkv_low[own_k]
    dq_part[own_q] = dq_low[own_q]
    for cp in sent:
        cp.wait()


def attend_back(do, st, q_all, kv_all, starts):
    return pl.pallas_call(
        attend_back_kernel,
        name="attend_back",
        out_shape=(sds((8, D, TOK), BF16), sds((8, 2 * KV, TOK), BF16)),
        in_specs=[VM] * 5,
        out_specs=(VM,) * 2,
        scratch_shapes=[
            pltpu.VMEM((8, D, TOK), BF16),
            pltpu.VMEM((8, 32, TOK), F32),
            pltpu.VMEM((3, 4, 256, HD), BF16),
            pltpu.VMEM((3, 4, 256, HD), BF16),
            pltpu.VMEM((256, 512), F32),
            pltpu.VMEM((2, D, 512), F32),
            pltpu.VMEM((4, 2 * KV, 256), F32),
            pltpu.VMEM((8, D, TOK), BF16),
            pltpu.VMEM((8, 2 * KV, TOK), BF16),
            DMA((2, 8)), DMA((2, 8)), DMA((8,)), DMA((8,)), DMA((8,)), DMA((8,)),
        ],
        compiler_params=params(3),
    )(do, st, q_all, kv_all, starts)


def weights_kernel(
    h1a, h1b, dqa, dqb, oa, ob, daa, dab, h2a, h2b, dga, dgb, dua, dub, hida, hidb, gma, gmb, g_out
):
    def both(a, b):
        return jnp.concatenate([a[...], b[...]], axis=0)

    h1t = both(h1a, h1b).T
    ot = jnp.concatenate([oa[...], ob[...]], axis=1)
    h2t = both(h2a, h2b).T
    gmt = both(gma, gmb).T
    for i in range(6):
        cols = slice(256 * i, 256 * i + 256)
        g_out[i] = dot(h2t, jnp.concatenate([dga[:, cols], dgb[:, cols]], axis=0), 1, 0).astype(BF16)
        g_out[6 + i] = dot(h2t, jnp.concatenate([dua[:, cols], dub[:, cols]], axis=0), 1, 0).astype(
            BF16
        )
        g_out[12 + i] = dot(
            gmt, jnp.concatenate([hida[:, cols], hidb[:, cols]], axis=0), 1, 0
        ).astype(BF16)
    dat = both(daa, dab).T
    pad = jnp.zeros((64, 256), BF16)
    for i in range(6):
        out = None
        if i < 4:
            rows = slice(256 * i, min(256 * i + 256, 960))
            rhs = jnp.concatenate([dqa[rows, :], dqb[rows, :]], axis=1)
            if i == 3:
                rhs = jnp.concatenate([rhs, pad], axis=0)
            out = dot(h1t, rhs, 1, 1)
        if i >= 3:
            if i == 3:
                rhs = jnp.concatenate([jnp.zeros((192, 256), BF16), dat[0:64]], axis=0)
            else:
                rhs = dat[64 + 256 * (i - 4) : 64 + 256 * (i - 3)]
            more = dot(ot, rhs, 1, 1)
            out = more if out is None else out + more
        g_out[18 + i] = out.astype(BF16)


def reduce_kernel(
    g_ref, gain_ref, out_ref, gain_out,
    from_core, half, one, two, three, gather, gain_in, gain_sum, cs, cr, s1, r1, s2, r2, s3, r3, s4, r4, s5, r5, s6, r6, gs, gr
):
    row, seq, n, w = place()
    core = lax.rem(w, 2)
    spot = (n // 2, w // 2, 2 * row + lax.rem(n, 2))

    def device(x, y, z, c):
        return (z // 2, ((x * 2 + lax.rem(z, 2)) * 4 + y) * 2 + c)

    def along(axis, k):
        to = list(spot)
        to[axis] = lax.rem(spot[axis] + k, 4)
        return device(*to, core), to[axis]

    partner = device(*spot, 1 - core)
    bar = pltpu.get_barrier_semaphore()
    pl.semaphore_signal(bar, inc=1, device_id=partner, device_id_type=MESH)
    for axis in range(3):
        for k in range(1, 4):
            pl.semaphore_signal(bar, inc=1, device_id=along(axis, k)[0], device_id_type=MESH)
    pl.semaphore_wait(bar, 10)

    def gain_round(i, peers, count, at):
        gain_in[i, at] = gain_sum[...]
        cps = []
        for k, peer in enumerate(peers):
            cp = remote(gain_sum, gain_in.at[i, at], gs.at[i, k], gr.at[i, k], peer)
            cp.start()
            cps.append(cp)
        for cp in cps:
            cp.wait()
        gain_sum[...] = sum(gain_in[i, j] for j in range(count))

    cps = []
    for p in range(3):
        cp = remote(
            g_ref.at[pl.ds(12 * (1 - core) + 4 * p, 4)], from_core.at[pl.ds(4 * p, 4)],
            cs.at[p], cr.at[p], partner
        )
        cp.start()
        cps.append(cp)
    gain_sum[...] = gain_ref[...]
    gain_round(0, [partner], 2, core)
    ones = []
    for p in range(3):
        cps[p].wait()
        for i in range(4):
            half[4 * p + i] = (
                g_ref[12 * core + 4 * p + i].astype(F32) + from_core[4 * p + i].astype(F32)
            ).astype(BF16)
        for k in range(1, 4):
            peer, at = along(p, k)
            cp = remote(half.at[4 * p + at], one.at[p, k - 1], s1.at[p, k], r1.at[p, k], peer)
            cp.start()
            ones.append(cp)
    gain_round(1, [along(0, k)[0] for k in range(1, 4)], 4, spot[0])
    twos = []
    for p in range(3):
        for cp in ones[3 * p : 3 * p + 3]:
            cp.wait()
        gather[p] = (
            half[4 * p + spot[p]].astype(F32) + sum(one[p, k].astype(F32) for k in range(3))
        ).astype(BF16)
        axis = (p + 1) % 3
        for k in range(1, 4):
            peer, at = along(axis, k)
            cp = remote(
                gather.at[p, pl.ds(144 * at, 144)], two.at[p, k - 1], s2.at[p, k], r2.at[p, k], peer
            )
            cp.start()
            twos.append(cp)
    gain_round(2, [along(1, k)[0] for k in range(1, 4)], 4, spot[1])
    threes = []
    for p in range(3):
        for cp in twos[3 * p : 3 * p + 3]:
            cp.wait()
        b = spot[(p + 1) % 3]
        c = spot[(p + 2) % 3]
        three[p, c] = (
            gather[p, pl.ds(pl.multiple_of(144 * b, 16), 144)].astype(F32)
            + sum(two[p, k].astype(F32) for k in range(3))
        ).astype(BF16)
        for k in range(1, 4):
            peer, at = along((p + 2) % 3, k)
            cp = remote(three.at[p, c], three.at[p, c], s3.at[p, k], r3.at[p, k], peer)
            cp.start()
            threes.append(cp)
    gain_round(3, [along(2, k)[0] for k in range(1, 4)], 4, spot[2])
    gain_out[...] = gain_sum[...]
    fours = []
    for p in range(3):
        for cp in threes[3 * p : 3 * p + 3]:
            cp.wait()
        b = spot[(p + 1) % 3]
        mine = one.at[p, 0, pl.ds(pl.multiple_of(144 * b, 16), 144)]
        mine[...] = sum(three[p, k].astype(F32) for k in range(4)).astype(BF16)
        for k in range(1, 4):
            peer, at = along((p + 1) % 3, k)
            cp = remote(mine, mine, s4.at[p, k], r4.at[p, k], peer)
            cp.start()
            fours.append(cp)
    fives = []
    for p in range(3):
        for cp in fours[3 * p : 3 * p + 3]:
            cp.wait()
        a = spot[p]
        slot = 12 * core + 4 * p + a
        out_ref[slot] = one[p, 0]
        for k in range(1, 4):
            peer, at = along(p, k)
            cp = remote(out_ref.at[slot], out_ref.at[slot], s5.at[p, k], r5.at[p, k], peer)
            cp.start()
            fives.append(cp)
    sixes = []
    for p in range(3):
        for cp in fives[3 * p : 3 * p + 3]:
            cp.wait()
        blocks = out_ref.at[pl.ds(12 * core + 4 * p, 4)]
        cp = remote(blocks, blocks, s6.at[p], r6.at[p], partner)
        cp.start()
        sixes.append(cp)
    for cp in sixes:
        cp.wait()


def reduce_all(grads, gains):
    return pl.pallas_call(
        reduce_kernel,
        name="reduce_all",
        out_shape=(sds((24, D, 256), BF16), sds((8, D), F32)),
        in_specs=[VM] * 2,
        out_specs=(VM,) * 2,
        scratch_shapes=[
            pltpu.VMEM((12, D, 256), BF16),
            pltpu.VMEM((12, D, 256), BF16),
            pltpu.VMEM((3, 3, D, 256), BF16),
            pltpu.VMEM((3, 3, 144, 256), BF16),
            pltpu.VMEM((3, 4, 144, 256), BF16),
            pltpu.VMEM((3, D, 256), BF16),
            pltpu.VMEM((4, 4, 8, D), F32),
            pltpu.VMEM((8, D), F32),
            DMA((3,)), DMA((3,)),
        ]
        + [DMA((3, 4))] * 10
        + [DMA((3,)), DMA((3,)), DMA((4, 4)), DMA((4, 4))],
        compiler_params=params(4, 56 << 20),
    )(grads, gains)


def mirror_pairs():
    pairs = []
    for seq in range(64):
        n, w = seq // 8, seq % 8
        pairs.append((seq, 8 * (7 - n) + w if w % 2 else seq))
    return pairs


def on_device(
    tokens, cotangent, segment_ids, gain_attn, wq, wk, wv, wo, gain_mlp, wg, wu, wd
):
    pairs = mirror_pairs()
    ga = gain_attn[None]
    gm = gain_mlp[None]
    cot = lax.ppermute(cotangent[0], "seq", pairs)
    x0, starts, pos = entry(tokens[0], segment_ids)
    freq = jnp.exp(jnp.arange(32, dtype=F32) * (-2.0 / HD) * math.log(10000.0))
    angle = freq[:, None] * pos.astype(F32)
    cos, sin = jnp.cos(angle), jnp.sin(angle)

    q0, kv0, h10 = local(
        project_kernel, "project", [Q_T, KV_T, H_S], [x0, ga, wq, wk, wv, cos, sin]
    )
    qa0, kva0, part, stat = attend(q0, kv0, starts)
    q1, kv1, h11, x1_in, m0, h20, inv0, gate0, up0, hid0, o0, lse0 = local(
        middle_kernel,
        "middle",
        [Q_T, KV_T, H_S, X_S, X_S, H_S, sds((TOK, TOK), F32), F_S, F_S, FB_S, sds((D, TOK), F32),
         sds((16, TOK), F32)],
        [part, stat, x0, ga, wq, wk, wv, wo, gm, wg, wu, wd, cos, sin],
    )
    qa1, kva1, part, stat = attend(q1, kv1, starts)
    x2, h21, hid1, ob1, do1, st1, gm1, dg1, du1, da1, dx1, ggm1 = local(
        turn_kernel,
        "turn",
        [X_S, H_S, FB_S, Q_T, Q_T, ST_S, H_S, FB_S, FB_S, H_S, X_S, G_S],
        [part, stat, x1_in, cot, wo, gm, wg, wu, wd],
        [pltpu.VMEM((D, TOK), F32), pltpu.VMEM((16, TOK), F32)],
    )
    output = lax.ppermute(x2, "seq", pairs)
    dq, dkv = attend_back(do1, st1, qa1, kva1, starts)
    dqkv1, gga1, do0, st0, gm0, dg0, du0, da0, dx0, ggm0 = local(
        between_kernel,
        "between",
        [sds((960, TOK), BF16), G_S, Q_T, ST_S, H_S, FB_S, FB_S, H_S, X_S, G_S],
        [dq, dkv, x1_in, dx1, ga, wq, wk, wv, cos, sin, m0, inv0, gate0, up0, wo, gm, wg, wu, wd,
         o0, lse0],
    )
    dq, dkv = attend_back(do0, st0, qa0, kva0, starts)
    dqkv0, gga0, g0 = local(
        last_kernel,
        "last",
        [sds((960, TOK), BF16), G_S, X_S],
        [dq, dkv, x0, dx0, ga, wq, wk, wv, cos, sin],
    )
    grad_tokens = lax.ppermute(g0, "seq", pairs)
    (grads,) = local(
        weights_kernel,
        "weights",
        [sds((24, D, 256), BF16)],
        [h10, h11, dqkv0, dqkv1, o0.astype(BF16), ob1, da0, da1, h20, h21, dg0, dg1, du0, du1,
         hid0, hid1, gm0, gm1],
    )
    gains = jnp.concatenate([gga0 + gga1, ggm0 + ggm1, jnp.zeros((6, D), F32)], axis=0)
    total, gains = reduce_all(grads, gains)

    def slab(first):
        return jnp.transpose(total[first : first + 6], (1, 0, 2)).reshape(D, FF).astype(F32)

    small = slab(18)
    return (
        output[None],
        grad_tokens[None],
        gains[0],
        small[:, 0:576],
        small[:, 576:768],
        small[:, 768:960],
        small[:, 960:1536],
        gains[1],
        slab(0),
        slab(6),
        jnp.transpose(total[12:18], (0, 2, 1)).reshape(FF, D).astype(F32),
    )


def solution(mesh):
    rows = P("rows", "seq", None)
    in_specs = (rows, rows, P("rows", "seq")) + (P(),) * 9
    out_specs = (rows, rows) + (P(),) * 9
    return jax.shard_map(
        on_device, mesh=mesh, in_specs=in_specs, out_specs=out_specs, check_vma=False
    )
```

```python
import functools
import math

import jax
import jax.numpy as jnp
from jax import lax
from jax.experimental import pallas as pl
from jax.experimental.pallas import tpu as pltpu
from jax.sharding import PartitionSpec as P

F32 = jnp.float32
BF16 = jnp.bfloat16
MESH = pl.DeviceIdType.MESH

D = 576
HEADS = 9
HD = 64
KV = 192
FF = 1536
TOK = 128
DOCS = 16
EPS = 1e-05
SCALE = 0.125
EXP_SCALE = SCALE * 1.4426950408889634
MASKED = -1e30
LOWEST = -1e20

VM = pl.BlockSpec(memory_space=pltpu.VMEM)
DMA = pltpu.SemaphoreType.DMA


def dot(a, b, ca, cb):
    return lax.dot_general(a, b, (((ca,), (cb,)), ((), ())), preferred_element_type=F32)


def sds(shape, dtype):
    return jax.ShapeDtypeStruct(shape, dtype)


def params(collective=None, limit=50 << 20):
    if collective is None:
        return pltpu.CompilerParams(vmem_limit_bytes=limit)
    return pltpu.CompilerParams(
        vmem_limit_bytes=limit, collective_id=collective, has_side_effects=True
    )


def place():
    seq = lax.axis_index("seq")
    row = lax.axis_index("rows")
    return row, seq, seq // 8, lax.rem(seq, 8)


def slot_of(w):
    return lax.rem(w, 2) * 4 + w // 2


def octet_of(n, w):
    return jnp.where(lax.rem(w, 2) == 0, n, 7 - n)


def greet(row, n, w):
    bar = pltpu.get_barrier_semaphore()
    for k in range(1, 8):
        pl.semaphore_signal(
            bar, inc=1, device_id=(row, 8 * n + lax.rem(w + k, 8)), device_id_type=MESH
        )
        pl.semaphore_signal(
            bar, inc=1, device_id=(row, 8 * lax.rem(n + k, 8) + w), device_id_type=MESH
        )
    return bar


def remote(src, dst, send, recv, target):
    return pltpu.make_async_remote_copy(
        src_ref=src,
        dst_ref=dst,
        send_sem=send,
        recv_sem=recv,
        device_id=target,
        device_id_type=MESH,
    )


def entry_kernel(
    tok_ref, cot_ref, ids_ref, x_ref, g_ref, starts_ref, pos_ref,
    tok_in, cot_in, ids_all, starts_all, ysend, yrecv, xsend, xrecv, tsend, trecv
):
    row, seq, n, w = place()
    core = lax.rem(w, 2)
    mirror = (row, 8 * (7 - n) + w)
    bar = greet(row, n, w)
    ids_all[seq] = ids_ref[...]
    pl.semaphore_wait(bar, 14)

    sent = []
    for k in range(1, 8):
        cp = remote(
            ids_all.at[seq], ids_all.at[seq], ysend.at[k], yrecv.at[k],
            (row, 8 * n + lax.rem(w + k, 8)),
        )
        cp.start()
        sent.append(cp)
    moves = [
        remote(tok_ref, tok_in, tsend.at[0], trecv.at[0], mirror),
        remote(cot_ref, cot_in, tsend.at[1], trecv.at[1], mirror),
    ]

    @pl.when(core == 1)
    def _():
        for move in moves:
            move.start()

    for cp in sent:
        cp.wait()
    own = ids_all.at[pl.ds(8 * n, 8)]
    sent = []
    for k in range(1, 8):
        cp = remote(own, own, xsend.at[k], xrecv.at[k], (row, 8 * lax.rem(n + k, 8) + w))
        cp.start()
        sent.append(cp)

    @pl.when(core == 0)
    def _():
        x_ref[...] = tok_ref[...].T
        g_ref[...] = cot_ref[...].T

    for cp in sent:
        cp.wait()

    ids = jnp.concatenate([ids_all[i] for i in range(64)], axis=0)
    total = jnp.zeros((64, TOK), jnp.int32)
    for doc in range(DOCS - 1):
        count = jnp.where(ids == doc, 1.0, 0.0)
        count = jnp.sum(jnp.sum(count, axis=0, keepdims=True), axis=1, keepdims=True)
        total = total + jnp.where(ids > doc, count.astype(jnp.int32), 0)
    starts_all[...] = total[:, None, :]
    for half in range(2):
        octet = n if half == 0 else 7 - n
        for y in range(4):
            starts_ref[half, :, TOK * y : TOK * y + TOK] = starts_all[8 * octet + 2 * y + half]
    mine = 8 * octet_of(n, w) + w
    pos_ref[...] = (
        mine * TOK + lax.broadcasted_iota(jnp.int32, (1, TOK), 1) - starts_all[mine]
    )

    @pl.when(core == 1)
    def _():
        for move in moves:
            move.wait()
        x_ref[...] = tok_in[...].T
        g_ref[...] = cot_in[...].T


def entry(tokens, cotangent, ids):
    return pl.pallas_call(
        entry_kernel,
        name="entry",
        out_shape=(
            sds((TOK, D), F32),
            sds((TOK, D), F32),
            sds((2, 1, 4 * TOK), jnp.int32),
            sds((1, TOK), jnp.int32),
        ),
        in_specs=[VM] * 3,
        out_specs=(VM,) * 4,
        scratch_shapes=[
            pltpu.VMEM((D, TOK), F32),
            pltpu.VMEM((D, TOK), F32),
            pltpu.VMEM((64, 1, TOK), jnp.int32),
            pltpu.VMEM((64, 1, TOK), jnp.int32),
        ]
        + [pltpu.SemaphoreType.DMA((8,))] * 4
        + [pltpu.SemaphoreType.DMA((2,))] * 2,
        compiler_params=params(1),
    )(tokens, cotangent, ids)


def norm_in(x, gain):
    inverse = lax.rsqrt(jnp.mean(x * x, axis=-1, keepdims=True) + EPS)
    return (x * inverse * gain).astype(BF16), inverse


def norm_back(x, inverse, gain, grad):
    scaled = grad * gain
    grad_gain = jnp.sum(grad * (x * inverse), axis=0, keepdims=True)
    inner = jnp.mean(scaled * x, axis=-1, keepdims=True)
    return inverse * scaled - x * (inverse * inverse * inverse) * inner, grad_gain


def project(x, gain, wq, wk, wv, cos, sin, q_out, kv_out, h_out):
    h, _ = norm_in(x, gain)
    h_out[...] = h
    qt = dot(h, wq, 1, 0).T
    for i in range(HEADS):
        a = qt[HD * i : HD * i + 32]
        b = qt[HD * i + 32 : HD * i + 64]
        q_out[HD * i : HD * i + 32, :] = (a * cos - b * sin).astype(BF16)
        q_out[HD * i + 32 : HD * i + 64, :] = (b * cos + a * sin).astype(BF16)
    kt = dot(wk, h, 1, 1)
    vt = dot(wv, h, 1, 1).astype(BF16)
    for i in range(3):
        a = kt[HD * i : HD * i + 32]
        b = kt[HD * i + 32 : HD * i + 64]
        kv_out[TOK * i : TOK * i + 32, :] = (a * cos - b * sin).astype(BF16)
        kv_out[TOK * i + 32 : TOK * i + 64, :] = (b * cos + a * sin).astype(BF16)
        kv_out[TOK * i + 64 : TOK * i + 128, :] = vt[HD * i : HD * i + 64]


def combine(part, stat, o_out, lse_out):
    for g in range(3):
        tops = [stat[i, 8 * g : 8 * g + 3, :] for i in range(4)]
        top = functools.reduce(jnp.maximum, tops)
        factors = [jnp.exp2((t - top) * EXP_SCALE) for t in tops]
        total = sum(f * stat[i, 8 * g + 4 : 8 * g + 7, :] for i, f in enumerate(factors))
        inverse = 1.0 / total
        factors = [f * inverse for f in factors]
        lse_out[3 * g : 3 * g + 3, :] = top + jnp.log2(total) * (1.0 / EXP_SCALE)
        for j in range(3):
            rows = slice(192 * g + HD * j, 192 * g + HD * j + HD)
            o_out[rows, :] = sum(
                part[i, rows, :].astype(F32) * factors[i][j : j + 1, :] for i in range(4)
            )


def feed_forward(x, o_t, wo, gain, wg, wu, wd):
    x1 = x + dot(o_t, wo, 0, 0)
    h2, inverse = norm_in(x1, gain)
    gate = dot(h2, wg, 1, 0)
    up = dot(h2, wu, 1, 0)
    hid = (gate * jax.nn.sigmoid(gate) * up).astype(BF16)
    return x1, h2, inverse, gate, up, hid, x1 + dot(hid, wd, 1, 1)


def feed_back(g, x1, inverse, gate, up, wo, gain, wg, wu, wd, o_ref, lse,
              do_out, stat_out, gm_out, dgate_out, dup_out, da_out):
    gm = g.astype(BF16)
    gm_out[...] = gm
    dhid = dot(gm, wd, 1, 0)
    sg = jax.nn.sigmoid(gate)
    dgate = (dhid * up * sg * (1.0 + gate * (1.0 - sg))).astype(BF16)
    dup = (dhid * gate * sg).astype(BF16)
    dgate_out[...] = dgate
    dup_out[...] = dup
    dh2 = dot(dgate, wg, 1, 1) + dot(dup, wu, 1, 1)
    dy, grad_gain = norm_back(x1, inverse, gain, dh2)
    dx1 = g + dy
    da = dx1.astype(BF16)
    da_out[...] = da
    do_t = dot(wo, da, 1, 1).astype(BF16)
    do_out[...] = do_t
    stat_out[...] = jnp.zeros(stat_out.shape, F32)
    stat_out[0:HEADS, :] = lse
    for h in range(HEADS):
        rows = slice(HD * h, HD * h + HD)
        stat_out[16 + h : 17 + h, :] = jnp.sum(
            do_t[rows].astype(F32) * o_ref[rows, :], axis=0, keepdims=True
        )
    return dx1, grad_gain


def project_back(dq_part, dkv_part, x, dx1, gain, wq, wk, wv, cos, sin, dqkv_out):
    for h in range(HEADS + 3):
        part, base, many = (dq_part, HD * h, 4) if h < HEADS else (dkv_part, TOK * (h - HEADS), 8)
        a = sum(part[i, base : base + 32, :].astype(F32) for i in range(many))
        b = sum(part[i, base + 32 : base + 64, :].astype(F32) for i in range(many))
        dqkv_out[HD * h : HD * h + 32, :] = (a * cos + b * sin).astype(BF16)
        dqkv_out[HD * h + 32 : HD * h + 64, :] = (b * cos - a * sin).astype(BF16)
    for g in range(3):
        base = TOK * g + HD
        dqkv_out[D + KV + HD * g : D + KV + HD * g + HD, :] = sum(
            dkv_part[i, base : base + HD, :].astype(F32) for i in range(8)
        ).astype(BF16)
    dh1 = (
        dot(dqkv_out[0:D, :], wq, 0, 1)
        + dot(dqkv_out[D : D + KV, :], wk, 0, 0)
        + dot(dqkv_out[D + KV :, :], wv, 0, 0)
    )
    inverse = lax.rsqrt(jnp.mean(x * x, axis=-1, keepdims=True) + EPS)
    dy, grad_gain = norm_back(x, inverse, gain, dh1)
    return dx1 + dy, grad_gain


Q_T = sds((D, TOK), BF16)
KV_T = sds((2 * KV, TOK), BF16)
H_S = sds((TOK, D), BF16)
X_S = sds((TOK, D), F32)
X_T = sds((D, TOK), F32)
F_S = sds((TOK, FF), F32)
FB_S = sds((TOK, FF), BF16)
ST_S = sds((32, TOK), F32)
G_S = sds((1, D), F32)


def project_kernel(x, gain, wq, wk, wv, cos, sin, q_out, kv_out, h_out):
    project(x[...], gain[...], wq[...], wk[...], wv[...], cos[...], sin[...], q_out, kv_out, h_out)


def middle_kernel(
    part, stat, x, ga, wq, wk, wv, wo, gm, wg, wu, wd, cos, sin,
    q_out, kv_out, h_out, x_out, x1_out, h2_out, inv_out, gate_out, up_out, hid_out, o_out, lse_out
):
    combine(part, stat, o_out, lse_out)
    x1, h2, inverse, gate, up, hid, x2 = feed_forward(
        x[...], o_out[...].astype(BF16), wo[...], gm[...], wg[...], wu[...], wd[...]
    )
    x1_out[...] = x1
    h2_out[...] = h2
    inv_out[...] = jnp.broadcast_to(inverse, inv_out.shape)
    gate_out[...] = gate
    up_out[...] = up
    hid_out[...] = hid
    x_out[...] = x2
    project(x2, ga[...], wq[...], wk[...], wv[...], cos[...], sin[...], q_out, kv_out, h_out)


def turn_kernel(
    part, stat, x, g, wo, gm, wg, wu, wd,
    x_out, h2_out, hid_out, ob_out, do_out, stat_out, gmo, dgate, dup, da, dx1_out, gg_out, o_s, lse_s
):
    combine(part, stat, o_s, lse_s)
    ob = o_s[...].astype(BF16)
    ob_out[...] = ob
    x1, h2, inverse, gate, up, hid, x2 = feed_forward(
        x[...], ob, wo[...], gm[...], wg[...], wu[...], wd[...]
    )
    h2_out[...] = h2
    hid_out[...] = hid
    x_out[...] = x2.T
    dx1, gg = feed_back(
        g[...], x1, inverse, gate, up, wo[...], gm[...], wg[...], wu[...], wd[...], o_s,
        lse_s[0:HEADS, :], do_out, stat_out, gmo, dgate, dup, da
    )
    dx1_out[...] = dx1
    gg_out[...] = gg


def between_kernel(
    dq, dkv, x, dx1, ga, wq, wk, wv, cos, sin, x1, inv, gate, up, wo, gm, wg, wu, wd, o, lse,
    dqkv_out, gga_out, do_out, stat_out, gmo, dgate, dup, da, dx1_out, ggm_out
):
    g, gga = project_back(
        dq, dkv, x[...], dx1[...], ga[...], wq[...], wk[...], wv[...], cos[...], sin[...], dqkv_out
    )
    gga_out[...] = gga
    dx0, ggm = feed_back(
        g, x1[...], inv[:, 0:1], gate[...], up[...], wo[...], gm[...], wg[...], wu[...], wd[...], o,
        lse[0:HEADS, :], do_out, stat_out, gmo, dgate, dup, da
    )
    dx1_out[...] = dx0
    ggm_out[...] = ggm


def last_kernel(dq, dkv, x, dx1, ga, wq, wk, wv, cos, sin, dqkv_out, gga_out, g_out):
    g, gga = project_back(
        dq, dkv, x[...], dx1[...], ga[...], wq[...], wk[...], wv[...], cos[...], sin[...], dqkv_out
    )
    gga_out[...] = gga
    g_out[...] = g.T


def local(kernel, name, outs, args, scratch=()):
    return pl.pallas_call(
        kernel,
        name=name,
        out_shape=tuple(outs),
        in_specs=[VM] * len(args),
        out_specs=(VM,) * len(outs),
        scratch_shapes=list(scratch),
        compiler_params=params(),
    )(*args)


W3 = 12 * TOK


class Spread:
    def __init__(self, row, n, w, send, recv):
        self.core = lax.rem(w, 2)
        self.y = w // 2
        self.own = self.core * 4 + self.y
        self.row, self.n = row, n
        self.partner = (row, 8 * n + 2 * self.y + 1 - self.core)
        self.send, self.recv = send, recv
        self.first, self.passed = {}, {}

    def chip(self, k):
        return (self.row, 8 * self.n + 2 * lax.rem(self.y + k, 4) + self.core)

    def start(self, part, ref):
        self.first[part], self.passed[part] = [], []
        for k in range(1, 4):
            cp = remote(ref(self.own), ref(self.own), self.send.at[part, k], self.recv.at[part, k],
                        self.chip(k))
            cp.start()
            self.first[part].append(cp)
        self.hand(part, ref, self.own, 4)

    def hand(self, part, ref, slot, k):
        cp = remote(ref(slot), ref(slot), self.send.at[part, k], self.recv.at[part, k], self.partner)
        cp.start()
        self.passed[part].append(cp)

    def forward(self, part, ref):
        for k in range(1, 4):
            self.first[part][k - 1].wait_recv()
            self.hand(part, ref, self.core * 4 + lax.rem(self.y + 4 - k, 4), 4 + k)

    def arrive(self, part):
        for cp in self.passed[part]:
            cp.wait_recv()

    def finish(self):
        for part in self.first:
            for cp in self.first[part] + self.passed[part]:
                cp.wait_send()


def turns(n):
    return (n + 2) // 2


def fill_masks(bias, starts_ref, n, w):
    turn = turns(n)

    def one(t, carry):
        sel = jnp.where(t >= turn, 1, 0)
        kc = jnp.where(t >= turn, t - turn, t)
        line = lax.broadcasted_iota(jnp.int32, (256, 1), 0)
        key = (2 * kc + line // TOK) * 1024 + w * TOK + lax.rem(line, TOK)
        col = lax.broadcasted_iota(jnp.int32, (1, 512), 1)
        octet = jnp.where(sel == 0, n, 7 - n)
        query = octet * 1024 + (2 * (col // TOK) + sel) * TOK + lax.rem(col, TOK)
        bias[t] = jnp.where((key >= starts_ref[sel]) & (key <= query), 0.0, MASKED)
        return carry

    lax.fori_loop(0, 5, one, 0)


def chunk_range(n, sel):
    turn = turns(n)
    return jnp.where(sel == 0, 0, turn), jnp.where(sel == 0, turn, 5 - turn)


def three_heads(ref, sel, g):
    return jnp.concatenate(
        [
            ref[4 * sel + y, HD * h : HD * h + HD, :]
            for h in range(3 * g, 3 * g + 3)
            for y in range(4)
        ],
        axis=1,
    )


def two_blocks(ref, kc, first):
    return jnp.concatenate([ref[2 * kc + i, first : first + HD, :] for i in range(2)], axis=1)


def by_chip(value, y):
    return jnp.concatenate(
        [value[:, 512 * j + TOK * y : 512 * j + TOK * y + TOK] for j in range(3)], axis=0
    )


def attend_kernel(
    q_ref, kv_ref, starts_ref, q_all, kv_all, part_ref, stat_ref,
    k_nat, bias, top, total, acc, o_send, o_recv, r_send, r_recv, o_y, s_y,
    qs, qr, ks, kr, ps, pr, ys, yr
):
    row, seq, n, w = place()
    bar = greet(row, n, w)
    core, y = lax.rem(w, 2), w // 2
    own_k = octet_of(n, w)
    queries = Spread(row, n, w, qs, qr)
    q_all[queries.own] = q_ref[...]
    kv_all[own_k] = kv_ref[...]
    pl.semaphore_wait(bar, 14)

    def q_part(g):
        return lambda slot: q_all.at[slot, pl.ds(192 * g, 192)]

    keys = {}
    for g in range(3):
        keys[g] = []
        for k in range(1, 8):
            block = kv_all.at[own_k, pl.ds(TOK * g, TOK)]
            cp = remote(
                block, block, ks.at[g, k], kr.at[g, k], (row, 8 * lax.rem(n + k, 8) + w)
            )
            cp.start()
            keys[g].append(cp)
        queries.start(g, q_part(g))
    fill_masks(bias, starts_ref, n, w)
    queries.forward(0, q_part(0))

    def phase(g, sel):
        base, count = chunk_range(n, sel)
        top[...] = jnp.full(top.shape, LOWEST, F32)
        total[...] = jnp.zeros(total.shape, F32)
        acc[...] = jnp.zeros(acc.shape, F32)

        def step(kc, carry):
            scores = dot(k_nat[kc], three_heads(q_all, sel, g), 1, 0)
            mask = bias[base + kc]
            weights, shrinks = [], []
            for j in range(3):
                cols = slice(512 * j, 512 * j + 512)
                s = scores[:, cols] + mask
                old = top[:, cols]
                new = jnp.maximum(old, jnp.max(s, axis=0, keepdims=True))
                p = jnp.exp2((s - new) * EXP_SCALE)
                shrink = jnp.exp2((old - new) * EXP_SCALE)
                top[:, cols] = new
                total[:, cols] = total[:, cols] * shrink + jnp.sum(p, axis=0, keepdims=True)
                weights.append(p.astype(BF16))
                shrinks.append(shrink)
            values = two_blocks(kv_all, kc, TOK * g + HD)
            acc[...] = acc[...] * jnp.concatenate(shrinks, axis=1) + dot(
                values, jnp.concatenate(weights, axis=1), 1, 0
            )
            return carry

        lax.fori_loop(0, count, step, 0)

    pairs, outs = [], []
    for g in range(3):
        for cp in keys[g]:
            cp.wait_recv()
        for j in range(8):
            k_nat[j // 2, (j % 2) * TOK : (j % 2) * TOK + TOK, :] = jnp.transpose(
                kv_all[j, TOK * g : TOK * g + HD, :]
            )
        queries.arrive(g)
        phase(g, 1 - core)
        o_send[g] = acc[...].astype(BF16)
        r_send[g, 0] = top[...]
        r_send[g, 1] = total[...]
        both = [
            remote(o_send.at[g], o_recv.at[g], ps.at[0, g], pr.at[0, g], queries.partner),
            remote(r_send.at[g], r_recv.at[g], ps.at[1, g], pr.at[1, g], queries.partner),
        ]
        for cp in both:
            cp.start()
        pairs += both
        if g < 2:
            queries.forward(g + 1, q_part(g + 1))
        phase(g, core)
        for cp in both:
            cp.wait_recv()
        new = jnp.maximum(top[...], r_recv[g, 0])
        mine = jnp.exp2((top[...] - new) * EXP_SCALE)
        theirs = jnp.exp2((r_recv[g, 0] - new) * EXP_SCALE)
        length = total[...] * mine + r_recv[g, 1] * theirs
        out = (acc[...] * mine + o_recv[g].astype(F32) * theirs).astype(BF16)
        for i in range(4):
            o_y[g, i] = by_chip(out, i)
            for j in range(3):
                cols = slice(512 * j + TOK * i, 512 * j + TOK * i + TOK)
                s_y[g, i, j : j + 1, :] = new[:, cols]
                s_y[g, i, 4 + j : 5 + j, :] = length[:, cols]
        for k in range(1, 4):
            to = lax.rem(y + k, 4)
            peer = queries.chip(k)
            for cp in (
                remote(o_y.at[g, to], part_ref.at[y, pl.ds(192 * g, 192)], ys.at[0, g, k],
                       yr.at[0, g, k], peer),
                remote(s_y.at[g, to], stat_ref.at[y, pl.ds(8 * g, 8)], ys.at[1, g, k],
                       yr.at[1, g, k], peer),
            ):
                cp.start()
                outs.append(cp)
        part_ref[y, 192 * g : 192 * g + 192, :] = o_y[g, y]
        stat_ref[y, 8 * g : 8 * g + 8, :] = s_y[g, y]
    queries.finish()
    for g in range(3):
        for cp in keys[g]:
            cp.wait_send()
    for cp in pairs:
        cp.wait_send()
    for cp in outs:
        cp.wait()


def attend(q, kv, starts):
    return pl.pallas_call(
        attend_kernel,
        name="attend",
        out_shape=(
            sds((8, D, TOK), BF16),
            sds((8, 2 * KV, TOK), BF16),
            sds((4, D, TOK), BF16),
            sds((4, 24, TOK), F32),
        ),
        in_specs=[VM] * 3,
        out_specs=(VM,) * 4,
        scratch_shapes=[
            pltpu.VMEM((4, 256, HD), BF16),
            pltpu.VMEM((5, 256, 512), F32),
            pltpu.VMEM((1, W3), F32),
            pltpu.VMEM((1, W3), F32),
            pltpu.VMEM((HD, W3), F32),
            pltpu.VMEM((3, HD, W3), BF16),
            pltpu.VMEM((3, HD, W3), BF16),
            pltpu.VMEM((3, 2, 1, W3), F32),
            pltpu.VMEM((3, 2, 1, W3), F32),
            pltpu.VMEM((3, 4, 192, TOK), BF16),
            pltpu.VMEM((3, 4, 8, TOK), F32),
            DMA((3, 8)), DMA((3, 8)), DMA((3, 8)), DMA((3, 8)),
            DMA((2, 3)), DMA((2, 3)), DMA((2, 3, 4)), DMA((2, 3, 4)),
        ],
        compiler_params=params(2),
    )(q, kv, starts)


def attend_back_kernel(
    do_ref, st_ref, q_all, kv_all, starts_ref, dq_part, dkv_part,
    do_all, st_all, k_nat, v_nat, bias, rows_s, dq, dkv, q_send, q_recv, q_y, kv_low,
    qs, qr, ks, kr, ps, pr, ys, yr
):
    row, seq, n, w = place()
    bar = greet(row, n, w)
    core, y = lax.rem(w, 2), w // 2
    own_k = octet_of(n, w)
    grads = Spread(row, n, w, qs, qr)
    do_all[grads.own] = do_ref[...]
    st_all[grads.own] = st_ref[...]
    pl.semaphore_wait(bar, 14)

    def part(g):
        return lambda slot: do_all.at[slot, pl.ds(192 * g, 192)]

    def stats(slot):
        return st_all.at[slot]

    grads.start(3, stats)
    for g in range(3):
        grads.start(g, part(g))
    fill_masks(bias, starts_ref, n, w)
    grads.forward(3, stats)
    grads.forward(0, part(0))

    def phase(g, sel):
        base, count = chunk_range(n, sel)
        dq[...] = jnp.zeros(dq.shape, F32)
        for i, first in enumerate((0, 16)):
            for j in range(3):
                for c in range(4):
                    at = 512 * j + TOK * c
                    line = first + 3 * g + j
                    rows_s[i, :, at : at + TOK] = st_all[4 * sel + c, line : line + 1, :]

        def step(kc, carry):
            qt = three_heads(q_all, sel, g)
            dt = three_heads(do_all, sel, g)
            scores = dot(k_nat[kc], qt, 1, 0)
            dp = dot(v_nat[kc], dt, 1, 0)
            mask = bias[base + kc]
            ps_, ds_ = [], []
            for j in range(3):
                cols = slice(512 * j, 512 * j + 512)
                p = jnp.exp2((scores[:, cols] + mask - rows_s[0, :, cols]) * EXP_SCALE)
                ds_.append((p * (dp[:, cols] - rows_s[1, :, cols])).astype(BF16))
                ps_.append(p.astype(BF16))
            p = jnp.concatenate(ps_, axis=1)
            ds = jnp.concatenate(ds_, axis=1)
            dkv[kc, 0:HD, :] += dot(ds, qt, 1, 1).T
            dkv[kc, HD:, :] += dot(p, dt, 1, 1).T
            dq[...] += dot(two_blocks(kv_all, kc, TOK * g), ds, 1, 0)
            return carry

        lax.fori_loop(0, count, step, 0)

    pairs, outs = [], []
    for g in range(3):
        dkv[...] = jnp.zeros(dkv.shape, F32)
        for j in range(8):
            at = slice((j % 2) * TOK, (j % 2) * TOK + TOK)
            k_nat[j // 2, at, :] = jnp.transpose(kv_all[j, TOK * g : TOK * g + HD, :])
            v_nat[j // 2, at, :] = jnp.transpose(kv_all[j, TOK * g + HD : TOK * g + TOK, :])
        if g == 0:
            grads.arrive(3)
        grads.arrive(g)
        phase(g, 1 - core)
        q_send[g] = (dq[...] * SCALE).astype(BF16)
        pair = remote(q_send.at[g], q_recv.at[g], ps.at[g], pr.at[g], grads.partner)
        pair.start()
        pairs.append(pair)
        if g < 2:
            grads.forward(g + 1, part(g + 1))
        phase(g, core)
        for j in range(8):
            cols = slice((j % 2) * TOK, (j % 2) * TOK + TOK)
            kv_low[g, j, 0:HD, :] = (dkv[j // 2, 0:HD, cols] * SCALE).astype(BF16)
            kv_low[g, j, HD:, :] = dkv[j // 2, HD:, cols].astype(BF16)
        for k in range(1, 8):
            to = lax.rem(n + k, 8)
            cp = remote(
                kv_low.at[g, octet_of(to, w)], dkv_part.at[n, pl.ds(TOK * g, TOK)], ks.at[g, k],
                kr.at[g, k], (row, 8 * to + w),
            )
            cp.start()
            outs.append(cp)
        pair.wait_recv()
        out = (dq[...] * SCALE + q_recv[g].astype(F32)).astype(BF16)
        for i in range(4):
            q_y[g, i] = by_chip(out, i)
        for k in range(1, 4):
            to = lax.rem(y + k, 4)
            cp = remote(q_y.at[g, to], dq_part.at[y, pl.ds(192 * g, 192)], ys.at[g, k], yr.at[g, k],
                        grads.chip(k))
            cp.start()
            outs.append(cp)
        dkv_part[n, TOK * g : TOK * g + TOK, :] = kv_low[g, own_k]
        dq_part[y, 192 * g : 192 * g + 192, :] = q_y[g, y]
    grads.finish()
    for cp in pairs:
        cp.wait_send()
    for cp in outs:
        cp.wait()


def attend_back(do, st, q_all, kv_all, starts):
    return pl.pallas_call(
        attend_back_kernel,
        name="attend_back",
        out_shape=(sds((4, D, TOK), BF16), sds((8, 2 * KV, TOK), BF16)),
        in_specs=[VM] * 5,
        out_specs=(VM,) * 2,
        scratch_shapes=[
            pltpu.VMEM((8, D, TOK), BF16),
            pltpu.VMEM((8, 32, TOK), F32),
            pltpu.VMEM((4, 256, HD), BF16),
            pltpu.VMEM((4, 256, HD), BF16),
            pltpu.VMEM((5, 256, 512), F32),
            pltpu.VMEM((2, 1, W3), F32),
            pltpu.VMEM((HD, W3), F32),
            pltpu.VMEM((4, TOK, 256), F32),
            pltpu.VMEM((3, HD, W3), BF16),
            pltpu.VMEM((3, HD, W3), BF16),
            pltpu.VMEM((3, 4, 192, TOK), BF16),
            pltpu.VMEM((3, 8, TOK, TOK), BF16),
            DMA((4, 8)), DMA((4, 8)), DMA((3, 8)), DMA((3, 8)),
            DMA((3,)), DMA((3,)), DMA((3, 4)), DMA((3, 4)),
        ],
        compiler_params=params(3),
    )(do, st, q_all, kv_all, starts)


def weights_kernel(
    h1a, h1b, dqa, dqb, oa, ob, daa, dab, h2a, h2b, dga, dgb, dua, dub, hida, hidb, gma, gmb, g_out
):
    def both(a, b):
        return jnp.concatenate([a[...], b[...]], axis=0)

    h1t = both(h1a, h1b).T
    ot = jnp.concatenate([oa[...], ob[...]], axis=1)
    h2t = both(h2a, h2b).T
    gmt = both(gma, gmb).T
    for i in range(6):
        cols = slice(256 * i, 256 * i + 256)
        g_out[i] = dot(h2t, jnp.concatenate([dga[:, cols], dgb[:, cols]], axis=0), 1, 0).astype(BF16)
        g_out[6 + i] = dot(h2t, jnp.concatenate([dua[:, cols], dub[:, cols]], axis=0), 1, 0).astype(
            BF16
        )
        g_out[12 + i] = dot(
            gmt, jnp.concatenate([hida[:, cols], hidb[:, cols]], axis=0), 1, 0
        ).astype(BF16)
    dat = both(daa, dab).T

    def rows(first, last):
        return jnp.concatenate([dqa[first:last, :], dqb[first:last, :]], axis=1)

    g_out[18] = dot(h1t, rows(0, 256), 1, 1).astype(BF16)
    g_out[19] = dot(h1t, rows(256, 512), 1, 1).astype(BF16)
    g_out[20, :, 0:128] = dot(h1t, rows(512, 640), 1, 1).astype(BF16)
    g_out[20, :, 128:256] = dot(ot, dat[0:128], 1, 1).astype(BF16)
    g_out[21] = dot(ot, dat[128:384], 1, 1).astype(BF16)
    low = jnp.concatenate([dat[384:576], jnp.zeros((64, 256), BF16)], axis=0)
    high = jnp.concatenate([jnp.zeros((192, 256), BF16), rows(640, 704)], axis=0)
    g_out[22] = (dot(ot, low, 1, 1) + dot(h1t, high, 1, 1)).astype(BF16)
    g_out[23] = dot(h1t, rows(704, 960), 1, 1).astype(BF16)


def spread_kernel(
    total, gate_out, up_out, down_out, q_out, k_out, v_out, o_out, big, small, kt, vt, sems
):
    cps = []
    for t, ref in enumerate((gate_out, up_out, down_out)):
        for i in range(6):
            cols = pl.ds(256 * i, 256)
            big[t, :, cols] = total[6 * t + i].astype(F32)
            cp = pltpu.make_async_copy(big.at[t, :, cols], ref.at[:, cols], sems.at[6 * t + i])
            cp.start()
            cps.append(cp)
    small[0, :, 0:256] = total[18].astype(F32)
    small[0, :, 256:512] = total[19].astype(F32)
    small[0, :, 512:576] = total[20, :, 0:64].astype(F32)
    small[1, :, 0:128] = total[20, :, 128:256].astype(F32)
    small[1, :, 128:384] = total[21].astype(F32)
    small[1, :, 384:576] = total[22, :, 0:192].astype(F32)
    kt[0:64, :] = total[20, :, 0:128].astype(F32).T[64:128]
    kt[64:128, :] = total[22, :, 128:256].astype(F32).T[64:128]
    last = total[23].astype(F32).T
    kt[128:192, :] = last[0:64]
    vt[...] = last[64:256]
    for i, (src, dst) in enumerate(
        ((small.at[0], q_out), (small.at[1], o_out), (kt, k_out), (vt, v_out))
    ):
        cp = pltpu.make_async_copy(src, dst, sems.at[18 + i])
        cp.start()
        cps.append(cp)
    for cp in cps:
        cp.wait()


def spread(total):
    anywhere = pl.BlockSpec(memory_space=pl.ANY)
    return pl.pallas_call(
        spread_kernel,
        name="spread",
        out_shape=(
            sds((D, FF), F32), sds((D, FF), F32), sds((D, FF), F32), sds((D, D), F32),
            sds((KV, D), F32), sds((KV, D), F32), sds((D, D), F32),
        ),
        in_specs=[VM],
        out_specs=(anywhere,) * 7,
        scratch_shapes=[
            pltpu.VMEM((3, D, FF), F32),
            pltpu.VMEM((2, D, D), F32),
            pltpu.VMEM((KV, D), F32),
            pltpu.VMEM((KV, D), F32),
            DMA((22,)),
        ],
        compiler_params=params(),
    )(total)


def reduce_kernel(
    g_ref, gain_ref, fin_ref, out_ref, gain_out, fin_out,
    fin_in, fs, fr, from_core, half, one, two, three, gather, gain_in, gain_sum, cs, cr, s1, r1, s2, r2, s3, r3, s4, r4, s5, r5, s6, r6, gs, gr
):
    row, seq, n, w = place()
    core = lax.rem(w, 2)
    spot = (n // 2, w // 2, 2 * row + lax.rem(n, 2))

    def device(x, y, z, c):
        return (z // 2, ((x * 2 + lax.rem(z, 2)) * 4 + y) * 2 + c)

    def along(axis, k):
        to = list(spot)
        to[axis] = lax.rem(spot[axis] + k, 4)
        return device(*to, core), to[axis]

    partner = device(*spot, 1 - core)
    bar = pltpu.get_barrier_semaphore()
    pl.semaphore_signal(bar, inc=1, device_id=partner, device_id_type=MESH)
    for axis in range(3):
        for k in range(1, 4):
            pl.semaphore_signal(bar, inc=1, device_id=along(axis, k)[0], device_id_type=MESH)
    mirror = device(3 - spot[0], spot[1], spot[2] // 2 * 2 + 1 - lax.rem(spot[2], 2), core)

    @pl.when(core == 1)
    def _():
        pl.semaphore_signal(bar, inc=1, device_id=mirror, device_id_type=MESH)
        pl.semaphore_wait(bar, 11)

    @pl.when(core == 0)
    def _():
        pl.semaphore_wait(bar, 10)

    moves = [remote(fin_ref.at[i], fin_in.at[i], fs.at[i], fr.at[i], mirror) for i in range(2)]

    def gain_round(i, peers, count, at):
        gain_in[i, at] = gain_sum[...]
        cps = []
        for k, peer in enumerate(peers):
            cp = remote(gain_sum, gain_in.at[i, at], gs.at[i, k], gr.at[i, k], peer)
            cp.start()
            cps.append(cp)
        for cp in cps:
            cp.wait()
        gain_sum[...] = sum(gain_in[i, j] for j in range(count))

    cps = []
    for p in range(3):
        cp = remote(
            g_ref.at[pl.ds(12 * (1 - core) + 4 * p, 4)], from_core.at[pl.ds(4 * p, 4)],
            cs.at[p], cr.at[p], partner
        )
        cp.start()
        cps.append(cp)

    @pl.when(core == 1)
    def _():
        for move in moves:
            move.start()

    gain_sum[...] = gain_ref[...]
    gain_round(0, [partner], 2, core)
    ones = []
    for p in range(3):
        cps[p].wait()
        for i in range(4):
            half[4 * p + i] = (
                g_ref[12 * core + 4 * p + i].astype(F32) + from_core[4 * p + i].astype(F32)
            ).astype(BF16)
        for k in range(1, 4):
            peer, at = along(p, k)
            cp = remote(half.at[4 * p + at], one.at[p, k - 1], s1.at[p, k], r1.at[p, k], peer)
            cp.start()
            ones.append(cp)
    gain_round(1, [along(0, k)[0] for k in range(1, 4)], 4, spot[0])
    twos = []
    for p in range(3):
        for cp in ones[3 * p : 3 * p + 3]:
            cp.wait()
        gather[p] = (
            half[4 * p + spot[p]].astype(F32) + sum(one[p, k].astype(F32) for k in range(3))
        ).astype(BF16)
        axis = (p + 1) % 3
        for k in range(1, 4):
            peer, at = along(axis, k)
            cp = remote(
                gather.at[p, pl.ds(144 * at, 144)], two.at[p, k - 1], s2.at[p, k], r2.at[p, k], peer
            )
            cp.start()
            twos.append(cp)
    gain_round(2, [along(1, k)[0] for k in range(1, 4)], 4, spot[1])
    threes = []
    for p in range(3):
        for cp in twos[3 * p : 3 * p + 3]:
            cp.wait()
        b = spot[(p + 1) % 3]
        c = spot[(p + 2) % 3]
        three[p, c] = (
            gather[p, pl.ds(pl.multiple_of(144 * b, 16), 144)].astype(F32)
            + sum(two[p, k].astype(F32) for k in range(3))
        ).astype(BF16)
        for k in range(1, 4):
            peer, at = along((p + 2) % 3, k)
            cp = remote(three.at[p, c], three.at[p, c], s3.at[p, k], r3.at[p, k], peer)
            cp.start()
            threes.append(cp)
    gain_round(3, [along(2, k)[0] for k in range(1, 4)], 4, spot[2])
    gain_out[...] = gain_sum[...]
    fours = []
    for p in range(3):
        for cp in threes[3 * p : 3 * p + 3]:
            cp.wait()
        b = spot[(p + 1) % 3]
        mine = one.at[p, 0, pl.ds(pl.multiple_of(144 * b, 16), 144)]
        mine[...] = sum(three[p, k].astype(F32) for k in range(4)).astype(BF16)
        for k in range(1, 4):
            peer, at = along((p + 1) % 3, k)
            cp = remote(mine, mine, s4.at[p, k], r4.at[p, k], peer)
            cp.start()
            fours.append(cp)
    fives = []
    for p in range(3):
        for cp in fours[3 * p : 3 * p + 3]:
            cp.wait()
        a = spot[p]
        slot = 12 * core + 4 * p + a
        out_ref[slot] = one[p, 0]
        for k in range(1, 4):
            peer, at = along(p, k)
            cp = remote(out_ref.at[slot], out_ref.at[slot], s5.at[p, k], r5.at[p, k], peer)
            cp.start()
            fives.append(cp)
    sixes = []
    for p in range(3):
        for cp in fives[3 * p : 3 * p + 3]:
            cp.wait()
        blocks = out_ref.at[pl.ds(12 * core + 4 * p, 4)]
        cp = remote(blocks, blocks, s6.at[p], r6.at[p], partner)
        cp.start()
        sixes.append(cp)

    @pl.when(core == 1)
    def _():
        for move in moves:
            move.wait()
        fin_out[...] = fin_in[...]

    @pl.when(core == 0)
    def _():
        fin_out[...] = fin_ref[...]

    for cp in sixes:
        cp.wait()


def reduce_all(grads, gains, final):
    return pl.pallas_call(
        reduce_kernel,
        name="reduce_all",
        out_shape=(sds((24, D, 256), BF16), sds((8, D), F32), sds((2, D, TOK), F32)),
        in_specs=[VM] * 3,
        out_specs=(VM,) * 3,
        scratch_shapes=[
            pltpu.VMEM((2, D, TOK), F32),
            DMA((2,)),
            DMA((2,)),
            pltpu.VMEM((12, D, 256), BF16),
            pltpu.VMEM((12, D, 256), BF16),
            pltpu.VMEM((3, 3, D, 256), BF16),
            pltpu.VMEM((3, 3, 144, 256), BF16),
            pltpu.VMEM((3, 4, 144, 256), BF16),
            pltpu.VMEM((3, D, 256), BF16),
            pltpu.VMEM((4, 4, 8, D), F32),
            pltpu.VMEM((8, D), F32),
            DMA((3,)), DMA((3,)),
        ]
        + [DMA((3, 4))] * 10
        + [DMA((3,)), DMA((3,)), DMA((4, 4)), DMA((4, 4))],
        compiler_params=params(4, 56 << 20),
    )(grads, gains, final)


def on_device(
    tokens, cotangent, segment_ids, gain_attn, wq, wk, wv, wo, gain_mlp, wg, wu, wd
):
    ga = gain_attn[None]
    gm = gain_mlp[None]
    wk, wv, wd = wk.T, wv.T, wd.T
    x0, cot, starts, pos = entry(tokens[0].T, cotangent[0].T, segment_ids)
    freq = jnp.exp(jnp.arange(32, dtype=F32) * (-2.0 / HD) * math.log(10000.0))
    angle = freq[:, None] * pos.astype(F32)
    cos, sin = jnp.cos(angle), jnp.sin(angle)

    q0, kv0, h10 = local(
        project_kernel, "project", [Q_T, KV_T, H_S], [x0, ga, wq, wk, wv, cos, sin]
    )
    qa0, kva0, part, stat = attend(q0, kv0, starts)
    q1, kv1, h11, x1_in, m0, h20, inv0, gate0, up0, hid0, o0, lse0 = local(
        middle_kernel,
        "middle",
        [Q_T, KV_T, H_S, X_S, X_S, H_S, sds((TOK, TOK), F32), F_S, F_S, FB_S, sds((D, TOK), F32),
         sds((16, TOK), F32)],
        [part, stat, x0, ga, wq, wk, wv, wo, gm, wg, wu, wd, cos, sin],
    )
    qa1, kva1, part, stat = attend(q1, kv1, starts)
    x2, h21, hid1, ob1, do1, st1, gm1, dg1, du1, da1, dx1, ggm1 = local(
        turn_kernel,
        "turn",
        [X_T, H_S, FB_S, Q_T, Q_T, ST_S, H_S, FB_S, FB_S, H_S, X_S, G_S],
        [part, stat, x1_in, cot, wo, gm, wg, wu, wd],
        [pltpu.VMEM((D, TOK), F32), pltpu.VMEM((16, TOK), F32)],
    )
    dq, dkv = attend_back(do1, st1, qa1, kva1, starts)
    dqkv1, gga1, do0, st0, gm0, dg0, du0, da0, dx0, ggm0 = local(
        between_kernel,
        "between",
        [sds((960, TOK), BF16), G_S, Q_T, ST_S, H_S, FB_S, FB_S, H_S, X_S, G_S],
        [dq, dkv, x1_in, dx1, ga, wq, wk, wv, cos, sin, m0, inv0, gate0, up0, wo, gm, wg, wu, wd,
         o0, lse0],
    )
    dq, dkv = attend_back(do0, st0, qa0, kva0, starts)
    dqkv0, gga0, g0 = local(
        last_kernel,
        "last",
        [sds((960, TOK), BF16), G_S, X_T],
        [dq, dkv, x0, dx0, ga, wq, wk, wv, cos, sin],
    )
    (grads,) = local(
        weights_kernel,
        "weights",
        [sds((24, D, 256), BF16)],
        [h10, h11, dqkv0, dqkv1, o0.astype(BF16), ob1, da0, da1, h20, h21, dg0, dg1, du0, du1,
         hid0, hid1, gm0, gm1],
    )
    gains = jnp.concatenate([gga0 + gga1, ggm0 + ggm1, jnp.zeros((6, D), F32)], axis=0)
    total, gains, final = reduce_all(grads, gains, jnp.stack([x2, g0]))
    gate, up, down, query, key, value, out = spread(total)
    return (
        final[0].T[None], final[1].T[None], gains[0], query, key.T, value.T, out, gains[1], gate, up,
        down.T,
    )


def solution(mesh):
    rows = P("rows", "seq", None)
    in_specs = (rows, rows, P("rows", "seq")) + (P(),) * 9
    out_specs = (rows, rows) + (P(),) * 9
    return jax.shard_map(
        on_device, mesh=mesh, in_specs=in_specs, out_specs=out_specs, check_vma=False
    )
```

```python
import functools
import math

import jax
import jax.numpy as jnp
from jax import lax
from jax.experimental import pallas as pl
from jax.experimental.pallas import tpu as pltpu
from jax.sharding import PartitionSpec as P

F32 = jnp.float32
BF16 = jnp.bfloat16
MESH = pl.DeviceIdType.MESH

D = 576
HEADS = 9
HD = 64
KV = 192
FF = 1536
TOK = 128
DOCS = 16
EPS = 1e-05
SCALE = 0.125
EXP_SCALE = SCALE * 1.4426950408889634
MASKED = -1e30
LOWEST = -1e20

VM = pl.BlockSpec(memory_space=pltpu.VMEM)
DMA = pltpu.SemaphoreType.DMA


def dot(a, b, ca, cb):
    return lax.dot_general(a, b, (((ca,), (cb,)), ((), ())), preferred_element_type=F32)


def sds(shape, dtype):
    return jax.ShapeDtypeStruct(shape, dtype)


def params(collective=None, limit=50 << 20):
    if collective is None:
        return pltpu.CompilerParams(vmem_limit_bytes=limit)
    return pltpu.CompilerParams(
        vmem_limit_bytes=limit, collective_id=collective, has_side_effects=True
    )


def place():
    seq = lax.axis_index("seq")
    row = lax.axis_index("rows")
    return row, seq, seq // 8, lax.rem(seq, 8)


def slot_of(w):
    return lax.rem(w, 2) * 4 + w // 2


def octet_of(n, w):
    return jnp.where(lax.rem(w, 2) == 0, n, 7 - n)


def greet(row, n, w):
    bar = pltpu.get_barrier_semaphore()
    for k in range(1, 8):
        pl.semaphore_signal(
            bar, inc=1, device_id=(row, 8 * n + lax.rem(w + k, 8)), device_id_type=MESH
        )
        pl.semaphore_signal(
            bar, inc=1, device_id=(row, 8 * lax.rem(n + k, 8) + w), device_id_type=MESH
        )
    return bar


def remote(src, dst, send, recv, target):
    return pltpu.make_async_remote_copy(
        src_ref=src,
        dst_ref=dst,
        send_sem=send,
        recv_sem=recv,
        device_id=target,
        device_id_type=MESH,
    )


def entry_kernel(
    tok_ref, cot_ref, ids_ref, x_ref, g_ref, starts_ref, pos_ref,
    tok_in, cot_in, ids_all, starts_all, ysend, yrecv, xsend, xrecv, tsend, trecv
):
    row, seq, n, w = place()
    core = lax.rem(w, 2)
    mirror = (row, 8 * (7 - n) + w)
    bar = greet(row, n, w)
    ids_all[seq] = ids_ref[...]
    pl.semaphore_wait(bar, 14)

    sent = []
    for k in range(1, 8):
        cp = remote(
            ids_all.at[seq], ids_all.at[seq], ysend.at[k], yrecv.at[k],
            (row, 8 * n + lax.rem(w + k, 8)),
        )
        cp.start()
        sent.append(cp)
    moves = [
        remote(tok_ref, tok_in, tsend.at[0], trecv.at[0], mirror),
        remote(cot_ref, cot_in, tsend.at[1], trecv.at[1], mirror),
    ]

    @pl.when(core == 1)
    def _():
        for move in moves:
            move.start()

    for cp in sent:
        cp.wait()
    own = ids_all.at[pl.ds(8 * n, 8)]
    sent = []
    for k in range(1, 8):
        cp = remote(own, own, xsend.at[k], xrecv.at[k], (row, 8 * lax.rem(n + k, 8) + w))
        cp.start()
        sent.append(cp)

    @pl.when(core == 0)
    def _():
        x_ref[...] = tok_ref[...].T
        g_ref[...] = cot_ref[...].T

    for cp in sent:
        cp.wait()

    ids = jnp.concatenate([ids_all[i] for i in range(64)], axis=0)
    total = jnp.zeros((64, TOK), jnp.int32)
    for doc in range(DOCS - 1):
        count = jnp.where(ids == doc, 1.0, 0.0)
        count = jnp.sum(jnp.sum(count, axis=0, keepdims=True), axis=1, keepdims=True)
        total = total + jnp.where(ids > doc, count.astype(jnp.int32), 0)
    starts_all[...] = total[:, None, :]
    for half in range(2):
        octet = n if half == 0 else 7 - n
        for y in range(4):
            starts_ref[half, :, TOK * y : TOK * y + TOK] = starts_all[8 * octet + 2 * y + half]
    mine = 8 * octet_of(n, w) + w
    pos_ref[...] = (
        mine * TOK + lax.broadcasted_iota(jnp.int32, (1, TOK), 1) - starts_all[mine]
    )

    @pl.when(core == 1)
    def _():
        for move in moves:
            move.wait()
        x_ref[...] = tok_in[...].T
        g_ref[...] = cot_in[...].T


def entry(tokens, cotangent, ids):
    return pl.pallas_call(
        entry_kernel,
        name="entry",
        out_shape=(
            sds((TOK, D), F32),
            sds((TOK, D), F32),
            sds((2, 1, 4 * TOK), jnp.int32),
            sds((1, TOK), jnp.int32),
        ),
        in_specs=[VM] * 3,
        out_specs=(VM,) * 4,
        scratch_shapes=[
            pltpu.VMEM((D, TOK), F32),
            pltpu.VMEM((D, TOK), F32),
            pltpu.VMEM((64, 1, TOK), jnp.int32),
            pltpu.VMEM((64, 1, TOK), jnp.int32),
        ]
        + [pltpu.SemaphoreType.DMA((8,))] * 4
        + [pltpu.SemaphoreType.DMA((2,))] * 2,
        compiler_params=params(1, 8 << 20),
    )(tokens, cotangent, ids)


def norm_in(x, gain):
    inverse = lax.rsqrt(jnp.mean(x * x, axis=-1, keepdims=True) + EPS)
    return (x * inverse * gain).astype(BF16), inverse


def norm_back(x, inverse, gain, grad):
    scaled = grad * gain
    grad_gain = jnp.sum(grad * (x * inverse), axis=0, keepdims=True)
    inner = jnp.mean(scaled * x, axis=-1, keepdims=True)
    return inverse * scaled - x * (inverse * inverse * inverse) * inner, grad_gain


def project(x, gain, wq, wk, wv, cos, sin, q_out, kv_out, h_out):
    h, _ = norm_in(x, gain)
    h_out[...] = h
    qt = dot(h, wq, 1, 0).T
    for i in range(HEADS):
        a = qt[HD * i : HD * i + 32]
        b = qt[HD * i + 32 : HD * i + 64]
        q_out[HD * i : HD * i + 32, :] = (a * cos - b * sin).astype(BF16)
        q_out[HD * i + 32 : HD * i + 64, :] = (b * cos + a * sin).astype(BF16)
    kt = dot(wk, h, 1, 1)
    vt = dot(wv, h, 1, 1).astype(BF16)
    for i in range(3):
        a = kt[HD * i : HD * i + 32]
        b = kt[HD * i + 32 : HD * i + 64]
        kv_out[TOK * i : TOK * i + 32, :] = (a * cos - b * sin).astype(BF16)
        kv_out[TOK * i + 32 : TOK * i + 64, :] = (b * cos + a * sin).astype(BF16)
        kv_out[TOK * i + 64 : TOK * i + 128, :] = vt[HD * i : HD * i + 64]


def combine(part, stat, o_out, lse_out):
    for g in range(3):
        tops = [stat[i, 8 * g : 8 * g + 3, :] for i in range(4)]
        top = functools.reduce(jnp.maximum, tops)
        factors = [jnp.exp2((t - top) * EXP_SCALE) for t in tops]
        total = sum(f * stat[i, 8 * g + 4 : 8 * g + 7, :] for i, f in enumerate(factors))
        inverse = 1.0 / total
        factors = [f * inverse for f in factors]
        lse_out[3 * g : 3 * g + 3, :] = top + jnp.log2(total) * (1.0 / EXP_SCALE)
        for j in range(3):
            rows = slice(192 * g + HD * j, 192 * g + HD * j + HD)
            o_out[rows, :] = sum(
                part[i, rows, :].astype(F32) * factors[i][j : j + 1, :] for i in range(4)
            )


def feed_forward(x, o_t, wo, gain, wg, wu, wd):
    x1 = x + dot(o_t, wo, 0, 0)
    h2, inverse = norm_in(x1, gain)
    gate = dot(h2, wg, 1, 0)
    up = dot(h2, wu, 1, 0)
    hid = (gate * jax.nn.sigmoid(gate) * up).astype(BF16)
    return x1, h2, inverse, gate, up, hid, x1 + dot(hid, wd, 1, 1)


def feed_back(g, x1, inverse, gate, up, wo, gain, wg, wu, wd, o_ref, lse,
              do_out, stat_out, gm_out, dgate_out, dup_out, da_out):
    gm = g.astype(BF16)
    gm_out[...] = gm
    dhid = dot(gm, wd, 1, 0)
    sg = jax.nn.sigmoid(gate)
    dgate = (dhid * up * sg * (1.0 + gate * (1.0 - sg))).astype(BF16)
    dup = (dhid * gate * sg).astype(BF16)
    dgate_out[...] = dgate
    dup_out[...] = dup
    dh2 = dot(dgate, wg, 1, 1) + dot(dup, wu, 1, 1)
    dy, grad_gain = norm_back(x1, inverse, gain, dh2)
    dx1 = g + dy
    da = dx1.astype(BF16)
    da_out[...] = da
    do_t = dot(wo, da, 1, 1).astype(BF16)
    do_out[...] = do_t
    stat_out[...] = jnp.zeros(stat_out.shape, F32)
    stat_out[0:HEADS, :] = lse
    for h in range(HEADS):
        rows = slice(HD * h, HD * h + HD)
        stat_out[16 + h : 17 + h, :] = jnp.sum(
            do_t[rows].astype(F32) * o_ref[rows, :], axis=0, keepdims=True
        )
    return dx1, grad_gain


def project_back(dq_part, dkv_part, x, dx1, gain, wq, wk, wv, cos, sin, dqkv_out):
    for h in range(HEADS + 3):
        part, base, many = (dq_part, HD * h, 4) if h < HEADS else (dkv_part, TOK * (h - HEADS), 8)
        a = sum(part[i, base : base + 32, :].astype(F32) for i in range(many))
        b = sum(part[i, base + 32 : base + 64, :].astype(F32) for i in range(many))
        dqkv_out[HD * h : HD * h + 32, :] = (a * cos + b * sin).astype(BF16)
        dqkv_out[HD * h + 32 : HD * h + 64, :] = (b * cos - a * sin).astype(BF16)
    for g in range(3):
        base = TOK * g + HD
        dqkv_out[D + KV + HD * g : D + KV + HD * g + HD, :] = sum(
            dkv_part[i, base : base + HD, :].astype(F32) for i in range(8)
        ).astype(BF16)
    dh1 = (
        dot(dqkv_out[0:D, :], wq, 0, 1)
        + dot(dqkv_out[D : D + KV, :], wk, 0, 0)
        + dot(dqkv_out[D + KV :, :], wv, 0, 0)
    )
    inverse = lax.rsqrt(jnp.mean(x * x, axis=-1, keepdims=True) + EPS)
    dy, grad_gain = norm_back(x, inverse, gain, dh1)
    return dx1 + dy, grad_gain


Q_T = sds((D, TOK), BF16)
KV_T = sds((2 * KV, TOK), BF16)
H_S = sds((TOK, D), BF16)
X_S = sds((TOK, D), F32)
X_T = sds((D, TOK), F32)
F_S = sds((TOK, FF), F32)
FB_S = sds((TOK, FF), BF16)
ST_S = sds((32, TOK), F32)
G_S = sds((1, D), F32)


def project_kernel(x, gain, wq, wk, wv, cos, sin, q_out, kv_out, h_out):
    project(x[...], gain[...], wq[...], wk[...], wv[...], cos[...], sin[...], q_out, kv_out, h_out)


def middle_kernel(
    part, stat, x, ga, wq, wk, wv, wo, gm, wg, wu, wd, cos, sin,
    q_out, kv_out, h_out, x_out, x1_out, h2_out, inv_out, gate_out, up_out, hid_out, o_out, lse_out
):
    combine(part, stat, o_out, lse_out)
    x1, h2, inverse, gate, up, hid, x2 = feed_forward(
        x[...], o_out[...].astype(BF16), wo[...], gm[...], wg[...], wu[...], wd[...]
    )
    x1_out[...] = x1
    h2_out[...] = h2
    inv_out[...] = jnp.broadcast_to(inverse, inv_out.shape)
    gate_out[...] = gate
    up_out[...] = up
    hid_out[...] = hid
    x_out[...] = x2
    project(x2, ga[...], wq[...], wk[...], wv[...], cos[...], sin[...], q_out, kv_out, h_out)


def turn_kernel(
    part, stat, x, g, wo, gm, wg, wu, wd,
    x_out, h2_out, hid_out, ob_out, do_out, stat_out, gmo, dgate, dup, da, dx1_out, gg_out, o_s, lse_s
):
    combine(part, stat, o_s, lse_s)
    ob = o_s[...].astype(BF16)
    ob_out[...] = ob
    x1, h2, inverse, gate, up, hid, x2 = feed_forward(
        x[...], ob, wo[...], gm[...], wg[...], wu[...], wd[...]
    )
    h2_out[...] = h2
    hid_out[...] = hid
    x_out[...] = x2.T
    dx1, gg = feed_back(
        g[...], x1, inverse, gate, up, wo[...], gm[...], wg[...], wu[...], wd[...], o_s,
        lse_s[0:HEADS, :], do_out, stat_out, gmo, dgate, dup, da
    )
    dx1_out[...] = dx1
    gg_out[...] = gg


def between_kernel(
    dq, dkv, x, dx1, ga, wq, wk, wv, cos, sin, x1, inv, gate, up, wo, gm, wg, wu, wd, o, lse,
    dqkv_out, gga_out, do_out, stat_out, gmo, dgate, dup, da, dx1_out, ggm_out
):
    g, gga = project_back(
        dq, dkv, x[...], dx1[...], ga[...], wq[...], wk[...], wv[...], cos[...], sin[...], dqkv_out
    )
    gga_out[...] = gga
    dx0, ggm = feed_back(
        g, x1[...], inv[:, 0:1], gate[...], up[...], wo[...], gm[...], wg[...], wu[...], wd[...], o,
        lse[0:HEADS, :], do_out, stat_out, gmo, dgate, dup, da
    )
    dx1_out[...] = dx0
    ggm_out[...] = ggm


def last_kernel(dq, dkv, x, dx1, ga, wq, wk, wv, cos, sin, dqkv_out, gga_out, g_out):
    g, gga = project_back(
        dq, dkv, x[...], dx1[...], ga[...], wq[...], wk[...], wv[...], cos[...], sin[...], dqkv_out
    )
    gga_out[...] = gga
    g_out[...] = g.T


def local(kernel, name, outs, args, scratch=(), limit=24 << 20):
    return pl.pallas_call(
        kernel,
        name=name,
        out_shape=tuple(outs),
        in_specs=[VM] * len(args),
        out_specs=(VM,) * len(outs),
        scratch_shapes=list(scratch),
        compiler_params=params(None, limit),
    )(*args)


class Torus:
    def __init__(self, row, n, w):
        self.core = lax.rem(w, 2)
        self.spot = (n // 2, w // 2, 2 * row + lax.rem(n, 2))
        self.partner = self.device(self.spot, 1 - self.core)

    def device(self, spot, core):
        x, y, z = spot
        return (z // 2, ((x * 2 + lax.rem(z, 2)) * 4 + y) * 2 + core)

    def along(self, axis, k):
        to = list(self.spot)
        to[axis] = lax.rem(self.spot[axis] + k, 4)
        return self.device(to, self.core), to[axis]


class Reduce:
    def __init__(self, torus, u, send, recv):
        self.torus, self.u, self.send, self.recv = torus, u, send, recv
        self.box = {}

    def go(self, stage, p, k, src, dst, peer):
        cp = remote(src, dst, self.send.at[stage, p, k], self.recv.at[stage, p, k], peer)
        cp.start()
        self.box.setdefault((stage, p), []).append(cp)

    def got(self, stage, p):
        for cp in self.box[stage, p]:
            cp.wait_recv()

    def finish(self):
        for cps in self.box.values():
            for cp in cps:
                cp.wait_send()

    def exchange(self, src, came):
        u, core = self.u, self.torus.core
        for p in range(3):
            self.go(
                0, p, 0, src.at[pl.ds(48 * u * (1 - core) + 16 * u * p, 16 * u)],
                came.at[pl.ds(16 * u * p, 16 * u)], self.torus.partner,
            )

    def first(self, p, src, came, half, one):
        u = self.u
        self.got(0, p)

        def quarter(i, carry):
            at = pl.ds(16 * u * p + 4 * u * i, 4 * u)
            mine = src[pl.ds(48 * u * self.torus.core + 16 * u * p + 4 * u * i, 4 * u)]
            half[at] = (mine.astype(F32) + came[at].astype(F32)).astype(BF16)
            return carry

        lax.fori_loop(0, 4, quarter, 0)
        for k in range(1, 4):
            peer, at = self.torus.along(p, k)
            self.go(1, p, k, half.at[pl.ds(16 * u * p + 4 * u * at, 4 * u)], one.at[p, k - 1], peer)

    def second(self, p, half, one, gather, two):
        u = self.u
        self.got(1, p)
        mine = half[pl.ds(16 * u * p + 4 * u * self.torus.spot[p], 4 * u)]
        gather[p] = (mine.astype(F32) + sum(one[p, k].astype(F32) for k in range(3))).astype(BF16)
        for k in range(1, 4):
            peer, at = self.torus.along((p + 1) % 3, k)
            self.go(2, p, k, gather.at[p, pl.ds(u * at, u)], two.at[p, k - 1], peer)

    def third(self, p, gather, two, three):
        u = self.u
        self.got(2, p)
        c = self.torus.spot[(p + 2) % 3]
        mine = gather[p, pl.ds(u * self.torus.spot[(p + 1) % 3], u)]
        three[p, c] = (mine.astype(F32) + sum(two[p, k].astype(F32) for k in range(3))).astype(BF16)
        for k in range(1, 4):
            self.go(3, p, k, three.at[p, c], three.at[p, c], self.torus.along((p + 2) % 3, k)[0])

    def fourth(self, p, three, mid):
        u = self.u
        self.got(3, p)
        at = pl.ds(u * self.torus.spot[(p + 1) % 3], u)
        mid[p, at] = sum(three[p, k].astype(F32) for k in range(4)).astype(BF16)
        for k in range(1, 4):
            self.go(4, p, k, mid.at[p, at], mid.at[p, at], self.torus.along((p + 1) % 3, k)[0])

    def fifth(self, p, mid, out):
        u = self.u
        at = pl.ds(48 * u * self.torus.core + 16 * u * p + 4 * u * self.torus.spot[p], 4 * u)
        out[at] = mid[p]
        for k in range(1, 4):
            self.go(5, p, k, out.at[at], out.at[at], self.torus.along(p, k)[0])

    def sixth(self, p, out):
        u = self.u
        self.got(5, p)
        at = pl.ds(48 * u * self.torus.core + 16 * u * p, 16 * u)
        self.go(6, p, 0, out.at[at], out.at[at], self.torus.partner)


def units(count, *lead):
    return tuple(lead) + (count, 16, 256)


EARLY, LATE = 7, 2


W3 = 12 * TOK


class Spread:
    def __init__(self, row, n, w, send, recv):
        self.core = lax.rem(w, 2)
        self.y = w // 2
        self.own = self.core * 4 + self.y
        self.row, self.n = row, n
        self.partner = (row, 8 * n + 2 * self.y + 1 - self.core)
        self.send, self.recv = send, recv
        self.first, self.passed = {}, {}

    def chip(self, k):
        return (self.row, 8 * self.n + 2 * lax.rem(self.y + k, 4) + self.core)

    def start(self, part, ref):
        self.first[part], self.passed[part] = [], []
        for k in range(1, 4):
            cp = remote(ref(self.own), ref(self.own), self.send.at[part, k], self.recv.at[part, k],
                        self.chip(k))
            cp.start()
            self.first[part].append(cp)
        self.hand(part, ref, self.own, 4)

    def hand(self, part, ref, slot, k):
        cp = remote(ref(slot), ref(slot), self.send.at[part, k], self.recv.at[part, k], self.partner)
        cp.start()
        self.passed[part].append(cp)

    def forward(self, part, ref):
        for k in range(1, 4):
            self.first[part][k - 1].wait_recv()
            self.hand(part, ref, self.core * 4 + lax.rem(self.y + 4 - k, 4), 4 + k)

    def arrive(self, part):
        for cp in self.passed[part]:
            cp.wait_recv()

    def finish(self):
        for part in self.first:
            for cp in self.first[part] + self.passed[part]:
                cp.wait_send()


def turns(n):
    return (n + 2) // 2


def fill_masks(bias, starts_ref, n, w):
    turn = turns(n)

    def one(t, carry):
        sel = jnp.where(t >= turn, 1, 0)
        kc = jnp.where(t >= turn, t - turn, t)
        line = lax.broadcasted_iota(jnp.int32, (256, 1), 0)
        key = (2 * kc + line // TOK) * 1024 + w * TOK + lax.rem(line, TOK)
        col = lax.broadcasted_iota(jnp.int32, (1, 512), 1)
        octet = jnp.where(sel == 0, n, 7 - n)
        query = octet * 1024 + (2 * (col // TOK) + sel) * TOK + lax.rem(col, TOK)
        bias[t] = jnp.where((key >= starts_ref[sel]) & (key <= query), 0.0, MASKED)
        return carry

    lax.fori_loop(0, 5, one, 0)


def chunk_range(n, sel):
    turn = turns(n)
    return jnp.where(sel == 0, 0, turn), jnp.where(sel == 0, turn, 5 - turn)


def three_heads(ref, sel, g):
    return jnp.concatenate(
        [
            ref[4 * sel + y, HD * h : HD * h + HD, :]
            for h in range(3 * g, 3 * g + 3)
            for y in range(4)
        ],
        axis=1,
    )


def two_blocks(ref, kc, first):
    return jnp.concatenate([ref[2 * kc + i, first : first + HD, :] for i in range(2)], axis=1)


def by_chip(value, y):
    return jnp.concatenate(
        [value[:, 512 * j + TOK * y : 512 * j + TOK * y + TOK] for j in range(3)], axis=0
    )


def attend_kernel(
    q_ref, kv_ref, starts_ref, q_all, kv_all, part_ref, stat_ref,
    k_nat, bias, top, total, acc, o_send, o_recv, r_send, r_recv, o_y, s_y,
    qs, qr, ks, kr, ps, pr, ys, yr
):
    row, seq, n, w = place()
    bar = greet(row, n, w)
    core, y = lax.rem(w, 2), w // 2
    own_k = octet_of(n, w)
    queries = Spread(row, n, w, qs, qr)
    q_all[queries.own] = q_ref[...]
    kv_all[own_k] = kv_ref[...]
    pl.semaphore_wait(bar, 14)

    def q_part(g):
        return lambda slot: q_all.at[slot, pl.ds(192 * g, 192)]

    keys = {}
    for g in range(3):
        keys[g] = []
        for k in range(1, 8):
            block = kv_all.at[own_k, pl.ds(TOK * g, TOK)]
            cp = remote(
                block, block, ks.at[g, k], kr.at[g, k], (row, 8 * lax.rem(n + k, 8) + w)
            )
            cp.start()
            keys[g].append(cp)
        queries.start(g, q_part(g))
    fill_masks(bias, starts_ref, n, w)
    queries.forward(0, q_part(0))

    def phase(g, sel):
        base, count = chunk_range(n, sel)
        top[...] = jnp.full(top.shape, LOWEST, F32)
        total[...] = jnp.zeros(total.shape, F32)
        acc[...] = jnp.zeros(acc.shape, F32)

        def step(kc, carry):
            scores = dot(k_nat[kc], three_heads(q_all, sel, g), 1, 0)
            mask = bias[base + kc]
            weights, shrinks = [], []
            for j in range(3):
                cols = slice(512 * j, 512 * j + 512)
                s = scores[:, cols] + mask
                old = top[:, cols]
                new = jnp.maximum(old, jnp.max(s, axis=0, keepdims=True))
                p = jnp.exp2((s - new) * EXP_SCALE)
                shrink = jnp.exp2((old - new) * EXP_SCALE)
                top[:, cols] = new
                total[:, cols] = total[:, cols] * shrink + jnp.sum(p, axis=0, keepdims=True)
                weights.append(p.astype(BF16))
                shrinks.append(shrink)
            values = two_blocks(kv_all, kc, TOK * g + HD)
            acc[...] = acc[...] * jnp.concatenate(shrinks, axis=1) + dot(
                values, jnp.concatenate(weights, axis=1), 1, 0
            )
            return carry

        lax.fori_loop(0, count, step, 0)

    pairs, outs = [], []
    for g in range(3):
        for cp in keys[g]:
            cp.wait_recv()
        for j in range(8):
            k_nat[j // 2, (j % 2) * TOK : (j % 2) * TOK + TOK, :] = jnp.transpose(
                kv_all[j, TOK * g : TOK * g + HD, :]
            )
        queries.arrive(g)
        phase(g, 1 - core)
        o_send[g] = acc[...].astype(BF16)
        r_send[g, 0] = top[...]
        r_send[g, 1] = total[...]
        both = [
            remote(o_send.at[g], o_recv.at[g], ps.at[0, g], pr.at[0, g], queries.partner),
            remote(r_send.at[g], r_recv.at[g], ps.at[1, g], pr.at[1, g], queries.partner),
        ]
        for cp in both:
            cp.start()
        pairs += both
        if g < 2:
            queries.forward(g + 1, q_part(g + 1))
        phase(g, core)
        for cp in both:
            cp.wait_recv()
        new = jnp.maximum(top[...], r_recv[g, 0])
        mine = jnp.exp2((top[...] - new) * EXP_SCALE)
        theirs = jnp.exp2((r_recv[g, 0] - new) * EXP_SCALE)
        length = total[...] * mine + r_recv[g, 1] * theirs
        out = (acc[...] * mine + o_recv[g].astype(F32) * theirs).astype(BF16)
        for i in range(4):
            o_y[g, i] = by_chip(out, i)
            for j in range(3):
                cols = slice(512 * j + TOK * i, 512 * j + TOK * i + TOK)
                s_y[g, i, j : j + 1, :] = new[:, cols]
                s_y[g, i, 4 + j : 5 + j, :] = length[:, cols]
        for k in range(1, 4):
            to = lax.rem(y + k, 4)
            peer = queries.chip(k)
            for cp in (
                remote(o_y.at[g, to], part_ref.at[y, pl.ds(192 * g, 192)], ys.at[0, g, k],
                       yr.at[0, g, k], peer),
                remote(s_y.at[g, to], stat_ref.at[y, pl.ds(8 * g, 8)], ys.at[1, g, k],
                       yr.at[1, g, k], peer),
            ):
                cp.start()
                outs.append(cp)
        part_ref[y, 192 * g : 192 * g + 192, :] = o_y[g, y]
        stat_ref[y, 8 * g : 8 * g + 8, :] = s_y[g, y]
    queries.finish()
    for g in range(3):
        for cp in keys[g]:
            cp.wait_send()
    for cp in pairs:
        cp.wait_send()
    for cp in outs:
        cp.wait()


def attend(q, kv, starts):
    return pl.pallas_call(
        attend_kernel,
        name="attend",
        out_shape=(
            sds((8, D, TOK), BF16),
            sds((8, 2 * KV, TOK), BF16),
            sds((4, D, TOK), BF16),
            sds((4, 24, TOK), F32),
        ),
        in_specs=[VM] * 3,
        out_specs=(VM,) * 4,
        scratch_shapes=[
            pltpu.VMEM((4, 256, HD), BF16),
            pltpu.VMEM((5, 256, 512), F32),
            pltpu.VMEM((1, W3), F32),
            pltpu.VMEM((1, W3), F32),
            pltpu.VMEM((HD, W3), F32),
            pltpu.VMEM((3, HD, W3), BF16),
            pltpu.VMEM((3, HD, W3), BF16),
            pltpu.VMEM((3, 2, 1, W3), F32),
            pltpu.VMEM((3, 2, 1, W3), F32),
            pltpu.VMEM((3, 4, 192, TOK), BF16),
            pltpu.VMEM((3, 4, 8, TOK), F32),
            DMA((3, 8)), DMA((3, 8)), DMA((3, 8)), DMA((3, 8)),
            DMA((2, 3)), DMA((2, 3)), DMA((2, 3, 4)), DMA((2, 3, 4)),
        ],
        compiler_params=params(2, 16 << 20),
    )(q, kv, starts)


def attend_back_kernel(
    carry_sum, do_ref, st_ref, q_all, kv_all, starts_ref, extra, dq_part, dkv_part, extra_out,
    do_all, st_all, k_nat, v_nat, bias, rows_s, dq, dkv, q_send, q_recv, q_y, kv_low,
    qs, qr, ks, kr, ps, pr, ys, yr, es, er, *more
):
    row, seq, n, w = place()
    bar = greet(row, n, w)
    torus = Torus(row, n, w)
    if carry_sum:
        came, half, one, gather, two, three = more
        for k in range(1, 4):
            pl.semaphore_signal(bar, inc=1, device_id=torus.along(2, k)[0], device_id_type=MESH)
        early = Reduce(torus, EARLY, es, er)
    else:
        (extra_in,) = more
        move = remote(extra, extra_in, es, er, (row, 8 * (7 - n) + w))
    core, y = lax.rem(w, 2), w // 2
    own_k = octet_of(n, w)
    grads = Spread(row, n, w, qs, qr)
    do_all[grads.own] = do_ref[...]
    st_all[grads.own] = st_ref[...]
    pl.semaphore_wait(bar, 17 if carry_sum else 14)

    def part(g):
        return lambda slot: do_all.at[slot, pl.ds(192 * g, 192)]

    def stats(slot):
        return st_all.at[slot]

    grads.start(3, stats)
    for g in range(3):
        grads.start(g, part(g))
    fill_masks(bias, starts_ref, n, w)
    if carry_sum:
        early.exchange(extra, came)
    grads.forward(3, stats)
    grads.forward(0, part(0))
    if carry_sum:
        for p in range(3):
            early.first(p, extra, came, half, one)
    else:

        @pl.when(core == 1)
        def _():
            move.start()

    def phase(g, sel):
        base, count = chunk_range(n, sel)
        dq[...] = jnp.zeros(dq.shape, F32)
        for i, first in enumerate((0, 16)):
            for j in range(3):
                for c in range(4):
                    at = 512 * j + TOK * c
                    line = first + 3 * g + j
                    rows_s[i, :, at : at + TOK] = st_all[4 * sel + c, line : line + 1, :]

        def step(kc, carry):
            qt = three_heads(q_all, sel, g)
            dt = three_heads(do_all, sel, g)
            scores = dot(k_nat[kc], qt, 1, 0)
            dp = dot(v_nat[kc], dt, 1, 0)
            mask = bias[base + kc]
            ps_, ds_ = [], []
            for j in range(3):
                cols = slice(512 * j, 512 * j + 512)
                p = jnp.exp2((scores[:, cols] + mask - rows_s[0, :, cols]) * EXP_SCALE)
                ds_.append((p * (dp[:, cols] - rows_s[1, :, cols])).astype(BF16))
                ps_.append(p.astype(BF16))
            p = jnp.concatenate(ps_, axis=1)
            ds = jnp.concatenate(ds_, axis=1)
            dkv[kc, 0:HD, :] += dot(ds, qt, 1, 1).T
            dkv[kc, HD:, :] += dot(p, dt, 1, 1).T
            dq[...] += dot(two_blocks(kv_all, kc, TOK * g), ds, 1, 0)
            return carry

        lax.fori_loop(0, count, step, 0)

    pairs, outs = [], []
    for g in range(3):
        dkv[...] = jnp.zeros(dkv.shape, F32)
        for j in range(8):
            at = slice((j % 2) * TOK, (j % 2) * TOK + TOK)
            k_nat[j // 2, at, :] = jnp.transpose(kv_all[j, TOK * g : TOK * g + HD, :])
            v_nat[j // 2, at, :] = jnp.transpose(kv_all[j, TOK * g + HD : TOK * g + TOK, :])
        if g == 0:
            grads.arrive(3)
        grads.arrive(g)
        phase(g, 1 - core)
        q_send[g] = (dq[...] * SCALE).astype(BF16)
        pair = remote(q_send.at[g], q_recv.at[g], ps.at[g], pr.at[g], grads.partner)
        pair.start()
        pairs.append(pair)
        if g < 2:
            grads.forward(g + 1, part(g + 1))
        elif carry_sum:
            for p in range(3):
                early.third(p, gather, two, three)
        phase(g, core)
        for j in range(8):
            cols = slice((j % 2) * TOK, (j % 2) * TOK + TOK)
            kv_low[g, j, 0:HD, :] = (dkv[j // 2, 0:HD, cols] * SCALE).astype(BF16)
            kv_low[g, j, HD:, :] = dkv[j // 2, HD:, cols].astype(BF16)
        for k in range(1, 8):
            to = lax.rem(n + k, 8)
            cp = remote(
                kv_low.at[g, octet_of(to, w)], dkv_part.at[n, pl.ds(TOK * g, TOK)], ks.at[g, k],
                kr.at[g, k], (row, 8 * to + w),
            )
            cp.start()
            outs.append(cp)
        pair.wait_recv()
        out = (dq[...] * SCALE + q_recv[g].astype(F32)).astype(BF16)
        for i in range(4):
            q_y[g, i] = by_chip(out, i)
        for k in range(1, 4):
            to = lax.rem(y + k, 4)
            cp = remote(q_y.at[g, to], dq_part.at[y, pl.ds(192 * g, 192)], ys.at[g, k], yr.at[g, k],
                        grads.chip(k))
            cp.start()
            outs.append(cp)
        dkv_part[n, TOK * g : TOK * g + TOK, :] = kv_low[g, own_k]
        dq_part[y, 192 * g : 192 * g + 192, :] = q_y[g, y]
        if carry_sum:
            for p in range(3):
                if g == 1:
                    early.second(p, half, one, gather, two)
                elif g == 2:
                    early.fourth(p, three, extra_out)
    grads.finish()
    for cp in pairs:
        cp.wait_send()
    for cp in outs:
        cp.wait()
    if carry_sum:
        for p in range(3):
            early.got(4, p)
        early.finish()
    else:

        @pl.when(core == 1)
        def _():
            move.wait()
            extra_out[...] = extra_in[...]

        @pl.when(core == 0)
        def _():
            extra_out[...] = extra[...]


def attend_back(do, st, q_all, kv_all, starts, extra, carry_sum):
    if carry_sum:
        u = EARLY
        extra_shape = sds(units(4 * u, 3), BF16)
        more = [DMA((5, 3, 4))] * 2 + [
            pltpu.VMEM(shape, BF16)
            for shape in (
                units(48 * u), units(48 * u), units(4 * u, 3, 3), units(4 * u, 3), units(u, 3, 3),
                units(u, 3, 4),
            )
        ]
    else:
        extra_shape = X_T
        more = [DMA, DMA, pltpu.VMEM((D, TOK), F32)]
    return pl.pallas_call(
        functools.partial(attend_back_kernel, carry_sum),
        name="attend_back_sum" if carry_sum else "attend_back",
        out_shape=(sds((4, D, TOK), BF16), sds((8, 2 * KV, TOK), BF16), extra_shape),
        in_specs=[VM] * 6,
        out_specs=(VM,) * 3,
        scratch_shapes=[
            pltpu.VMEM((8, D, TOK), BF16),
            pltpu.VMEM((8, 32, TOK), F32),
            pltpu.VMEM((4, 256, HD), BF16),
            pltpu.VMEM((4, 256, HD), BF16),
            pltpu.VMEM((5, 256, 512), F32),
            pltpu.VMEM((2, 1, W3), F32),
            pltpu.VMEM((HD, W3), F32),
            pltpu.VMEM((4, TOK, 256), F32),
            pltpu.VMEM((3, HD, W3), BF16),
            pltpu.VMEM((3, HD, W3), BF16),
            pltpu.VMEM((3, 4, 192, TOK), BF16),
            pltpu.VMEM((3, 8, TOK, TOK), BF16),
            DMA((4, 8)), DMA((4, 8)), DMA((3, 8)), DMA((3, 8)),
            DMA((3,)), DMA((3,)), DMA((3, 4)), DMA((3, 4)),
        ]
        + more,
        compiler_params=params(5, 32 << 20) if carry_sum else params(3, 16 << 20),
    )(do, st, q_all, kv_all, starts, extra)


def both_rows(a, b):
    return jnp.concatenate([a[...], b[...]], axis=0)


def as_units(value):
    return value.astype(BF16).reshape(units(value.shape[0] // 16))


def early_kernel(oa, ob, daa, dab, h2a, h2b, dga, dgb, dua, dub, hida, hidb, gma, gmb, g_out):
    ot = jnp.concatenate([oa[...], ob[...]], axis=1)
    h2t = both_rows(h2a, h2b).T
    gmt = both_rows(gma, gmb).T
    for i in range(6):
        cols = slice(256 * i, 256 * i + 256)
        for t, (lhs, a, b) in enumerate(((h2t, dga, dgb), (h2t, dua, dub), (gmt, hida, hidb))):
            rhs = jnp.concatenate([a[:, cols], b[:, cols]], axis=0)
            g_out[36 * (6 * t + i) : 36 * (6 * t + i) + 36] = as_units(dot(lhs, rhs, 1, 0))
    da = both_rows(daa[:, 128:384], dab[:, 128:384])
    g_out[648:672] = as_units(dot(ot[0:384], da, 1, 0))


def late_kernel(h1a, h1b, dqa, dqb, oa, ob, daa, dab, g_out):
    h1t = both_rows(h1a, h1b).T
    ot = jnp.concatenate([oa[...], ob[...]], axis=1)
    dat = both_rows(daa, dab).T

    def rows(first, last):
        return jnp.concatenate([dqa[first:last, :], dqb[first:last, :]], axis=1)

    g_out[0:36] = as_units(dot(h1t, rows(0, 256), 1, 1))
    g_out[36:72] = as_units(dot(h1t, rows(256, 512), 1, 1))
    mixed = [dot(h1t, rows(512, 640), 1, 1), dot(ot, dat[0:128], 1, 1)]
    g_out[72:108] = as_units(jnp.concatenate(mixed, axis=1))
    g_out[108:120] = as_units(dot(ot[384:576], dat[128:384], 1, 1))
    low = jnp.concatenate([dat[384:576], jnp.zeros((64, 256), BF16)], axis=0)
    high = jnp.concatenate([jnp.zeros((192, 256), BF16), rows(640, 704)], axis=0)
    g_out[120:156] = as_units(dot(ot, low, 1, 1) + dot(h1t, high, 1, 1))
    g_out[156:192] = as_units(dot(h1t, rows(704, 960), 1, 1))


def spread_kernel(
    early, late, gate_out, up_out, down_out, q_out, k_out, v_out, o_out, big, small, kt, vt, sems
):
    def block(ref, first, count=36):
        return ref[first : first + count].reshape(16 * count, 256).astype(F32)

    cps = []
    for t, ref in enumerate((gate_out, up_out, down_out)):
        for i in range(6):
            cols = pl.ds(256 * i, 256)
            big[t, :, cols] = block(early, 36 * (6 * t + i))
            cp = pltpu.make_async_copy(big.at[t, :, cols], ref.at[:, cols], sems.at[6 * t + i])
            cp.start()
            cps.append(cp)
    small[0, :, 0:256] = block(late, 0)
    small[0, :, 256:512] = block(late, 36)
    mixed = block(late, 72)
    small[0, :, 512:576] = mixed[:, 0:64]
    small[1, :, 0:128] = mixed[:, 128:256]
    kt[0:64, :] = mixed[:, 0:128].T[64:128]
    small[1, 0:384, 128:384] = block(early, 648, 24)
    small[1, 384:576, 128:384] = block(late, 108, 12)
    mixed = block(late, 120)
    small[1, :, 384:576] = mixed[:, 0:192]
    kt[64:128, :] = mixed[:, 128:256].T[64:128]
    last = block(late, 156).T
    kt[128:192, :] = last[0:64]
    vt[...] = last[64:256]
    for i, (src, dst) in enumerate(
        ((small.at[0], q_out), (small.at[1], o_out), (kt, k_out), (vt, v_out))
    ):
        cp = pltpu.make_async_copy(src, dst, sems.at[18 + i])
        cp.start()
        cps.append(cp)
    for cp in cps:
        cp.wait()


def spread(early, late):
    anywhere = pl.BlockSpec(memory_space=pl.ANY)
    return pl.pallas_call(
        spread_kernel,
        name="spread",
        out_shape=(
            sds((D, FF), F32), sds((D, FF), F32), sds((D, FF), F32), sds((D, D), F32),
            sds((KV, D), F32), sds((KV, D), F32), sds((D, D), F32),
        ),
        in_specs=[VM] * 2,
        out_specs=(anywhere,) * 7,
        scratch_shapes=[
            pltpu.VMEM((3, D, FF), F32),
            pltpu.VMEM((2, D, D), F32),
            pltpu.VMEM((KV, D), F32),
            pltpu.VMEM((KV, D), F32),
            DMA((22,)),
        ],
        compiler_params=params(None, 30 << 20),
    )(early, late)


def reduce_kernel(
    mid_ref, late_ref, gain_ref, fin_ref, early_out, late_out, gain_out, fin_out,
    came, half, one, gather, two, three, mid, gain_in, gain_sum, fin_in,
    s_e, r_e, s_l, r_l, gs, gr, fs, fr
):
    row, seq, n, w = place()
    torus = Torus(row, n, w)
    core = torus.core
    bar = pltpu.get_barrier_semaphore()
    pl.semaphore_signal(bar, inc=1, device_id=torus.partner, device_id_type=MESH)
    for axis in range(3):
        for k in range(1, 4):
            pl.semaphore_signal(bar, inc=1, device_id=torus.along(axis, k)[0], device_id_type=MESH)
    mirror = (row, 8 * (7 - n) + w)

    @pl.when(core == 1)
    def _():
        pl.semaphore_signal(bar, inc=1, device_id=mirror, device_id_type=MESH)
        pl.semaphore_wait(bar, 11)

    @pl.when(core == 0)
    def _():
        pl.semaphore_wait(bar, 10)

    early = Reduce(torus, EARLY, s_e, r_e)
    late = Reduce(torus, LATE, s_l, r_l)
    late.exchange(late_ref, came)
    for p in range(3):
        early.fifth(p, mid_ref, early_out)
    move = remote(fin_ref, fin_in, fs, fr, mirror)

    @pl.when(core == 1)
    def _():
        move.start()

    gains = []

    def gain_round(i, peers, count, at):
        gain_in[i, at] = gain_sum[i]
        for k, peer in enumerate(peers):
            cp = remote(gain_sum.at[i], gain_in.at[i, at], gs.at[i, k], gr.at[i, k], peer)
            cp.start()
            gains.append(cp)

    def gain_total(i, peers, count):
        for cp in gains[-peers:]:
            cp.wait_recv()
        return sum(gain_in[i, j] for j in range(count))

    def axis_peers(axis):
        return [torus.along(axis, k)[0] for k in range(1, 4)]

    gain_sum[0] = gain_ref[...]
    gain_round(0, [torus.partner], 2, core)
    for p in range(3):
        late.first(p, late_ref, came, half, one)
    gain_sum[1] = gain_total(0, 1, 2)
    gain_round(1, axis_peers(0), 4, torus.spot[0])
    for p in range(3):
        late.second(p, half, one, gather, two)
    for p in range(3):
        early.sixth(p, early_out)
    gain_sum[2] = gain_total(1, 3, 4)
    gain_round(2, axis_peers(1), 4, torus.spot[1])
    for p in range(3):
        late.third(p, gather, two, three)
    gain_sum[3] = gain_total(2, 3, 4)
    gain_round(3, axis_peers(2), 4, torus.spot[2])
    for p in range(3):
        late.fourth(p, three, mid)
    gain_out[...] = gain_total(3, 3, 4)
    for p in range(3):
        late.got(4, p)
        late.fifth(p, mid, late_out)
    for p in range(3):
        late.sixth(p, late_out)

    @pl.when(core == 1)
    def _():
        move.wait()
        fin_out[...] = fin_in[...]

    @pl.when(core == 0)
    def _():
        fin_out[...] = fin_ref[...]

    for cp in gains:
        cp.wait_send()
    for p in range(3):
        early.got(6, p)
        late.got(6, p)
    early.finish()
    late.finish()


def reduce_all(mid, late, gains, final):
    u = LATE
    return pl.pallas_call(
        reduce_kernel,
        name="reduce_all",
        out_shape=(
            sds(units(96 * EARLY), BF16), sds(units(96 * LATE), BF16), sds((8, D), F32), X_T
        ),
        in_specs=[VM] * 4,
        out_specs=(VM,) * 4,
        scratch_shapes=[
            pltpu.VMEM(shape, BF16)
            for shape in (
                units(48 * u), units(48 * u), units(4 * u, 3, 3), units(4 * u, 3), units(u, 3, 3),
                units(u, 3, 4), units(4 * u, 3),
            )
        ]
        + [
            pltpu.VMEM((4, 4, 8, D), F32),
            pltpu.VMEM((4, 8, D), F32),
            pltpu.VMEM((D, TOK), F32),
        ]
        + [DMA((7, 3, 4))] * 4
        + [DMA((4, 4)), DMA((4, 4)), DMA, DMA],
        compiler_params=params(4, 20 << 20),
    )(mid, late, gains, final)


def on_device(
    tokens, cotangent, segment_ids, gain_attn, wq, wk, wv, wo, gain_mlp, wg, wu, wd
):
    ga = gain_attn[None]
    gm = gain_mlp[None]
    wk, wv, wd = wk.T, wv.T, wd.T
    x0, cot, starts, pos = entry(tokens[0].T, cotangent[0].T, segment_ids)
    freq = jnp.exp(jnp.arange(32, dtype=F32) * (-2.0 / HD) * math.log(10000.0))
    angle = freq[:, None] * pos.astype(F32)
    cos, sin = jnp.cos(angle), jnp.sin(angle)

    q0, kv0, h10 = local(
        project_kernel, "project", [Q_T, KV_T, H_S], [x0, ga, wq, wk, wv, cos, sin]
    )
    qa0, kva0, part, stat = attend(q0, kv0, starts)
    q1, kv1, h11, x1_in, m0, h20, inv0, gate0, up0, hid0, o0, lse0 = local(
        middle_kernel,
        "middle",
        [Q_T, KV_T, H_S, X_S, X_S, H_S, sds((TOK, TOK), F32), F_S, F_S, FB_S, sds((D, TOK), F32),
         sds((16, TOK), F32)],
        [part, stat, x0, ga, wq, wk, wv, wo, gm, wg, wu, wd, cos, sin],
    )
    qa1, kva1, part, stat = attend(q1, kv1, starts)
    x2, h21, hid1, ob1, do1, st1, gm1, dg1, du1, da1, dx1, ggm1 = local(
        turn_kernel,
        "turn",
        [X_T, H_S, FB_S, Q_T, Q_T, ST_S, H_S, FB_S, FB_S, H_S, X_S, G_S],
        [part, stat, x1_in, cot, wo, gm, wg, wu, wd],
        [pltpu.VMEM((D, TOK), F32), pltpu.VMEM((16, TOK), F32)],
    )
    dq, dkv, output = attend_back(do1, st1, qa1, kva1, starts, x2, False)
    dqkv1, gga1, do0, st0, gm0, dg0, du0, da0, dx0, ggm0 = local(
        between_kernel,
        "between",
        [sds((960, TOK), BF16), G_S, Q_T, ST_S, H_S, FB_S, FB_S, H_S, X_S, G_S],
        [dq, dkv, x1_in, dx1, ga, wq, wk, wv, cos, sin, m0, inv0, gate0, up0, wo, gm, wg, wu, wd,
         o0, lse0],
    )
    ob0 = o0.astype(BF16)
    (early,) = local(
        early_kernel,
        "early",
        [sds(units(96 * EARLY), BF16)],
        [ob0, ob1, da0, da1, h20, h21, dg0, dg1, du0, du1, hid0, hid1, gm0, gm1],
    )
    dq, dkv, mid = attend_back(do0, st0, qa0, kva0, starts, early, True)
    dqkv0, gga0, g0 = local(
        last_kernel,
        "last",
        [sds((960, TOK), BF16), G_S, X_T],
        [dq, dkv, x0, dx0, ga, wq, wk, wv, cos, sin],
    )
    (late,) = local(
        late_kernel,
        "late",
        [sds(units(96 * LATE), BF16)],
        [h10, h11, dqkv0, dqkv1, ob0, ob1, da0, da1],
    )
    gains = jnp.concatenate([gga0 + gga1, ggm0 + ggm1, jnp.zeros((6, D), F32)], axis=0)
    early, late, gains, grad_tokens = reduce_all(mid, late, gains, g0)
    gate, up, down, query, key, value, out = spread(early, late)
    return (
        output.T[None], grad_tokens.T[None], gains[0], query, key.T, value.T, out, gains[1], gate, up,
        down.T,
    )


def solution(mesh):
    rows = P("rows", "seq", None)
    in_specs = (rows, rows, P("rows", "seq")) + (P(),) * 9
    out_specs = (rows, rows) + (P(),) * 9
    return jax.shard_map(
        on_device, mesh=mesh, in_specs=in_specs, out_specs=out_specs, check_vma=False
    )
```

```python
import functools
import math

import jax
import jax.numpy as jnp
from jax import lax
from jax.experimental import pallas as pl
from jax.experimental.pallas import tpu as pltpu
from jax.sharding import PartitionSpec as P

F32 = jnp.float32
BF16 = jnp.bfloat16
MESH = pl.DeviceIdType.MESH

D = 576
HEADS = 9
HD = 64
KV = 192
FF = 1536
TOK = 128
DOCS = 16
EPS = 1e-05
SCALE = 0.125
EXP_SCALE = SCALE * 1.4426950408889634
MASKED = -1e30
LOWEST = -1e20

VM = pl.BlockSpec(memory_space=pltpu.VMEM)
DMA = pltpu.SemaphoreType.DMA


def dot(a, b, ca, cb):
    return lax.dot_general(a, b, (((ca,), (cb,)), ((), ())), preferred_element_type=F32)


def sds(shape, dtype):
    return jax.ShapeDtypeStruct(shape, dtype)


def params(collective=None, limit=50 << 20):
    if collective is None:
        return pltpu.CompilerParams(vmem_limit_bytes=limit)
    return pltpu.CompilerParams(
        vmem_limit_bytes=limit, collective_id=collective, has_side_effects=True
    )


def cost(us):
    return pl.CostEstimate(flops=us * 1000000000, bytes_accessed=us * 1000000, transcendentals=0)


def place():
    seq = lax.axis_index("seq")
    row = lax.axis_index("rows")
    return row, seq, seq // 8, lax.rem(seq, 8)


def slot_of(w):
    return lax.rem(w, 2) * 4 + w // 2


def octet_of(n, w):
    return jnp.where(lax.rem(w, 2) == 0, n, 7 - n)


def greet(row, n, w):
    bar = pltpu.get_barrier_semaphore()
    for k in range(1, 8):
        pl.semaphore_signal(
            bar, inc=1, device_id=(row, 8 * n + lax.rem(w + k, 8)), device_id_type=MESH
        )
        pl.semaphore_signal(
            bar, inc=1, device_id=(row, 8 * lax.rem(n + k, 8) + w), device_id_type=MESH
        )
    return bar


def remote(src, dst, send, recv, target):
    return pltpu.make_async_remote_copy(
        src_ref=src,
        dst_ref=dst,
        send_sem=send,
        recv_sem=recv,
        device_id=target,
        device_id_type=MESH,
    )


def as_row(ref):
    return ref[...].reshape(1, D)


def norm_in(x, gain):
    inverse = lax.rsqrt(jnp.mean(x * x, axis=-1, keepdims=True) + EPS)
    return (x * inverse * gain).astype(BF16), inverse


def norm_back(x, inverse, gain, grad):
    scaled = grad * gain
    grad_gain = jnp.sum(grad * (x * inverse), axis=0, keepdims=True)
    inner = jnp.mean(scaled * x, axis=-1, keepdims=True)
    return inverse * scaled - x * (inverse * inverse * inverse) * inner, grad_gain


def project(x, gain, wq, wk, wv, h_out):
    h, _ = norm_in(x, gain)
    h_out[...] = h
    return dot(h, wq[...], 1, 0).T, dot(wk[...], h, 1, 1), dot(wv[...], h, 1, 1).astype(BF16)


def rotate(qt, kt, vt, cos, sin, q_out, kv_out):
    for i in range(HEADS):
        a = qt[HD * i : HD * i + 32]
        b = qt[HD * i + 32 : HD * i + 64]
        q_out[HD * i : HD * i + 32, :] = (a * cos - b * sin).astype(BF16)
        q_out[HD * i + 32 : HD * i + 64, :] = (b * cos + a * sin).astype(BF16)
    for i in range(3):
        a = kt[HD * i : HD * i + 32]
        b = kt[HD * i + 32 : HD * i + 64]
        kv_out[TOK * i : TOK * i + 32, :] = (a * cos - b * sin).astype(BF16)
        kv_out[TOK * i + 32 : TOK * i + 64, :] = (b * cos + a * sin).astype(BF16)
        kv_out[TOK * i + 64 : TOK * i + 128, :] = vt[HD * i : HD * i + 64]


def combine(part, stat, o_out, lse_out):
    for g in range(3):
        tops = [stat[i, 8 * g : 8 * g + 3, :] for i in range(4)]
        top = functools.reduce(jnp.maximum, tops)
        factors = [jnp.exp2((t - top) * EXP_SCALE) for t in tops]
        total = sum(f * stat[i, 8 * g + 4 : 8 * g + 7, :] for i, f in enumerate(factors))
        inverse = 1.0 / total
        factors = [f * inverse for f in factors]
        lse_out[3 * g : 3 * g + 3, :] = top + jnp.log2(total) * (1.0 / EXP_SCALE)
        for j in range(3):
            rows = slice(192 * g + HD * j, 192 * g + HD * j + HD)
            o_out[rows, :] = sum(
                part[i, rows, :].astype(F32) * factors[i][j : j + 1, :] for i in range(4)
            )


def feed_forward(x, o_t, wo, gain, wg, wu, wd):
    x1 = x + dot(o_t, wo[...], 0, 0)
    h2, inverse = norm_in(x1, gain)
    gate = dot(h2, wg[...], 1, 0)
    up = dot(h2, wu[...], 1, 0)
    hid = (gate * jax.nn.sigmoid(gate) * up).astype(BF16)
    return x1, h2, inverse, gate, up, hid, x1 + dot(hid, wd[...], 1, 1)


def feed_back(g, x1, inverse, gate, up, wo, gain, wg, wu, wd, o_ref, lse,
              do_out, stat_out, gm_out, dgate_out, dup_out, da_out):
    gm = g.astype(BF16)
    gm_out[...] = gm
    dhid = dot(gm, wd[...], 1, 0)
    sg = jax.nn.sigmoid(gate)
    dgate = (dhid * up * sg * (1.0 + gate * (1.0 - sg))).astype(BF16)
    dup = (dhid * gate * sg).astype(BF16)
    dgate_out[...] = dgate
    dup_out[...] = dup
    dh2 = dot(dgate, wg[...], 1, 1) + dot(dup, wu[...], 1, 1)
    dy, grad_gain = norm_back(x1, inverse, gain, dh2)
    dx1 = g + dy
    da = dx1.astype(BF16)
    da_out[...] = da
    do_t = dot(wo[...], da, 1, 1).astype(BF16)
    do_out[...] = do_t
    stat_out[...] = jnp.zeros(stat_out.shape, F32)
    stat_out[0:HEADS, :] = lse
    for h in range(HEADS):
        rows = slice(HD * h, HD * h + HD)
        stat_out[16 + h : 17 + h, :] = jnp.sum(
            do_t[rows].astype(F32) * o_ref[rows, :], axis=0, keepdims=True
        )
    return dx1, grad_gain


def project_back(dq_part, dkv_part, x, dx1, gain, wq, wk, wv, cos, sin, dqkv_out):
    for h in range(HEADS + 3):
        part, base, many = (dq_part, HD * h, 4) if h < HEADS else (dkv_part, TOK * (h - HEADS), 8)
        a = sum(part[i, base : base + 32, :].astype(F32) for i in range(many))
        b = sum(part[i, base + 32 : base + 64, :].astype(F32) for i in range(many))
        dqkv_out[HD * h : HD * h + 32, :] = (a * cos + b * sin).astype(BF16)
        dqkv_out[HD * h + 32 : HD * h + 64, :] = (b * cos - a * sin).astype(BF16)
    for g in range(3):
        base = TOK * g + HD
        dqkv_out[D + KV + HD * g : D + KV + HD * g + HD, :] = sum(
            dkv_part[i, base : base + HD, :].astype(F32) for i in range(8)
        ).astype(BF16)
    dh1 = (
        dot(dqkv_out[0:D, :], wq[...], 0, 1)
        + dot(dqkv_out[D : D + KV, :], wk[...], 0, 0)
        + dot(dqkv_out[D + KV :, :], wv[...], 0, 0)
    )
    inverse = lax.rsqrt(jnp.mean(x * x, axis=-1, keepdims=True) + EPS)
    dy, grad_gain = norm_back(x, inverse, gain, dh1)
    return dx1 + dy, grad_gain


Q_T = sds((D, TOK), BF16)
KV_T = sds((2 * KV, TOK), BF16)
H_S = sds((TOK, D), BF16)
X_S = sds((TOK, D), F32)
X_T = sds((D, TOK), F32)
F_S = sds((TOK, FF), F32)
FB_S = sds((TOK, FF), BF16)
ST_S = sds((32, TOK), F32)
G_S = sds((1, D), F32)


ANY = pl.BlockSpec(memory_space=pl.ANY)
HBM = pl.BlockSpec(memory_space=pltpu.HBM)


class Lazy:
    def __init__(self, src, buf, sem):
        self.copy = pltpu.make_async_copy(src, buf, sem)
        self.copy.start()
        self.buf, self.waited = buf, False

    def ref(self):
        if not self.waited:
            self.copy.wait()
            self.waited = True
        return self.buf

    def __getitem__(self, index):
        return self.ref()[index]


def fetch(srcs, bufs, sems):
    return [Lazy(src, buf, sems.at[i]) for i, (src, buf) in enumerate(zip(srcs, bufs))]


def buffers(*arrays):
    return [pltpu.VMEM(a.shape, a.dtype) for a in arrays] + [DMA((len(arrays),))]


def mirrored(ctx, src, dst, send, recv):
    move = remote(src, dst, send.at[0], recv, (ctx.row, 8 * (7 - ctx.n) + ctx.w))
    stay = pltpu.make_async_copy(src, dst, send.at[1])

    def both(if_one, if_zero):
        pl.when(ctx.core == 1)(if_one)
        pl.when(ctx.core == 0)(if_zero)

    return lambda: both(move.start, stay.start), lambda: both(move.wait, stay.wait)


def first_part(ctx, ins, outs, scratch):
    tok, ids_ref, ga, wq, wk, wv = ins
    x_out, h_out, starts_ref, cos_ref, sin_ref, q_save, kv_save = outs
    (tok_in, ids_all, starts_all, ysend, yrecv, xsend, xrecv, tsend, trecv,
     bq, bk, bv, bsem, ssem) = scratch
    row, n, w = ctx.row, ctx.n, ctx.w
    seq = 8 * n + w
    get_ids = pltpu.make_async_copy(ids_ref, ids_all.at[seq], ssem.at[0])
    get_ids.start()
    wq, wk, wv = fetch([wq, wk, wv], [bq, bk, bv], bsem)
    get_ids.wait()
    ctx.ready()
    start, wait = mirrored(ctx, tok, tok_in, tsend, trecv)
    start()
    sent = []
    for k in range(1, 8):
        cp = remote(
            ids_all.at[seq], ids_all.at[seq], ysend.at[k], yrecv.at[k],
            (row, 8 * n + lax.rem(w + k, 8)),
        )
        cp.start()
        sent.append(cp)
    for cp in sent:
        cp.wait()
    own = ids_all.at[pl.ds(8 * n, 8)]
    sent = []
    for k in range(1, 8):
        cp = remote(own, own, xsend.at[k], xrecv.at[k], (row, 8 * lax.rem(n + k, 8) + w))
        cp.start()
        sent.append(cp)
    wait()
    x = tok_in[...].T
    x_out[...] = x
    raw = project(x, as_row(ga), wq, wk, wv, h_out)
    for cp in sent:
        cp.wait()

    ids = jnp.concatenate([ids_all[i] for i in range(64)], axis=0)
    total = jnp.zeros((64, TOK), jnp.int32)
    for doc in range(DOCS - 1):
        count = jnp.where(ids == doc, 1.0, 0.0)
        count = jnp.sum(jnp.sum(count, axis=0, keepdims=True), axis=1, keepdims=True)
        total = total + jnp.where(ids > doc, count.astype(jnp.int32), 0)
    starts_all[...] = total[:, None, :]
    for half in range(2):
        octet = n if half == 0 else 7 - n
        for y in range(4):
            starts_ref[half, :, TOK * y : TOK * y + TOK] = starts_all[8 * octet + 2 * y + half]
    mine = 8 * octet_of(n, w) + w
    pos = mine * TOK + lax.broadcasted_iota(jnp.int32, (1, TOK), 1) - starts_all[mine]
    line = lax.broadcasted_iota(jnp.int32, (32, TOK), 0).astype(F32)
    angle = jnp.exp(line * (-2.0 / HD) * math.log(10000.0)) * pos.astype(F32)
    cos_ref[...] = jnp.cos(angle)
    sin_ref[...] = jnp.sin(angle)
    rotate(*raw, cos_ref[...], sin_ref[...], ctx.q_own, ctx.kv_own)

    saves = [
        pltpu.make_async_copy(ctx.q_all, q_save, ssem.at[1]),
        pltpu.make_async_copy(ctx.kv_all, kv_save, ssem.at[2]),
    ]

    def arrived():
        for cp in saves:
            cp.start()

    def end():
        for cp in saves:
            cp.wait()

    return None, arrived, end


def middle_part(ctx, ins, outs, scratch):
    part, stat, x, cot, ga, wq, wk, wv, wo, gm, wg, wu, wd, cos, sin = ins
    g_out, h_out, x_out, x1_out, h2_out, inv_out, gate_out, up_out, hid_out, o_out, lse_out = outs
    gate_s, up_s, ssem, cot_in, csend, crecv = scratch
    start, wait = mirrored(ctx, cot, cot_in, csend, crecv)
    saves = [
        pltpu.make_async_copy(gate_s, gate_out, ssem.at[0]),
        pltpu.make_async_copy(up_s, up_out, ssem.at[1]),
    ]
    combine(part, stat, o_out, lse_out)
    x1, h2, inverse, gate, up, hid, x2 = feed_forward(
        x[...], o_out[...].astype(BF16), wo, as_row(gm), wg, wu, wd
    )
    x_out[...] = x2
    raw = project(x2, as_row(ga), wq, wk, wv, h_out)
    rotate(*raw, cos[...], sin[...], ctx.q_own, ctx.kv_own)
    ctx.ready()

    def late():
        x1_out[...] = x1
        h2_out[...] = h2
        inv_out[...] = jnp.broadcast_to(inverse, inv_out.shape)
        gate_s[...] = gate
        up_s[...] = up
        hid_out[...] = hid
        for cp in saves:
            cp.start()
        start()

    def end():
        for cp in saves:
            cp.wait()
        wait()
        g_out[...] = cot_in[...].T

    return late, None, end


def turn_part(ctx, ins, outs, scratch):
    part, stat, x, g, wo, gm, wg, wu, wd = ins
    h2_out, hid_out, ob_out, gmo, dgate, dup, da, dx1_out, gg_out = outs
    o_s, lse_s = scratch
    combine(part, stat, o_s, lse_s)
    ob = o_s[...].astype(BF16)
    ob_out[...] = ob
    x1, h2, inverse, gate, up, hid, x2 = feed_forward(
        x[...], ob, wo, as_row(gm), wg, wu, wd
    )
    h2_out[...] = h2
    hid_out[...] = hid
    ctx.extra[...] = x2.T
    dx1, gg = feed_back(
        g[...], x1, inverse, gate, up, wo, as_row(gm), wg, wu, wd, o_s,
        lse_s[0:HEADS, :], ctx.do_own, ctx.st_own, gmo, dgate, dup, da
    )
    dx1_out[...] = dx1
    gg_out[...] = gg


def between_part(ctx, ins, outs, scratch):
    (dq, dkv, x, dx1, ga, wq, wk, wv, cos, sin, x1, inv, gate, up, wo, gm, wg, wu, wd, o, lse,
     ob1, da1, h20, h21, dg1, du1, hid0, hid1, gm1) = ins
    dqkv_out, gga_out, da, dx1_out, ggm_out, ob_out = outs
    gmo, dgate, dup = scratch
    g, gga = project_back(
        dq, dkv, x[...], dx1[...], as_row(ga), wq, wk, wv, cos[...], sin[...], dqkv_out
    )
    gga_out[...] = gga
    dx0, ggm = feed_back(
        g, x1[...], inv[:, 0:1], gate[...], up[...], wo, as_row(gm), wg, wu, wd, o,
        lse[0:HEADS, :], ctx.do_own, ctx.st_own, gmo, dgate, dup, da
    )
    dx1_out[...] = dx0
    ggm_out[...] = ggm
    ob_out[...] = o[...].astype(BF16)

    def grads():
        early_grads(
            ob_out, ob1, da, da1, h20, h21, dgate, dg1, dup, du1, hid0, hid1, gmo, gm1, ctx.extra
        )

    return grads


class Torus:
    def __init__(self, row, n, w):
        self.core = lax.rem(w, 2)
        self.spot = (n // 2, w // 2, 2 * row + lax.rem(n, 2))
        self.partner = self.device(self.spot, 1 - self.core)

    def device(self, spot, core):
        x, y, z = spot
        return (z // 2, ((x * 2 + lax.rem(z, 2)) * 4 + y) * 2 + core)

    def along(self, axis, k):
        to = list(self.spot)
        to[axis] = lax.rem(self.spot[axis] + k, 4)
        return self.device(to, self.core), to[axis]


class Reduce:
    def __init__(self, torus, u, send, recv):
        self.torus, self.u, self.send, self.recv = torus, u, send, recv
        self.box = {}

    def go(self, stage, p, k, src, dst, peer):
        cp = remote(src, dst, self.send.at[stage, p, k], self.recv.at[stage, p, k], peer)
        cp.start()
        self.box.setdefault((stage, p), []).append(cp)

    def got(self, stage, p):
        for cp in self.box[stage, p]:
            cp.wait_recv()

    def finish(self):
        for cps in self.box.values():
            for cp in cps:
                cp.wait_send()

    def exchange(self, src, came):
        u, core = self.u, self.torus.core
        for p in range(3):
            self.go(
                0, p, 0, src.at[pl.ds(48 * u * (1 - core) + 16 * u * p, 16 * u)],
                came.at[pl.ds(16 * u * p, 16 * u)], self.torus.partner,
            )

    def first(self, p, src, came, half, one):
        u = self.u
        self.got(0, p)

        def quarter(i, carry):
            at = pl.ds(16 * u * p + 4 * u * i, 4 * u)
            mine = src[pl.ds(48 * u * self.torus.core + 16 * u * p + 4 * u * i, 4 * u)]
            half[at] = (mine.astype(F32) + came[at].astype(F32)).astype(BF16)
            return carry

        lax.fori_loop(0, 4, quarter, 0)
        for k in range(1, 4):
            peer, at = self.torus.along(p, k)
            self.go(1, p, k, half.at[pl.ds(16 * u * p + 4 * u * at, 4 * u)], one.at[p, k - 1], peer)

    def second(self, p, half, one, gather, two):
        u = self.u
        self.got(1, p)
        mine = half[pl.ds(16 * u * p + 4 * u * self.torus.spot[p], 4 * u)]
        gather[p] = (mine.astype(F32) + sum(one[p, k].astype(F32) for k in range(3))).astype(BF16)
        for k in range(1, 4):
            peer, at = self.torus.along((p + 1) % 3, k)
            self.go(2, p, k, gather.at[p, pl.ds(u * at, u)], two.at[p, k - 1], peer)

    def third(self, p, gather, two, three):
        u = self.u
        self.got(2, p)
        c = self.torus.spot[(p + 2) % 3]
        mine = gather[p, pl.ds(u * self.torus.spot[(p + 1) % 3], u)]
        three[p, c] = (mine.astype(F32) + sum(two[p, k].astype(F32) for k in range(3))).astype(BF16)
        for k in range(1, 4):
            self.go(3, p, k, three.at[p, c], three.at[p, c], self.torus.along((p + 2) % 3, k)[0])

    def fourth(self, p, three, mid):
        u = self.u
        self.got(3, p)
        at = pl.ds(u * self.torus.spot[(p + 1) % 3], u)
        mid[p, at] = sum(three[p, k].astype(F32) for k in range(4)).astype(BF16)
        for k in range(1, 4):
            self.go(4, p, k, mid.at[p, at], mid.at[p, at], self.torus.along((p + 1) % 3, k)[0])

    def fifth(self, p, mid, out):
        u = self.u
        at = pl.ds(48 * u * self.torus.core + 16 * u * p + 4 * u * self.torus.spot[p], 4 * u)
        out[at] = mid[p]
        for k in range(1, 4):
            self.go(5, p, k, out.at[at], out.at[at], self.torus.along(p, k)[0])

    def sixth(self, p, out):
        u = self.u
        self.got(5, p)
        at = pl.ds(48 * u * self.torus.core + 16 * u * p, 16 * u)
        self.go(6, p, 0, out.at[at], out.at[at], self.torus.partner)


def units(count, *lead):
    return tuple(lead) + (count, 16, 256)


EARLY, LATE = 7, 2


W3 = 12 * TOK


class Spread:
    def __init__(self, row, n, w, send, recv):
        self.core = lax.rem(w, 2)
        self.y = w // 2
        self.own = self.core * 4 + self.y
        self.row, self.n = row, n
        self.partner = (row, 8 * n + 2 * self.y + 1 - self.core)
        self.send, self.recv = send, recv
        self.first, self.passed = {}, {}

    def chip(self, k):
        return (self.row, 8 * self.n + 2 * lax.rem(self.y + k, 4) + self.core)

    def start(self, part, ref):
        self.first[part], self.passed[part] = [], []
        for k in range(1, 4):
            cp = remote(ref(self.own), ref(self.own), self.send.at[part, k], self.recv.at[part, k],
                        self.chip(k))
            cp.start()
            self.first[part].append(cp)
        self.hand(part, ref, self.own, 4)

    def hand(self, part, ref, slot, k):
        cp = remote(ref(slot), ref(slot), self.send.at[part, k], self.recv.at[part, k], self.partner)
        cp.start()
        self.passed[part].append(cp)

    def forward(self, part, ref):
        for k in range(1, 4):
            self.first[part][k - 1].wait_recv()
            self.hand(part, ref, self.core * 4 + lax.rem(self.y + 4 - k, 4), 4 + k)

    def arrive(self, part):
        for cp in self.passed[part]:
            cp.wait_recv()

    def finish(self):
        for part in self.first:
            for cp in self.first[part] + self.passed[part]:
                cp.wait_send()


def turns(n):
    return (n + 2) // 2


def fill_masks(bias, starts_ref, n, w):
    turn = turns(n)

    def one(t, carry):
        sel = jnp.where(t >= turn, 1, 0)
        kc = jnp.where(t >= turn, t - turn, t)
        line = lax.broadcasted_iota(jnp.int32, (256, 1), 0)
        key = (2 * kc + line // TOK) * 1024 + w * TOK + lax.rem(line, TOK)
        col = lax.broadcasted_iota(jnp.int32, (1, 512), 1)
        octet = jnp.where(sel == 0, n, 7 - n)
        query = octet * 1024 + (2 * (col // TOK) + sel) * TOK + lax.rem(col, TOK)
        bias[t] = jnp.where((key >= starts_ref[sel]) & (key <= query), 0.0, MASKED)
        return carry

    lax.fori_loop(0, 5, one, 0)


def chunk_range(n, sel):
    turn = turns(n)
    return jnp.where(sel == 0, 0, turn), jnp.where(sel == 0, turn, 5 - turn)


def three_heads(ref, sel, g):
    return jnp.concatenate(
        [
            ref[4 * sel + y, HD * h : HD * h + HD, :]
            for h in range(3 * g, 3 * g + 3)
            for y in range(4)
        ],
        axis=1,
    )


def two_blocks(ref, kc, first):
    return jnp.concatenate([ref[2 * kc + i, first : first + HD, :] for i in range(2)], axis=1)


def by_chip(value, y):
    return jnp.concatenate(
        [value[:, 512 * j + TOK * y : 512 * j + TOK * y + TOK] for j in range(3)], axis=0
    )


class Context:
    pass


def attend_kernel(first, n_in, n_out, *refs):
    ins, refs = refs[:n_in], refs[n_in:]
    outs, refs = refs[:n_out], refs[n_out:]
    if first:
        part_ref, stat_ref, q_all, kv_all = refs[:4]
    else:
        q_all, kv_all, part_ref, stat_ref = refs[:4]
    (k_nat, bias, top, total, acc, o_send, o_recv, r_send, r_recv, o_y, s_y,
     qs, qr, ks, kr, ps, pr, ys, yr) = refs[4:23]
    starts_ref = outs[2] if first else ins[-1]
    row, seq, n, w = place()
    bar = greet(row, n, w)
    core, y = lax.rem(w, 2), w // 2
    own_k = octet_of(n, w)
    queries = Spread(row, n, w, qs, qr)
    ctx = Context()
    ctx.row, ctx.n, ctx.w, ctx.core = row, n, w, core
    ctx.q_own, ctx.kv_own = q_all.at[queries.own], kv_all.at[own_k]
    ctx.q_all, ctx.kv_all = q_all, kv_all
    ctx.ready = lambda: pl.semaphore_wait(bar, 14)
    if first:
        late, arrived, end = first_part(ctx, ins, outs, refs[23:])
    else:
        late, arrived, end = middle_part(ctx, ins[:-1], outs, refs[23:])

    def q_part(g):
        return lambda slot: q_all.at[slot, pl.ds(192 * g, 192)]

    keys = {}
    for g in range(3):
        keys[g] = []
        for k in range(1, 8):
            block = kv_all.at[own_k, pl.ds(TOK * g, TOK)]
            cp = remote(
                block, block, ks.at[g, k], kr.at[g, k], (row, 8 * lax.rem(n + k, 8) + w)
            )
            cp.start()
            keys[g].append(cp)
        queries.start(g, q_part(g))
    fill_masks(bias, starts_ref, n, w)
    queries.forward(0, q_part(0))

    def phase(g, sel):
        base, count = chunk_range(n, sel)
        top[...] = jnp.full(top.shape, LOWEST, F32)
        total[...] = jnp.zeros(total.shape, F32)
        acc[...] = jnp.zeros(acc.shape, F32)

        def step(kc, carry):
            scores = dot(k_nat[kc], three_heads(q_all, sel, g), 1, 0)
            mask = bias[base + kc]
            weights, shrinks = [], []
            for j in range(3):
                cols = slice(512 * j, 512 * j + 512)
                s = scores[:, cols] + mask
                old = top[:, cols]
                new = jnp.maximum(old, jnp.max(s, axis=0, keepdims=True))
                p = jnp.exp2((s - new) * EXP_SCALE)
                shrink = jnp.exp2((old - new) * EXP_SCALE)
                top[:, cols] = new
                total[:, cols] = total[:, cols] * shrink + jnp.sum(p, axis=0, keepdims=True)
                weights.append(p.astype(BF16))
                shrinks.append(shrink)
            values = two_blocks(kv_all, kc, TOK * g + HD)
            acc[...] = acc[...] * jnp.concatenate(shrinks, axis=1) + dot(
                values, jnp.concatenate(weights, axis=1), 1, 0
            )
            return carry

        lax.fori_loop(0, count, step, 0)

    pairs, flying = [], []
    for g in range(3):
        for cp in keys[g]:
            cp.wait_recv()
        for j in range(8):
            k_nat[j // 2, (j % 2) * TOK : (j % 2) * TOK + TOK, :] = jnp.transpose(
                kv_all[j, TOK * g : TOK * g + HD, :]
            )
        queries.arrive(g)
        if g == 2 and arrived is not None:
            arrived()
        phase(g, 1 - core)
        o_send[g] = acc[...].astype(BF16)
        r_send[g, 0] = top[...]
        r_send[g, 1] = total[...]
        both = [
            remote(o_send.at[g], o_recv.at[g], ps.at[0, g], pr.at[0, g], queries.partner),
            remote(r_send.at[g], r_recv.at[g], ps.at[1, g], pr.at[1, g], queries.partner),
        ]
        for cp in both:
            cp.start()
        pairs += both
        if g < 2:
            queries.forward(g + 1, q_part(g + 1))
        if g == 0 and late is not None:
            late()
        phase(g, core)
        for cp in both:
            cp.wait_recv()
        new = jnp.maximum(top[...], r_recv[g, 0])
        mine = jnp.exp2((top[...] - new) * EXP_SCALE)
        theirs = jnp.exp2((r_recv[g, 0] - new) * EXP_SCALE)
        length = total[...] * mine + r_recv[g, 1] * theirs
        out = (acc[...] * mine + o_recv[g].astype(F32) * theirs).astype(BF16)
        for i in range(4):
            o_y[g, i] = by_chip(out, i)
            for j in range(3):
                cols = slice(512 * j + TOK * i, 512 * j + TOK * i + TOK)
                s_y[g, i, j : j + 1, :] = new[:, cols]
                s_y[g, i, 4 + j : 5 + j, :] = length[:, cols]
        for k in range(1, 4):
            to = lax.rem(y + k, 4)
            peer = queries.chip(k)
            for cp in (
                remote(o_y.at[g, to], part_ref.at[y, pl.ds(192 * g, 192)], ys.at[0, g, k],
                       yr.at[0, g, k], peer),
                remote(s_y.at[g, to], stat_ref.at[y, pl.ds(8 * g, 8)], ys.at[1, g, k],
                       yr.at[1, g, k], peer),
            ):
                cp.start()
                flying.append(cp)
        part_ref[y, 192 * g : 192 * g + 192, :] = o_y[g, y]
        stat_ref[y, 8 * g : 8 * g + 8, :] = s_y[g, y]
    queries.finish()
    for g in range(3):
        for cp in keys[g]:
            cp.wait_send()
    for cp in pairs:
        cp.wait_send()
    for cp in flying:
        cp.wait()
    if end is not None:
        end()


GATHERED = [((8, D, TOK), BF16), ((8, 2 * KV, TOK), BF16)]


def attend(first, ins, specs, outs, scratch, collective, limit):
    count = len(outs)
    here = [] if first else [sds(*a) for a in GATHERED]
    there = [pltpu.VMEM(*a) for a in GATHERED] if first else []
    outs = outs + [(o, VM) for o in here + [sds((4, D, TOK), BF16), sds((4, 24, TOK), F32)]]
    return pl.pallas_call(
        functools.partial(attend_kernel, first, len(ins), count),
        name="attend_first" if first else "attend",
        out_shape=tuple(o for o, _ in outs),
        in_specs=specs,
        out_specs=tuple(spec for _, spec in outs),
        scratch_shapes=there
        + [
            pltpu.VMEM((4, 256, HD), BF16),
            pltpu.VMEM((5, 256, 512), F32),
            pltpu.VMEM((1, W3), F32),
            pltpu.VMEM((1, W3), F32),
            pltpu.VMEM((HD, W3), F32),
            pltpu.VMEM((3, HD, W3), BF16),
            pltpu.VMEM((3, HD, W3), BF16),
            pltpu.VMEM((3, 2, 1, W3), F32),
            pltpu.VMEM((3, 2, 1, W3), F32),
            pltpu.VMEM((3, 4, 192, TOK), BF16),
            pltpu.VMEM((3, 4, 8, TOK), F32),
            DMA((3, 8)), DMA((3, 8)), DMA((3, 8)), DMA((3, 8)),
            DMA((2, 3)), DMA((2, 3)), DMA((2, 3, 4)), DMA((2, 3, 4)),
        ]
        + scratch,
        compiler_params=params(collective, limit),
        cost_estimate=cost(30),
    )(*ins)


def attend_back_kernel(carry_sum, n_in, n_out, n_more, *refs):
    ins, refs = refs[:n_in], refs[n_in:]
    outs, refs = refs[:n_out], refs[n_out:]
    (dq_part, dkv_part, extra_out, do_all, st_all, k_nat, v_nat, bias, rows_s, dq, dkv, q_send,
     q_recv, q_y, kv_low, extra, qs, qr, ks, kr, ps, pr, ys, yr, es, er) = refs[:26]
    more, scratch = refs[26 : 26 + n_more], refs[26 + n_more :]
    q_all, kv_all, starts_ref = ins[-3:]
    ctx = Context()
    ctx.q_all, ctx.kv_all = q_all, kv_all
    row, seq, n, w = place()
    bar = greet(row, n, w)
    torus = Torus(row, n, w)
    if carry_sum:
        came, one, gather, two, three = more
        half = extra.at[pl.ds(48 * EARLY * lax.rem(w, 2), 48 * EARLY)]
        for k in range(1, 4):
            pl.semaphore_signal(bar, inc=1, device_id=torus.along(2, k)[0], device_id_type=MESH)
        early = Reduce(torus, EARLY, es, er)
    else:
        (extra_in,) = more
        move = remote(extra, extra_in, es, er, (row, 8 * (7 - n) + w))
    core, y = lax.rem(w, 2), w // 2
    own_k = octet_of(n, w)
    grads = Spread(row, n, w, qs, qr)
    ctx.do_own, ctx.st_own, ctx.extra = do_all.at[grads.own], st_all.at[grads.own], extra
    make = between_part if carry_sum else turn_part
    grads_of = make(ctx, ins[:-3], outs, scratch)
    pl.semaphore_wait(bar, 17 if carry_sum else 14)

    def part(g):
        return lambda slot: do_all.at[slot, pl.ds(192 * g, 192)]

    def stats(slot):
        return st_all.at[slot]

    grads.start(3, stats)
    for g in range(3):
        grads.start(g, part(g))
    fill_masks(bias, starts_ref, n, w)
    if carry_sum:
        grads_of()
        early.exchange(extra, came)
    grads.forward(3, stats)
    grads.forward(0, part(0))
    if carry_sum:
        for p in range(3):
            early.first(p, extra, came, half, one)
    if not carry_sum:

        @pl.when(core == 1)
        def _():
            move.start()

    def phase(g, sel):
        base, count = chunk_range(n, sel)
        dq[...] = jnp.zeros(dq.shape, F32)
        for i, first in enumerate((0, 16)):
            for j in range(3):
                for c in range(4):
                    at = 512 * j + TOK * c
                    line = first + 3 * g + j
                    rows_s[i, :, at : at + TOK] = st_all[4 * sel + c, line : line + 1, :]

        def step(kc, carry):
            qt = three_heads(q_all, sel, g)
            dt = three_heads(do_all, sel, g)
            scores = dot(k_nat[kc], qt, 1, 0)
            dp = dot(v_nat[kc], dt, 1, 0)
            mask = bias[base + kc]
            ps_, ds_ = [], []
            for j in range(3):
                cols = slice(512 * j, 512 * j + 512)
                p = jnp.exp2((scores[:, cols] + mask - rows_s[0, :, cols]) * EXP_SCALE)
                ds_.append((p * (dp[:, cols] - rows_s[1, :, cols])).astype(BF16))
                ps_.append(p.astype(BF16))
            p = jnp.concatenate(ps_, axis=1)
            ds = jnp.concatenate(ds_, axis=1)
            dkv[kc, 0:HD, :] += dot(ds, qt, 1, 1).T
            dkv[kc, HD:, :] += dot(p, dt, 1, 1).T
            dq[...] += dot(two_blocks(kv_all, kc, TOK * g), ds, 1, 0)
            return carry

        lax.fori_loop(0, count, step, 0)

    pairs, flying = [], []
    for g in range(3):
        dkv[...] = jnp.zeros(dkv.shape, F32)
        for j in range(8):
            at = slice((j % 2) * TOK, (j % 2) * TOK + TOK)
            k_nat[j // 2, at, :] = jnp.transpose(kv_all[j, TOK * g : TOK * g + HD, :])
            v_nat[j // 2, at, :] = jnp.transpose(kv_all[j, TOK * g + HD : TOK * g + TOK, :])
        if g == 0:
            grads.arrive(3)
        grads.arrive(g)
        phase(g, 1 - core)
        q_send[g] = (dq[...] * SCALE).astype(BF16)
        pair = remote(q_send.at[g], q_recv.at[g], ps.at[g], pr.at[g], grads.partner)
        pair.start()
        pairs.append(pair)
        if g < 2:
            grads.forward(g + 1, part(g + 1))
        elif carry_sum:
            for p in range(3):
                early.third(p, gather, two, three)
        phase(g, core)
        for j in range(8):
            cols = slice((j % 2) * TOK, (j % 2) * TOK + TOK)
            kv_low[g, j, 0:HD, :] = (dkv[j // 2, 0:HD, cols] * SCALE).astype(BF16)
            kv_low[g, j, HD:, :] = dkv[j // 2, HD:, cols].astype(BF16)
        for k in range(1, 8):
            to = lax.rem(n + k, 8)
            cp = remote(
                kv_low.at[g, octet_of(to, w)], dkv_part.at[n, pl.ds(TOK * g, TOK)], ks.at[g, k],
                kr.at[g, k], (row, 8 * to + w),
            )
            cp.start()
            flying.append(cp)
        pair.wait_recv()
        out = (dq[...] * SCALE + q_recv[g].astype(F32)).astype(BF16)
        for i in range(4):
            q_y[g, i] = by_chip(out, i)
        for k in range(1, 4):
            to = lax.rem(y + k, 4)
            cp = remote(q_y.at[g, to], dq_part.at[y, pl.ds(192 * g, 192)], ys.at[g, k], yr.at[g, k],
                        grads.chip(k))
            cp.start()
            flying.append(cp)
        dkv_part[n, TOK * g : TOK * g + TOK, :] = kv_low[g, own_k]
        dq_part[y, 192 * g : 192 * g + 192, :] = q_y[g, y]
        if carry_sum:
            for p in range(3):
                if g == 1:
                    early.second(p, half, one, gather, two)
                elif g == 2:
                    early.fourth(p, three, extra_out)
    grads.finish()
    for cp in pairs:
        cp.wait_send()
    for cp in flying:
        cp.wait()
    if carry_sum:
        for p in range(3):
            early.got(4, p)
        early.finish()
    else:

        @pl.when(core == 1)
        def _():
            move.wait()
            extra_out[...] = extra_in[...]

        @pl.when(core == 0)
        def _():
            extra_out[...] = extra[...]


def attend_back(carry_sum, ins, specs, outs, scratch, limit):
    if carry_sum:
        u = EARLY
        extra_shape = sds(units(4 * u, 3), BF16)
        extra = pltpu.VMEM(units(96 * u), BF16)
        sems = [DMA((5, 3, 4))] * 2
        more = [
            pltpu.VMEM(shape, BF16)
            for shape in (
                units(48 * u), units(4 * u, 3, 3), units(4 * u, 3), units(u, 3, 3), units(u, 3, 4),
            )
        ]
    else:
        extra_shape = X_T
        extra = pltpu.VMEM((D, TOK), F32)
        sems = [DMA, DMA]
        more = [pltpu.VMEM((D, TOK), F32)]
    return pl.pallas_call(
        functools.partial(attend_back_kernel, carry_sum, len(ins), len(outs), len(more)),
        name="attend_back_sum" if carry_sum else "attend_back",
        out_shape=tuple(outs + [sds((4, D, TOK), BF16), sds((8, 2 * KV, TOK), BF16), extra_shape]),
        in_specs=specs,
        out_specs=(VM,) * (len(outs) + 3),
        scratch_shapes=[
            pltpu.VMEM((8, D, TOK), BF16),
            pltpu.VMEM((8, 32, TOK), F32),
            pltpu.VMEM((4, 256, HD), BF16),
            pltpu.VMEM((4, 256, HD), BF16),
            pltpu.VMEM((5, 256, 512), F32),
            pltpu.VMEM((2, 1, W3), F32),
            pltpu.VMEM((HD, W3), F32),
            pltpu.VMEM((4, TOK, 256), F32),
            pltpu.VMEM((3, HD, W3), BF16),
            pltpu.VMEM((3, HD, W3), BF16),
            pltpu.VMEM((3, 4, 192, TOK), BF16),
            pltpu.VMEM((3, 8, TOK, TOK), BF16),
            extra,
            DMA((4, 8)), DMA((4, 8)), DMA((3, 8)), DMA((3, 8)),
            DMA((3,)), DMA((3,)), DMA((3, 4)), DMA((3, 4)),
        ]
        + sems
        + more
        + scratch,
        compiler_params=params(5 if carry_sum else 3, limit),
        cost_estimate=cost(40),
    )(*ins)


def both_rows(a, b):
    return jnp.concatenate([a[...], b[...]], axis=0)


def as_units(value):
    return value.astype(BF16).reshape(units(value.shape[0] // 16))


def early_grads(oa, ob, daa, dab, h2a, h2b, dga, dgb, dua, dub, hida, hidb, gma, gmb, g_out):
    ot = jnp.concatenate([oa[...], ob[...]], axis=1)
    h2t = both_rows(h2a, h2b).T
    gmt = both_rows(gma, gmb).T
    for i in range(6):
        cols = slice(256 * i, 256 * i + 256)
        for t, (lhs, a, b) in enumerate(((h2t, dga, dgb), (h2t, dua, dub), (gmt, hida, hidb))):
            rhs = jnp.concatenate([a[:, cols], b[:, cols]], axis=0)
            g_out[36 * (6 * t + i) : 36 * (6 * t + i) + 36] = as_units(dot(lhs, rhs, 1, 0))
    da = both_rows(daa[:, 128:384], dab[:, 128:384])
    g_out[648:672] = as_units(dot(ot[0:384], da, 1, 0))


def late_grads(h1a, h1b, dqa, dqb, oa, ob, daa, dab, g_out):
    h1t = both_rows(h1a, h1b).T
    ot = jnp.concatenate([oa[...], ob[...]], axis=1)
    dat = both_rows(daa, dab).T

    def rows(first, last):
        return jnp.concatenate([dqa[first:last, :], dqb[first:last, :]], axis=1)

    g_out[0:36] = as_units(dot(h1t, rows(0, 256), 1, 1))
    g_out[36:72] = as_units(dot(h1t, rows(256, 512), 1, 1))
    mixed = [dot(h1t, rows(512, 640), 1, 1), dot(ot, dat[0:128], 1, 1)]
    g_out[72:108] = as_units(jnp.concatenate(mixed, axis=1))
    g_out[108:120] = as_units(dot(ot[384:576], dat[128:384], 1, 1))
    low = jnp.concatenate([dat[384:576], jnp.zeros((64, 256), BF16)], axis=0)
    high = jnp.concatenate([jnp.zeros((192, 256), BF16), rows(640, 704)], axis=0)
    g_out[120:156] = as_units(dot(ot, low, 1, 1) + dot(h1t, high, 1, 1))
    g_out[156:192] = as_units(dot(h1t, rows(704, 960), 1, 1))


def spread_kernel(
    early, late, x_in, g_in, x_out, g_out, gate_out, up_out, down_out, q_out, k_out, v_out, o_out, big, small, kt, vt, sems
):
    def block(ref, first, count=36):
        return ref[first : first + count].reshape(16 * count, 256).astype(F32)

    cps = [
        pltpu.make_async_copy(x_in, x_out, sems.at[22]),
        pltpu.make_async_copy(g_in, g_out, sems.at[23]),
    ]
    for cp in cps:
        cp.start()
    for t, ref in enumerate((gate_out, up_out, down_out)):
        for i in range(6):
            cols = pl.ds(256 * i, 256)
            big[t, :, cols] = block(early, 36 * (6 * t + i))
            cp = pltpu.make_async_copy(big.at[t, :, cols], ref.at[:, cols], sems.at[6 * t + i])
            cp.start()
            cps.append(cp)
    small[0, :, 0:256] = block(late, 0)
    small[0, :, 256:512] = block(late, 36)
    mixed = block(late, 72)
    small[0, :, 512:576] = mixed[:, 0:64]
    small[1, :, 0:128] = mixed[:, 128:256]
    kt[0:64, :] = mixed[:, 0:128].T[64:128]
    small[1, 0:384, 128:384] = block(early, 648, 24)
    small[1, 384:576, 128:384] = block(late, 108, 12)
    mixed = block(late, 120)
    small[1, :, 384:576] = mixed[:, 0:192]
    kt[64:128, :] = mixed[:, 128:256].T[64:128]
    last = block(late, 156).T
    kt[128:192, :] = last[0:64]
    vt[...] = last[64:256]
    for i, (src, dst) in enumerate(
        ((small.at[0], q_out), (small.at[1], o_out), (kt, k_out), (vt, v_out))
    ):
        cp = pltpu.make_async_copy(src, dst, sems.at[18 + i])
        cp.start()
        cps.append(cp)
    for cp in cps:
        cp.wait()


def spread(*ins):
    return pl.pallas_call(
        spread_kernel,
        name="spread",
        out_shape=(
            X_T, X_T, sds((D, FF), F32), sds((D, FF), F32), sds((D, FF), F32), sds((D, D), F32),
            sds((KV, D), F32), sds((KV, D), F32), sds((D, D), F32),
        ),
        in_specs=[VM] * 4,
        out_specs=(ANY,) * 9,
        scratch_shapes=[
            pltpu.VMEM((3, D, FF), F32),
            pltpu.VMEM((2, D, D), F32),
            pltpu.VMEM((KV, D), F32),
            pltpu.VMEM((KV, D), F32),
            DMA((24,)),
        ],
        compiler_params=params(None, 30 << 20),
    )(*ins)


def reduce_kernel(
    mid_ref, dq, dkv, x, dx1, ga, wq, wk, wv, cos, sin, h10, h11, dqkv1, ob0, ob1, da0, da1,
    gga1, ggm0, ggm1, early_out, late_out, gain_out, fin_out,
    late_ref, came, half, one, gather, two, three, mid, gain_in, gain_sum, fin_ref, fin_in, dqkv0,
    s_e, r_e, s_l, r_l, gs, gr, fs, fr
):
    row, seq, n, w = place()
    torus = Torus(row, n, w)
    core = torus.core
    bar = pltpu.get_barrier_semaphore()
    pl.semaphore_signal(bar, inc=1, device_id=torus.partner, device_id_type=MESH)
    for axis in range(3):
        for k in range(1, 4):
            pl.semaphore_signal(bar, inc=1, device_id=torus.along(axis, k)[0], device_id_type=MESH)
    mirror = (row, 8 * (7 - n) + w)
    g, gga0 = project_back(
        dq, dkv, x[...], dx1[...], as_row(ga), wq, wk, wv, cos[...], sin[...], dqkv0
    )
    fin_ref[...] = g.T
    gain_sum[0] = jnp.concatenate(
        [gga0 + gga1[...], ggm0[...] + ggm1[...], jnp.zeros((6, D), F32)], axis=0
    )

    @pl.when(core == 1)
    def _():
        pl.semaphore_signal(bar, inc=1, device_id=mirror, device_id_type=MESH)
        pl.semaphore_wait(bar, 11)

    @pl.when(core == 0)
    def _():
        pl.semaphore_wait(bar, 10)

    early = Reduce(torus, EARLY, s_e, r_e)
    late = Reduce(torus, LATE, s_l, r_l)
    for p in range(3):
        early.fifth(p, mid_ref, early_out)
    late_grads(h10, h11, dqkv0, dqkv1, ob0, ob1, da0, da1, late_ref)
    late.exchange(late_ref, came)
    move = remote(fin_ref, fin_in, fs, fr, mirror)

    @pl.when(core == 1)
    def _():
        move.start()

    gains = []

    def gain_round(i, peers, count, at):
        gain_in[i, at] = gain_sum[i]
        for k, peer in enumerate(peers):
            cp = remote(gain_sum.at[i], gain_in.at[i, at], gs.at[i, k], gr.at[i, k], peer)
            cp.start()
            gains.append(cp)

    def gain_total(i, peers, count):
        for cp in gains[-peers:]:
            cp.wait_recv()
        return sum(gain_in[i, j] for j in range(count))

    def axis_peers(axis):
        return [torus.along(axis, k)[0] for k in range(1, 4)]

    gain_round(0, [torus.partner], 2, core)
    for p in range(3):
        late.first(p, late_ref, came, half, one)
    gain_sum[1] = gain_total(0, 1, 2)
    gain_round(1, axis_peers(0), 4, torus.spot[0])
    for p in range(3):
        late.second(p, half, one, gather, two)
    for p in range(3):
        early.sixth(p, early_out)
    gain_sum[2] = gain_total(1, 3, 4)
    gain_round(2, axis_peers(1), 4, torus.spot[1])
    for p in range(3):
        late.third(p, gather, two, three)
    gain_sum[3] = gain_total(2, 3, 4)
    gain_round(3, axis_peers(2), 4, torus.spot[2])
    for p in range(3):
        late.fourth(p, three, mid)
    gain_out[...] = gain_total(3, 3, 4)
    for p in range(3):
        late.got(4, p)
        late.fifth(p, mid, late_out)
    for p in range(3):
        late.sixth(p, late_out)

    @pl.when(core == 1)
    def _():
        move.wait()
        fin_out[...] = fin_in[...]

    @pl.when(core == 0)
    def _():
        fin_out[...] = fin_ref[...]

    for cp in gains:
        cp.wait_send()
    for p in range(3):
        early.got(6, p)
        late.got(6, p)
    early.finish()
    late.finish()


def reduce_all(*ins):
    u = LATE
    return pl.pallas_call(
        reduce_kernel,
        name="reduce_all",
        out_shape=(
            sds(units(96 * EARLY), BF16), sds(units(96 * LATE), BF16), sds((8, D), F32), X_T
        ),
        in_specs=[VM] * len(ins),
        out_specs=(VM,) * 4,
        scratch_shapes=[
            pltpu.VMEM(shape, BF16)
            for shape in (
                units(96 * u), units(48 * u), units(48 * u), units(4 * u, 3, 3), units(4 * u, 3), units(u, 3, 3),
                units(u, 3, 4), units(4 * u, 3),
            )
        ]
        + [
            pltpu.VMEM((4, 4, 8, D), F32),
            pltpu.VMEM((4, 8, D), F32),
            pltpu.VMEM((D, TOK), F32),
            pltpu.VMEM((D, TOK), F32),
            pltpu.VMEM((960, TOK), BF16),
        ]
        + [DMA((7, 3, 4))] * 4
        + [DMA((4, 4)), DMA((4, 4)), DMA, DMA],
        compiler_params=params(4, 24 << 20),
        cost_estimate=cost(40),
    )(*ins)


def on_device(
    tokens, cotangent, segment_ids, gain_attn, wq, wk, wv, wo, gain_mlp, wg, wu, wd
):
    ga, gm = gain_attn, gain_mlp
    wk, wv, wd = wk.T, wv.T, wd.T
    w_q, w_k, w_v = sds((D, D), BF16), sds((KV, D), BF16), sds((KV, D), BF16)
    table = sds((32, TOK), F32)
    x0, h10, starts, cos, sin, qa0, kva0, part, stat = attend(
        True,
        [tokens[0].T, segment_ids, ga, wq, wk, wv],
        [HBM, HBM, VM, HBM, HBM, HBM],
        [(o, VM) for o in (X_S, H_S, sds((2, 1, 4 * TOK), jnp.int32), table, table)]
        + [(sds(*a), HBM) for a in GATHERED],
        [
            pltpu.VMEM((D, TOK), F32),
            pltpu.VMEM((64, 1, TOK), jnp.int32),
            pltpu.VMEM((64, 1, TOK), jnp.int32),
        ]
        + [DMA((8,))] * 4
        + [DMA((2,)), DMA]
        + buffers(w_q, w_k, w_v)
        + [DMA((3,))],
        1,
        20 << 20,
    )
    cot, h11, x1, m0, h20, inv0, gate0, up0, hid0, o0, lse0, qa1, kva1, part, stat = attend(
        False,
        [part, stat, x0, cotangent[0].T, ga, wq, wk, wv, wo, gm, wg, wu, wd, cos, sin, starts],
        [VM] * 16,
        [(o, VM) for o in (X_S, H_S, X_S, X_S, H_S, sds((TOK, TOK), F32))]
        + [(F_S, HBM), (F_S, HBM)]
        + [(o, VM) for o in (FB_S, sds((D, TOK), F32), sds((16, TOK), F32))],
        [pltpu.VMEM((TOK, FF), F32), pltpu.VMEM((TOK, FF), F32), DMA((2,)), pltpu.VMEM((D, TOK), F32),
         DMA((2,)), DMA],
        2,
        20 << 20,
    )
    h21, hid1, ob1, gm1, dg1, du1, da1, dx1, ggm1, dq, dkv, output = attend_back(
        False,
        [part, stat, x1, cot, wo, gm, wg, wu, wd, qa1, kva1, starts],
        [VM] * 12,
        [H_S, FB_S, Q_T, H_S, FB_S, FB_S, H_S, X_S, G_S],
        [pltpu.VMEM((D, TOK), F32), pltpu.VMEM((16, TOK), F32)],
        20 << 20,
    )
    dqkv1, gga1, da0, dx0, ggm0, ob0, dq, dkv, mid = attend_back(
        True,
        [dq, dkv, x1, dx1, ga, wq, wk, wv, cos, sin, m0, inv0, gate0, up0, wo, gm, wg, wu, wd, o0,
         lse0, ob1, da1, h20, h21, dg1, du1, hid0, hid1, gm1, qa0, kva0, starts],
        [VM] * 33,
        [sds((960, TOK), BF16), G_S, H_S, X_S, G_S, Q_T],
        [pltpu.VMEM((TOK, D), BF16), pltpu.VMEM((TOK, FF), BF16), pltpu.VMEM((TOK, FF), BF16)],
        28 << 20,
    )
    early, late, gains, grad_tokens = reduce_all(
        mid, dq, dkv, x0, dx0, ga, wq, wk, wv, cos, sin, h10, h11, dqkv1, ob0, ob1, da0, da1, gga1,
        ggm0, ggm1
    )
    output, grad_tokens, gate, up, down, query, key, value, out = spread(
        early, late, output, grad_tokens
    )
    return (
        output.T[None], grad_tokens.T[None], gains[0], query, key.T, value.T, out, gains[1], gate, up,
        down.T,
    )


def solution(mesh):
    rows = P("rows", "seq", None)
    in_specs = (rows, rows, P("rows", "seq")) + (P(),) * 9
    out_specs = (rows, rows) + (P(),) * 9
    return jax.shard_map(
        on_device, mesh=mesh, in_specs=in_specs, out_specs=out_specs, check_vma=False
    )
```

```python
import functools
import math

import jax
import jax.numpy as jnp
from jax import lax
from jax.experimental import pallas as pl
from jax.experimental.pallas import tpu as pltpu
from jax.sharding import PartitionSpec as P

F32 = jnp.float32
BF16 = jnp.bfloat16
MESH = pl.DeviceIdType.MESH

D = 576
HEADS = 9
HD = 64
KV = 192
FF = 1536
TOK = 128
DOCS = 16
EPS = 1e-05
SCALE = 0.125
EXP_SCALE = SCALE * 1.4426950408889634
MASKED = -1e30
LOWEST = -1e20

VM = pl.BlockSpec(memory_space=pltpu.VMEM)
DMA = pltpu.SemaphoreType.DMA


def dot(a, b, ca, cb):
    return lax.dot_general(a, b, (((ca,), (cb,)), ((), ())), preferred_element_type=F32)


def sds(shape, dtype):
    return jax.ShapeDtypeStruct(shape, dtype)


def params(collective=None, limit=50 << 20):
    if collective is None:
        return pltpu.CompilerParams(vmem_limit_bytes=limit)
    return pltpu.CompilerParams(
        vmem_limit_bytes=limit, collective_id=collective, has_side_effects=True
    )


def cost(us):
    return pl.CostEstimate(flops=us * 1000000000, bytes_accessed=us * 1000000, transcendentals=0)


def place():
    seq = lax.axis_index("seq")
    row = lax.axis_index("rows")
    return row, seq, seq // 8, lax.rem(seq, 8)


def slot_of(w):
    return lax.rem(w, 2) * 4 + w // 2


def octet_of(n, w):
    return jnp.where(lax.rem(w, 2) == 0, n, 7 - n)


def greet(row, n, w):
    bar = pltpu.get_barrier_semaphore()
    for k in range(1, 8):
        pl.semaphore_signal(
            bar, inc=1, device_id=(row, 8 * n + lax.rem(w + k, 8)), device_id_type=MESH
        )
        pl.semaphore_signal(
            bar, inc=1, device_id=(row, 8 * lax.rem(n + k, 8) + w), device_id_type=MESH
        )
    return bar


def remote(src, dst, send, recv, target):
    return pltpu.make_async_remote_copy(
        src_ref=src,
        dst_ref=dst,
        send_sem=send,
        recv_sem=recv,
        device_id=target,
        device_id_type=MESH,
    )


def as_row(ref):
    return ref[...].reshape(1, D)


def norm_in(x, gain):
    inverse = lax.rsqrt(jnp.mean(x * x, axis=-1, keepdims=True) + EPS)
    return (x * inverse * gain).astype(BF16), inverse


def norm_back(x, inverse, gain, grad):
    scaled = grad * gain
    grad_gain = jnp.sum(grad * (x * inverse), axis=0, keepdims=True)
    inner = jnp.mean(scaled * x, axis=-1, keepdims=True)
    return inverse * scaled - x * (inverse * inverse * inverse) * inner, grad_gain


def project(x, gain, wq, wk, wv, h_out):
    h, _ = norm_in(x, gain)
    h_out[...] = h
    return dot(h, wq[...], 1, 0).T, dot(wk[...], h, 1, 1), dot(wv[...], h, 1, 1).astype(BF16)


def rotate(qt, kt, vt, cos, sin, q_out, kv_out):
    for i in range(HEADS):
        a = qt[HD * i : HD * i + 32]
        b = qt[HD * i + 32 : HD * i + 64]
        q_out[HD * i : HD * i + 32, :] = (a * cos - b * sin).astype(BF16)
        q_out[HD * i + 32 : HD * i + 64, :] = (b * cos + a * sin).astype(BF16)
    for i in range(3):
        a = kt[HD * i : HD * i + 32]
        b = kt[HD * i + 32 : HD * i + 64]
        kv_out[TOK * i : TOK * i + 32, :] = (a * cos - b * sin).astype(BF16)
        kv_out[TOK * i + 32 : TOK * i + 64, :] = (b * cos + a * sin).astype(BF16)
        kv_out[TOK * i + 64 : TOK * i + 128, :] = vt[HD * i : HD * i + 64]


def combine(part, stat, o_out, lse_out):
    for g in range(3):
        tops = [stat[i, 8 * g : 8 * g + 3, :] for i in range(4)]
        top = functools.reduce(jnp.maximum, tops)
        factors = [jnp.exp2((t - top) * EXP_SCALE) for t in tops]
        total = sum(f * stat[i, 8 * g + 4 : 8 * g + 7, :] for i, f in enumerate(factors))
        inverse = 1.0 / total
        factors = [f * inverse for f in factors]
        lse_out[3 * g : 3 * g + 3, :] = top + jnp.log2(total) * (1.0 / EXP_SCALE)
        for j in range(3):
            rows = slice(192 * g + HD * j, 192 * g + HD * j + HD)
            o_out[rows, :] = sum(
                part[i, rows, :].astype(F32) * factors[i][j : j + 1, :] for i in range(4)
            )


def feed_forward(x, o_t, wo, gain, wg, wu, wd):
    x1 = x + dot(o_t, wo[...], 0, 0)
    h2, inverse = norm_in(x1, gain)
    gate = dot(h2, wg[...], 1, 0)
    up = dot(h2, wu[...], 1, 0)
    hid = (gate * jax.nn.sigmoid(gate) * up).astype(BF16)
    return x1, h2, inverse, gate, up, hid, x1 + dot(hid, wd[...], 1, 1)


def feed_back(g, x1, inverse, gate, up, wo, gain, wg, wu, wd, o_ref, lse,
              do_out, stat_out, gm_out, dgate_out, dup_out, da_out):
    gm = g.astype(BF16)
    gm_out[...] = gm
    dhid = dot(gm, wd[...], 1, 0)
    sg = jax.nn.sigmoid(gate)
    dgate = (dhid * up * sg * (1.0 + gate * (1.0 - sg))).astype(BF16)
    dup = (dhid * gate * sg).astype(BF16)
    dgate_out[...] = dgate
    dup_out[...] = dup
    dh2 = dot(dgate, wg[...], 1, 1) + dot(dup, wu[...], 1, 1)
    dy, grad_gain = norm_back(x1, inverse, gain, dh2)
    dx1 = g + dy
    da = dx1.astype(BF16)
    da_out[...] = da
    do_t = dot(wo[...], da, 1, 1).astype(BF16)
    do_out[...] = do_t
    stat_out[...] = jnp.zeros(stat_out.shape, F32)
    stat_out[0:HEADS, :] = lse
    for h in range(HEADS):
        rows = slice(HD * h, HD * h + HD)
        stat_out[16 + h : 17 + h, :] = jnp.sum(
            do_t[rows].astype(F32) * o_ref[rows, :], axis=0, keepdims=True
        )
    return dx1, grad_gain


def project_back(dq_part, dkv_part, x, dx1, gain, wq, wk, wv, cos, sin, dqkv_out):
    for h in range(HEADS + 3):
        part, base, many = (dq_part, HD * h, 4) if h < HEADS else (dkv_part, TOK * (h - HEADS), 8)
        a = sum(part[i, base : base + 32, :].astype(F32) for i in range(many))
        b = sum(part[i, base + 32 : base + 64, :].astype(F32) for i in range(many))
        dqkv_out[HD * h : HD * h + 32, :] = (a * cos + b * sin).astype(BF16)
        dqkv_out[HD * h + 32 : HD * h + 64, :] = (b * cos - a * sin).astype(BF16)
    for g in range(3):
        base = TOK * g + HD
        dqkv_out[D + KV + HD * g : D + KV + HD * g + HD, :] = sum(
            dkv_part[i, base : base + HD, :].astype(F32) for i in range(8)
        ).astype(BF16)
    dh1 = (
        dot(dqkv_out[0:D, :], wq[...], 0, 1)
        + dot(dqkv_out[D : D + KV, :], wk[...], 0, 0)
        + dot(dqkv_out[D + KV :, :], wv[...], 0, 0)
    )
    inverse = lax.rsqrt(jnp.mean(x * x, axis=-1, keepdims=True) + EPS)
    dy, grad_gain = norm_back(x, inverse, gain, dh1)
    return dx1 + dy, grad_gain


Q_T = sds((D, TOK), BF16)
KV_T = sds((2 * KV, TOK), BF16)
H_S = sds((TOK, D), BF16)
X_S = sds((TOK, D), F32)
X_T = sds((D, TOK), F32)
F_S = sds((TOK, FF), F32)
FB_S = sds((TOK, FF), BF16)
ST_S = sds((32, TOK), F32)
G_S = sds((1, D), F32)


ANY = pl.BlockSpec(memory_space=pl.ANY)
HBM = pl.BlockSpec(memory_space=pltpu.HBM)


class Lazy:
    def __init__(self, src, buf, sem):
        self.copy = pltpu.make_async_copy(src, buf, sem)
        self.copy.start()
        self.buf, self.waited = buf, False

    def ref(self):
        if not self.waited:
            self.copy.wait()
            self.waited = True
        return self.buf

    def __getitem__(self, index):
        return self.ref()[index]


def fetch(srcs, bufs, sems):
    return [Lazy(src, buf, sems.at[i]) for i, (src, buf) in enumerate(zip(srcs, bufs))]


def buffers(*arrays):
    return [pltpu.VMEM(a.shape, a.dtype) for a in arrays] + [DMA((len(arrays),))]


def begin_kernel(out):
    out[...] = jnp.zeros(out.shape, F32)


def begin():
    return pl.pallas_call(
        begin_kernel,
        name="begin",
        out_shape=sds((8, TOK), F32),
        out_specs=VM,
        compiler_params=params(None, 1 << 20),
        cost_estimate=cost(30),
    )()


def mirrored(ctx, src, dst, send, recv):
    move = remote(src, dst, send.at[0], recv, (ctx.row, 8 * (7 - ctx.n) + ctx.w))
    stay = pltpu.make_async_copy(src, dst, send.at[1])

    def both(if_one, if_zero):
        pl.when(ctx.core == 1)(if_one)
        pl.when(ctx.core == 0)(if_zero)

    return lambda: both(move.start, stay.start), lambda: both(move.wait, stay.wait)


def first_part(ctx, ins, outs, scratch):
    tok, ids_ref, ga, wq, wk, wv, _ = ins
    x_out, h_out, starts_ref, cos_ref, sin_ref, q_save, kv_save = outs
    (tok_in, ids_all, starts_all, ysend, yrecv, xsend, xrecv, tsend, trecv,
     bq, bk, bv, bsem, ssem) = scratch
    row, n, w = ctx.row, ctx.n, ctx.w
    seq = 8 * n + w
    get_ids = pltpu.make_async_copy(ids_ref, ids_all.at[seq], ssem.at[0])
    get_ids.start()
    wq, wk, wv = fetch([wq, wk, wv], [bq, bk, bv], bsem)
    get_ids.wait()
    ctx.ready()
    start, wait = mirrored(ctx, tok, tok_in, tsend, trecv)
    start()
    sent = []
    for k in range(1, 8):
        cp = remote(
            ids_all.at[seq], ids_all.at[seq], ysend.at[k], yrecv.at[k],
            (row, 8 * n + lax.rem(w + k, 8)),
        )
        cp.start()
        sent.append(cp)
    for cp in sent:
        cp.wait()
    own = ids_all.at[pl.ds(8 * n, 8)]
    sent = []
    for k in range(1, 8):
        cp = remote(own, own, xsend.at[k], xrecv.at[k], (row, 8 * lax.rem(n + k, 8) + w))
        cp.start()
        sent.append(cp)
    wait()
    x = tok_in[...].T
    x_out[...] = x
    raw = project(x, as_row(ga), wq, wk, wv, h_out)
    for cp in sent:
        cp.wait()

    ids = jnp.concatenate([ids_all[i] for i in range(64)], axis=0)
    total = jnp.zeros((64, TOK), jnp.int32)
    for doc in range(DOCS - 1):
        count = jnp.where(ids == doc, 1.0, 0.0)
        count = jnp.sum(jnp.sum(count, axis=0, keepdims=True), axis=1, keepdims=True)
        total = total + jnp.where(ids > doc, count.astype(jnp.int32), 0)
    starts_all[...] = total[:, None, :]
    for half in range(2):
        octet = n if half == 0 else 7 - n
        for y in range(4):
            starts_ref[half, :, TOK * y : TOK * y + TOK] = starts_all[8 * octet + 2 * y + half]
    mine = 8 * octet_of(n, w) + w
    pos = mine * TOK + lax.broadcasted_iota(jnp.int32, (1, TOK), 1) - starts_all[mine]
    line = lax.broadcasted_iota(jnp.int32, (32, TOK), 0).astype(F32)
    angle = jnp.exp(line * (-2.0 / HD) * math.log(10000.0)) * pos.astype(F32)
    cos_ref[...] = jnp.cos(angle)
    sin_ref[...] = jnp.sin(angle)
    rotate(*raw, cos_ref[...], sin_ref[...], ctx.q_own, ctx.kv_own)

    saves = [
        pltpu.make_async_copy(ctx.q_all, q_save, ssem.at[1]),
        pltpu.make_async_copy(ctx.kv_all, kv_save, ssem.at[2]),
    ]

    def arrived():
        for cp in saves:
            cp.start()

    def end():
        for cp in saves:
            cp.wait()

    return None, arrived, end


def middle_part(ctx, ins, outs, scratch):
    part, stat, x, cot, ga, wq, wk, wv, wo, gm, wg, wu, wd, cos, sin = ins
    g_out, h_out, x_out, x1_out, h2_out, inv_out, gate_out, up_out, hid_out, o_out, lse_out = outs
    gate_s, up_s, ssem, cot_in, csend, crecv = scratch
    start, wait = mirrored(ctx, cot, cot_in, csend, crecv)
    saves = [
        pltpu.make_async_copy(gate_s, gate_out, ssem.at[0]),
        pltpu.make_async_copy(up_s, up_out, ssem.at[1]),
    ]
    combine(part, stat, o_out, lse_out)
    x1, h2, inverse, gate, up, hid, x2 = feed_forward(
        x[...], o_out[...].astype(BF16), wo, as_row(gm), wg, wu, wd
    )
    x_out[...] = x2
    raw = project(x2, as_row(ga), wq, wk, wv, h_out)
    rotate(*raw, cos[...], sin[...], ctx.q_own, ctx.kv_own)
    ctx.ready()

    def late():
        x1_out[...] = x1
        h2_out[...] = h2
        inv_out[...] = jnp.broadcast_to(inverse, inv_out.shape)
        gate_s[...] = gate
        up_s[...] = up
        hid_out[...] = hid
        for cp in saves:
            cp.start()
        start()

    def end():
        for cp in saves:
            cp.wait()
        wait()
        g_out[...] = cot_in[...].T

    return late, None, end


def turn_part(ctx, ins, outs, scratch):
    part, stat, x, g, wo, gm, wg, wu, wd = ins
    h2_out, hid_out, ob_out, gmo, dgate, dup, da, dx1_out, gg_out = outs
    o_s, lse_s = scratch
    combine(part, stat, o_s, lse_s)
    ob = o_s[...].astype(BF16)
    ob_out[...] = ob
    x1, h2, inverse, gate, up, hid, x2 = feed_forward(
        x[...], ob, wo, as_row(gm), wg, wu, wd
    )
    h2_out[...] = h2
    hid_out[...] = hid
    ctx.extra[...] = x2.T
    dx1, gg = feed_back(
        g[...], x1, inverse, gate, up, wo, as_row(gm), wg, wu, wd, o_s,
        lse_s[0:HEADS, :], ctx.do_own, ctx.st_own, gmo, dgate, dup, da
    )
    dx1_out[...] = dx1
    gg_out[...] = gg


def between_part(ctx, ins, outs, scratch):
    (dq, dkv, x, dx1, ga, wq, wk, wv, cos, sin, x1, inv, gate, up, wo, gm, wg, wu, wd, o, lse,
     ob1, da1, h20, h21, dg1, du1, hid0, hid1, gm1) = ins
    dqkv_out, gga_out, da, dx1_out, ggm_out, ob_out = outs
    gmo, dgate, dup = scratch
    g, gga = project_back(
        dq, dkv, x[...], dx1[...], as_row(ga), wq, wk, wv, cos[...], sin[...], dqkv_out
    )
    gga_out[...] = gga
    dx0, ggm = feed_back(
        g, x1[...], inv[:, 0:1], gate[...], up[...], wo, as_row(gm), wg, wu, wd, o,
        lse[0:HEADS, :], ctx.do_own, ctx.st_own, gmo, dgate, dup, da
    )
    dx1_out[...] = dx0
    ggm_out[...] = ggm
    ob_out[...] = o[...].astype(BF16)

    def grads():
        early_grads(
            ob_out, ob1, da, da1, h20, h21, dgate, dg1, dup, du1, hid0, hid1, gmo, gm1, ctx.extra
        )

    return grads


class Torus:
    def __init__(self, row, n, w):
        self.core = lax.rem(w, 2)
        self.spot = (n // 2, w // 2, 2 * row + lax.rem(n, 2))
        self.partner = self.device(self.spot, 1 - self.core)

    def device(self, spot, core):
        x, y, z = spot
        return (z // 2, ((x * 2 + lax.rem(z, 2)) * 4 + y) * 2 + core)

    def along(self, axis, k):
        to = list(self.spot)
        to[axis] = lax.rem(self.spot[axis] + k, 4)
        return self.device(to, self.core), to[axis]


class Reduce:
    def __init__(self, torus, u, send, recv):
        self.torus, self.u, self.send, self.recv = torus, u, send, recv
        self.box = {}

    def go(self, stage, p, k, src, dst, peer):
        cp = remote(src, dst, self.send.at[stage, p, k], self.recv.at[stage, p, k], peer)
        cp.start()
        self.box.setdefault((stage, p), []).append(cp)

    def got(self, stage, p):
        for cp in self.box[stage, p]:
            cp.wait_recv()

    def finish(self):
        for cps in self.box.values():
            for cp in cps:
                cp.wait_send()

    def exchange(self, src, came):
        u, core = self.u, self.torus.core
        for p in range(3):
            self.go(
                0, p, 0, src.at[pl.ds(48 * u * (1 - core) + 16 * u * p, 16 * u)],
                came.at[pl.ds(16 * u * p, 16 * u)], self.torus.partner,
            )

    def first(self, p, src, came, half, one):
        u = self.u
        self.got(0, p)

        def quarter(i, carry):
            at = pl.ds(16 * u * p + 4 * u * i, 4 * u)
            mine = src[pl.ds(48 * u * self.torus.core + 16 * u * p + 4 * u * i, 4 * u)]
            half[at] = (mine.astype(F32) + came[at].astype(F32)).astype(BF16)
            return carry

        lax.fori_loop(0, 4, quarter, 0)
        for k in range(1, 4):
            peer, at = self.torus.along(p, k)
            self.go(1, p, k, half.at[pl.ds(16 * u * p + 4 * u * at, 4 * u)], one.at[p, k - 1], peer)

    def second(self, p, half, one, gather, two):
        u = self.u
        self.got(1, p)
        mine = half[pl.ds(16 * u * p + 4 * u * self.torus.spot[p], 4 * u)]
        gather[p] = (mine.astype(F32) + sum(one[p, k].astype(F32) for k in range(3))).astype(BF16)
        for k in range(1, 4):
            peer, at = self.torus.along((p + 1) % 3, k)
            self.go(2, p, k, gather.at[p, pl.ds(u * at, u)], two.at[p, k - 1], peer)

    def third(self, p, gather, two, three):
        u = self.u
        self.got(2, p)
        c = self.torus.spot[(p + 2) % 3]
        mine = gather[p, pl.ds(u * self.torus.spot[(p + 1) % 3], u)]
        three[p, c] = (mine.astype(F32) + sum(two[p, k].astype(F32) for k in range(3))).astype(BF16)
        for k in range(1, 4):
            self.go(3, p, k, three.at[p, c], three.at[p, c], self.torus.along((p + 2) % 3, k)[0])

    def fourth(self, p, three, mid):
        u = self.u
        self.got(3, p)
        at = pl.ds(u * self.torus.spot[(p + 1) % 3], u)
        mid[p, at] = sum(three[p, k].astype(F32) for k in range(4)).astype(BF16)
        for k in range(1, 4):
            self.go(4, p, k, mid.at[p, at], mid.at[p, at], self.torus.along((p + 1) % 3, k)[0])

    def fifth(self, p, mid, out):
        u = self.u
        at = pl.ds(48 * u * self.torus.core + 16 * u * p + 4 * u * self.torus.spot[p], 4 * u)
        out[at] = mid[p]
        for k in range(1, 4):
            self.go(5, p, k, out.at[at], out.at[at], self.torus.along(p, k)[0])

    def sixth(self, p, out):
        u = self.u
        self.got(5, p)
        at = pl.ds(48 * u * self.torus.core + 16 * u * p, 16 * u)
        self.go(6, p, 0, out.at[at], out.at[at], self.torus.partner)


def units(count, *lead):
    return tuple(lead) + (count, 16, 256)


EARLY, LATE = 7, 2


W3 = 12 * TOK


class Spread:
    def __init__(self, row, n, w, send, recv):
        self.core = lax.rem(w, 2)
        self.y = w // 2
        self.own = self.core * 4 + self.y
        self.row, self.n = row, n
        self.partner = (row, 8 * n + 2 * self.y + 1 - self.core)
        self.send, self.recv = send, recv
        self.first, self.passed = {}, {}

    def chip(self, k):
        return (self.row, 8 * self.n + 2 * lax.rem(self.y + k, 4) + self.core)

    def start(self, part, ref):
        self.first[part], self.passed[part] = [], []
        for k in range(1, 4):
            cp = remote(ref(self.own), ref(self.own), self.send.at[part, k], self.recv.at[part, k],
                        self.chip(k))
            cp.start()
            self.first[part].append(cp)
        self.hand(part, ref, self.own, 4)

    def hand(self, part, ref, slot, k):
        cp = remote(ref(slot), ref(slot), self.send.at[part, k], self.recv.at[part, k], self.partner)
        cp.start()
        self.passed[part].append(cp)

    def forward(self, part, ref):
        for k in range(1, 4):
            self.first[part][k - 1].wait_recv()
            self.hand(part, ref, self.core * 4 + lax.rem(self.y + 4 - k, 4), 4 + k)

    def arrive(self, part):
        for cp in self.passed[part]:
            cp.wait_recv()

    def finish(self):
        for part in self.first:
            for cp in self.first[part] + self.passed[part]:
                cp.wait_send()


def turns(n):
    return (n + 2) // 2


def fill_masks(bias, starts_ref, n, w):
    turn = turns(n)

    def one(t, carry):
        sel = jnp.where(t >= turn, 1, 0)
        kc = jnp.where(t >= turn, t - turn, t)
        line = lax.broadcasted_iota(jnp.int32, (256, 1), 0)
        key = (2 * kc + line // TOK) * 1024 + w * TOK + lax.rem(line, TOK)
        col = lax.broadcasted_iota(jnp.int32, (1, 512), 1)
        octet = jnp.where(sel == 0, n, 7 - n)
        query = octet * 1024 + (2 * (col // TOK) + sel) * TOK + lax.rem(col, TOK)
        bias[t] = jnp.where((key >= starts_ref[sel]) & (key <= query), 0.0, MASKED)
        return carry

    lax.fori_loop(0, 5, one, 0)


def over_keys(n, sel, step):
    octet = jnp.where(sel == 0, n, 7 - n)
    base = jnp.where(sel == 0, 0, turns(n))
    whole = (octet + 1) // 2

    def chunk(kc, carry):
        step(base + kc, kc, 2 * TOK)
        return carry

    lax.fori_loop(0, whole, chunk, 0)

    @pl.when(lax.rem(octet + 1, 2) == 1)
    def _():
        step(base + whole, whole, TOK)


def three_heads(ref, sel, g):
    return jnp.concatenate(
        [
            ref[4 * sel + y, HD * h : HD * h + HD, :]
            for h in range(3 * g, 3 * g + 3)
            for y in range(4)
        ],
        axis=1,
    )


def key_blocks(ref, kc, first, keys):
    return jnp.concatenate(
        [ref[2 * kc + i, first : first + HD, :] for i in range(keys // TOK)], axis=1
    )


def by_chip(value, y):
    return jnp.concatenate(
        [value[:, 512 * j + TOK * y : 512 * j + TOK * y + TOK] for j in range(3)], axis=0
    )


class Context:
    pass


def attend_kernel(first, n_in, n_out, *refs):
    ins, refs = refs[:n_in], refs[n_in:]
    outs, refs = refs[:n_out], refs[n_out:]
    if first:
        part_ref, stat_ref, q_all, kv_all = refs[:4]
    else:
        q_all, kv_all, part_ref, stat_ref = refs[:4]
    (k_nat, bias, top, total, acc, o_send, o_recv, r_send, r_recv, o_y, s_y,
     qs, qr, ks, kr, ps, pr, ys, yr) = refs[4:23]
    starts_ref = outs[2] if first else ins[-1]
    row, seq, n, w = place()
    bar = greet(row, n, w)
    core, y = lax.rem(w, 2), w // 2
    own_k = octet_of(n, w)
    queries = Spread(row, n, w, qs, qr)
    ctx = Context()
    ctx.row, ctx.n, ctx.w, ctx.core = row, n, w, core
    ctx.q_own, ctx.kv_own = q_all.at[queries.own], kv_all.at[own_k]
    ctx.q_all, ctx.kv_all = q_all, kv_all
    ctx.ready = lambda: pl.semaphore_wait(bar, 14)
    if first:
        late, arrived, end = first_part(ctx, ins, outs, refs[23:])
    else:
        late, arrived, end = middle_part(ctx, ins[:-1], outs, refs[23:])

    def q_part(g):
        return lambda slot: q_all.at[slot, pl.ds(192 * g, 192)]

    keys = {}
    for g in range(3):
        keys[g] = []
        for k in range(1, 8):
            block = kv_all.at[own_k, pl.ds(TOK * g, TOK)]
            cp = remote(
                block, block, ks.at[g, k], kr.at[g, k], (row, 8 * lax.rem(n + k, 8) + w)
            )
            cp.start()
            keys[g].append(cp)
        queries.start(g, q_part(g))
    fill_masks(bias, starts_ref, n, w)
    queries.forward(0, q_part(0))

    def phase(g, sel):
        top[...] = jnp.full(top.shape, LOWEST, F32)
        total[...] = jnp.zeros(total.shape, F32)
        acc[...] = jnp.zeros(acc.shape, F32)

        def step(at, kc, keys):
            scores = dot(k_nat[kc, 0:keys], three_heads(q_all, sel, g), 1, 0)
            mask = bias[at, 0:keys]
            weights, shrinks = [], []
            for j in range(3):
                cols = slice(512 * j, 512 * j + 512)
                s = scores[:, cols] + mask
                old = top[:, cols]
                new = jnp.maximum(old, jnp.max(s, axis=0, keepdims=True))
                p = jnp.exp2((s - new) * EXP_SCALE)
                shrink = jnp.exp2((old - new) * EXP_SCALE)
                top[:, cols] = new
                total[:, cols] = total[:, cols] * shrink + jnp.sum(p, axis=0, keepdims=True)
                weights.append(p.astype(BF16))
                shrinks.append(shrink)
            values = key_blocks(kv_all, kc, TOK * g + HD, keys)
            acc[...] = acc[...] * jnp.concatenate(shrinks, axis=1) + dot(
                values, jnp.concatenate(weights, axis=1), 1, 0
            )

        over_keys(n, sel, step)

    pairs, flying = [], []
    for g in range(3):
        for cp in keys[g]:
            cp.wait_recv()
        for j in range(8):
            k_nat[j // 2, (j % 2) * TOK : (j % 2) * TOK + TOK, :] = jnp.transpose(
                kv_all[j, TOK * g : TOK * g + HD, :]
            )
        queries.arrive(g)
        if g == 2 and arrived is not None:
            arrived()
        phase(g, 1 - core)
        o_send[g] = acc[...].astype(BF16)
        r_send[g, 0] = top[...]
        r_send[g, 1] = total[...]
        both = [
            remote(o_send.at[g], o_recv.at[g], ps.at[0, g], pr.at[0, g], queries.partner),
            remote(r_send.at[g], r_recv.at[g], ps.at[1, g], pr.at[1, g], queries.partner),
        ]
        for cp in both:
            cp.start()
        pairs += both
        if g < 2:
            queries.forward(g + 1, q_part(g + 1))
        if g == 0 and late is not None:
            late()
        phase(g, core)
        for cp in both:
            cp.wait_recv()
        new = jnp.maximum(top[...], r_recv[g, 0])
        mine = jnp.exp2((top[...] - new) * EXP_SCALE)
        theirs = jnp.exp2((r_recv[g, 0] - new) * EXP_SCALE)
        length = total[...] * mine + r_recv[g, 1] * theirs
        out = (acc[...] * mine + o_recv[g].astype(F32) * theirs).astype(BF16)
        for i in range(4):
            o_y[g, i] = by_chip(out, i)
            for j in range(3):
                cols = slice(512 * j + TOK * i, 512 * j + TOK * i + TOK)
                s_y[g, i, j : j + 1, :] = new[:, cols]
                s_y[g, i, 4 + j : 5 + j, :] = length[:, cols]
        for k in range(1, 4):
            to = lax.rem(y + k, 4)
            peer = queries.chip(k)
            for cp in (
                remote(o_y.at[g, to], part_ref.at[y, pl.ds(192 * g, 192)], ys.at[0, g, k],
                       yr.at[0, g, k], peer),
                remote(s_y.at[g, to], stat_ref.at[y, pl.ds(8 * g, 8)], ys.at[1, g, k],
                       yr.at[1, g, k], peer),
            ):
                cp.start()
                flying.append(cp)
        part_ref[y, 192 * g : 192 * g + 192, :] = o_y[g, y]
        stat_ref[y, 8 * g : 8 * g + 8, :] = s_y[g, y]
    queries.finish()
    for g in range(3):
        for cp in keys[g]:
            cp.wait_send()
    for cp in pairs:
        cp.wait_send()
    for cp in flying:
        cp.wait()
    if end is not None:
        end()


GATHERED = [((8, D, TOK), BF16), ((8, 2 * KV, TOK), BF16)]


def attend(first, ins, specs, outs, scratch, collective, limit):
    count = len(outs)
    here = [] if first else [sds(*a) for a in GATHERED]
    there = [pltpu.VMEM(*a) for a in GATHERED] if first else []
    outs = outs + [(o, VM) for o in here + [sds((4, D, TOK), BF16), sds((4, 24, TOK), F32)]]
    return pl.pallas_call(
        functools.partial(attend_kernel, first, len(ins), count),
        name="attend_first" if first else "attend",
        out_shape=tuple(o for o, _ in outs),
        in_specs=specs,
        out_specs=tuple(spec for _, spec in outs),
        scratch_shapes=there
        + [
            pltpu.VMEM((4, 256, HD), BF16),
            pltpu.VMEM((5, 256, 512), F32),
            pltpu.VMEM((1, W3), F32),
            pltpu.VMEM((1, W3), F32),
            pltpu.VMEM((HD, W3), F32),
            pltpu.VMEM((3, HD, W3), BF16),
            pltpu.VMEM((3, HD, W3), BF16),
            pltpu.VMEM((3, 2, 1, W3), F32),
            pltpu.VMEM((3, 2, 1, W3), F32),
            pltpu.VMEM((3, 4, 192, TOK), BF16),
            pltpu.VMEM((3, 4, 8, TOK), F32),
            DMA((3, 8)), DMA((3, 8)), DMA((3, 8)), DMA((3, 8)),
            DMA((2, 3)), DMA((2, 3)), DMA((2, 3, 4)), DMA((2, 3, 4)),
        ]
        + scratch,
        compiler_params=params(collective, limit),
        cost_estimate=cost(30),
    )(*ins)


def attend_back_kernel(carry_sum, n_in, n_out, n_more, *refs):
    ins, refs = refs[:n_in], refs[n_in:]
    outs, refs = refs[:n_out], refs[n_out:]
    (dq_part, dkv_part, extra_out, do_all, st_all, k_nat, v_nat, bias, rows_s, dq, dkv, q_send,
     q_recv, q_y, kv_low, extra, qs, qr, ks, kr, ps, pr, ys, yr, es, er) = refs[:26]
    more, scratch = refs[26 : 26 + n_more], refs[26 + n_more :]
    q_all, kv_all, starts_ref = ins[-3:]
    ctx = Context()
    ctx.q_all, ctx.kv_all = q_all, kv_all
    row, seq, n, w = place()
    bar = greet(row, n, w)
    torus = Torus(row, n, w)
    if carry_sum:
        came, one, gather, two, three = more
        half = extra.at[pl.ds(48 * EARLY * lax.rem(w, 2), 48 * EARLY)]
        for k in range(1, 4):
            pl.semaphore_signal(bar, inc=1, device_id=torus.along(2, k)[0], device_id_type=MESH)
        early = Reduce(torus, EARLY, es, er)
    else:
        (extra_in,) = more
        move = remote(extra, extra_in, es, er, (row, 8 * (7 - n) + w))
    core, y = lax.rem(w, 2), w // 2
    own_k = octet_of(n, w)
    grads = Spread(row, n, w, qs, qr)
    ctx.do_own, ctx.st_own, ctx.extra = do_all.at[grads.own], st_all.at[grads.own], extra
    make = between_part if carry_sum else turn_part
    grads_of = make(ctx, ins[:-3], outs, scratch)
    pl.semaphore_wait(bar, 17 if carry_sum else 14)

    def part(g):
        return lambda slot: do_all.at[slot, pl.ds(192 * g, 192)]

    def stats(slot):
        return st_all.at[slot]

    grads.start(3, stats)
    for g in range(3):
        grads.start(g, part(g))
    if carry_sum:
        grads_of()
        early.exchange(extra, came)
    fill_masks(bias, starts_ref, n, w)
    for g in range(3):
        for j in range(8):
            at = slice((j % 2) * TOK, (j % 2) * TOK + TOK)
            k_nat[g, j // 2, at, :] = jnp.transpose(kv_all[j, TOK * g : TOK * g + HD, :])
            v_nat[g, j // 2, at, :] = jnp.transpose(kv_all[j, TOK * g + HD : TOK * g + TOK, :])
    grads.forward(3, stats)
    grads.forward(0, part(0))
    if carry_sum:
        for p in range(3):
            early.first(p, extra, came, half, one)
    if not carry_sum:

        @pl.when(core == 1)
        def _():
            move.start()

    def phase(g, sel):
        dq[...] = jnp.zeros(dq.shape, F32)
        for i, first in enumerate((0, 16)):
            for j in range(3):
                for c in range(4):
                    at = 512 * j + TOK * c
                    line = first + 3 * g + j
                    rows_s[i, :, at : at + TOK] = st_all[4 * sel + c, line : line + 1, :]

        def step(at, kc, keys):
            qt = three_heads(q_all, sel, g)
            dt = three_heads(do_all, sel, g)
            scores = dot(k_nat[g, kc, 0:keys], qt, 1, 0)
            dp = dot(v_nat[g, kc, 0:keys], dt, 1, 0)
            mask = bias[at, 0:keys]
            ps_, ds_ = [], []
            for j in range(3):
                cols = slice(512 * j, 512 * j + 512)
                p = jnp.exp2((scores[:, cols] + mask - rows_s[0, :, cols]) * EXP_SCALE)
                ds_.append((p * (dp[:, cols] - rows_s[1, :, cols])).astype(BF16))
                ps_.append(p.astype(BF16))
            p = jnp.concatenate(ps_, axis=1)
            ds = jnp.concatenate(ds_, axis=1)
            dkv[kc, 0:HD, 0:keys] += dot(ds, qt, 1, 1).T
            dkv[kc, HD:, 0:keys] += dot(p, dt, 1, 1).T
            dq[...] += dot(key_blocks(kv_all, kc, TOK * g, keys), ds, 1, 0)

        over_keys(n, sel, step)

    pairs, flying = [], []
    for g in range(3):
        dkv[...] = jnp.zeros(dkv.shape, F32)
        if g == 0:
            grads.arrive(3)
        grads.arrive(g)
        phase(g, 1 - core)
        q_send[g] = (dq[...] * SCALE).astype(BF16)
        pair = remote(q_send.at[g], q_recv.at[g], ps.at[g], pr.at[g], grads.partner)
        pair.start()
        pairs.append(pair)
        if g == 1 and carry_sum:
            for p in range(3):
                early.second(p, half, one, gather, two)
        if g < 2:
            grads.forward(g + 1, part(g + 1))
        elif carry_sum:
            for p in range(3):
                early.third(p, gather, two, three)
        phase(g, core)
        for j in range(8):
            cols = slice((j % 2) * TOK, (j % 2) * TOK + TOK)
            kv_low[g, j, 0:HD, :] = (dkv[j // 2, 0:HD, cols] * SCALE).astype(BF16)
            kv_low[g, j, HD:, :] = dkv[j // 2, HD:, cols].astype(BF16)
        for k in range(1, 8):
            to = lax.rem(n + k, 8)
            cp = remote(
                kv_low.at[g, octet_of(to, w)], dkv_part.at[n, pl.ds(TOK * g, TOK)], ks.at[g, k],
                kr.at[g, k], (row, 8 * to + w),
            )
            cp.start()
            flying.append(cp)
        pair.wait_recv()
        out = (dq[...] * SCALE + q_recv[g].astype(F32)).astype(BF16)
        for i in range(4):
            q_y[g, i] = by_chip(out, i)
        for k in range(1, 4):
            to = lax.rem(y + k, 4)
            cp = remote(q_y.at[g, to], dq_part.at[y, pl.ds(192 * g, 192)], ys.at[g, k], yr.at[g, k],
                        grads.chip(k))
            cp.start()
            flying.append(cp)
        dkv_part[n, TOK * g : TOK * g + TOK, :] = kv_low[g, own_k]
        dq_part[y, 192 * g : 192 * g + 192, :] = q_y[g, y]
        if carry_sum:
            for p in range(3):
                if g == 2:
                    early.fourth(p, three, extra_out)
    grads.finish()
    for cp in pairs:
        cp.wait_send()
    for cp in flying:
        cp.wait()
    if carry_sum:
        for p in range(3):
            early.got(4, p)
        early.finish()
    else:

        @pl.when(core == 1)
        def _():
            move.wait()
            extra_out[...] = extra_in[...]

        @pl.when(core == 0)
        def _():
            extra_out[...] = extra[...]


def attend_back(carry_sum, ins, specs, outs, scratch, limit):
    if carry_sum:
        u = EARLY
        extra_shape = sds(units(4 * u, 3), BF16)
        extra = pltpu.VMEM(units(96 * u), BF16)
        sems = [DMA((5, 3, 4))] * 2
        more = [
            pltpu.VMEM(shape, BF16)
            for shape in (
                units(48 * u), units(4 * u, 3, 3), units(4 * u, 3), units(u, 3, 3), units(u, 3, 4),
            )
        ]
    else:
        extra_shape = X_T
        extra = pltpu.VMEM((D, TOK), F32)
        sems = [DMA, DMA]
        more = [pltpu.VMEM((D, TOK), F32)]
    return pl.pallas_call(
        functools.partial(attend_back_kernel, carry_sum, len(ins), len(outs), len(more)),
        name="attend_back_sum" if carry_sum else "attend_back",
        out_shape=tuple(outs + [sds((4, D, TOK), BF16), sds((8, 2 * KV, TOK), BF16), extra_shape]),
        in_specs=specs,
        out_specs=(VM,) * (len(outs) + 3),
        scratch_shapes=[
            pltpu.VMEM((8, D, TOK), BF16),
            pltpu.VMEM((8, 32, TOK), F32),
            pltpu.VMEM((3, 4, 256, HD), BF16),
            pltpu.VMEM((3, 4, 256, HD), BF16),
            pltpu.VMEM((5, 256, 512), F32),
            pltpu.VMEM((2, 1, W3), F32),
            pltpu.VMEM((HD, W3), F32),
            pltpu.VMEM((4, TOK, 256), F32),
            pltpu.VMEM((3, HD, W3), BF16),
            pltpu.VMEM((3, HD, W3), BF16),
            pltpu.VMEM((3, 4, 192, TOK), BF16),
            pltpu.VMEM((3, 8, TOK, TOK), BF16),
            extra,
            DMA((4, 8)), DMA((4, 8)), DMA((3, 8)), DMA((3, 8)),
            DMA((3,)), DMA((3,)), DMA((3, 4)), DMA((3, 4)),
        ]
        + sems
        + more
        + scratch,
        compiler_params=params(5 if carry_sum else 3, limit),
        cost_estimate=cost(40),
    )(*ins)


def both_rows(a, b):
    return jnp.concatenate([a[...], b[...]], axis=0)


def as_units(value):
    return value.astype(BF16).reshape(units(value.shape[0] // 16))


def early_grads(oa, ob, daa, dab, h2a, h2b, dga, dgb, dua, dub, hida, hidb, gma, gmb, g_out):
    ot = jnp.concatenate([oa[...], ob[...]], axis=1)
    h2t = both_rows(h2a, h2b).T
    gmt = both_rows(gma, gmb).T
    for i in range(6):
        cols = slice(256 * i, 256 * i + 256)
        for t, (lhs, a, b) in enumerate(((h2t, dga, dgb), (h2t, dua, dub), (gmt, hida, hidb))):
            rhs = jnp.concatenate([a[:, cols], b[:, cols]], axis=0)
            g_out[36 * (6 * t + i) : 36 * (6 * t + i) + 36] = as_units(dot(lhs, rhs, 1, 0))
    da = both_rows(daa[:, 128:384], dab[:, 128:384])
    g_out[648:672] = as_units(dot(ot[0:384], da, 1, 0))


def late_grads(h1a, h1b, dqa, dqb, oa, ob, daa, dab, g_out):
    h1t = both_rows(h1a, h1b).T
    ot = jnp.concatenate([oa[...], ob[...]], axis=1)
    dat = both_rows(daa, dab).T

    def rows(first, last):
        return jnp.concatenate([dqa[first:last, :], dqb[first:last, :]], axis=1)

    g_out[0:36] = as_units(dot(h1t, rows(0, 256), 1, 1))
    g_out[36:72] = as_units(dot(h1t, rows(256, 512), 1, 1))
    mixed = [dot(h1t, rows(512, 640), 1, 1), dot(ot, dat[0:128], 1, 1)]
    g_out[72:108] = as_units(jnp.concatenate(mixed, axis=1))
    g_out[108:120] = as_units(dot(ot[384:576], dat[128:384], 1, 1))
    low = jnp.concatenate([dat[384:576], jnp.zeros((64, 256), BF16)], axis=0)
    high = jnp.concatenate([jnp.zeros((192, 256), BF16), rows(640, 704)], axis=0)
    g_out[120:156] = as_units(dot(ot, low, 1, 1) + dot(h1t, high, 1, 1))
    g_out[156:192] = as_units(dot(h1t, rows(704, 960), 1, 1))


def spread_kernel(
    early, late, x_in, g_in, gains, ga_out, gm_out, x_out, g_out, gate_out, up_out, down_out, q_out, k_out, v_out, o_out, big, small, kt, vt, sems
):
    def block(ref, first, count=36):
        return ref[first : first + count].reshape(16 * count, 256).astype(F32)

    ga_out[...] = gains[0:1, :].reshape(D)
    gm_out[...] = gains[1:2, :].reshape(D)
    cps = [
        pltpu.make_async_copy(x_in, x_out, sems.at[22]),
        pltpu.make_async_copy(g_in, g_out, sems.at[23]),
    ]
    for cp in cps:
        cp.start()
    for t, ref in enumerate((gate_out, up_out, down_out)):
        for i in range(6):
            cols = pl.ds(256 * i, 256)
            big[t, :, cols] = block(early, 36 * (6 * t + i))
            cp = pltpu.make_async_copy(big.at[t, :, cols], ref.at[:, cols], sems.at[6 * t + i])
            cp.start()
            cps.append(cp)
    small[0, :, 0:256] = block(late, 0)
    small[0, :, 256:512] = block(late, 36)
    mixed = block(late, 72)
    small[0, :, 512:576] = mixed[:, 0:64]
    small[1, :, 0:128] = mixed[:, 128:256]
    kt[0:64, :] = mixed[:, 0:128].T[64:128]
    small[1, 0:384, 128:384] = block(early, 648, 24)
    small[1, 384:576, 128:384] = block(late, 108, 12)
    mixed = block(late, 120)
    small[1, :, 384:576] = mixed[:, 0:192]
    kt[64:128, :] = mixed[:, 128:256].T[64:128]
    last = block(late, 156).T
    kt[128:192, :] = last[0:64]
    vt[...] = last[64:256]
    for i, (src, dst) in enumerate(
        ((small.at[0], q_out), (small.at[1], o_out), (kt, k_out), (vt, v_out))
    ):
        cp = pltpu.make_async_copy(src, dst, sems.at[18 + i])
        cp.start()
        cps.append(cp)
    for cp in cps:
        cp.wait()


def spread(*ins):
    return pl.pallas_call(
        spread_kernel,
        name="spread",
        out_shape=(
            sds((D,), F32), sds((D,), F32), X_T, X_T, sds((D, FF), F32), sds((D, FF), F32), sds((D, FF), F32), sds((D, D), F32),
            sds((KV, D), F32), sds((KV, D), F32), sds((D, D), F32),
        ),
        in_specs=[VM] * 5,
        out_specs=(VM,) * 2 + (ANY,) * 9,
        scratch_shapes=[
            pltpu.VMEM((3, D, FF), F32),
            pltpu.VMEM((2, D, D), F32),
            pltpu.VMEM((KV, D), F32),
            pltpu.VMEM((KV, D), F32),
            DMA((24,)),
        ],
        compiler_params=params(None, 30 << 20),
    )(*ins)


def reduce_kernel(
    mid_ref, dq, dkv, x, dx1, ga, wq, wk, wv, cos, sin, h10, h11, dqkv1, ob0, ob1, da0, da1,
    gga1, ggm0, ggm1, early_out, late_out, gain_out, fin_out,
    late_ref, came, half, one, gather, two, three, mid, gain_in, gain_sum, fin_ref, fin_in, dqkv0,
    s_e, r_e, s_l, r_l, gs, gr, fs, fr
):
    row, seq, n, w = place()
    torus = Torus(row, n, w)
    core = torus.core
    bar = pltpu.get_barrier_semaphore()
    pl.semaphore_signal(bar, inc=1, device_id=torus.partner, device_id_type=MESH)
    for axis in range(3):
        for k in range(1, 4):
            pl.semaphore_signal(bar, inc=1, device_id=torus.along(axis, k)[0], device_id_type=MESH)
    mirror = (row, 8 * (7 - n) + w)
    g, gga0 = project_back(
        dq, dkv, x[...], dx1[...], as_row(ga), wq, wk, wv, cos[...], sin[...], dqkv0
    )
    fin_ref[...] = g.T
    late_grads(h10, h11, dqkv0, dqkv1, ob0, ob1, da0, da1, late_ref)
    gain_sum[0] = jnp.concatenate(
        [gga0 + gga1[...], ggm0[...] + ggm1[...], jnp.zeros((6, D), F32)], axis=0
    )

    @pl.when(core == 1)
    def _():
        pl.semaphore_signal(bar, inc=1, device_id=mirror, device_id_type=MESH)
        pl.semaphore_wait(bar, 11)

    @pl.when(core == 0)
    def _():
        pl.semaphore_wait(bar, 10)

    early = Reduce(torus, EARLY, s_e, r_e)
    late = Reduce(torus, LATE, s_l, r_l)
    late.exchange(late_ref, came)
    move = remote(fin_ref, fin_in, fs, fr, mirror)

    @pl.when(core == 1)
    def _():
        move.start()

    gains = []

    def gain_round(i, peers, count, at):
        gain_in[i, at] = gain_sum[i]
        for k, peer in enumerate(peers):
            cp = remote(gain_sum.at[i], gain_in.at[i, at], gs.at[i, k], gr.at[i, k], peer)
            cp.start()
            gains.append(cp)

    def gain_total(i, peers, count):
        for cp in gains[-peers:]:
            cp.wait_recv()
        return sum(gain_in[i, j] for j in range(count))

    def axis_peers(axis):
        return [torus.along(axis, k)[0] for k in range(1, 4)]

    gain_round(0, [torus.partner], 2, core)
    for p in range(3):
        late.first(p, late_ref, came, half, one)
    for p in range(3):
        early.fifth(p, mid_ref, early_out)
    gain_sum[1] = gain_total(0, 1, 2)
    gain_round(1, axis_peers(0), 4, torus.spot[0])
    for p in range(3):
        late.second(p, half, one, gather, two)
    gain_sum[2] = gain_total(1, 3, 4)
    gain_round(2, axis_peers(1), 4, torus.spot[1])
    for p in range(3):
        late.third(p, gather, two, three)
    gain_sum[3] = gain_total(2, 3, 4)
    gain_round(3, axis_peers(2), 4, torus.spot[2])
    for p in range(3):
        late.fourth(p, three, mid)
    for p in range(3):
        early.sixth(p, early_out)
    gain_out[...] = gain_total(3, 3, 4)
    for p in range(3):
        late.got(4, p)
        late.fifth(p, mid, late_out)
    for p in range(3):
        late.sixth(p, late_out)

    @pl.when(core == 1)
    def _():
        move.wait()
        fin_out[...] = fin_in[...]

    @pl.when(core == 0)
    def _():
        fin_out[...] = fin_ref[...]

    for cp in gains:
        cp.wait_send()
    for p in range(3):
        early.got(6, p)
        late.got(6, p)
    early.finish()
    late.finish()


def reduce_all(*ins):
    u = LATE
    return pl.pallas_call(
        reduce_kernel,
        name="reduce_all",
        out_shape=(
            sds(units(96 * EARLY), BF16), sds(units(96 * LATE), BF16), sds((8, D), F32), X_T
        ),
        in_specs=[VM] * len(ins),
        out_specs=(VM,) * 4,
        scratch_shapes=[
            pltpu.VMEM(shape, BF16)
            for shape in (
                units(96 * u), units(48 * u), units(48 * u), units(4 * u, 3, 3), units(4 * u, 3), units(u, 3, 3),
                units(u, 3, 4), units(4 * u, 3),
            )
        ]
        + [
            pltpu.VMEM((4, 4, 8, D), F32),
            pltpu.VMEM((4, 8, D), F32),
            pltpu.VMEM((D, TOK), F32),
            pltpu.VMEM((D, TOK), F32),
            pltpu.VMEM((960, TOK), BF16),
        ]
        + [DMA((7, 3, 4))] * 4
        + [DMA((4, 4)), DMA((4, 4)), DMA, DMA],
        compiler_params=params(4, 24 << 20),
        cost_estimate=cost(40),
    )(*ins)


def on_device(
    tokens, cotangent, segment_ids, gain_attn, wq, wk, wv, wo, gain_mlp, wg, wu, wd
):
    ga, gm = gain_attn, gain_mlp
    wk, wv, wd = wk.T, wv.T, wd.T
    w_q, w_k, w_v = sds((D, D), BF16), sds((KV, D), BF16), sds((KV, D), BF16)
    table = sds((32, TOK), F32)
    x0, h10, starts, cos, sin, qa0, kva0, part, stat = attend(
        True,
        [tokens[0].T, segment_ids, ga, wq, wk, wv, begin()],
        [HBM, HBM, VM, HBM, HBM, HBM, VM],
        [(o, VM) for o in (X_S, H_S, sds((2, 1, 4 * TOK), jnp.int32), table, table)]
        + [(sds(*a), HBM) for a in GATHERED],
        [
            pltpu.VMEM((D, TOK), F32),
            pltpu.VMEM((64, 1, TOK), jnp.int32),
            pltpu.VMEM((64, 1, TOK), jnp.int32),
        ]
        + [DMA((8,))] * 4
        + [DMA((2,)), DMA]
        + buffers(w_q, w_k, w_v)
        + [DMA((3,))],
        1,
        20 << 20,
    )
    cot, h11, x1, m0, h20, inv0, gate0, up0, hid0, o0, lse0, qa1, kva1, part, stat = attend(
        False,
        [part, stat, x0, cotangent[0].T, ga, wq, wk, wv, wo, gm, wg, wu, wd, cos, sin, starts],
        [VM] * 16,
        [(o, VM) for o in (X_S, H_S, X_S, X_S, H_S, sds((TOK, TOK), F32))]
        + [(F_S, HBM), (F_S, HBM)]
        + [(o, VM) for o in (FB_S, sds((D, TOK), F32), sds((16, TOK), F32))],
        [pltpu.VMEM((TOK, FF), F32), pltpu.VMEM((TOK, FF), F32), DMA((2,)), pltpu.VMEM((D, TOK), F32),
         DMA((2,)), DMA],
        2,
        20 << 20,
    )
    h21, hid1, ob1, gm1, dg1, du1, da1, dx1, ggm1, dq, dkv, output = attend_back(
        False,
        [part, stat, x1, cot, wo, gm, wg, wu, wd, qa1, kva1, starts],
        [VM] * 12,
        [H_S, FB_S, Q_T, H_S, FB_S, FB_S, H_S, X_S, G_S],
        [pltpu.VMEM((D, TOK), F32), pltpu.VMEM((16, TOK), F32)],
        20 << 20,
    )
    dqkv1, gga1, da0, dx0, ggm0, ob0, dq, dkv, mid = attend_back(
        True,
        [dq, dkv, x1, dx1, ga, wq, wk, wv, cos, sin, m0, inv0, gate0, up0, wo, gm, wg, wu, wd, o0,
         lse0, ob1, da1, h20, h21, dg1, du1, hid0, hid1, gm1, qa0, kva0, starts],
        [VM] * 33,
        [sds((960, TOK), BF16), G_S, H_S, X_S, G_S, Q_T],
        [pltpu.VMEM((TOK, D), BF16), pltpu.VMEM((TOK, FF), BF16), pltpu.VMEM((TOK, FF), BF16)],
        28 << 20,
    )
    early, late, gains, grad_tokens = reduce_all(
        mid, dq, dkv, x0, dx0, ga, wq, wk, wv, cos, sin, h10, h11, dqkv1, ob0, ob1, da0, da1, gga1,
        ggm0, ggm1
    )
    gga, ggm, output, grad_tokens, gate, up, down, query, key, value, out = spread(
        early, late, output, grad_tokens, gains
    )
    return (
        output.T[None], grad_tokens.T[None], gga, query, key.T, value.T, out, ggm, gate, up,
        down.T,
    )


def solution(mesh):
    rows = P("rows", "seq", None)
    in_specs = (rows, rows, P("rows", "seq")) + (P(),) * 9
    out_specs = (rows, rows) + (P(),) * 9
    return jax.shard_map(
        on_device, mesh=mesh, in_specs=in_specs, out_specs=out_specs, check_vma=False
    )
```

```python
import functools
import math

import jax
import jax.numpy as jnp
from jax import lax
from jax.experimental import pallas as pl
from jax.experimental.pallas import tpu as pltpu
from jax.sharding import PartitionSpec as P

F32 = jnp.float32
BF16 = jnp.bfloat16
MESH = pl.DeviceIdType.MESH

D = 576
HEADS = 9
HD = 64
KV = 192
FF = 1536
TOK = 128
DOCS = 16
EPS = 1e-05
SCALE = 0.125
EXP_SCALE = SCALE * 1.4426950408889634
MASKED = -1e30
LOWEST = -1e20

VM = pl.BlockSpec(memory_space=pltpu.VMEM)
DMA = pltpu.SemaphoreType.DMA


def dot(a, b, ca, cb):
    return lax.dot_general(a, b, (((ca,), (cb,)), ((), ())), preferred_element_type=F32)


def sds(shape, dtype):
    return jax.ShapeDtypeStruct(shape, dtype)


def params(collective=None, limit=50 << 20):
    if collective is None:
        return pltpu.CompilerParams(vmem_limit_bytes=limit)
    return pltpu.CompilerParams(
        vmem_limit_bytes=limit, collective_id=collective, has_side_effects=True
    )


def cost(us):
    return pl.CostEstimate(flops=us * 1000000000, bytes_accessed=us * 1000000, transcendentals=0)


def place():
    seq = lax.axis_index("seq")
    row = lax.axis_index("rows")
    return row, seq, seq // 8, lax.rem(seq, 8)


def slot_of(w):
    return lax.rem(w, 2) * 4 + w // 2


def octet_of(n, w):
    return jnp.where(lax.rem(w, 2) == 0, n, 7 - n)


def greet(row, n, w):
    bar = pltpu.get_barrier_semaphore()
    for k in range(1, 8):
        pl.semaphore_signal(
            bar, inc=1, device_id=(row, 8 * n + lax.rem(w + k, 8)), device_id_type=MESH
        )
        pl.semaphore_signal(
            bar, inc=1, device_id=(row, 8 * lax.rem(n + k, 8) + w), device_id_type=MESH
        )
    return bar


def remote(src, dst, send, recv, target):
    return pltpu.make_async_remote_copy(
        src_ref=src,
        dst_ref=dst,
        send_sem=send,
        recv_sem=recv,
        device_id=target,
        device_id_type=MESH,
    )


def as_row(ref):
    return ref[...].reshape(1, D)


def norm_in(x, gain):
    inverse = lax.rsqrt(jnp.mean(x * x, axis=-1, keepdims=True) + EPS)
    return (x * inverse * gain).astype(BF16), inverse


def norm_back(x, inverse, gain, grad):
    scaled = grad * gain
    grad_gain = jnp.sum(grad * (x * inverse), axis=0, keepdims=True)
    inner = jnp.mean(scaled * x, axis=-1, keepdims=True)
    return inverse * scaled - x * (inverse * inverse * inverse) * inner, grad_gain


def project(x, gain, wq, wk, wv, h_out):
    h, _ = norm_in(x, gain)
    h_out[...] = h
    return dot(h, wq[...], 1, 0).T, dot(wk[...], h, 1, 1), dot(wv[...], h, 1, 1).astype(BF16)


def rotate(qt, kt, vt, cos, sin, q_out, kv_out):
    scaled_cos, scaled_sin = cos * EXP_SCALE, sin * EXP_SCALE
    for i in range(HEADS):
        a = qt[HD * i : HD * i + 32]
        b = qt[HD * i + 32 : HD * i + 64]
        q_out[HD * i : HD * i + 32, :] = (a * scaled_cos - b * scaled_sin).astype(BF16)
        q_out[HD * i + 32 : HD * i + 64, :] = (b * scaled_cos + a * scaled_sin).astype(BF16)
    for i in range(3):
        a = kt[HD * i : HD * i + 32]
        b = kt[HD * i + 32 : HD * i + 64]
        kv_out[TOK * i : TOK * i + 32, :] = (a * cos - b * sin).astype(BF16)
        kv_out[TOK * i + 32 : TOK * i + 64, :] = (b * cos + a * sin).astype(BF16)
        kv_out[TOK * i + 64 : TOK * i + 128, :] = vt[HD * i : HD * i + 64]


def combine(part, stat, o_out, lse_out):
    for g in range(3):
        tops = [stat[i, 8 * g : 8 * g + 3, :] for i in range(4)]
        top = functools.reduce(jnp.maximum, tops)
        factors = [jnp.exp2(t - top) for t in tops]
        total = sum(f * stat[i, 8 * g + 4 : 8 * g + 7, :] for i, f in enumerate(factors))
        inverse = 1.0 / total
        factors = [f * inverse for f in factors]
        lse_out[3 * g : 3 * g + 3, :] = top + jnp.log2(total)
        for j in range(3):
            rows = slice(192 * g + HD * j, 192 * g + HD * j + HD)
            o_out[rows, :] = sum(
                part[i, rows, :].astype(F32) * factors[i][j : j + 1, :] for i in range(4)
            )


def feed_forward(x, o_t, wo, gain, wg, wu, wd):
    x1 = x + dot(o_t, wo[...], 0, 0)
    h2, inverse = norm_in(x1, gain)
    gate = dot(h2, wg[...], 1, 0)
    up = dot(h2, wu[...], 1, 0)
    hid = (gate * jax.nn.sigmoid(gate) * up).astype(BF16)
    return x1, h2, inverse, gate, up, hid, x1 + dot(hid, wd[...], 1, 1)


def feed_back(g, x1, inverse, gate, up, wo, gain, wg, wu, wd, o_ref, lse,
              do_out, stat_out, gm_out, dgate_out, dup_out, da_out):
    gm = g.astype(BF16)
    gm_out[...] = gm
    dhid = dot(gm, wd[...], 1, 0)
    sg = jax.nn.sigmoid(gate)
    dgate = (dhid * up * sg * (1.0 + gate * (1.0 - sg))).astype(BF16)
    dup = (dhid * gate * sg).astype(BF16)
    dgate_out[...] = dgate
    dup_out[...] = dup
    dh2 = dot(dgate, wg[...], 1, 1) + dot(dup, wu[...], 1, 1)
    dy, grad_gain = norm_back(x1, inverse, gain, dh2)
    dx1 = g + dy
    da = dx1.astype(BF16)
    da_out[...] = da
    do_t = dot(wo[...], da, 1, 1).astype(BF16)
    do_out[...] = do_t
    stat_out[...] = jnp.zeros(stat_out.shape, F32)
    stat_out[0:HEADS, :] = lse
    for h in range(HEADS):
        rows = slice(HD * h, HD * h + HD)
        stat_out[16 + h : 17 + h, :] = jnp.sum(
            do_t[rows].astype(F32) * o_ref[rows, :], axis=0, keepdims=True
        )
    return dx1, grad_gain


def project_back(dq_part, dkv_part, x, dx1, gain, wq, wk, wv, cos, sin, dqkv_out):
    for h in range(HEADS + 3):
        part, base, many = (dq_part, HD * h, 4) if h < HEADS else (dkv_part, TOK * (h - HEADS), 8)
        a = sum(part[i, base : base + 32, :].astype(F32) for i in range(many))
        b = sum(part[i, base + 32 : base + 64, :].astype(F32) for i in range(many))
        dqkv_out[HD * h : HD * h + 32, :] = (a * cos + b * sin).astype(BF16)
        dqkv_out[HD * h + 32 : HD * h + 64, :] = (b * cos - a * sin).astype(BF16)
    for g in range(3):
        base = TOK * g + HD
        dqkv_out[D + KV + HD * g : D + KV + HD * g + HD, :] = sum(
            dkv_part[i, base : base + HD, :].astype(F32) for i in range(8)
        ).astype(BF16)
    dh1 = (
        dot(dqkv_out[0:D, :], wq[...], 0, 1)
        + dot(dqkv_out[D : D + KV, :], wk[...], 0, 0)
        + dot(dqkv_out[D + KV :, :], wv[...], 0, 0)
    )
    inverse = lax.rsqrt(jnp.mean(x * x, axis=-1, keepdims=True) + EPS)
    dy, grad_gain = norm_back(x, inverse, gain, dh1)
    return dx1 + dy, grad_gain


Q_T = sds((D, TOK), BF16)
KV_T = sds((2 * KV, TOK), BF16)
H_S = sds((TOK, D), BF16)
X_S = sds((TOK, D), F32)
X_T = sds((D, TOK), F32)
F_S = sds((TOK, FF), F32)
FB_S = sds((TOK, FF), BF16)
ST_S = sds((32, TOK), F32)
G_S = sds((1, D), F32)


ANY = pl.BlockSpec(memory_space=pl.ANY)
HBM = pl.BlockSpec(memory_space=pltpu.HBM)


class Lazy:
    def __init__(self, src, buf, sem):
        self.copy = pltpu.make_async_copy(src, buf, sem)
        self.copy.start()
        self.buf, self.waited = buf, False

    def ref(self):
        if not self.waited:
            self.copy.wait()
            self.waited = True
        return self.buf

    def __getitem__(self, index):
        return self.ref()[index]


def fetch(srcs, bufs, sems):
    return [Lazy(src, buf, sems.at[i]) for i, (src, buf) in enumerate(zip(srcs, bufs))]


def buffers(*arrays):
    return [pltpu.VMEM(a.shape, a.dtype) for a in arrays] + [DMA((len(arrays),))]


def begin_kernel(out):
    out[...] = jnp.zeros(out.shape, F32)


def begin():
    return pl.pallas_call(
        begin_kernel,
        name="begin",
        out_shape=sds((8, TOK), F32),
        out_specs=VM,
        compiler_params=params(None, 1 << 20),
        cost_estimate=cost(30),
    )()


def mirrored(ctx, src, dst, send, recv):
    move = remote(src, dst, send.at[0], recv, (ctx.row, 8 * (7 - ctx.n) + ctx.w))
    stay = pltpu.make_async_copy(src, dst, send.at[1])

    def both(if_one, if_zero):
        pl.when(ctx.core == 1)(if_one)
        pl.when(ctx.core == 0)(if_zero)

    return lambda: both(move.start, stay.start), lambda: both(move.wait, stay.wait)


def first_part(ctx, ins, outs, scratch):
    tok, ids_ref, ga, wq, wk, wv, _ = ins
    x_out, h_out, starts_ref, cos_ref, sin_ref, q_save, kv_save = outs
    (tok_in, ids_all, starts_all, ysend, yrecv, xsend, xrecv, tsend, trecv,
     bq, bk, bv, bsem, ssem) = scratch
    row, n, w = ctx.row, ctx.n, ctx.w
    seq = 8 * n + w
    get_ids = pltpu.make_async_copy(ids_ref, ids_all.at[seq], ssem.at[0])
    get_ids.start()
    wq, wk, wv = fetch([wq, wk, wv], [bq, bk, bv], bsem)
    get_ids.wait()
    ctx.ready()
    start, wait = mirrored(ctx, tok, tok_in, tsend, trecv)
    start()
    sent = []
    for k in range(1, 8):
        cp = remote(
            ids_all.at[seq], ids_all.at[seq], ysend.at[k], yrecv.at[k],
            (row, 8 * n + lax.rem(w + k, 8)),
        )
        cp.start()
        sent.append(cp)
    for cp in sent:
        cp.wait()
    own = ids_all.at[pl.ds(8 * n, 8)]
    sent = []
    for k in range(1, 8):
        cp = remote(own, own, xsend.at[k], xrecv.at[k], (row, 8 * lax.rem(n + k, 8) + w))
        cp.start()
        sent.append(cp)
    wait()
    x = tok_in[...].T
    x_out[...] = x
    raw = project(x, as_row(ga), wq, wk, wv, h_out)
    for cp in sent:
        cp.wait()

    ids = jnp.concatenate([ids_all[i] for i in range(64)], axis=0)
    total = jnp.zeros((64, TOK), jnp.int32)
    for doc in range(DOCS - 1):
        count = jnp.where(ids == doc, 1.0, 0.0)
        count = jnp.sum(jnp.sum(count, axis=0, keepdims=True), axis=1, keepdims=True)
        total = total + jnp.where(ids > doc, count.astype(jnp.int32), 0)
    starts_all[...] = total[:, None, :]
    for half in range(2):
        octet = n if half == 0 else 7 - n
        for y in range(4):
            starts_ref[half, :, TOK * y : TOK * y + TOK] = starts_all[8 * octet + 2 * y + half]
    mine = 8 * octet_of(n, w) + w
    pos = mine * TOK + lax.broadcasted_iota(jnp.int32, (1, TOK), 1) - starts_all[mine]
    line = lax.broadcasted_iota(jnp.int32, (32, TOK), 0).astype(F32)
    angle = jnp.exp(line * (-2.0 / HD) * math.log(10000.0)) * pos.astype(F32)
    cos_ref[...] = jnp.cos(angle)
    sin_ref[...] = jnp.sin(angle)
    rotate(*raw, cos_ref[...], sin_ref[...], ctx.q_own, ctx.kv_own)

    saves = [
        pltpu.make_async_copy(ctx.q_all, q_save, ssem.at[1]),
        pltpu.make_async_copy(ctx.kv_all, kv_save, ssem.at[2]),
    ]

    def arrived():
        for cp in saves:
            cp.start()

    def end():
        for cp in saves:
            cp.wait()

    return None, arrived, end


def middle_part(ctx, ins, outs, scratch):
    part, stat, x, cot, ga, wq, wk, wv, wo, gm, wg, wu, wd, cos, sin = ins
    g_out, h_out, x_out, x1_out, h2_out, inv_out, gate_out, up_out, hid_out, o_out, lse_out = outs
    gate_s, up_s, ssem, cot_in, csend, crecv = scratch
    start, wait = mirrored(ctx, cot, cot_in, csend, crecv)
    saves = [
        pltpu.make_async_copy(gate_s, gate_out, ssem.at[0]),
        pltpu.make_async_copy(up_s, up_out, ssem.at[1]),
    ]
    combine(part, stat, o_out, lse_out)
    x1, h2, inverse, gate, up, hid, x2 = feed_forward(
        x[...], o_out[...].astype(BF16), wo, as_row(gm), wg, wu, wd
    )
    x_out[...] = x2
    raw = project(x2, as_row(ga), wq, wk, wv, h_out)
    rotate(*raw, cos[...], sin[...], ctx.q_own, ctx.kv_own)
    ctx.ready()

    def late():
        x1_out[...] = x1
        h2_out[...] = h2
        inv_out[...] = jnp.broadcast_to(inverse, inv_out.shape)
        gate_s[...] = gate
        up_s[...] = up
        hid_out[...] = hid
        for cp in saves:
            cp.start()
        start()

    def end():
        for cp in saves:
            cp.wait()
        wait()
        g_out[...] = cot_in[...].T

    return late, None, end


def turn_part(ctx, ins, outs, scratch):
    part, stat, x, g, wo, gm, wg, wu, wd = ins
    h2_out, hid_out, ob_out, gmo, dgate, dup, da, dx1_out, gg_out = outs
    o_s, lse_s = scratch
    combine(part, stat, o_s, lse_s)
    ob = o_s[...].astype(BF16)
    ob_out[...] = ob
    x1, h2, inverse, gate, up, hid, x2 = feed_forward(
        x[...], ob, wo, as_row(gm), wg, wu, wd
    )
    h2_out[...] = h2
    hid_out[...] = hid
    ctx.extra[...] = x2.T
    dx1, gg = feed_back(
        g[...], x1, inverse, gate, up, wo, as_row(gm), wg, wu, wd, o_s,
        lse_s[0:HEADS, :], ctx.do_own, ctx.st_own, gmo, dgate, dup, da
    )
    dx1_out[...] = dx1
    gg_out[...] = gg


def between_part(ctx, ins, outs, scratch):
    (dq, dkv, x, dx1, ga, wq, wk, wv, cos, sin, x1, inv, gate, up, wo, gm, wg, wu, wd, o, lse,
     ob1, da1, h20, h21, dg1, du1, hid0, hid1, gm1) = ins
    dqkv_out, gga_out, da, dx1_out, ggm_out, ob_out = outs
    gmo, dgate, dup = scratch
    g, gga = project_back(
        dq, dkv, x[...], dx1[...], as_row(ga), wq, wk, wv, cos[...], sin[...], dqkv_out
    )
    gga_out[...] = gga
    dx0, ggm = feed_back(
        g, x1[...], inv[:, 0:1], gate[...], up[...], wo, as_row(gm), wg, wu, wd, o,
        lse[0:HEADS, :], ctx.do_own, ctx.st_own, gmo, dgate, dup, da
    )
    dx1_out[...] = dx0
    ggm_out[...] = ggm
    ob_out[...] = o[...].astype(BF16)

    def grads():
        early_grads(
            ob_out, ob1, da, da1, h20, h21, dgate, dg1, dup, du1, hid0, hid1, gmo, gm1, ctx.extra
        )

    return grads


class Torus:
    def __init__(self, row, n, w):
        self.core = lax.rem(w, 2)
        self.spot = (n // 2, w // 2, 2 * row + lax.rem(n, 2))
        self.partner = self.device(self.spot, 1 - self.core)

    def device(self, spot, core):
        x, y, z = spot
        return (z // 2, ((x * 2 + lax.rem(z, 2)) * 4 + y) * 2 + core)

    def along(self, axis, k):
        to = list(self.spot)
        to[axis] = lax.rem(self.spot[axis] + k, 4)
        return self.device(to, self.core), to[axis]


class Reduce:
    def __init__(self, torus, u, send, recv):
        self.torus, self.u, self.send, self.recv = torus, u, send, recv
        self.box = {}

    def go(self, stage, p, k, src, dst, peer):
        cp = remote(src, dst, self.send.at[stage, p, k], self.recv.at[stage, p, k], peer)
        cp.start()
        self.box.setdefault((stage, p), []).append(cp)

    def got(self, stage, p):
        for cp in self.box[stage, p]:
            cp.wait_recv()

    def finish(self):
        for cps in self.box.values():
            for cp in cps:
                cp.wait_send()

    def exchange(self, src, came):
        u, core = self.u, self.torus.core
        for p in range(3):
            self.go(
                0, p, 0, src.at[pl.ds(48 * u * (1 - core) + 16 * u * p, 16 * u)],
                came.at[pl.ds(16 * u * p, 16 * u)], self.torus.partner,
            )

    def first(self, p, src, came, half, one):
        u = self.u
        self.got(0, p)

        def quarter(i, carry):
            at = pl.ds(16 * u * p + 4 * u * i, 4 * u)
            mine = src[pl.ds(48 * u * self.torus.core + 16 * u * p + 4 * u * i, 4 * u)]
            half[at] = (mine.astype(F32) + came[at].astype(F32)).astype(BF16)
            return carry

        lax.fori_loop(0, 4, quarter, 0)
        for k in range(1, 4):
            peer, at = self.torus.along(p, k)
            self.go(1, p, k, half.at[pl.ds(16 * u * p + 4 * u * at, 4 * u)], one.at[p, k - 1], peer)

    def second(self, p, half, one, gather, two):
        u = self.u
        self.got(1, p)
        mine = half[pl.ds(16 * u * p + 4 * u * self.torus.spot[p], 4 * u)]
        gather[p] = (mine.astype(F32) + sum(one[p, k].astype(F32) for k in range(3))).astype(BF16)
        for k in range(1, 4):
            peer, at = self.torus.along((p + 1) % 3, k)
            self.go(2, p, k, gather.at[p, pl.ds(u * at, u)], two.at[p, k - 1], peer)

    def third(self, p, gather, two, three):
        u = self.u
        self.got(2, p)
        c = self.torus.spot[(p + 2) % 3]
        mine = gather[p, pl.ds(u * self.torus.spot[(p + 1) % 3], u)]
        three[p, c] = (mine.astype(F32) + sum(two[p, k].astype(F32) for k in range(3))).astype(BF16)
        for k in range(1, 4):
            self.go(3, p, k, three.at[p, c], three.at[p, c], self.torus.along((p + 2) % 3, k)[0])

    def fourth(self, p, three, mid):
        u = self.u
        self.got(3, p)
        at = pl.ds(u * self.torus.spot[(p + 1) % 3], u)
        mid[p, at] = sum(three[p, k].astype(F32) for k in range(4)).astype(BF16)
        for k in range(1, 4):
            self.go(4, p, k, mid.at[p, at], mid.at[p, at], self.torus.along((p + 1) % 3, k)[0])

    def fifth(self, p, mid, out, chunk=0, chunks=1):
        u = self.u
        size = 4 * u // chunks
        base = 48 * u * self.torus.core + 16 * u * p + 4 * u * self.torus.spot[p]
        at = pl.ds(base + size * chunk, size)
        out[at] = mid[p, size * chunk : size * chunk + size]
        for k in range(1, 4):
            self.go(7 + chunk, p, k, out.at[at], out.at[at], self.torus.along(p, k)[0])

    def sixth(self, p, out, chunks=1):
        u = self.u
        for chunk in range(chunks):
            self.got(7 + chunk, p)
        at = pl.ds(48 * u * self.torus.core + 16 * u * p, 16 * u)
        self.go(6, p, 0, out.at[at], out.at[at], self.torus.partner)


def units(count, *lead):
    return tuple(lead) + (count, 16, 256)


EARLY, LATE = 7, 2


W3 = 12 * TOK


class Spread:
    def __init__(self, row, n, w, send, recv):
        self.core = lax.rem(w, 2)
        self.y = w // 2
        self.own = self.core * 4 + self.y
        self.row, self.n = row, n
        self.partner = (row, 8 * n + 2 * self.y + 1 - self.core)
        self.send, self.recv = send, recv
        self.first, self.passed = {}, {}

    def chip(self, k):
        return (self.row, 8 * self.n + 2 * lax.rem(self.y + k, 4) + self.core)

    def start(self, part, ref):
        self.first[part], self.passed[part] = [], []
        for k in range(1, 4):
            cp = remote(ref(self.own), ref(self.own), self.send.at[part, k], self.recv.at[part, k],
                        self.chip(k))
            cp.start()
            self.first[part].append(cp)
        self.hand(part, ref, self.own, 4)

    def hand(self, part, ref, slot, k):
        cp = remote(ref(slot), ref(slot), self.send.at[part, k], self.recv.at[part, k], self.partner)
        cp.start()
        self.passed[part].append(cp)

    def forward(self, part, ref):
        for k in range(1, 4):
            self.first[part][k - 1].wait_recv()
            self.hand(part, ref, self.core * 4 + lax.rem(self.y + 4 - k, 4), 4 + k)

    def arrive(self, part):
        for cp in self.passed[part]:
            cp.wait_recv()

    def finish(self):
        for part in self.first:
            for cp in self.first[part] + self.passed[part]:
                cp.wait_send()


def turns(n):
    return (n + 2) // 2


def fill_masks(bias, starts_ref, n, w):
    turn = turns(n)

    def one(t, carry):
        sel = jnp.where(t >= turn, 1, 0)
        kc = jnp.where(t >= turn, t - turn, t)
        line = lax.broadcasted_iota(jnp.int32, (256, 1), 0)
        key = (2 * kc + line // TOK) * 1024 + w * TOK + lax.rem(line, TOK)
        col = lax.broadcasted_iota(jnp.int32, (1, 512), 1)
        octet = jnp.where(sel == 0, n, 7 - n)
        query = octet * 1024 + (2 * (col // TOK) + sel) * TOK + lax.rem(col, TOK)
        bias[t] = jnp.where((key >= starts_ref[sel]) & (key <= query), 0.0, MASKED)
        return carry

    lax.fori_loop(0, 5, one, 0)


def over_keys(n, sel, step):
    octet = jnp.where(sel == 0, n, 7 - n)
    base = jnp.where(sel == 0, 0, turns(n))
    whole = (octet + 1) // 2

    def chunk(kc, carry):
        step(base + kc, kc, 2 * TOK)
        return carry

    lax.fori_loop(0, whole, chunk, 0)

    @pl.when(lax.rem(octet + 1, 2) == 1)
    def _():
        step(base + whole, whole, TOK)


def three_heads(ref, sel, g):
    return jnp.concatenate(
        [
            ref[4 * sel + y, HD * h : HD * h + HD, :]
            for h in range(3 * g, 3 * g + 3)
            for y in range(4)
        ],
        axis=1,
    )


def key_blocks(ref, kc, first, keys):
    return jnp.concatenate(
        [ref[2 * kc + i, first : first + HD, :] for i in range(keys // TOK)], axis=1
    )


def by_chip(value, y):
    return jnp.concatenate(
        [value[:, 512 * j + TOK * y : 512 * j + TOK * y + TOK] for j in range(3)], axis=0
    )


class Context:
    pass


def attend_kernel(first, n_in, n_out, *refs):
    ins, refs = refs[:n_in], refs[n_in:]
    outs, refs = refs[:n_out], refs[n_out:]
    if first:
        part_ref, stat_ref, q_all, kv_all = refs[:4]
    else:
        q_all, kv_all, part_ref, stat_ref = refs[:4]
    (k_nat, bias, top, total, acc, o_send, o_recv, r_send, r_recv, o_y, s_y,
     qs, qr, ks, kr, ps, pr, ys, yr) = refs[4:23]
    starts_ref = outs[2] if first else ins[-1]
    row, seq, n, w = place()
    bar = greet(row, n, w)
    core, y = lax.rem(w, 2), w // 2
    own_k = octet_of(n, w)
    queries = Spread(row, n, w, qs, qr)
    ctx = Context()
    ctx.row, ctx.n, ctx.w, ctx.core = row, n, w, core
    ctx.q_own, ctx.kv_own = q_all.at[queries.own], kv_all.at[own_k]
    ctx.q_all, ctx.kv_all = q_all, kv_all
    ctx.ready = lambda: pl.semaphore_wait(bar, 14)
    if first:
        late, arrived, end = first_part(ctx, ins, outs, refs[23:])
    else:
        late, arrived, end = middle_part(ctx, ins[:-1], outs, refs[23:])

    def q_part(g):
        return lambda slot: q_all.at[slot, pl.ds(192 * g, 192)]

    keys = {}
    for g in range(3):
        keys[g] = []
        for k in range(1, 8):
            block = kv_all.at[own_k, pl.ds(TOK * g, TOK)]
            cp = remote(
                block, block, ks.at[g, k], kr.at[g, k], (row, 8 * lax.rem(n + k, 8) + w)
            )
            cp.start()
            keys[g].append(cp)
        queries.start(g, q_part(g))
    fill_masks(bias, starts_ref, n, w)
    queries.forward(0, q_part(0))

    def phase(g, sel):
        top[...] = jnp.full(top.shape, LOWEST, F32)
        total[...] = jnp.zeros(total.shape, F32)
        acc[...] = jnp.zeros(acc.shape, F32)

        def step(at, kc, keys):
            scores = dot(k_nat[kc, 0:keys], three_heads(q_all, sel, g), 1, 0)
            mask = bias[at, 0:keys]
            weights, shrinks = [], []
            for j in range(3):
                cols = slice(512 * j, 512 * j + 512)
                s = scores[:, cols] + mask
                old = top[:, cols]
                new = jnp.maximum(old, jnp.max(s, axis=0, keepdims=True))
                p = jnp.exp2(s - new)
                shrink = jnp.exp2(old - new)
                top[:, cols] = new
                total[:, cols] = total[:, cols] * shrink + jnp.sum(p, axis=0, keepdims=True)
                weights.append(p.astype(BF16))
                shrinks.append(shrink)
            values = key_blocks(kv_all, kc, TOK * g + HD, keys)
            acc[...] = acc[...] * jnp.concatenate(shrinks, axis=1) + dot(
                values, jnp.concatenate(weights, axis=1), 1, 0
            )

        over_keys(n, sel, step)

    pairs, flying = [], []
    for g in range(3):
        for cp in keys[g]:
            cp.wait_recv()
        for j in range(8):
            k_nat[j // 2, (j % 2) * TOK : (j % 2) * TOK + TOK, :] = jnp.transpose(
                kv_all[j, TOK * g : TOK * g + HD, :]
            )
        queries.arrive(g)
        if g == 2 and arrived is not None:
            arrived()
        phase(g, 1 - core)
        o_send[g] = acc[...].astype(BF16)
        r_send[g, 0] = top[...]
        r_send[g, 1] = total[...]
        both = [
            remote(o_send.at[g], o_recv.at[g], ps.at[0, g], pr.at[0, g], queries.partner),
            remote(r_send.at[g], r_recv.at[g], ps.at[1, g], pr.at[1, g], queries.partner),
        ]
        for cp in both:
            cp.start()
        pairs += both
        if g < 2:
            queries.forward(g + 1, q_part(g + 1))
        if g == 0 and late is not None:
            late()
        phase(g, core)
        for cp in both:
            cp.wait_recv()
        new = jnp.maximum(top[...], r_recv[g, 0])
        mine = jnp.exp2(top[...] - new)
        theirs = jnp.exp2(r_recv[g, 0] - new)
        length = total[...] * mine + r_recv[g, 1] * theirs
        out = (acc[...] * mine + o_recv[g].astype(F32) * theirs).astype(BF16)
        for i in range(4):
            o_y[g, i] = by_chip(out, i)
            for j in range(3):
                cols = slice(512 * j + TOK * i, 512 * j + TOK * i + TOK)
                s_y[g, i, j : j + 1, :] = new[:, cols]
                s_y[g, i, 4 + j : 5 + j, :] = length[:, cols]
        for k in range(1, 4):
            to = lax.rem(y + k, 4)
            peer = queries.chip(k)
            for cp in (
                remote(o_y.at[g, to], part_ref.at[y, pl.ds(192 * g, 192)], ys.at[0, g, k],
                       yr.at[0, g, k], peer),
                remote(s_y.at[g, to], stat_ref.at[y, pl.ds(8 * g, 8)], ys.at[1, g, k],
                       yr.at[1, g, k], peer),
            ):
                cp.start()
                flying.append(cp)
        part_ref[y, 192 * g : 192 * g + 192, :] = o_y[g, y]
        stat_ref[y, 8 * g : 8 * g + 8, :] = s_y[g, y]
    queries.finish()
    for g in range(3):
        for cp in keys[g]:
            cp.wait_send()
    for cp in pairs:
        cp.wait_send()
    for cp in flying:
        cp.wait()
    if end is not None:
        end()


GATHERED = [((8, D, TOK), BF16), ((8, 2 * KV, TOK), BF16)]


def attend(first, ins, specs, outs, scratch, collective, limit):
    count = len(outs)
    here = [] if first else [sds(*a) for a in GATHERED]
    there = [pltpu.VMEM(*a) for a in GATHERED] if first else []
    outs = outs + [(o, VM) for o in here + [sds((4, D, TOK), BF16), sds((4, 24, TOK), F32)]]
    return pl.pallas_call(
        functools.partial(attend_kernel, first, len(ins), count),
        name="attend_first" if first else "attend",
        out_shape=tuple(o for o, _ in outs),
        in_specs=specs,
        out_specs=tuple(spec for _, spec in outs),
        scratch_shapes=there
        + [
            pltpu.VMEM((4, 256, HD), BF16),
            pltpu.VMEM((5, 256, 512), F32),
            pltpu.VMEM((1, W3), F32),
            pltpu.VMEM((1, W3), F32),
            pltpu.VMEM((HD, W3), F32),
            pltpu.VMEM((3, HD, W3), BF16),
            pltpu.VMEM((3, HD, W3), BF16),
            pltpu.VMEM((3, 2, 1, W3), F32),
            pltpu.VMEM((3, 2, 1, W3), F32),
            pltpu.VMEM((3, 4, 192, TOK), BF16),
            pltpu.VMEM((3, 4, 8, TOK), F32),
            DMA((3, 8)), DMA((3, 8)), DMA((3, 8)), DMA((3, 8)),
            DMA((2, 3)), DMA((2, 3)), DMA((2, 3, 4)), DMA((2, 3, 4)),
        ]
        + scratch,
        compiler_params=params(collective, limit),
        cost_estimate=cost(30),
    )(*ins)


def attend_back_kernel(carry_sum, n_in, n_out, n_more, *refs):
    ins, refs = refs[:n_in], refs[n_in:]
    outs, refs = refs[:n_out], refs[n_out:]
    (dq_part, dkv_part, extra_out, do_all, st_all, k_nat, v_nat, bias, rows_s, dq, dq_other, dkv, q_send,
     q_recv, q_y, kv_low, extra, qs, qr, ks, kr, ps, pr, ys, yr, es, er) = refs[:27]
    more, scratch = refs[27 : 27 + n_more], refs[27 + n_more :]
    q_all, kv_all, starts_ref = ins[-3:]
    ctx = Context()
    ctx.q_all, ctx.kv_all = q_all, kv_all
    row, seq, n, w = place()
    bar = greet(row, n, w)
    torus = Torus(row, n, w)
    if carry_sum:
        came, one, gather, two, three = more
        half = extra.at[pl.ds(48 * EARLY * lax.rem(w, 2), 48 * EARLY)]
        for k in range(1, 4):
            pl.semaphore_signal(bar, inc=1, device_id=torus.along(2, k)[0], device_id_type=MESH)
        early = Reduce(torus, EARLY, es, er)
    else:
        (extra_in,) = more
        move = remote(extra, extra_in, es, er, (row, 8 * (7 - n) + w))
    core, y = lax.rem(w, 2), w // 2
    own_k = octet_of(n, w)
    grads = Spread(row, n, w, qs, qr)
    ctx.do_own, ctx.st_own, ctx.extra = do_all.at[grads.own], st_all.at[grads.own], extra
    make = between_part if carry_sum else turn_part
    grads_of = make(ctx, ins[:-3], outs, scratch)
    pl.semaphore_wait(bar, 17 if carry_sum else 14)

    def part(g):
        return lambda slot: do_all.at[slot, pl.ds(192 * g, 192)]

    def stats(slot):
        return st_all.at[slot]

    grads.start(3, stats)
    for g in range(3):
        grads.start(g, part(g))
    if carry_sum:
        grads_of()
        early.exchange(extra, came)
    fill_masks(bias, starts_ref, n, w)
    for g in range(3):
        for j in range(8):
            at = slice((j % 2) * TOK, (j % 2) * TOK + TOK)
            k_nat[g, j // 2, at, :] = jnp.transpose(kv_all[j, TOK * g : TOK * g + HD, :])
            v_nat[g, j // 2, at, :] = jnp.transpose(kv_all[j, TOK * g + HD : TOK * g + TOK, :])
    grads.forward(3, stats)
    grads.forward(0, part(0))
    if carry_sum:
        for p in range(3):
            early.first(p, extra, came, half, one)
    if not carry_sum:

        @pl.when(core == 1)
        def _():
            move.start()

    def phase(g, sel, dq):
        dq[...] = jnp.zeros(dq.shape, F32)
        for i, first in enumerate((0, 16)):
            for j in range(3):
                for c in range(4):
                    at = 512 * j + TOK * c
                    line = first + 3 * g + j
                    rows_s[i, :, at : at + TOK] = st_all[4 * sel + c, line : line + 1, :]

        def step(at, kc, keys):
            qt = three_heads(q_all, sel, g)
            dt = three_heads(do_all, sel, g)
            scores = dot(k_nat[g, kc, 0:keys], qt, 1, 0)
            dp = dot(v_nat[g, kc, 0:keys], dt, 1, 0)
            mask = bias[at, 0:keys]
            ps_, ds_ = [], []
            for j in range(3):
                cols = slice(512 * j, 512 * j + 512)
                p = jnp.exp2(scores[:, cols] + mask - rows_s[0, :, cols])
                ds_.append((p * (dp[:, cols] - rows_s[1, :, cols])).astype(BF16))
                ps_.append(p.astype(BF16))
            p = jnp.concatenate(ps_, axis=1)
            ds = jnp.concatenate(ds_, axis=1)
            dkv[kc, 0:HD, 0:keys] += dot(ds, qt, 1, 1).T
            dkv[kc, HD:, 0:keys] += dot(p, dt, 1, 1).T
            dq[...] += dot(key_blocks(kv_all, kc, TOK * g, keys), ds, 1, 0)

        over_keys(n, sel, step)

    pairs, flying = [], []
    for g in range(3):
        dkv[...] = jnp.zeros(dkv.shape, F32)
        if g == 0:
            phase(g, core, dq)
            grads.forward(1, part(1))
            grads.arrive(3)
        grads.arrive(g)
        phase(g, 1 - core, dq_other)
        q_send[g] = (dq_other[...] * SCALE).astype(BF16)
        pair = remote(q_send.at[g], q_recv.at[g], ps.at[g], pr.at[g], grads.partner)
        pair.start()
        pairs.append(pair)
        if g == 1 and carry_sum:
            for p in range(3):
                early.second(p, half, one, gather, two)
        if g == 1:
            grads.forward(2, part(2))
        elif g == 2 and carry_sum:
            for p in range(3):
                early.third(p, gather, two, three)
        if g > 0:
            phase(g, core, dq)
        for j in range(8):
            cols = slice((j % 2) * TOK, (j % 2) * TOK + TOK)
            kv_low[g, j, 0:HD, :] = (dkv[j // 2, 0:HD, cols] * (SCALE / EXP_SCALE)).astype(BF16)
            kv_low[g, j, HD:, :] = dkv[j // 2, HD:, cols].astype(BF16)
        for k in range(1, 8):
            to = lax.rem(n + k, 8)
            cp = remote(
                kv_low.at[g, octet_of(to, w)], dkv_part.at[n, pl.ds(TOK * g, TOK)], ks.at[g, k],
                kr.at[g, k], (row, 8 * to + w),
            )
            cp.start()
            flying.append(cp)
        pair.wait_recv()
        out = (dq[...] * SCALE + q_recv[g].astype(F32)).astype(BF16)
        for i in range(4):
            q_y[g, i] = by_chip(out, i)
        for k in range(1, 4):
            to = lax.rem(y + k, 4)
            cp = remote(q_y.at[g, to], dq_part.at[y, pl.ds(192 * g, 192)], ys.at[g, k], yr.at[g, k],
                        grads.chip(k))
            cp.start()
            flying.append(cp)
        dkv_part[n, TOK * g : TOK * g + TOK, :] = kv_low[g, own_k]
        dq_part[y, 192 * g : 192 * g + 192, :] = q_y[g, y]
        if carry_sum:
            for p in range(3):
                if g == 2:
                    early.fourth(p, three, extra_out)
    grads.finish()
    for cp in pairs:
        cp.wait_send()
    for cp in flying:
        cp.wait()
    if carry_sum:
        for p in range(3):
            early.got(4, p)
        early.finish()
    else:

        @pl.when(core == 1)
        def _():
            move.wait()
            extra_out[...] = extra_in[...]

        @pl.when(core == 0)
        def _():
            extra_out[...] = extra[...]


def attend_back(carry_sum, ins, specs, outs, scratch, limit):
    if carry_sum:
        u = EARLY
        extra_shape = sds(units(4 * u, 3), BF16)
        extra = pltpu.VMEM(units(96 * u), BF16)
        sems = [DMA((5, 3, 4))] * 2
        more = [
            pltpu.VMEM(shape, BF16)
            for shape in (
                units(48 * u), units(4 * u, 3, 3), units(4 * u, 3), units(u, 3, 3), units(u, 3, 4),
            )
        ]
    else:
        extra_shape = X_T
        extra = pltpu.VMEM((D, TOK), F32)
        sems = [DMA, DMA]
        more = [pltpu.VMEM((D, TOK), F32)]
    return pl.pallas_call(
        functools.partial(attend_back_kernel, carry_sum, len(ins), len(outs), len(more)),
        name="attend_back_sum" if carry_sum else "attend_back",
        out_shape=tuple(outs + [sds((4, D, TOK), BF16), sds((8, 2 * KV, TOK), BF16), extra_shape]),
        in_specs=specs,
        out_specs=(VM,) * (len(outs) + 3),
        scratch_shapes=[
            pltpu.VMEM((8, D, TOK), BF16),
            pltpu.VMEM((8, 32, TOK), F32),
            pltpu.VMEM((3, 4, 256, HD), BF16),
            pltpu.VMEM((3, 4, 256, HD), BF16),
            pltpu.VMEM((5, 256, 512), F32),
            pltpu.VMEM((2, 1, W3), F32),
            pltpu.VMEM((HD, W3), F32),
            pltpu.VMEM((HD, W3), F32),
            pltpu.VMEM((4, TOK, 256), F32),
            pltpu.VMEM((3, HD, W3), BF16),
            pltpu.VMEM((3, HD, W3), BF16),
            pltpu.VMEM((3, 4, 192, TOK), BF16),
            pltpu.VMEM((3, 8, TOK, TOK), BF16),
            extra,
            DMA((4, 8)), DMA((4, 8)), DMA((3, 8)), DMA((3, 8)),
            DMA((3,)), DMA((3,)), DMA((3, 4)), DMA((3, 4)),
        ]
        + sems
        + more
        + scratch,
        compiler_params=params(5 if carry_sum else 3, limit),
        cost_estimate=cost(40),
    )(*ins)


def both_rows(a, b):
    return jnp.concatenate([a[...], b[...]], axis=0)


def as_units(value):
    return value.astype(BF16).reshape(units(value.shape[0] // 16))


def early_grads(oa, ob, daa, dab, h2a, h2b, dga, dgb, dua, dub, hida, hidb, gma, gmb, g_out):
    ot = jnp.concatenate([oa[...], ob[...]], axis=1)
    h2t = both_rows(h2a, h2b).T
    gmt = both_rows(gma, gmb).T
    for i in range(6):
        cols = slice(256 * i, 256 * i + 256)
        for t, (lhs, a, b) in enumerate(((h2t, dga, dgb), (h2t, dua, dub), (gmt, hida, hidb))):
            rhs = jnp.concatenate([a[:, cols], b[:, cols]], axis=0)
            g_out[36 * (6 * t + i) : 36 * (6 * t + i) + 36] = as_units(dot(lhs, rhs, 1, 0))
    da = both_rows(daa[:, 128:384], dab[:, 128:384])
    g_out[648:672] = as_units(dot(ot[0:384], da, 1, 0))


def late_grads(h1a, h1b, dqa, dqb, oa, ob, daa, dab, g_out):
    h1t = both_rows(h1a, h1b).T
    ot = jnp.concatenate([oa[...], ob[...]], axis=1)
    dat = both_rows(daa, dab).T

    def rows(first, last):
        return jnp.concatenate([dqa[first:last, :], dqb[first:last, :]], axis=1)

    g_out[0:36] = as_units(dot(h1t, rows(0, 256), 1, 1))
    g_out[36:72] = as_units(dot(h1t, rows(256, 512), 1, 1))
    mixed = [dot(h1t, rows(512, 640), 1, 1), dot(ot, dat[0:128], 1, 1)]
    g_out[72:108] = as_units(jnp.concatenate(mixed, axis=1))
    g_out[108:120] = as_units(dot(ot[384:576], dat[128:384], 1, 1))
    low = jnp.concatenate([dat[384:576], jnp.zeros((64, 256), BF16)], axis=0)
    high = jnp.concatenate([jnp.zeros((192, 256), BF16), rows(640, 704)], axis=0)
    g_out[120:156] = as_units(dot(ot, low, 1, 1) + dot(h1t, high, 1, 1))
    g_out[156:192] = as_units(dot(h1t, rows(704, 960), 1, 1))


def spread_kernel(
    early, late, x_in, g_in, gains, ga_out, gm_out, x_out, g_out, gate_out, up_out, down_out, q_out, k_out, v_out, o_out, big, small, kt, vt, sems
):
    def block(ref, first, count=36):
        return ref[first : first + count].reshape(16 * count, 256).astype(F32)

    ga_out[...] = gains[0:1, :].reshape(D)
    gm_out[...] = gains[1:2, :].reshape(D)
    cps = [
        pltpu.make_async_copy(x_in, x_out, sems.at[22]),
        pltpu.make_async_copy(g_in, g_out, sems.at[23]),
    ]
    for cp in cps:
        cp.start()
    for t, ref in enumerate((gate_out, up_out, down_out)):
        for i in range(6):
            rows = pl.ds(96 * i, 96)
            for c in range(6):
                big[t, rows, 256 * c : 256 * c + 256] = block(early, 36 * (6 * t + c) + 6 * i, 6)
            cp = pltpu.make_async_copy(big.at[t, rows], ref.at[rows], sems.at[6 * t + i])
            cp.start()
            cps.append(cp)
    small[0, :, 0:256] = block(late, 0)
    small[0, :, 256:512] = block(late, 36)
    mixed = block(late, 72)
    small[0, :, 512:576] = mixed[:, 0:64]
    small[1, :, 0:128] = mixed[:, 128:256]
    kt[0:64, :] = mixed[:, 0:128].T[64:128]
    small[1, 0:384, 128:384] = block(early, 648, 24)
    small[1, 384:576, 128:384] = block(late, 108, 12)
    mixed = block(late, 120)
    small[1, :, 384:576] = mixed[:, 0:192]
    kt[64:128, :] = mixed[:, 128:256].T[64:128]
    last = block(late, 156).T
    kt[128:192, :] = last[0:64]
    vt[...] = last[64:256]
    for i, (src, dst) in enumerate(
        ((small.at[0], q_out), (small.at[1], o_out), (kt, k_out), (vt, v_out))
    ):
        cp = pltpu.make_async_copy(src, dst, sems.at[18 + i])
        cp.start()
        cps.append(cp)
    for cp in cps:
        cp.wait()


def spread(*ins):
    return pl.pallas_call(
        spread_kernel,
        name="spread",
        out_shape=(
            sds((D,), F32), sds((D,), F32), X_T, X_T, sds((D, FF), F32), sds((D, FF), F32), sds((D, FF), F32), sds((D, D), F32),
            sds((KV, D), F32), sds((KV, D), F32), sds((D, D), F32),
        ),
        in_specs=[VM] * 5,
        out_specs=(VM,) * 2 + (ANY,) * 9,
        scratch_shapes=[
            pltpu.VMEM((3, D, FF), F32),
            pltpu.VMEM((2, D, D), F32),
            pltpu.VMEM((KV, D), F32),
            pltpu.VMEM((KV, D), F32),
            DMA((24,)),
        ],
        compiler_params=params(None, 30 << 20),
    )(*ins)


def reduce_kernel(
    mid_ref, dq, dkv, x, dx1, ga, wq, wk, wv, cos, sin, h10, h11, dqkv1, ob0, ob1, da0, da1,
    gga1, ggm0, ggm1, early_out, late_out, gain_out, fin_out,
    late_ref, came, half, one, gather, two, three, mid, gain_in, gain_sum, fin_ref, fin_in, dqkv0,
    s_e, r_e, s_l, r_l, gs, gr, fs, fr
):
    row, seq, n, w = place()
    torus = Torus(row, n, w)
    core = torus.core
    bar = pltpu.get_barrier_semaphore()
    pl.semaphore_signal(bar, inc=1, device_id=torus.partner, device_id_type=MESH)
    for axis in range(3):
        for k in range(1, 4):
            pl.semaphore_signal(bar, inc=1, device_id=torus.along(axis, k)[0], device_id_type=MESH)
    mirror = (row, 8 * (7 - n) + w)
    g, gga0 = project_back(
        dq, dkv, x[...], dx1[...], as_row(ga), wq, wk, wv, cos[...], sin[...], dqkv0
    )
    fin_ref[...] = g.T
    late_grads(h10, h11, dqkv0, dqkv1, ob0, ob1, da0, da1, late_ref)
    gain_sum[0] = jnp.concatenate(
        [gga0 + gga1[...], ggm0[...] + ggm1[...], jnp.zeros((6, D), F32)], axis=0
    )

    @pl.when(core == 1)
    def _():
        pl.semaphore_signal(bar, inc=1, device_id=mirror, device_id_type=MESH)
        pl.semaphore_wait(bar, 11)

    @pl.when(core == 0)
    def _():
        pl.semaphore_wait(bar, 10)

    early = Reduce(torus, EARLY, s_e, r_e)
    late = Reduce(torus, LATE, s_l, r_l)
    late.exchange(late_ref, came)

    def early_chunk(chunk):
        for p in range(3):
            early.fifth(p, mid_ref, early_out, chunk, 4)

    early_chunk(0)
    move = remote(fin_ref, fin_in, fs, fr, mirror)

    @pl.when(core == 1)
    def _():
        move.start()

    gains = []

    def gain_round(i, peers, count, at):
        gain_in[i, at] = gain_sum[i]
        for k, peer in enumerate(peers):
            cp = remote(gain_sum.at[i], gain_in.at[i, at], gs.at[i, k], gr.at[i, k], peer)
            cp.start()
            gains.append(cp)

    def gain_total(i, peers, count):
        for cp in gains[-peers:]:
            cp.wait_recv()
        return sum(gain_in[i, j] for j in range(count))

    def axis_peers(axis):
        return [torus.along(axis, k)[0] for k in range(1, 4)]

    gain_round(0, [torus.partner], 2, core)
    for p in range(3):
        late.first(p, late_ref, came, half, one)
    early_chunk(1)
    gain_sum[1] = gain_total(0, 1, 2)
    gain_round(1, axis_peers(0), 4, torus.spot[0])
    for p in range(3):
        late.second(p, half, one, gather, two)
    early_chunk(2)
    gain_sum[2] = gain_total(1, 3, 4)
    gain_round(2, axis_peers(1), 4, torus.spot[1])
    for p in range(3):
        late.third(p, gather, two, three)
    early_chunk(3)
    gain_sum[3] = gain_total(2, 3, 4)
    gain_round(3, axis_peers(2), 4, torus.spot[2])
    for p in range(3):
        late.fourth(p, three, mid)
    for p in range(3):
        early.sixth(p, early_out, 4)
    gain_out[...] = gain_total(3, 3, 4)
    for p in range(3):
        late.got(4, p)
        late.fifth(p, mid, late_out)
    for p in range(3):
        late.sixth(p, late_out)

    @pl.when(core == 1)
    def _():
        move.wait()
        fin_out[...] = fin_in[...]

    @pl.when(core == 0)
    def _():
        fin_out[...] = fin_ref[...]

    for cp in gains:
        cp.wait_send()
    for p in range(3):
        early.got(6, p)
        late.got(6, p)
    early.finish()
    late.finish()


def reduce_all(*ins):
    u = LATE
    return pl.pallas_call(
        reduce_kernel,
        name="reduce_all",
        out_shape=(
            sds(units(96 * EARLY), BF16), sds(units(96 * LATE), BF16), sds((8, D), F32), X_T
        ),
        in_specs=[VM] * len(ins),
        out_specs=(VM,) * 4,
        scratch_shapes=[
            pltpu.VMEM(shape, BF16)
            for shape in (
                units(96 * u), units(48 * u), units(48 * u), units(4 * u, 3, 3), units(4 * u, 3), units(u, 3, 3),
                units(u, 3, 4), units(4 * u, 3),
            )
        ]
        + [
            pltpu.VMEM((4, 4, 8, D), F32),
            pltpu.VMEM((4, 8, D), F32),
            pltpu.VMEM((D, TOK), F32),
            pltpu.VMEM((D, TOK), F32),
            pltpu.VMEM((960, TOK), BF16),
        ]
        + [DMA((11, 3, 4))] * 4
        + [DMA((4, 4)), DMA((4, 4)), DMA, DMA],
        compiler_params=params(4, 24 << 20),
        cost_estimate=cost(40),
    )(*ins)


def on_device(
    tokens, cotangent, segment_ids, gain_attn, wq, wk, wv, wo, gain_mlp, wg, wu, wd
):
    ga, gm = gain_attn, gain_mlp
    wk, wv, wd = wk.T, wv.T, wd.T
    w_q, w_k, w_v = sds((D, D), BF16), sds((KV, D), BF16), sds((KV, D), BF16)
    table = sds((32, TOK), F32)
    x0, h10, starts, cos, sin, qa0, kva0, part, stat = attend(
        True,
        [tokens[0].T, segment_ids, ga, wq, wk, wv, begin()],
        [HBM, HBM, VM, HBM, HBM, HBM, VM],
        [(o, VM) for o in (X_S, H_S, sds((2, 1, 4 * TOK), jnp.int32), table, table)]
        + [(sds(*a), HBM) for a in GATHERED],
        [
            pltpu.VMEM((D, TOK), F32),
            pltpu.VMEM((64, 1, TOK), jnp.int32),
            pltpu.VMEM((64, 1, TOK), jnp.int32),
        ]
        + [DMA((8,))] * 4
        + [DMA((2,)), DMA]
        + buffers(w_q, w_k, w_v)
        + [DMA((3,))],
        1,
        20 << 20,
    )
    cot, h11, x1, m0, h20, inv0, gate0, up0, hid0, o0, lse0, qa1, kva1, part, stat = attend(
        False,
        [part, stat, x0, cotangent[0].T, ga, wq, wk, wv, wo, gm, wg, wu, wd, cos, sin, starts],
        [VM] * 16,
        [(o, VM) for o in (X_S, H_S, X_S, X_S, H_S, sds((TOK, TOK), F32))]
        + [(F_S, HBM), (F_S, HBM)]
        + [(o, VM) for o in (FB_S, sds((D, TOK), F32), sds((16, TOK), F32))],
        [pltpu.VMEM((TOK, FF), F32), pltpu.VMEM((TOK, FF), F32), DMA((2,)), pltpu.VMEM((D, TOK), F32),
         DMA((2,)), DMA],
        2,
        20 << 20,
    )
    h21, hid1, ob1, gm1, dg1, du1, da1, dx1, ggm1, dq, dkv, output = attend_back(
        False,
        [part, stat, x1, cot, wo, gm, wg, wu, wd, qa1, kva1, starts],
        [VM] * 12,
        [H_S, FB_S, Q_T, H_S, FB_S, FB_S, H_S, X_S, G_S],
        [pltpu.VMEM((D, TOK), F32), pltpu.VMEM((16, TOK), F32)],
        20 << 20,
    )
    dqkv1, gga1, da0, dx0, ggm0, ob0, dq, dkv, mid = attend_back(
        True,
        [dq, dkv, x1, dx1, ga, wq, wk, wv, cos, sin, m0, inv0, gate0, up0, wo, gm, wg, wu, wd, o0,
         lse0, ob1, da1, h20, h21, dg1, du1, hid0, hid1, gm1, qa0, kva0, starts],
        [VM] * 33,
        [sds((960, TOK), BF16), G_S, H_S, X_S, G_S, Q_T],
        [pltpu.VMEM((TOK, D), BF16), pltpu.VMEM((TOK, FF), BF16), pltpu.VMEM((TOK, FF), BF16)],
        28 << 20,
    )
    early, late, gains, grad_tokens = reduce_all(
        mid, dq, dkv, x0, dx0, ga, wq, wk, wv, cos, sin, h10, h11, dqkv1, ob0, ob1, da0, da1, gga1,
        ggm0, ggm1
    )
    gga, ggm, output, grad_tokens, gate, up, down, query, key, value, out = spread(
        early, late, output, grad_tokens, gains
    )
    return (
        output.T[None], grad_tokens.T[None], gga, query, key.T, value.T, out, ggm, gate, up,
        down.T,
    )


def solution(mesh):
    rows = P("rows", "seq", None)
    in_specs = (rows, rows, P("rows", "seq")) + (P(),) * 9
    out_specs = (rows, rows) + (P(),) * 9
    return jax.shard_map(
        on_device, mesh=mesh, in_specs=in_specs, out_specs=out_specs, check_vma=False
    )
```

```python
import functools
import math

import jax
import jax.numpy as jnp
from jax import lax
from jax.experimental import pallas as pl
from jax.experimental.pallas import tpu as pltpu
from jax.sharding import PartitionSpec as P

F32 = jnp.float32
BF16 = jnp.bfloat16
MESH = pl.DeviceIdType.MESH

D = 576
HEADS = 9
HD = 64
KV = 192
FF = 1536
TOK = 128
DOCS = 16
EPS = 1e-05
SCALE = 0.125
EXP_SCALE = SCALE * 1.4426950408889634
MASKED = -1e30
LOWEST = -1e20

VM = pl.BlockSpec(memory_space=pltpu.VMEM)
DMA = pltpu.SemaphoreType.DMA


def dot(a, b, ca, cb):
    return lax.dot_general(a, b, (((ca,), (cb,)), ((), ())), preferred_element_type=F32)


def sds(shape, dtype):
    return jax.ShapeDtypeStruct(shape, dtype)


def params(collective=None, limit=50 << 20):
    if collective is None:
        return pltpu.CompilerParams(vmem_limit_bytes=limit)
    return pltpu.CompilerParams(
        vmem_limit_bytes=limit, collective_id=collective, has_side_effects=True
    )


def cost(us):
    return pl.CostEstimate(flops=us * 1000000000, bytes_accessed=us * 1000000, transcendentals=0)


def place():
    seq = lax.axis_index("seq")
    row = lax.axis_index("rows")
    return row, seq, seq // 8, lax.rem(seq, 8)


def slot_of(w):
    return lax.rem(w, 2) * 4 + w // 2


def octet_of(n, w):
    return jnp.where(lax.rem(w, 2) == 0, n, 7 - n)


def greet(row, n, w):
    bar = pltpu.get_barrier_semaphore()
    for k in range(1, 8):
        pl.semaphore_signal(
            bar, inc=1, device_id=(row, 8 * n + lax.rem(w + k, 8)), device_id_type=MESH
        )
        pl.semaphore_signal(
            bar, inc=1, device_id=(row, 8 * lax.rem(n + k, 8) + w), device_id_type=MESH
        )
    return bar


def remote(src, dst, send, recv, target):
    return pltpu.make_async_remote_copy(
        src_ref=src,
        dst_ref=dst,
        send_sem=send,
        recv_sem=recv,
        device_id=target,
        device_id_type=MESH,
    )


def as_row(ref):
    return ref[...].reshape(1, D)


def norm_in(x, gain):
    inverse = lax.rsqrt(jnp.mean(x * x, axis=-1, keepdims=True) + EPS)
    return (x * inverse * gain).astype(BF16), inverse


def norm_back(x, inverse, gain, grad):
    scaled = grad * gain
    grad_gain = jnp.sum(grad * (x * inverse), axis=0, keepdims=True)
    inner = jnp.mean(scaled * x, axis=-1, keepdims=True)
    return inverse * scaled - x * (inverse * inverse * inverse) * inner, grad_gain


def project(x, gain, wq, wk, wv, h_out):
    h, _ = norm_in(x, gain)
    h_out[...] = h
    return dot(h, wq[...], 1, 0).T, dot(wk[...], h, 1, 1), dot(wv[...], h, 1, 1).astype(BF16)


def rotate(qt, kt, vt, cos, sin, q_out, kv_out):
    scaled_cos, scaled_sin = cos * EXP_SCALE, sin * EXP_SCALE
    for i in range(HEADS):
        a = qt[HD * i : HD * i + 32]
        b = qt[HD * i + 32 : HD * i + 64]
        q_out[HD * i : HD * i + 32, :] = (a * scaled_cos - b * scaled_sin).astype(BF16)
        q_out[HD * i + 32 : HD * i + 64, :] = (b * scaled_cos + a * scaled_sin).astype(BF16)
    for i in range(3):
        a = kt[HD * i : HD * i + 32]
        b = kt[HD * i + 32 : HD * i + 64]
        kv_out[TOK * i : TOK * i + 32, :] = (a * cos - b * sin).astype(BF16)
        kv_out[TOK * i + 32 : TOK * i + 64, :] = (b * cos + a * sin).astype(BF16)
        kv_out[TOK * i + 64 : TOK * i + 128, :] = vt[HD * i : HD * i + 64]


def combine(part, stat, o_out, lse_out):
    for g in range(3):
        tops = [stat[i, 8 * g : 8 * g + 3, :] for i in range(4)]
        top = functools.reduce(jnp.maximum, tops)
        factors = [jnp.exp2(t - top) for t in tops]
        total = sum(f * stat[i, 8 * g + 4 : 8 * g + 7, :] for i, f in enumerate(factors))
        inverse = 1.0 / total
        factors = [f * inverse for f in factors]
        lse_out[3 * g : 3 * g + 3, :] = top + jnp.log2(total)
        for j in range(3):
            rows = slice(192 * g + HD * j, 192 * g + HD * j + HD)
            o_out[rows, :] = sum(
                part[i, rows, :].astype(F32) * factors[i][j : j + 1, :] for i in range(4)
            )


def feed_forward(x, o_t, wo, gain, wg, wu, wd):
    x1 = x + dot(o_t, wo[...], 0, 0)
    h2, inverse = norm_in(x1, gain)
    gate = dot(h2, wg[...], 1, 0)
    up = dot(h2, wu[...], 1, 0)
    hid = (gate * jax.nn.sigmoid(gate) * up).astype(BF16)
    return x1, h2, inverse, gate, up, hid, x1 + dot(hid, wd[...], 1, 1)


def feed_back(g, x1, inverse, gate, up, wo, gain, wg, wu, wd, o_ref, lse,
              do_out, stat_out, gm_out, dgate_out, dup_out, da_out):
    gm = g.astype(BF16)
    gm_out[...] = gm
    dhid = dot(gm, wd[...], 1, 0)
    sg = jax.nn.sigmoid(gate)
    dgate = (dhid * up * sg * (1.0 + gate * (1.0 - sg))).astype(BF16)
    dup = (dhid * gate * sg).astype(BF16)
    dgate_out[...] = dgate
    dup_out[...] = dup
    dh2 = dot(dgate, wg[...], 1, 1) + dot(dup, wu[...], 1, 1)
    dy, grad_gain = norm_back(x1, inverse, gain, dh2)
    dx1 = g + dy
    da = dx1.astype(BF16)
    da_out[...] = da
    do_t = dot(wo[...], da, 1, 1).astype(BF16)
    do_out[...] = do_t
    stat_out[...] = jnp.zeros(stat_out.shape, F32)
    stat_out[0:HEADS, :] = lse
    for h in range(HEADS):
        rows = slice(HD * h, HD * h + HD)
        stat_out[16 + h : 17 + h, :] = jnp.sum(
            do_t[rows].astype(F32) * o_ref[rows, :], axis=0, keepdims=True
        )
    return dx1, grad_gain


def project_back(dq_part, dkv_part, x, dx1, gain, wq, wk, wv, cos, sin, dqkv_out):
    for h in range(HEADS + 3):
        part, base, many = (dq_part, HD * h, 4) if h < HEADS else (dkv_part, TOK * (h - HEADS), 8)
        a = sum(part[i, base : base + 32, :].astype(F32) for i in range(many))
        b = sum(part[i, base + 32 : base + 64, :].astype(F32) for i in range(many))
        dqkv_out[HD * h : HD * h + 32, :] = (a * cos + b * sin).astype(BF16)
        dqkv_out[HD * h + 32 : HD * h + 64, :] = (b * cos - a * sin).astype(BF16)
    for g in range(3):
        base = TOK * g + HD
        dqkv_out[D + KV + HD * g : D + KV + HD * g + HD, :] = sum(
            dkv_part[i, base : base + HD, :].astype(F32) for i in range(8)
        ).astype(BF16)
    dh1 = (
        dot(dqkv_out[0:D, :], wq[...], 0, 1)
        + dot(dqkv_out[D : D + KV, :], wk[...], 0, 0)
        + dot(dqkv_out[D + KV :, :], wv[...], 0, 0)
    )
    inverse = lax.rsqrt(jnp.mean(x * x, axis=-1, keepdims=True) + EPS)
    dy, grad_gain = norm_back(x, inverse, gain, dh1)
    return dx1 + dy, grad_gain


Q_T = sds((D, TOK), BF16)
KV_T = sds((2 * KV, TOK), BF16)
H_S = sds((TOK, D), BF16)
X_S = sds((TOK, D), F32)
X_T = sds((D, TOK), F32)
F_S = sds((TOK, FF), F32)
FB_S = sds((TOK, FF), BF16)
ST_S = sds((32, TOK), F32)
G_S = sds((1, D), F32)


ANY = pl.BlockSpec(memory_space=pl.ANY)
HBM = pl.BlockSpec(memory_space=pltpu.HBM)


class Lazy:
    def __init__(self, src, buf, sem):
        self.copy = pltpu.make_async_copy(src, buf, sem)
        self.copy.start()
        self.buf, self.waited = buf, False

    def ref(self):
        if not self.waited:
            self.copy.wait()
            self.waited = True
        return self.buf

    def __getitem__(self, index):
        return self.ref()[index]


def fetch(srcs, bufs, sems):
    return [Lazy(src, buf, sems.at[i]) for i, (src, buf) in enumerate(zip(srcs, bufs))]


def buffers(*arrays):
    return [pltpu.VMEM(a.shape, a.dtype) for a in arrays] + [DMA((len(arrays),))]


def begin_kernel(out):
    out[...] = jnp.zeros(out.shape, F32)


def begin():
    return pl.pallas_call(
        begin_kernel,
        name="begin",
        out_shape=sds((8, TOK), F32),
        out_specs=VM,
        compiler_params=params(None, 1 << 20),
        cost_estimate=cost(30),
    )()


def mirrored(ctx, src, dst, send, recv):
    move = remote(src, dst, send.at[0], recv, (ctx.row, 8 * (7 - ctx.n) + ctx.w))
    stay = pltpu.make_async_copy(src, dst, send.at[1])

    def both(if_one, if_zero):
        pl.when(ctx.core == 1)(if_one)
        pl.when(ctx.core == 0)(if_zero)

    return lambda: both(move.start, stay.start), lambda: both(move.wait, stay.wait)


def first_part(ctx, ins, outs, scratch):
    tok, ids_ref, ga, wq, wk, wv, _ = ins
    x_out, h_out, starts_ref, cos_ref, sin_ref, q_save, kv_save = outs
    (tok_in, ids_all, starts_all, ysend, yrecv, xsend, xrecv, tsend, trecv,
     bq, bk, bv, bsem, ssem) = scratch
    row, n, w = ctx.row, ctx.n, ctx.w
    seq = 8 * n + w
    get_ids = pltpu.make_async_copy(ids_ref, ids_all.at[seq], ssem.at[0])
    get_ids.start()
    wq, wk, wv = fetch([wq, wk, wv], [bq, bk, bv], bsem)
    get_ids.wait()
    ctx.ready()
    start, wait = mirrored(ctx, tok, tok_in, tsend, trecv)
    start()
    sent = []
    for k in range(1, 8):
        cp = remote(
            ids_all.at[seq], ids_all.at[seq], ysend.at[k], yrecv.at[k],
            (row, 8 * n + lax.rem(w + k, 8)),
        )
        cp.start()
        sent.append(cp)
    for cp in sent:
        cp.wait()
    own = ids_all.at[pl.ds(8 * n, 8)]
    sent = []
    for k in range(1, 8):
        cp = remote(own, own, xsend.at[k], xrecv.at[k], (row, 8 * lax.rem(n + k, 8) + w))
        cp.start()
        sent.append(cp)
    wait()
    x = tok_in[...].T
    x_out[...] = x
    raw = project(x, as_row(ga), wq, wk, wv, h_out)
    for cp in sent:
        cp.wait()

    ids = jnp.concatenate([ids_all[i] for i in range(64)], axis=0)
    total = jnp.zeros((64, TOK), jnp.int32)
    for doc in range(DOCS - 1):
        count = jnp.where(ids == doc, 1.0, 0.0)
        count = jnp.sum(jnp.sum(count, axis=0, keepdims=True), axis=1, keepdims=True)
        total = total + jnp.where(ids > doc, count.astype(jnp.int32), 0)
    starts_all[...] = total[:, None, :]
    for half in range(2):
        octet = n if half == 0 else 7 - n
        for y in range(4):
            starts_ref[half, :, TOK * y : TOK * y + TOK] = starts_all[8 * octet + 2 * y + half]
    mine = 8 * octet_of(n, w) + w
    pos = mine * TOK + lax.broadcasted_iota(jnp.int32, (1, TOK), 1) - starts_all[mine]
    line = lax.broadcasted_iota(jnp.int32, (32, TOK), 0).astype(F32)
    angle = jnp.exp(line * (-2.0 / HD) * math.log(10000.0)) * pos.astype(F32)
    cos_ref[...] = jnp.cos(angle)
    sin_ref[...] = jnp.sin(angle)
    rotate(*raw, cos_ref[...], sin_ref[...], ctx.q_own, ctx.kv_own)

    saves = [
        pltpu.make_async_copy(ctx.q_all, q_save, ssem.at[1]),
        pltpu.make_async_copy(ctx.kv_all, kv_save, ssem.at[2]),
    ]

    def arrived():
        for cp in saves:
            cp.start()

    def end():
        for cp in saves:
            cp.wait()

    return None, arrived, end


def middle_part(ctx, ins, outs, scratch):
    part, stat, x, cot, ga, wq, wk, wv, wo, gm, wg, wu, wd, cos, sin = ins
    g_out, h_out, x_out, x1_out, h2_out, inv_out, gate_out, up_out, hid_out, o_out, lse_out = outs
    gate_s, up_s, ssem, cot_in, csend, crecv = scratch
    start, wait = mirrored(ctx, cot, cot_in, csend, crecv)
    saves = [
        pltpu.make_async_copy(gate_s, gate_out, ssem.at[0]),
        pltpu.make_async_copy(up_s, up_out, ssem.at[1]),
    ]
    combine(part, stat, o_out, lse_out)
    x1, h2, inverse, gate, up, hid, x2 = feed_forward(
        x[...], o_out[...].astype(BF16), wo, as_row(gm), wg, wu, wd
    )
    x_out[...] = x2
    raw = project(x2, as_row(ga), wq, wk, wv, h_out)
    rotate(*raw, cos[...], sin[...], ctx.q_own, ctx.kv_own)
    ctx.ready()

    def late():
        x1_out[...] = x1
        h2_out[...] = h2
        inv_out[...] = jnp.broadcast_to(inverse, inv_out.shape)
        gate_s[...] = gate
        up_s[...] = up
        hid_out[...] = hid
        for cp in saves:
            cp.start()
        start()

    def end():
        for cp in saves:
            cp.wait()
        wait()
        g_out[...] = cot_in[...].T

    return late, None, end


def turn_part(ctx, ins, outs, scratch):
    part, stat, x, g, wo, gm, wg, wu, wd = ins
    h2_out, hid_out, ob_out, gmo, dgate, dup, da, dx1_out, gg_out = outs
    o_s, lse_s = scratch
    combine(part, stat, o_s, lse_s)
    ob = o_s[...].astype(BF16)
    ob_out[...] = ob
    x1, h2, inverse, gate, up, hid, x2 = feed_forward(
        x[...], ob, wo, as_row(gm), wg, wu, wd
    )
    h2_out[...] = h2
    hid_out[...] = hid
    ctx.extra[...] = x2.T
    dx1, gg = feed_back(
        g[...], x1, inverse, gate, up, wo, as_row(gm), wg, wu, wd, o_s,
        lse_s[0:HEADS, :], ctx.do_own, ctx.st_own, gmo, dgate, dup, da
    )
    dx1_out[...] = dx1
    gg_out[...] = gg


def between_part(ctx, ins, outs, scratch):
    (dq, dkv, x, dx1, ga, wq, wk, wv, cos, sin, x1, inv, gate, up, wo, gm, wg, wu, wd, o, lse,
     ob1, da1, h20, h21, dg1, du1, hid0, hid1, gm1) = ins
    dqkv_out, gga_out, da, dx1_out, ggm_out, ob_out = outs
    gmo, dgate, dup = scratch
    g, gga = project_back(
        dq, dkv, x[...], dx1[...], as_row(ga), wq, wk, wv, cos[...], sin[...], dqkv_out
    )
    gga_out[...] = gga
    dx0, ggm = feed_back(
        g, x1[...], inv[:, 0:1], gate[...], up[...], wo, as_row(gm), wg, wu, wd, o,
        lse[0:HEADS, :], ctx.do_own, ctx.st_own, gmo, dgate, dup, da
    )
    dx1_out[...] = dx0
    ggm_out[...] = ggm
    ob_out[...] = o[...].astype(BF16)

    def grads():
        early_grads(
            ob_out, ob1, da, da1, h20, h21, dgate, dg1, dup, du1, hid0, hid1, gmo, gm1, ctx.extra
        )

    return grads


class Torus:
    def __init__(self, row, n, w):
        self.core = lax.rem(w, 2)
        self.spot = (n // 2, w // 2, 2 * row + lax.rem(n, 2))
        self.partner = self.device(self.spot, 1 - self.core)

    def device(self, spot, core):
        x, y, z = spot
        return (z // 2, ((x * 2 + lax.rem(z, 2)) * 4 + y) * 2 + core)

    def along(self, axis, k):
        to = list(self.spot)
        to[axis] = lax.rem(self.spot[axis] + k, 4)
        return self.device(to, self.core), to[axis]


class Reduce:
    def __init__(self, torus, u, send, recv):
        self.torus, self.u, self.send, self.recv = torus, u, send, recv
        self.box = {}

    def go(self, stage, p, k, src, dst, peer):
        cp = remote(src, dst, self.send.at[stage, p, k], self.recv.at[stage, p, k], peer)
        cp.start()
        self.box.setdefault((stage, p), []).append(cp)

    def got(self, stage, p):
        for cp in self.box[stage, p]:
            cp.wait_recv()

    def finish(self):
        for cps in self.box.values():
            for cp in cps:
                cp.wait_send()

    def exchange(self, src, came):
        u, core = self.u, self.torus.core
        for p in range(3):
            self.go(
                0, p, 0, src.at[pl.ds(48 * u * (1 - core) + 16 * u * p, 16 * u)],
                came.at[pl.ds(16 * u * p, 16 * u)], self.torus.partner,
            )

    def first(self, p, src, came, half, one):
        u = self.u
        self.got(0, p)

        def quarter(i, carry):
            at = pl.ds(16 * u * p + 4 * u * i, 4 * u)
            mine = src[pl.ds(48 * u * self.torus.core + 16 * u * p + 4 * u * i, 4 * u)]
            half[at] = (mine.astype(F32) + came[at].astype(F32)).astype(BF16)
            return carry

        lax.fori_loop(0, 4, quarter, 0)
        for k in range(1, 4):
            peer, at = self.torus.along(p, k)
            self.go(1, p, k, half.at[pl.ds(16 * u * p + 4 * u * at, 4 * u)], one.at[p, k - 1], peer)

    def second(self, p, half, one, gather, two):
        u = self.u
        self.got(1, p)
        mine = half[pl.ds(16 * u * p + 4 * u * self.torus.spot[p], 4 * u)]
        gather[p] = (mine.astype(F32) + sum(one[p, k].astype(F32) for k in range(3))).astype(BF16)
        for k in range(1, 4):
            peer, at = self.torus.along((p + 1) % 3, k)
            self.go(2, p, k, gather.at[p, pl.ds(u * at, u)], two.at[p, k - 1], peer)

    def third(self, p, gather, two, three):
        u = self.u
        self.got(2, p)
        c = self.torus.spot[(p + 2) % 3]
        mine = gather[p, pl.ds(u * self.torus.spot[(p + 1) % 3], u)]
        three[p, c] = (mine.astype(F32) + sum(two[p, k].astype(F32) for k in range(3))).astype(BF16)
        for k in range(1, 4):
            self.go(3, p, k, three.at[p, c], three.at[p, c], self.torus.along((p + 2) % 3, k)[0])

    def fourth(self, p, three, mid):
        u = self.u
        if (3, p) in self.box:
            self.got(3, p)
        at = pl.ds(u * self.torus.spot[(p + 1) % 3], u)
        mid[p, at] = sum(three[p, k].astype(F32) for k in range(4)).astype(BF16)
        for k in range(1, 4):
            self.go(4, p, k, mid.at[p, at], mid.at[p, at], self.torus.along((p + 1) % 3, k)[0])

    def fifth(self, p, mid, out, chunk=0, chunks=1):
        u = self.u
        size = 4 * u // chunks
        base = 48 * u * self.torus.core + 16 * u * p + 4 * u * self.torus.spot[p]
        at = pl.ds(base + size * chunk, size)
        out[at] = mid[p, size * chunk : size * chunk + size]
        for k in range(1, 4):
            self.go(7 + chunk, p, k, out.at[at], out.at[at], self.torus.along(p, k)[0])

    def sixth(self, p, out, chunks=1):
        u = self.u
        for chunk in range(chunks):
            self.got(7 + chunk, p)
        at = pl.ds(48 * u * self.torus.core + 16 * u * p, 16 * u)
        self.go(6, p, 0, out.at[at], out.at[at], self.torus.partner)


def units(count, *lead):
    return tuple(lead) + (count, 16, 256)


EARLY, LATE = 7, 2


W3 = 12 * TOK


class Spread:
    def __init__(self, row, n, w, send, recv):
        self.core = lax.rem(w, 2)
        self.y = w // 2
        self.own = self.core * 4 + self.y
        self.row, self.n = row, n
        self.partner = (row, 8 * n + 2 * self.y + 1 - self.core)
        self.send, self.recv = send, recv
        self.first, self.passed = {}, {}

    def chip(self, k):
        return (self.row, 8 * self.n + 2 * lax.rem(self.y + k, 4) + self.core)

    def start(self, part, ref):
        self.first[part], self.passed[part] = [], []
        for k in range(1, 4):
            cp = remote(ref(self.own), ref(self.own), self.send.at[part, k], self.recv.at[part, k],
                        self.chip(k))
            cp.start()
            self.first[part].append(cp)
        self.hand(part, ref, self.own, 4)

    def hand(self, part, ref, slot, k):
        cp = remote(ref(slot), ref(slot), self.send.at[part, k], self.recv.at[part, k], self.partner)
        cp.start()
        self.passed[part].append(cp)

    def forward(self, part, ref):
        for k in range(1, 4):
            self.first[part][k - 1].wait_recv()
            self.hand(part, ref, self.core * 4 + lax.rem(self.y + 4 - k, 4), 4 + k)

    def arrive(self, part):
        for cp in self.passed[part]:
            cp.wait_recv()

    def finish(self):
        for part in self.first:
            for cp in self.first[part] + self.passed[part]:
                cp.wait_send()


def turns(n):
    return (n + 2) // 2


def fill_masks(bias, starts_ref, n, w):
    turn = turns(n)

    def one(t, carry):
        sel = jnp.where(t >= turn, 1, 0)
        kc = jnp.where(t >= turn, t - turn, t)
        line = lax.broadcasted_iota(jnp.int32, (256, 1), 0)
        key = (2 * kc + line // TOK) * 1024 + w * TOK + lax.rem(line, TOK)
        col = lax.broadcasted_iota(jnp.int32, (1, 512), 1)
        octet = jnp.where(sel == 0, n, 7 - n)
        query = octet * 1024 + (2 * (col // TOK) + sel) * TOK + lax.rem(col, TOK)
        bias[t] = jnp.where((key >= starts_ref[sel]) & (key <= query), 0.0, MASKED)
        return carry

    lax.fori_loop(0, 5, one, 0)


def over_keys(n, sel, step):
    octet = jnp.where(sel == 0, n, 7 - n)
    base = jnp.where(sel == 0, 0, turns(n))
    whole = (octet + 1) // 2

    def chunk(kc, carry):
        step(base + kc, kc, 2 * TOK)
        return carry

    lax.fori_loop(0, whole, chunk, 0)

    @pl.when(lax.rem(octet + 1, 2) == 1)
    def _():
        step(base + whole, whole, TOK)


def three_heads(ref, sel, g):
    return jnp.concatenate(
        [
            ref[4 * sel + y, HD * h : HD * h + HD, :]
            for h in range(3 * g, 3 * g + 3)
            for y in range(4)
        ],
        axis=1,
    )


def key_blocks(ref, kc, first, keys):
    return jnp.concatenate(
        [ref[2 * kc + i, first : first + HD, :] for i in range(keys // TOK)], axis=1
    )


def by_chip(value, y):
    return jnp.concatenate(
        [value[:, 512 * j + TOK * y : 512 * j + TOK * y + TOK] for j in range(3)], axis=0
    )


class Context:
    pass


def attend_kernel(first, n_in, n_out, *refs):
    ins, refs = refs[:n_in], refs[n_in:]
    outs, refs = refs[:n_out], refs[n_out:]
    if first:
        part_ref, stat_ref, q_all, kv_all = refs[:4]
    else:
        q_all, kv_all, part_ref, stat_ref = refs[:4]
    (k_nat, bias, top, total, acc, o_send, o_recv, r_send, r_recv, o_y, s_y,
     qs, qr, ks, kr, ps, pr, ys, yr) = refs[4:23]
    starts_ref = outs[2] if first else ins[-1]
    row, seq, n, w = place()
    bar = greet(row, n, w)
    core, y = lax.rem(w, 2), w // 2
    own_k = octet_of(n, w)
    queries = Spread(row, n, w, qs, qr)
    ctx = Context()
    ctx.row, ctx.n, ctx.w, ctx.core = row, n, w, core
    ctx.q_own, ctx.kv_own = q_all.at[queries.own], kv_all.at[own_k]
    ctx.q_all, ctx.kv_all = q_all, kv_all
    ctx.ready = lambda: pl.semaphore_wait(bar, 14)
    if first:
        late, arrived, end = first_part(ctx, ins, outs, refs[23:])
    else:
        late, arrived, end = middle_part(ctx, ins[:-1], outs, refs[23:])

    def q_part(g):
        return lambda slot: q_all.at[slot, pl.ds(192 * g, 192)]

    keys = {}
    for g in range(3):
        keys[g] = []
        for k in range(1, 8):
            block = kv_all.at[own_k, pl.ds(TOK * g, TOK)]
            cp = remote(
                block, block, ks.at[g, k], kr.at[g, k], (row, 8 * lax.rem(n + k, 8) + w)
            )
            cp.start()
            keys[g].append(cp)
        queries.start(g, q_part(g))
    fill_masks(bias, starts_ref, n, w)
    queries.forward(0, q_part(0))

    def phase(g, sel):
        top[...] = jnp.full(top.shape, LOWEST, F32)
        total[...] = jnp.zeros(total.shape, F32)
        acc[...] = jnp.zeros(acc.shape, F32)

        def step(at, kc, keys):
            scores = dot(k_nat[kc, 0:keys], three_heads(q_all, sel, g), 1, 0)
            mask = bias[at, 0:keys]
            weights, shrinks = [], []
            for j in range(3):
                cols = slice(512 * j, 512 * j + 512)
                s = scores[:, cols] + mask
                old = top[:, cols]
                new = jnp.maximum(old, jnp.max(s, axis=0, keepdims=True))
                p = jnp.exp2(s - new)
                shrink = jnp.exp2(old - new)
                top[:, cols] = new
                total[:, cols] = total[:, cols] * shrink + jnp.sum(p, axis=0, keepdims=True)
                weights.append(p.astype(BF16))
                shrinks.append(shrink)
            values = key_blocks(kv_all, kc, TOK * g + HD, keys)
            acc[...] = acc[...] * jnp.concatenate(shrinks, axis=1) + dot(
                values, jnp.concatenate(weights, axis=1), 1, 0
            )

        over_keys(n, sel, step)

    pairs, flying = [], []
    for g in range(3):
        for cp in keys[g]:
            cp.wait_recv()
        for j in range(8):
            k_nat[j // 2, (j % 2) * TOK : (j % 2) * TOK + TOK, :] = jnp.transpose(
                kv_all[j, TOK * g : TOK * g + HD, :]
            )
        queries.arrive(g)
        if g == 2 and arrived is not None:
            arrived()
        phase(g, 1 - core)
        o_send[g] = acc[...].astype(BF16)
        r_send[g, 0] = top[...]
        r_send[g, 1] = total[...]
        both = [
            remote(o_send.at[g], o_recv.at[g], ps.at[0, g], pr.at[0, g], queries.partner),
            remote(r_send.at[g], r_recv.at[g], ps.at[1, g], pr.at[1, g], queries.partner),
        ]
        for cp in both:
            cp.start()
        pairs += both
        if g < 2:
            queries.forward(g + 1, q_part(g + 1))
        if g == 0 and late is not None:
            late()
        phase(g, core)
        for cp in both:
            cp.wait_recv()
        new = jnp.maximum(top[...], r_recv[g, 0])
        mine = jnp.exp2(top[...] - new)
        theirs = jnp.exp2(r_recv[g, 0] - new)
        length = total[...] * mine + r_recv[g, 1] * theirs
        out = (acc[...] * mine + o_recv[g].astype(F32) * theirs).astype(BF16)
        for i in range(4):
            o_y[g, i] = by_chip(out, i)
            for j in range(3):
                cols = slice(512 * j + TOK * i, 512 * j + TOK * i + TOK)
                s_y[g, i, j : j + 1, :] = new[:, cols]
                s_y[g, i, 4 + j : 5 + j, :] = length[:, cols]
        for k in range(1, 4):
            to = lax.rem(y + k, 4)
            peer = queries.chip(k)
            for cp in (
                remote(o_y.at[g, to], part_ref.at[y, pl.ds(192 * g, 192)], ys.at[0, g, k],
                       yr.at[0, g, k], peer),
                remote(s_y.at[g, to], stat_ref.at[y, pl.ds(8 * g, 8)], ys.at[1, g, k],
                       yr.at[1, g, k], peer),
            ):
                cp.start()
                flying.append(cp)
        part_ref[y, 192 * g : 192 * g + 192, :] = o_y[g, y]
        stat_ref[y, 8 * g : 8 * g + 8, :] = s_y[g, y]
    queries.finish()
    for g in range(3):
        for cp in keys[g]:
            cp.wait_send()
    for cp in pairs:
        cp.wait_send()
    for cp in flying:
        cp.wait()
    if end is not None:
        end()


GATHERED = [((8, D, TOK), BF16), ((8, 2 * KV, TOK), BF16)]


def attend(first, ins, specs, outs, scratch, collective, limit):
    count = len(outs)
    here = [] if first else [sds(*a) for a in GATHERED]
    there = [pltpu.VMEM(*a) for a in GATHERED] if first else []
    outs = outs + [(o, VM) for o in here + [sds((4, D, TOK), BF16), sds((4, 24, TOK), F32)]]
    return pl.pallas_call(
        functools.partial(attend_kernel, first, len(ins), count),
        name="attend_first" if first else "attend",
        out_shape=tuple(o for o, _ in outs),
        in_specs=specs,
        out_specs=tuple(spec for _, spec in outs),
        scratch_shapes=there
        + [
            pltpu.VMEM((4, 256, HD), BF16),
            pltpu.VMEM((5, 256, 512), F32),
            pltpu.VMEM((1, W3), F32),
            pltpu.VMEM((1, W3), F32),
            pltpu.VMEM((HD, W3), F32),
            pltpu.VMEM((3, HD, W3), BF16),
            pltpu.VMEM((3, HD, W3), BF16),
            pltpu.VMEM((3, 2, 1, W3), F32),
            pltpu.VMEM((3, 2, 1, W3), F32),
            pltpu.VMEM((3, 4, 192, TOK), BF16),
            pltpu.VMEM((3, 4, 8, TOK), F32),
            DMA((3, 8)), DMA((3, 8)), DMA((3, 8)), DMA((3, 8)),
            DMA((2, 3)), DMA((2, 3)), DMA((2, 3, 4)), DMA((2, 3, 4)),
        ]
        + scratch,
        compiler_params=params(collective, limit),
        cost_estimate=cost(30),
    )(*ins)


def attend_back_kernel(carry_sum, n_in, n_out, n_more, *refs):
    ins, refs = refs[:n_in], refs[n_in:]
    outs, refs = refs[:n_out], refs[n_out:]
    (dq_part, dkv_part, extra_out, do_all, st_all, k_nat, v_nat, bias, rows_s, dq, dq_other, dkv, q_send,
     q_recv, q_y, kv_low, extra, qs, qr, ks, kr, ps, pr, ys, yr, es, er) = refs[:27]
    more, scratch = refs[27 : 27 + n_more], refs[27 + n_more :]
    q_all, kv_all, starts_ref = ins[-3:]
    ctx = Context()
    ctx.q_all, ctx.kv_all = q_all, kv_all
    row, seq, n, w = place()
    bar = greet(row, n, w)
    torus = Torus(row, n, w)
    if carry_sum:
        came, one, gather, two = more
        half = extra.at[pl.ds(48 * EARLY * lax.rem(w, 2), 48 * EARLY)]
        for k in range(1, 4):
            pl.semaphore_signal(bar, inc=1, device_id=torus.along(2, k)[0], device_id_type=MESH)
        early = Reduce(torus, EARLY, es, er)
    else:
        (extra_in,) = more
        move = remote(extra, extra_in, es, er, (row, 8 * (7 - n) + w))
    core, y = lax.rem(w, 2), w // 2
    own_k = octet_of(n, w)
    grads = Spread(row, n, w, qs, qr)
    ctx.do_own, ctx.st_own, ctx.extra = do_all.at[grads.own], st_all.at[grads.own], extra
    make = between_part if carry_sum else turn_part
    grads_of = make(ctx, ins[:-3], outs, scratch)
    pl.semaphore_wait(bar, 17 if carry_sum else 14)

    def part(g):
        return lambda slot: do_all.at[slot, pl.ds(192 * g, 192)]

    def stats(slot):
        return st_all.at[slot]

    grads.start(3, stats)
    for g in range(3):
        grads.start(g, part(g))
    if carry_sum:
        grads_of()
        early.exchange(extra, came)
    fill_masks(bias, starts_ref, n, w)
    for g in range(3):
        for j in range(8):
            at = slice((j % 2) * TOK, (j % 2) * TOK + TOK)
            k_nat[g, j // 2, at, :] = jnp.transpose(kv_all[j, TOK * g : TOK * g + HD, :])
            v_nat[g, j // 2, at, :] = jnp.transpose(kv_all[j, TOK * g + HD : TOK * g + TOK, :])
    grads.forward(3, stats)
    grads.forward(0, part(0))
    if carry_sum:
        for p in range(3):
            early.first(p, extra, came, half, one)
    if not carry_sum:

        @pl.when(core == 1)
        def _():
            move.start()

    def phase(g, sel, dq):
        dq[...] = jnp.zeros(dq.shape, F32)
        for i, first in enumerate((0, 16)):
            for j in range(3):
                for c in range(4):
                    at = 512 * j + TOK * c
                    line = first + 3 * g + j
                    rows_s[i, :, at : at + TOK] = st_all[4 * sel + c, line : line + 1, :]

        def step(at, kc, keys):
            qt = three_heads(q_all, sel, g)
            dt = three_heads(do_all, sel, g)
            scores = dot(k_nat[g, kc, 0:keys], qt, 1, 0)
            dp = dot(v_nat[g, kc, 0:keys], dt, 1, 0)
            mask = bias[at, 0:keys]
            ps_, ds_ = [], []
            for j in range(3):
                cols = slice(512 * j, 512 * j + 512)
                p = jnp.exp2(scores[:, cols] + mask - rows_s[0, :, cols])
                ds_.append((p * (dp[:, cols] - rows_s[1, :, cols])).astype(BF16))
                ps_.append(p.astype(BF16))
            p = jnp.concatenate(ps_, axis=1)
            ds = jnp.concatenate(ds_, axis=1)
            dkv[kc, 0:HD, 0:keys] += dot(ds, qt, 1, 1).T
            dkv[kc, HD:, 0:keys] += dot(p, dt, 1, 1).T
            dq[...] += dot(key_blocks(kv_all, kc, TOK * g, keys), ds, 1, 0)

        over_keys(n, sel, step)

    pairs, flying = [], []
    for g in range(3):
        dkv[...] = jnp.zeros(dkv.shape, F32)
        if g == 0:
            phase(g, core, dq)
            grads.forward(1, part(1))
            grads.arrive(3)
        grads.arrive(g)
        phase(g, 1 - core, dq_other)
        q_send[g] = (dq_other[...] * SCALE).astype(BF16)
        pair = remote(q_send.at[g], q_recv.at[g], ps.at[g], pr.at[g], grads.partner)
        pair.start()
        pairs.append(pair)
        if g == 1:
            grads.forward(2, part(2))
        if g == 2 and carry_sum:
            for p in range(3):
                early.second(p, half, one, gather, two)
        if g > 0:
            phase(g, core, dq)
        for j in range(8):
            cols = slice((j % 2) * TOK, (j % 2) * TOK + TOK)
            kv_low[g, j, 0:HD, :] = (dkv[j // 2, 0:HD, cols] * (SCALE / EXP_SCALE)).astype(BF16)
            kv_low[g, j, HD:, :] = dkv[j // 2, HD:, cols].astype(BF16)
        for k in range(1, 8):
            to = lax.rem(n + k, 8)
            cp = remote(
                kv_low.at[g, octet_of(to, w)], dkv_part.at[n, pl.ds(TOK * g, TOK)], ks.at[g, k],
                kr.at[g, k], (row, 8 * to + w),
            )
            cp.start()
            flying.append(cp)
        pair.wait_recv()
        out = (dq[...] * SCALE + q_recv[g].astype(F32)).astype(BF16)
        for i in range(4):
            q_y[g, i] = by_chip(out, i)
        for k in range(1, 4):
            to = lax.rem(y + k, 4)
            cp = remote(q_y.at[g, to], dq_part.at[y, pl.ds(192 * g, 192)], ys.at[g, k], yr.at[g, k],
                        grads.chip(k))
            cp.start()
            flying.append(cp)
        dkv_part[n, TOK * g : TOK * g + TOK, :] = kv_low[g, own_k]
        dq_part[y, 192 * g : 192 * g + 192, :] = q_y[g, y]
        if carry_sum:
            for p in range(3):
                if g == 2:
                    early.third(p, gather, two, extra_out)
    grads.finish()
    for cp in pairs:
        cp.wait_send()
    for cp in flying:
        cp.wait()
    if carry_sum:
        for p in range(3):
            early.got(3, p)
        early.finish()
    else:

        @pl.when(core == 1)
        def _():
            move.wait()
            extra_out[...] = extra_in[...]

        @pl.when(core == 0)
        def _():
            extra_out[...] = extra[...]


def attend_back(carry_sum, ins, specs, outs, scratch, limit):
    if carry_sum:
        u = EARLY
        extra_shape = sds(units(u, 3, 4), BF16)
        extra = pltpu.VMEM(units(96 * u), BF16)
        sems = [DMA((5, 3, 4))] * 2
        more = [
            pltpu.VMEM(shape, BF16)
            for shape in (
                units(48 * u), units(4 * u, 3, 3), units(4 * u, 3), units(u, 3, 3),
            )
        ]
    else:
        extra_shape = X_T
        extra = pltpu.VMEM((D, TOK), F32)
        sems = [DMA, DMA]
        more = [pltpu.VMEM((D, TOK), F32)]
    return pl.pallas_call(
        functools.partial(attend_back_kernel, carry_sum, len(ins), len(outs), len(more)),
        name="attend_back_sum" if carry_sum else "attend_back",
        out_shape=tuple(outs + [sds((4, D, TOK), BF16), sds((8, 2 * KV, TOK), BF16), extra_shape]),
        in_specs=specs,
        out_specs=(VM,) * (len(outs) + 3),
        scratch_shapes=[
            pltpu.VMEM((8, D, TOK), BF16),
            pltpu.VMEM((8, 32, TOK), F32),
            pltpu.VMEM((3, 4, 256, HD), BF16),
            pltpu.VMEM((3, 4, 256, HD), BF16),
            pltpu.VMEM((5, 256, 512), F32),
            pltpu.VMEM((2, 1, W3), F32),
            pltpu.VMEM((HD, W3), F32),
            pltpu.VMEM((HD, W3), F32),
            pltpu.VMEM((4, TOK, 256), F32),
            pltpu.VMEM((3, HD, W3), BF16),
            pltpu.VMEM((3, HD, W3), BF16),
            pltpu.VMEM((3, 4, 192, TOK), BF16),
            pltpu.VMEM((3, 8, TOK, TOK), BF16),
            extra,
            DMA((4, 8)), DMA((4, 8)), DMA((3, 8)), DMA((3, 8)),
            DMA((3,)), DMA((3,)), DMA((3, 4)), DMA((3, 4)),
        ]
        + sems
        + more
        + scratch,
        compiler_params=params(5 if carry_sum else 3, limit),
        cost_estimate=cost(40),
    )(*ins)


def both_rows(a, b):
    return jnp.concatenate([a[...], b[...]], axis=0)


def as_units(value):
    return value.astype(BF16).reshape(units(value.shape[0] // 16))


def early_grads(oa, ob, daa, dab, h2a, h2b, dga, dgb, dua, dub, hida, hidb, gma, gmb, g_out):
    ot = jnp.concatenate([oa[...], ob[...]], axis=1)
    h2t = both_rows(h2a, h2b).T
    gmt = both_rows(gma, gmb).T
    for i in range(6):
        cols = slice(256 * i, 256 * i + 256)
        for t, (lhs, a, b) in enumerate(((h2t, dga, dgb), (h2t, dua, dub), (gmt, hida, hidb))):
            rhs = jnp.concatenate([a[:, cols], b[:, cols]], axis=0)
            g_out[36 * (6 * t + i) : 36 * (6 * t + i) + 36] = as_units(dot(lhs, rhs, 1, 0))
    da = both_rows(daa[:, 128:384], dab[:, 128:384])
    g_out[648:672] = as_units(dot(ot[0:384], da, 1, 0))


def late_grads(h1a, h1b, dqa, dqb, oa, ob, daa, dab, g_out):
    h1t = both_rows(h1a, h1b).T
    ot = jnp.concatenate([oa[...], ob[...]], axis=1)
    dat = both_rows(daa, dab).T

    def rows(first, last):
        return jnp.concatenate([dqa[first:last, :], dqb[first:last, :]], axis=1)

    g_out[0:36] = as_units(dot(h1t, rows(0, 256), 1, 1))
    g_out[36:72] = as_units(dot(h1t, rows(256, 512), 1, 1))
    mixed = [dot(h1t, rows(512, 640), 1, 1), dot(ot, dat[0:128], 1, 1)]
    g_out[72:108] = as_units(jnp.concatenate(mixed, axis=1))
    g_out[108:120] = as_units(dot(ot[384:576], dat[128:384], 1, 1))
    low = jnp.concatenate([dat[384:576], jnp.zeros((64, 256), BF16)], axis=0)
    high = jnp.concatenate([jnp.zeros((192, 256), BF16), rows(640, 704)], axis=0)
    g_out[120:156] = as_units(dot(ot, low, 1, 1) + dot(h1t, high, 1, 1))
    g_out[156:192] = as_units(dot(h1t, rows(704, 960), 1, 1))


def spread_kernel(
    early, late, x_in, g_in, gains, ga_out, gm_out, x_out, g_out, gate_out, up_out, down_out, q_out, k_out, v_out, o_out, big, small, kt, vt, sems
):
    def block(ref, first, count=36):
        return ref[first : first + count].reshape(16 * count, 256).astype(F32)

    ga_out[...] = gains[0:1, :].reshape(D)
    gm_out[...] = gains[1:2, :].reshape(D)
    cps = [
        pltpu.make_async_copy(x_in, x_out, sems.at[22]),
        pltpu.make_async_copy(g_in, g_out, sems.at[23]),
    ]
    for cp in cps:
        cp.start()
    for t, ref in enumerate((gate_out, up_out, down_out)):
        for i in range(6):
            rows = pl.ds(96 * i, 96)
            for c in range(6):
                big[t, rows, 256 * c : 256 * c + 256] = block(early, 36 * (6 * t + c) + 6 * i, 6)
            cp = pltpu.make_async_copy(big.at[t, rows], ref.at[rows], sems.at[6 * t + i])
            cp.start()
            cps.append(cp)
    small[0, :, 0:256] = block(late, 0)
    small[0, :, 256:512] = block(late, 36)
    mixed = block(late, 72)
    small[0, :, 512:576] = mixed[:, 0:64]
    small[1, :, 0:128] = mixed[:, 128:256]
    kt[0:64, :] = mixed[:, 0:128].T[64:128]
    small[1, 0:384, 128:384] = block(early, 648, 24)
    small[1, 384:576, 128:384] = block(late, 108, 12)
    mixed = block(late, 120)
    small[1, :, 384:576] = mixed[:, 0:192]
    kt[64:128, :] = mixed[:, 128:256].T[64:128]
    last = block(late, 156).T
    kt[128:192, :] = last[0:64]
    vt[...] = last[64:256]
    for i, (src, dst) in enumerate(
        ((small.at[0], q_out), (small.at[1], o_out), (kt, k_out), (vt, v_out))
    ):
        cp = pltpu.make_async_copy(src, dst, sems.at[18 + i])
        cp.start()
        cps.append(cp)
    for cp in cps:
        cp.wait()


def spread(*ins):
    return pl.pallas_call(
        spread_kernel,
        name="spread",
        out_shape=(
            sds((D,), F32), sds((D,), F32), X_T, X_T, sds((D, FF), F32), sds((D, FF), F32), sds((D, FF), F32), sds((D, D), F32),
            sds((KV, D), F32), sds((KV, D), F32), sds((D, D), F32),
        ),
        in_specs=[VM] * 5,
        out_specs=(VM,) * 2 + (ANY,) * 9,
        scratch_shapes=[
            pltpu.VMEM((3, D, FF), F32),
            pltpu.VMEM((2, D, D), F32),
            pltpu.VMEM((KV, D), F32),
            pltpu.VMEM((KV, D), F32),
            DMA((24,)),
        ],
        compiler_params=params(None, 30 << 20),
    )(*ins)


def reduce_kernel(
    mid_ref, dq, dkv, x, dx1, ga, wq, wk, wv, cos, sin, h10, h11, dqkv1, ob0, ob1, da0, da1,
    gga1, ggm0, ggm1, early_out, late_out, gain_out, fin_out,
    late_ref, early_mid, came, half, one, gather, two, three, mid, gain_in, gain_sum, fin_ref, fin_in, dqkv0,
    s_e, r_e, s_l, r_l, gs, gr, fs, fr
):
    row, seq, n, w = place()
    torus = Torus(row, n, w)
    core = torus.core
    bar = pltpu.get_barrier_semaphore()
    pl.semaphore_signal(bar, inc=1, device_id=torus.partner, device_id_type=MESH)
    for axis in range(3):
        for k in range(1, 4):
            pl.semaphore_signal(bar, inc=1, device_id=torus.along(axis, k)[0], device_id_type=MESH)
    mirror = (row, 8 * (7 - n) + w)
    g, gga0 = project_back(
        dq, dkv, x[...], dx1[...], as_row(ga), wq, wk, wv, cos[...], sin[...], dqkv0
    )
    fin_ref[...] = g.T
    late_grads(h10, h11, dqkv0, dqkv1, ob0, ob1, da0, da1, late_ref)
    gain_sum[0] = jnp.concatenate(
        [gga0 + gga1[...], ggm0[...] + ggm1[...], jnp.zeros((6, D), F32)], axis=0
    )

    @pl.when(core == 1)
    def _():
        pl.semaphore_signal(bar, inc=1, device_id=mirror, device_id_type=MESH)
        pl.semaphore_wait(bar, 11)

    @pl.when(core == 0)
    def _():
        pl.semaphore_wait(bar, 10)

    early = Reduce(torus, EARLY, s_e, r_e)
    late = Reduce(torus, LATE, s_l, r_l)
    late.exchange(late_ref, came)

    def early_chunk(chunk):
        for p in range(3):
            if chunk == 0:
                early.got(4, p)
            early.fifth(p, early_mid, early_out, chunk, 4)

    for p in range(3):
        early.fourth(p, mid_ref, early_mid)
    move = remote(fin_ref, fin_in, fs, fr, mirror)

    @pl.when(core == 1)
    def _():
        move.start()

    gains = []

    def gain_round(i, peers, count, at):
        gain_in[i, at] = gain_sum[i]
        for k, peer in enumerate(peers):
            cp = remote(gain_sum.at[i], gain_in.at[i, at], gs.at[i, k], gr.at[i, k], peer)
            cp.start()
            gains.append(cp)

    def gain_total(i, peers, count):
        for cp in gains[-peers:]:
            cp.wait_recv()
        return sum(gain_in[i, j] for j in range(count))

    def axis_peers(axis):
        return [torus.along(axis, k)[0] for k in range(1, 4)]

    gain_round(0, [torus.partner], 2, core)
    for p in range(3):
        late.first(p, late_ref, came, half, one)
    early_chunk(0)
    gain_sum[1] = gain_total(0, 1, 2)
    gain_round(1, axis_peers(0), 4, torus.spot[0])
    for p in range(3):
        late.second(p, half, one, gather, two)
    early_chunk(1)
    gain_sum[2] = gain_total(1, 3, 4)
    gain_round(2, axis_peers(1), 4, torus.spot[1])
    for p in range(3):
        late.third(p, gather, two, three)
    early_chunk(2)
    gain_sum[3] = gain_total(2, 3, 4)
    gain_round(3, axis_peers(2), 4, torus.spot[2])
    for p in range(3):
        late.fourth(p, three, mid)
    early_chunk(3)
    for p in range(3):
        early.sixth(p, early_out, 4)
    gain_out[...] = gain_total(3, 3, 4)
    for p in range(3):
        late.got(4, p)
        late.fifth(p, mid, late_out)
    for p in range(3):
        late.sixth(p, late_out)

    @pl.when(core == 1)
    def _():
        move.wait()
        fin_out[...] = fin_in[...]

    @pl.when(core == 0)
    def _():
        fin_out[...] = fin_ref[...]

    for cp in gains:
        cp.wait_send()
    for p in range(3):
        early.got(6, p)
        late.got(6, p)
    early.finish()
    late.finish()


def reduce_all(*ins):
    u = LATE
    return pl.pallas_call(
        reduce_kernel,
        name="reduce_all",
        out_shape=(
            sds(units(96 * EARLY), BF16), sds(units(96 * LATE), BF16), sds((8, D), F32), X_T
        ),
        in_specs=[VM] * len(ins),
        out_specs=(VM,) * 4,
        scratch_shapes=[
            pltpu.VMEM(shape, BF16)
            for shape in (
                units(96 * u), units(4 * EARLY, 3), units(48 * u), units(48 * u), units(4 * u, 3, 3), units(4 * u, 3), units(u, 3, 3),
                units(u, 3, 4), units(4 * u, 3),
            )
        ]
        + [
            pltpu.VMEM((4, 4, 8, D), F32),
            pltpu.VMEM((4, 8, D), F32),
            pltpu.VMEM((D, TOK), F32),
            pltpu.VMEM((D, TOK), F32),
            pltpu.VMEM((960, TOK), BF16),
        ]
        + [DMA((11, 3, 4))] * 4
        + [DMA((4, 4)), DMA((4, 4)), DMA, DMA],
        compiler_params=params(4, 24 << 20),
        cost_estimate=cost(40),
    )(*ins)


def on_device(
    tokens, cotangent, segment_ids, gain_attn, wq, wk, wv, wo, gain_mlp, wg, wu, wd
):
    ga, gm = gain_attn, gain_mlp
    wk, wv, wd = wk.T, wv.T, wd.T
    w_q, w_k, w_v = sds((D, D), BF16), sds((KV, D), BF16), sds((KV, D), BF16)
    table = sds((32, TOK), F32)
    x0, h10, starts, cos, sin, qa0, kva0, part, stat = attend(
        True,
        [tokens[0].T, segment_ids, ga, wq, wk, wv, begin()],
        [HBM, HBM, VM, HBM, HBM, HBM, VM],
        [(o, VM) for o in (X_S, H_S, sds((2, 1, 4 * TOK), jnp.int32), table, table)]
        + [(sds(*a), HBM) for a in GATHERED],
        [
            pltpu.VMEM((D, TOK), F32),
            pltpu.VMEM((64, 1, TOK), jnp.int32),
            pltpu.VMEM((64, 1, TOK), jnp.int32),
        ]
        + [DMA((8,))] * 4
        + [DMA((2,)), DMA]
        + buffers(w_q, w_k, w_v)
        + [DMA((3,))],
        1,
        20 << 20,
    )
    cot, h11, x1, m0, h20, inv0, gate0, up0, hid0, o0, lse0, qa1, kva1, part, stat = attend(
        False,
        [part, stat, x0, cotangent[0].T, ga, wq, wk, wv, wo, gm, wg, wu, wd, cos, sin, starts],
        [VM] * 16,
        [(o, VM) for o in (X_S, H_S, X_S, X_S, H_S, sds((TOK, TOK), F32))]
        + [(F_S, HBM), (F_S, HBM)]
        + [(o, VM) for o in (FB_S, sds((D, TOK), F32), sds((16, TOK), F32))],
        [pltpu.VMEM((TOK, FF), F32), pltpu.VMEM((TOK, FF), F32), DMA((2,)), pltpu.VMEM((D, TOK), F32),
         DMA((2,)), DMA],
        2,
        20 << 20,
    )
    h21, hid1, ob1, gm1, dg1, du1, da1, dx1, ggm1, dq, dkv, output = attend_back(
        False,
        [part, stat, x1, cot, wo, gm, wg, wu, wd, qa1, kva1, starts],
        [VM] * 12,
        [H_S, FB_S, Q_T, H_S, FB_S, FB_S, H_S, X_S, G_S],
        [pltpu.VMEM((D, TOK), F32), pltpu.VMEM((16, TOK), F32)],
        20 << 20,
    )
    dqkv1, gga1, da0, dx0, ggm0, ob0, dq, dkv, mid = attend_back(
        True,
        [dq, dkv, x1, dx1, ga, wq, wk, wv, cos, sin, m0, inv0, gate0, up0, wo, gm, wg, wu, wd, o0,
         lse0, ob1, da1, h20, h21, dg1, du1, hid0, hid1, gm1, qa0, kva0, starts],
        [VM] * 33,
        [sds((960, TOK), BF16), G_S, H_S, X_S, G_S, Q_T],
        [pltpu.VMEM((TOK, D), BF16), pltpu.VMEM((TOK, FF), BF16), pltpu.VMEM((TOK, FF), BF16)],
        28 << 20,
    )
    early, late, gains, grad_tokens = reduce_all(
        mid, dq, dkv, x0, dx0, ga, wq, wk, wv, cos, sin, h10, h11, dqkv1, ob0, ob1, da0, da1, gga1,
        ggm0, ggm1
    )
    gga, ggm, output, grad_tokens, gate, up, down, query, key, value, out = spread(
        early, late, output, grad_tokens, gains
    )
    return (
        output.T[None], grad_tokens.T[None], gga, query, key.T, value.T, out, ggm, gate, up,
        down.T,
    )


def solution(mesh):
    rows = P("rows", "seq", None)
    in_specs = (rows, rows, P("rows", "seq")) + (P(),) * 9
    out_specs = (rows, rows) + (P(),) * 9
    return jax.shard_map(
        on_device, mesh=mesh, in_specs=in_specs, out_specs=out_specs, check_vma=False
    )
```

```python
import functools
import math

import jax
import jax.numpy as jnp
from jax import lax
from jax.experimental import pallas as pl
from jax.experimental.pallas import tpu as pltpu
from jax.sharding import PartitionSpec as P

F32 = jnp.float32
BF16 = jnp.bfloat16
MESH = pl.DeviceIdType.MESH

D = 576
HEADS = 9
HD = 64
KV = 192
FF = 1536
TOK = 128
DOCS = 16
EPS = 1e-05
SCALE = 0.125
EXP_SCALE = SCALE * 1.4426950408889634
MASKED = -1e30
LOWEST = -1e20

VM = pl.BlockSpec(memory_space=pltpu.VMEM)
DMA = pltpu.SemaphoreType.DMA


def dot(a, b, ca, cb):
    return lax.dot_general(a, b, (((ca,), (cb,)), ((), ())), preferred_element_type=F32)


def sds(shape, dtype):
    return jax.ShapeDtypeStruct(shape, dtype)


def params(collective=None, limit=50 << 20):
    if collective is None:
        return pltpu.CompilerParams(vmem_limit_bytes=limit)
    return pltpu.CompilerParams(
        vmem_limit_bytes=limit, collective_id=collective, has_side_effects=True
    )


def cost(us):
    return pl.CostEstimate(flops=us * 1000000000, bytes_accessed=us * 1000000, transcendentals=0)


def place():
    seq = lax.axis_index("seq")
    row = lax.axis_index("rows")
    return row, seq, seq // 8, lax.rem(seq, 8)


def slot_of(w):
    return lax.rem(w, 2) * 4 + w // 2


def octet_of(n, w):
    return jnp.where(lax.rem(w, 2) == 0, n, 7 - n)


def greet(row, n, w):
    bar = pltpu.get_barrier_semaphore()
    for k in range(1, 8):
        pl.semaphore_signal(
            bar, inc=1, device_id=(row, 8 * n + lax.rem(w + k, 8)), device_id_type=MESH
        )
        pl.semaphore_signal(
            bar, inc=1, device_id=(row, 8 * lax.rem(n + k, 8) + w), device_id_type=MESH
        )
    return bar


def remote(src, dst, send, recv, target):
    return pltpu.make_async_remote_copy(
        src_ref=src,
        dst_ref=dst,
        send_sem=send,
        recv_sem=recv,
        device_id=target,
        device_id_type=MESH,
    )


def as_row(ref):
    return ref[...]


def norm_in(x, gain):
    inverse = lax.rsqrt(jnp.mean(x * x, axis=-1, keepdims=True) + EPS)
    return (x * inverse * gain).astype(BF16), inverse


def norm_back(x, inverse, gain, grad):
    scaled = grad * gain
    grad_gain = jnp.sum(grad * (x * inverse), axis=0, keepdims=True)
    inner = jnp.mean(scaled * x, axis=-1, keepdims=True)
    return inverse * scaled - x * (inverse * inverse * inverse) * inner, grad_gain


def project(x, gain, wq, wk, wv, h_out):
    h, _ = norm_in(x, gain)
    h_out[...] = h
    return dot(h, wq[...], 1, 0).T, dot(wk[...], h, 1, 1), dot(wv[...], h, 1, 1).astype(BF16)


def rotate(qt, kt, vt, cos, sin, q_out, kv_out):
    scaled_cos, scaled_sin = cos * EXP_SCALE, sin * EXP_SCALE
    for i in range(HEADS):
        a = qt[HD * i : HD * i + 32]
        b = qt[HD * i + 32 : HD * i + 64]
        q_out[HD * i : HD * i + 32, :] = (a * scaled_cos - b * scaled_sin).astype(BF16)
        q_out[HD * i + 32 : HD * i + 64, :] = (b * scaled_cos + a * scaled_sin).astype(BF16)
    for i in range(3):
        a = kt[HD * i : HD * i + 32]
        b = kt[HD * i + 32 : HD * i + 64]
        kv_out[TOK * i : TOK * i + 32, :] = (a * cos - b * sin).astype(BF16)
        kv_out[TOK * i + 32 : TOK * i + 64, :] = (b * cos + a * sin).astype(BF16)
        kv_out[TOK * i + 64 : TOK * i + 128, :] = vt[HD * i : HD * i + 64]


def combine(part, stat, o_out, lse_out):
    for g in range(3):
        tops = [stat[i, 8 * g : 8 * g + 3, :] for i in range(4)]
        top = functools.reduce(jnp.maximum, tops)
        factors = [jnp.exp2(t - top) for t in tops]
        total = sum(f * stat[i, 8 * g + 4 : 8 * g + 7, :] for i, f in enumerate(factors))
        inverse = 1.0 / total
        factors = [f * inverse for f in factors]
        lse_out[3 * g : 3 * g + 3, :] = top + jnp.log2(total)
        for j in range(3):
            rows = slice(192 * g + HD * j, 192 * g + HD * j + HD)
            o_out[rows, :] = sum(
                part[i, rows, :].astype(F32) * factors[i][j : j + 1, :] for i in range(4)
            )


def feed_forward(x, o_t, wo, gain, wg, wu, wd):
    x1 = x + dot(o_t, wo[...], 0, 0)
    h2, inverse = norm_in(x1, gain)
    gate = dot(h2, wg[...], 1, 0)
    up = dot(h2, wu[...], 1, 0)
    hid = (gate * jax.nn.sigmoid(gate) * up).astype(BF16)
    return x1, h2, inverse, gate, up, hid, x1 + dot(hid, wd[...], 1, 1)


def feed_back(g, x1, inverse, gate, up, wo, gain, wg, wu, wd, o_ref, lse,
              do_out, stat_out, gm_out, dgate_out, dup_out, da_out):
    gm = g.astype(BF16)
    gm_out[...] = gm
    dhid = dot(gm, wd[...], 1, 0)
    sg = jax.nn.sigmoid(gate)
    dgate = (dhid * up * sg * (1.0 + gate * (1.0 - sg))).astype(BF16)
    dup = (dhid * gate * sg).astype(BF16)
    dgate_out[...] = dgate
    dup_out[...] = dup
    dh2 = dot(dgate, wg[...], 1, 1) + dot(dup, wu[...], 1, 1)
    dy, grad_gain = norm_back(x1, inverse, gain, dh2)
    dx1 = g + dy
    da = dx1.astype(BF16)
    da_out[...] = da
    do_t = dot(wo[...], da, 1, 1).astype(BF16)
    do_out[...] = do_t
    stat_out[...] = jnp.zeros(stat_out.shape, F32)
    stat_out[0:HEADS, :] = lse
    for h in range(HEADS):
        rows = slice(HD * h, HD * h + HD)
        stat_out[16 + h : 17 + h, :] = jnp.sum(
            do_t[rows].astype(F32) * o_ref[rows, :], axis=0, keepdims=True
        )
    return dx1, grad_gain


def project_back(dq_part, dkv_part, x, dx1, gain, wq, wk, wv, cos, sin, dqkv_out):
    for h in range(HEADS + 3):
        part, base, many = (dq_part, HD * h, 4) if h < HEADS else (dkv_part, TOK * (h - HEADS), 8)
        a = sum(part[i, base : base + 32, :].astype(F32) for i in range(many))
        b = sum(part[i, base + 32 : base + 64, :].astype(F32) for i in range(many))
        dqkv_out[HD * h : HD * h + 32, :] = (a * cos + b * sin).astype(BF16)
        dqkv_out[HD * h + 32 : HD * h + 64, :] = (b * cos - a * sin).astype(BF16)
    for g in range(3):
        base = TOK * g + HD
        dqkv_out[D + KV + HD * g : D + KV + HD * g + HD, :] = sum(
            dkv_part[i, base : base + HD, :].astype(F32) for i in range(8)
        ).astype(BF16)
    dh1 = (
        dot(dqkv_out[0:D, :], wq[...], 0, 1)
        + dot(dqkv_out[D : D + KV, :], wk[...], 0, 0)
        + dot(dqkv_out[D + KV :, :], wv[...], 0, 0)
    )
    inverse = lax.rsqrt(jnp.mean(x * x, axis=-1, keepdims=True) + EPS)
    dy, grad_gain = norm_back(x, inverse, gain, dh1)
    return dx1 + dy, grad_gain


Q_T = sds((D, TOK), BF16)
KV_T = sds((2 * KV, TOK), BF16)
H_S = sds((TOK, D), BF16)
X_S = sds((TOK, D), F32)
X_T = sds((D, TOK), F32)
F_S = sds((TOK, FF), F32)
FB_S = sds((TOK, FF), BF16)
ST_S = sds((32, TOK), F32)
G_S = sds((1, D), F32)


ANY = pl.BlockSpec(memory_space=pl.ANY)
HBM = pl.BlockSpec(memory_space=pltpu.HBM)


class Lazy:
    def __init__(self, src, buf, sem):
        self.copy = pltpu.make_async_copy(src, buf, sem)
        self.copy.start()
        self.buf, self.waited = buf, False

    def ref(self):
        if not self.waited:
            self.copy.wait()
            self.waited = True
        return self.buf

    def __getitem__(self, index):
        return self.ref()[index]


def fetch(srcs, bufs, sems):
    return [Lazy(src, buf, sems.at[i]) for i, (src, buf) in enumerate(zip(srcs, bufs))]


def buffers(*arrays):
    return [pltpu.VMEM(a.shape, a.dtype) for a in arrays] + [DMA((len(arrays),))]


def begin_kernel(out):
    out[...] = jnp.zeros(out.shape, F32)


def begin():
    return pl.pallas_call(
        begin_kernel,
        name="begin",
        out_shape=sds((8, TOK), F32),
        out_specs=VM,
        compiler_params=params(None, 1 << 20),
        cost_estimate=cost(30),
    )()


def mirrored(ctx, src, dst, send, recv):
    move = remote(src, dst, send.at[0], recv, (ctx.row, 8 * (7 - ctx.n) + ctx.w))
    stay = pltpu.make_async_copy(src, dst, send.at[1])

    def both(if_one, if_zero):
        pl.when(ctx.core == 1)(if_one)
        pl.when(ctx.core == 0)(if_zero)

    return lambda: both(move.start, stay.start), lambda: both(move.wait, stay.wait)


def first_part(ctx, ins, outs, scratch):
    tok, ids_ref, ga, wq, wk, wv, _ = ins
    x_out, h_out, starts_ref, cos_ref, sin_ref, q_save, kv_save = outs
    (tok_in, ids_all, starts_all, ysend, yrecv, xsend, xrecv, tsend, trecv,
     bq, bk, bv, bsem, ssem) = scratch
    row, n, w = ctx.row, ctx.n, ctx.w
    seq = 8 * n + w
    get_ids = pltpu.make_async_copy(ids_ref, ids_all.at[seq], ssem.at[0])
    get_ids.start()
    wq, wk, wv = fetch([wq, wk, wv], [bq, bk, bv], bsem)
    get_ids.wait()
    ctx.ready()
    start, wait = mirrored(ctx, tok, tok_in, tsend, trecv)
    start()
    sent = []
    for k in range(1, 8):
        cp = remote(
            ids_all.at[seq], ids_all.at[seq], ysend.at[k], yrecv.at[k],
            (row, 8 * n + lax.rem(w + k, 8)),
        )
        cp.start()
        sent.append(cp)
    for cp in sent:
        cp.wait()
    own = ids_all.at[pl.ds(8 * n, 8)]
    sent = []
    for k in range(1, 8):
        cp = remote(own, own, xsend.at[k], xrecv.at[k], (row, 8 * lax.rem(n + k, 8) + w))
        cp.start()
        sent.append(cp)
    wait()
    x = tok_in[...].T
    x_out[...] = x
    raw = project(x, as_row(ga), wq, wk, wv, h_out)
    for cp in sent:
        cp.wait()

    ids = jnp.concatenate([ids_all[i] for i in range(64)], axis=0)
    total = jnp.zeros((64, TOK), jnp.int32)
    for doc in range(DOCS - 1):
        count = jnp.where(ids == doc, 1.0, 0.0)
        count = jnp.sum(jnp.sum(count, axis=0, keepdims=True), axis=1, keepdims=True)
        total = total + jnp.where(ids > doc, count.astype(jnp.int32), 0)
    starts_all[...] = total[:, None, :]
    for half in range(2):
        octet = n if half == 0 else 7 - n
        for y in range(4):
            starts_ref[half, :, TOK * y : TOK * y + TOK] = starts_all[8 * octet + 2 * y + half]
    mine = 8 * octet_of(n, w) + w
    pos = mine * TOK + lax.broadcasted_iota(jnp.int32, (1, TOK), 1) - starts_all[mine]
    line = lax.broadcasted_iota(jnp.int32, (32, TOK), 0).astype(F32)
    angle = jnp.exp(line * (-2.0 / HD) * math.log(10000.0)) * pos.astype(F32)
    cos_ref[...] = jnp.cos(angle)
    sin_ref[...] = jnp.sin(angle)
    rotate(*raw, cos_ref[...], sin_ref[...], ctx.q_own, ctx.kv_own)

    saves = [
        pltpu.make_async_copy(ctx.q_all, q_save, ssem.at[1]),
        pltpu.make_async_copy(ctx.kv_all, kv_save, ssem.at[2]),
    ]

    def arrived():
        for cp in saves:
            cp.start()

    def end():
        for cp in saves:
            cp.wait()

    return None, arrived, end


def middle_part(ctx, ins, outs, scratch):
    part, stat, x, cot, ga, wq, wk, wv, wo, gm, wg, wu, wd, cos, sin = ins
    g_out, h_out, x_out, x1_out, h2_out, inv_out, gate_out, up_out, hid_out, o_out, lse_out = outs
    gate_s, up_s, ssem, cot_in, csend, crecv = scratch
    start, wait = mirrored(ctx, cot, cot_in, csend, crecv)
    saves = [
        pltpu.make_async_copy(gate_s, gate_out, ssem.at[0]),
        pltpu.make_async_copy(up_s, up_out, ssem.at[1]),
    ]
    combine(part, stat, o_out, lse_out)
    x1, h2, inverse, gate, up, hid, x2 = feed_forward(
        x[...], o_out[...].astype(BF16), wo, as_row(gm), wg, wu, wd
    )
    x_out[...] = x2
    raw = project(x2, as_row(ga), wq, wk, wv, h_out)
    rotate(*raw, cos[...], sin[...], ctx.q_own, ctx.kv_own)
    ctx.ready()

    def late():
        x1_out[...] = x1
        h2_out[...] = h2
        inv_out[...] = jnp.broadcast_to(inverse, inv_out.shape)
        gate_s[...] = gate
        up_s[...] = up
        hid_out[...] = hid
        for cp in saves:
            cp.start()
        start()

    def end():
        for cp in saves:
            cp.wait()
        wait()
        g_out[...] = cot_in[...].T

    return late, None, end


def turn_part(ctx, ins, outs, scratch):
    part, stat, x, g, wo, gm, wg, wu, wd = ins
    h2_out, hid_out, ob_out, gmo, dgate, dup, da, dx1_out, gg_out = outs
    o_s, lse_s = scratch
    combine(part, stat, o_s, lse_s)
    ob = o_s[...].astype(BF16)
    ob_out[...] = ob
    x1, h2, inverse, gate, up, hid, x2 = feed_forward(
        x[...], ob, wo, as_row(gm), wg, wu, wd
    )
    h2_out[...] = h2
    hid_out[...] = hid
    ctx.extra[...] = x2.T
    dx1, gg = feed_back(
        g[...], x1, inverse, gate, up, wo, as_row(gm), wg, wu, wd, o_s,
        lse_s[0:HEADS, :], ctx.do_own, ctx.st_own, gmo, dgate, dup, da
    )
    dx1_out[...] = dx1
    gg_out[...] = gg


def between_part(ctx, ins, outs, scratch):
    (dq, dkv, x, dx1, ga, wq, wk, wv, cos, sin, x1, inv, gate, up, wo, gm, wg, wu, wd, o, lse,
     ob1, da1, h20, h21, dg1, du1, hid0, hid1, gm1) = ins
    dqkv_out, gga_out, da, dx1_out, ggm_out, ob_out = outs
    gmo, dgate, dup = scratch
    g, gga = project_back(
        dq, dkv, x[...], dx1[...], as_row(ga), wq, wk, wv, cos[...], sin[...], dqkv_out
    )
    gga_out[...] = gga
    dx0, ggm = feed_back(
        g, x1[...], inv[:, 0:1], gate[...], up[...], wo, as_row(gm), wg, wu, wd, o,
        lse[0:HEADS, :], ctx.do_own, ctx.st_own, gmo, dgate, dup, da
    )
    dx1_out[...] = dx0
    ggm_out[...] = ggm
    ob_out[...] = o[...].astype(BF16)

    def grads():
        early_grads(
            ob_out, ob1, da, da1, h20, h21, dgate, dg1, dup, du1, hid0, hid1, gmo, gm1, ctx.extra
        )

    return grads


class Torus:
    def __init__(self, row, n, w):
        self.core = lax.rem(w, 2)
        self.spot = (n // 2, w // 2, 2 * row + lax.rem(n, 2))
        self.partner = self.device(self.spot, 1 - self.core)

    def device(self, spot, core):
        x, y, z = spot
        return (z // 2, ((x * 2 + lax.rem(z, 2)) * 4 + y) * 2 + core)

    def along(self, axis, k):
        to = list(self.spot)
        to[axis] = lax.rem(self.spot[axis] + k, 4)
        return self.device(to, self.core), to[axis]


class Reduce:
    def __init__(self, torus, u, send, recv):
        self.torus, self.u, self.send, self.recv = torus, u, send, recv
        self.box = {}

    def go(self, stage, p, k, src, dst, peer):
        cp = remote(src, dst, self.send.at[stage, p, k], self.recv.at[stage, p, k], peer)
        cp.start()
        self.box.setdefault((stage, p), []).append(cp)

    def got(self, stage, p):
        for cp in self.box[stage, p]:
            cp.wait_recv()

    def finish(self):
        for cps in self.box.values():
            for cp in cps:
                cp.wait_send()

    def exchange(self, src, came):
        u, core = self.u, self.torus.core
        for p in range(3):
            self.go(
                0, p, 0, src.at[pl.ds(48 * u * (1 - core) + 16 * u * p, 16 * u)],
                came.at[pl.ds(16 * u * p, 16 * u)], self.torus.partner,
            )

    def first(self, p, src, came, half, one):
        u = self.u
        self.got(0, p)

        def quarter(i, carry):
            at = pl.ds(16 * u * p + 4 * u * i, 4 * u)
            mine = src[pl.ds(48 * u * self.torus.core + 16 * u * p + 4 * u * i, 4 * u)]
            half[at] = (mine.astype(F32) + came[at].astype(F32)).astype(BF16)
            return carry

        lax.fori_loop(0, 4, quarter, 0)
        for k in range(1, 4):
            peer, at = self.torus.along(p, k)
            self.go(1, p, k, half.at[pl.ds(16 * u * p + 4 * u * at, 4 * u)], one.at[p, k - 1], peer)

    def second(self, p, half, one, gather, two):
        u = self.u
        self.got(1, p)
        mine = half[pl.ds(16 * u * p + 4 * u * self.torus.spot[p], 4 * u)]
        gather[p] = (mine.astype(F32) + sum(one[p, k].astype(F32) for k in range(3))).astype(BF16)
        for k in range(1, 4):
            peer, at = self.torus.along((p + 1) % 3, k)
            self.go(2, p, k, gather.at[p, pl.ds(u * at, u)], two.at[p, k - 1], peer)

    def third(self, p, gather, two, three):
        u = self.u
        self.got(2, p)
        c = self.torus.spot[(p + 2) % 3]
        mine = gather[p, pl.ds(u * self.torus.spot[(p + 1) % 3], u)]
        three[p, c] = (mine.astype(F32) + sum(two[p, k].astype(F32) for k in range(3))).astype(BF16)
        for k in range(1, 4):
            self.go(3, p, k, three.at[p, c], three.at[p, c], self.torus.along((p + 2) % 3, k)[0])

    def fourth(self, p, three, mid):
        u = self.u
        if (3, p) in self.box:
            self.got(3, p)
        at = pl.ds(u * self.torus.spot[(p + 1) % 3], u)
        mid[p, at] = sum(three[p, k].astype(F32) for k in range(4)).astype(BF16)
        for k in range(1, 4):
            self.go(4, p, k, mid.at[p, at], mid.at[p, at], self.torus.along((p + 1) % 3, k)[0])

    def fifth(self, p, mid, out, chunk=0, chunks=1):
        u = self.u
        size = 4 * u // chunks
        base = 48 * u * self.torus.core + 16 * u * p + 4 * u * self.torus.spot[p]
        at = pl.ds(base + size * chunk, size)
        out[at] = mid[p, size * chunk : size * chunk + size]
        for k in range(1, 4):
            self.go(7 + chunk, p, k, out.at[at], out.at[at], self.torus.along(p, k)[0])

    def sixth(self, p, out, chunks=1):
        u = self.u
        for chunk in range(chunks):
            self.got(7 + chunk, p)
        at = pl.ds(48 * u * self.torus.core + 16 * u * p, 16 * u)
        self.go(6, p, 0, out.at[at], out.at[at], self.torus.partner)


def units(count, *lead):
    return tuple(lead) + (count, 16, 256)


EARLY, LATE = 7, 2


W3 = 12 * TOK


class Spread:
    def __init__(self, row, n, w, send, recv):
        self.core = lax.rem(w, 2)
        self.y = w // 2
        self.own = self.core * 4 + self.y
        self.row, self.n = row, n
        self.partner = (row, 8 * n + 2 * self.y + 1 - self.core)
        self.send, self.recv = send, recv
        self.first, self.passed = {}, {}

    def chip(self, k):
        return (self.row, 8 * self.n + 2 * lax.rem(self.y + k, 4) + self.core)

    def start(self, part, ref):
        self.first[part], self.passed[part] = [], []
        for k in range(1, 4):
            cp = remote(ref(self.own), ref(self.own), self.send.at[part, k], self.recv.at[part, k],
                        self.chip(k))
            cp.start()
            self.first[part].append(cp)
        self.hand(part, ref, self.own, 4)

    def hand(self, part, ref, slot, k):
        cp = remote(ref(slot), ref(slot), self.send.at[part, k], self.recv.at[part, k], self.partner)
        cp.start()
        self.passed[part].append(cp)

    def forward(self, part, ref):
        for k in range(1, 4):
            self.first[part][k - 1].wait_recv()
            self.hand(part, ref, self.core * 4 + lax.rem(self.y + 4 - k, 4), 4 + k)

    def arrive(self, part):
        for cp in self.passed[part]:
            cp.wait_recv()

    def finish(self):
        for part in self.first:
            for cp in self.first[part] + self.passed[part]:
                cp.wait_send()


def turns(n):
    return (n + 2) // 2


def fill_masks(bias, starts_ref, n, w):
    turn = turns(n)

    def one(t, carry):
        sel = jnp.where(t >= turn, 1, 0)
        kc = jnp.where(t >= turn, t - turn, t)
        line = lax.broadcasted_iota(jnp.int32, (256, 1), 0)
        key = (2 * kc + line // TOK) * 1024 + w * TOK + lax.rem(line, TOK)
        col = lax.broadcasted_iota(jnp.int32, (1, 512), 1)
        octet = jnp.where(sel == 0, n, 7 - n)
        query = octet * 1024 + (2 * (col // TOK) + sel) * TOK + lax.rem(col, TOK)
        bias[t] = jnp.where((key >= starts_ref[sel]) & (key <= query), 0.0, MASKED)
        return carry

    lax.fori_loop(0, 5, one, 0)


def over_keys(n, sel, step):
    octet = jnp.where(sel == 0, n, 7 - n)
    base = jnp.where(sel == 0, 0, turns(n))
    whole = (octet + 1) // 2

    def chunk(kc, carry):
        step(base + kc, kc, 2 * TOK)
        return carry

    lax.fori_loop(0, whole, chunk, 0)

    @pl.when(lax.rem(octet + 1, 2) == 1)
    def _():
        step(base + whole, whole, TOK)


def three_heads(ref, sel, g):
    return jnp.concatenate(
        [
            ref[4 * sel + y, HD * h : HD * h + HD, :]
            for h in range(3 * g, 3 * g + 3)
            for y in range(4)
        ],
        axis=1,
    )


def key_blocks(ref, kc, first, keys):
    return jnp.concatenate(
        [ref[2 * kc + i, first : first + HD, :] for i in range(keys // TOK)], axis=1
    )


def by_chip(value, y):
    return jnp.concatenate(
        [value[:, 512 * j + TOK * y : 512 * j + TOK * y + TOK] for j in range(3)], axis=0
    )


class Context:
    pass


def attend_kernel(first, n_in, n_out, *refs):
    ins, refs = refs[:n_in], refs[n_in:]
    outs, refs = refs[:n_out], refs[n_out:]
    if first:
        part_ref, stat_ref, q_all, kv_all = refs[:4]
    else:
        q_all, kv_all, part_ref, stat_ref = refs[:4]
    (k_nat, bias, top, total, acc, o_send, o_recv, r_send, r_recv, o_y, s_y,
     qs, qr, ks, kr, ps, pr, ys, yr) = refs[4:23]
    starts_ref = outs[2] if first else ins[-1]
    row, seq, n, w = place()
    bar = greet(row, n, w)
    core, y = lax.rem(w, 2), w // 2
    own_k = octet_of(n, w)
    queries = Spread(row, n, w, qs, qr)
    ctx = Context()
    ctx.row, ctx.n, ctx.w, ctx.core = row, n, w, core
    ctx.q_own, ctx.kv_own = q_all.at[queries.own], kv_all.at[own_k]
    ctx.q_all, ctx.kv_all = q_all, kv_all
    ctx.ready = lambda: pl.semaphore_wait(bar, 14)
    if first:
        late, arrived, end = first_part(ctx, ins, outs, refs[23:])
    else:
        late, arrived, end = middle_part(ctx, ins[:-1], outs, refs[23:])

    def q_part(g):
        return lambda slot: q_all.at[slot, pl.ds(192 * g, 192)]

    keys = {}
    for g in range(3):
        keys[g] = []
        for k in range(1, 8):
            block = kv_all.at[own_k, pl.ds(TOK * g, TOK)]
            cp = remote(
                block, block, ks.at[g, k], kr.at[g, k], (row, 8 * lax.rem(n + k, 8) + w)
            )
            cp.start()
            keys[g].append(cp)
        queries.start(g, q_part(g))
    fill_masks(bias, starts_ref, n, w)
    queries.forward(0, q_part(0))

    def phase(g, sel):
        top[...] = jnp.full(top.shape, LOWEST, F32)
        total[...] = jnp.zeros(total.shape, F32)
        acc[...] = jnp.zeros(acc.shape, F32)

        def step(at, kc, keys):
            scores = dot(k_nat[kc, 0:keys], three_heads(q_all, sel, g), 1, 0)
            mask = bias[at, 0:keys]
            weights, shrinks = [], []
            for j in range(3):
                cols = slice(512 * j, 512 * j + 512)
                s = scores[:, cols] + mask
                old = top[:, cols]
                new = jnp.maximum(old, jnp.max(s, axis=0, keepdims=True))
                p = jnp.exp2(s - new)
                shrink = jnp.exp2(old - new)
                top[:, cols] = new
                total[:, cols] = total[:, cols] * shrink + jnp.sum(p, axis=0, keepdims=True)
                weights.append(p.astype(BF16))
                shrinks.append(shrink)
            values = key_blocks(kv_all, kc, TOK * g + HD, keys)
            acc[...] = acc[...] * jnp.concatenate(shrinks, axis=1) + dot(
                values, jnp.concatenate(weights, axis=1), 1, 0
            )

        over_keys(n, sel, step)

    pairs, flying = [], []
    for g in range(3):
        for cp in keys[g]:
            cp.wait_recv()
        for j in range(8):
            k_nat[j // 2, (j % 2) * TOK : (j % 2) * TOK + TOK, :] = jnp.transpose(
                kv_all[j, TOK * g : TOK * g + HD, :]
            )
        queries.arrive(g)
        if g == 2 and arrived is not None:
            arrived()
        phase(g, 1 - core)
        o_send[g] = acc[...].astype(BF16)
        r_send[g, 0] = top[...]
        r_send[g, 1] = total[...]
        both = [
            remote(o_send.at[g], o_recv.at[g], ps.at[0, g], pr.at[0, g], queries.partner),
            remote(r_send.at[g], r_recv.at[g], ps.at[1, g], pr.at[1, g], queries.partner),
        ]
        for cp in both:
            cp.start()
        pairs += both
        if g < 2:
            queries.forward(g + 1, q_part(g + 1))
        if g == 0 and late is not None:
            late()
        phase(g, core)
        for cp in both:
            cp.wait_recv()
        new = jnp.maximum(top[...], r_recv[g, 0])
        mine = jnp.exp2(top[...] - new)
        theirs = jnp.exp2(r_recv[g, 0] - new)
        length = total[...] * mine + r_recv[g, 1] * theirs
        out = (acc[...] * mine + o_recv[g].astype(F32) * theirs).astype(BF16)
        for i in range(4):
            o_y[g, i] = by_chip(out, i)
            for j in range(3):
                cols = slice(512 * j + TOK * i, 512 * j + TOK * i + TOK)
                s_y[g, i, j : j + 1, :] = new[:, cols]
                s_y[g, i, 4 + j : 5 + j, :] = length[:, cols]
        for k in range(1, 4):
            to = lax.rem(y + k, 4)
            peer = queries.chip(k)
            for cp in (
                remote(o_y.at[g, to], part_ref.at[y, pl.ds(192 * g, 192)], ys.at[0, g, k],
                       yr.at[0, g, k], peer),
                remote(s_y.at[g, to], stat_ref.at[y, pl.ds(8 * g, 8)], ys.at[1, g, k],
                       yr.at[1, g, k], peer),
            ):
                cp.start()
                flying.append(cp)
        part_ref[y, 192 * g : 192 * g + 192, :] = o_y[g, y]
        stat_ref[y, 8 * g : 8 * g + 8, :] = s_y[g, y]
    queries.finish()
    for g in range(3):
        for cp in keys[g]:
            cp.wait_send()
    for cp in pairs:
        cp.wait_send()
    for cp in flying:
        cp.wait()
    if end is not None:
        end()


GATHERED = [((8, D, TOK), BF16), ((8, 2 * KV, TOK), BF16)]


def attend(first, ins, specs, outs, scratch, collective, limit):
    count = len(outs)
    here = [] if first else [sds(*a) for a in GATHERED]
    there = [pltpu.VMEM(*a) for a in GATHERED] if first else []
    outs = outs + [(o, VM) for o in here + [sds((4, D, TOK), BF16), sds((4, 24, TOK), F32)]]
    return pl.pallas_call(
        functools.partial(attend_kernel, first, len(ins), count),
        name="attend_first" if first else "attend",
        out_shape=tuple(o for o, _ in outs),
        in_specs=specs,
        out_specs=tuple(spec for _, spec in outs),
        scratch_shapes=there
        + [
            pltpu.VMEM((4, 256, HD), BF16),
            pltpu.VMEM((5, 256, 512), F32),
            pltpu.VMEM((1, W3), F32),
            pltpu.VMEM((1, W3), F32),
            pltpu.VMEM((HD, W3), F32),
            pltpu.VMEM((3, HD, W3), BF16),
            pltpu.VMEM((3, HD, W3), BF16),
            pltpu.VMEM((3, 2, 1, W3), F32),
            pltpu.VMEM((3, 2, 1, W3), F32),
            pltpu.VMEM((3, 4, 192, TOK), BF16),
            pltpu.VMEM((3, 4, 8, TOK), F32),
            DMA((3, 8)), DMA((3, 8)), DMA((3, 8)), DMA((3, 8)),
            DMA((2, 3)), DMA((2, 3)), DMA((2, 3, 4)), DMA((2, 3, 4)),
        ]
        + scratch,
        compiler_params=params(collective, limit),
        cost_estimate=cost(30),
    )(*ins)


def attend_back_kernel(carry_sum, n_in, n_out, n_more, *refs):
    ins, refs = refs[:n_in], refs[n_in:]
    outs, refs = refs[:n_out], refs[n_out:]
    (dq_part, dkv_part, extra_out, do_all, st_all, k_nat, v_nat, bias, rows_s, dq, dq_other, dkv, q_send,
     q_recv, q_y, kv_low, extra, qs, qr, ks, kr, ps, pr, ys, yr, es, er) = refs[:27]
    more, scratch = refs[27 : 27 + n_more], refs[27 + n_more :]
    q_all, kv_all, starts_ref = ins[-3:]
    ctx = Context()
    ctx.q_all, ctx.kv_all = q_all, kv_all
    row, seq, n, w = place()
    bar = greet(row, n, w)
    torus = Torus(row, n, w)
    if carry_sum:
        came, one, gather, two = more
        half = extra.at[pl.ds(48 * EARLY * lax.rem(w, 2), 48 * EARLY)]
        for k in range(1, 4):
            pl.semaphore_signal(bar, inc=1, device_id=torus.along(2, k)[0], device_id_type=MESH)
        early = Reduce(torus, EARLY, es, er)
    else:
        (extra_in,) = more
        move = remote(extra, extra_in, es, er, (row, 8 * (7 - n) + w))
    core, y = lax.rem(w, 2), w // 2
    own_k = octet_of(n, w)
    grads = Spread(row, n, w, qs, qr)
    ctx.do_own, ctx.st_own, ctx.extra = do_all.at[grads.own], st_all.at[grads.own], extra
    make = between_part if carry_sum else turn_part
    grads_of = make(ctx, ins[:-3], outs, scratch)
    pl.semaphore_wait(bar, 17 if carry_sum else 14)

    def part(g):
        return lambda slot: do_all.at[slot, pl.ds(192 * g, 192)]

    def stats(slot):
        return st_all.at[slot]

    grads.start(3, stats)
    for g in range(3):
        grads.start(g, part(g))
    if carry_sum:
        grads_of()
        early.exchange(extra, came)
    fill_masks(bias, starts_ref, n, w)
    for g in range(3):
        for j in range(8):
            at = slice((j % 2) * TOK, (j % 2) * TOK + TOK)
            k_nat[g, j // 2, at, :] = jnp.transpose(kv_all[j, TOK * g : TOK * g + HD, :])
            v_nat[g, j // 2, at, :] = jnp.transpose(kv_all[j, TOK * g + HD : TOK * g + TOK, :])
    grads.forward(3, stats)
    grads.forward(0, part(0))
    if carry_sum:
        for p in range(3):
            early.first(p, extra, came, half, one)
    if not carry_sum:

        @pl.when(core == 1)
        def _():
            move.start()

    def phase(g, sel, dq):
        dq[...] = jnp.zeros(dq.shape, F32)
        for i, first in enumerate((0, 16)):
            for j in range(3):
                for c in range(4):
                    at = 512 * j + TOK * c
                    line = first + 3 * g + j
                    rows_s[i, :, at : at + TOK] = st_all[4 * sel + c, line : line + 1, :]

        def step(at, kc, keys):
            qt = three_heads(q_all, sel, g)
            dt = three_heads(do_all, sel, g)
            scores = dot(k_nat[g, kc, 0:keys], qt, 1, 0)
            dp = dot(v_nat[g, kc, 0:keys], dt, 1, 0)
            mask = bias[at, 0:keys]
            ps_, ds_ = [], []
            for j in range(3):
                cols = slice(512 * j, 512 * j + 512)
                p = jnp.exp2(scores[:, cols] + mask - rows_s[0, :, cols])
                ds_.append((p * (dp[:, cols] - rows_s[1, :, cols])).astype(BF16))
                ps_.append(p.astype(BF16))
            p = jnp.concatenate(ps_, axis=1)
            ds = jnp.concatenate(ds_, axis=1)
            dkv[kc, 0:HD, 0:keys] += dot(ds, qt, 1, 1).T
            dkv[kc, HD:, 0:keys] += dot(p, dt, 1, 1).T
            dq[...] += dot(key_blocks(kv_all, kc, TOK * g, keys), ds, 1, 0)

        over_keys(n, sel, step)

    pairs, flying = [], []
    for g in range(3):
        dkv[...] = jnp.zeros(dkv.shape, F32)
        if g == 0:
            phase(g, core, dq)
            grads.forward(1, part(1))
            grads.arrive(3)
        grads.arrive(g)
        phase(g, 1 - core, dq_other)
        q_send[g] = (dq_other[...] * SCALE).astype(BF16)
        pair = remote(q_send.at[g], q_recv.at[g], ps.at[g], pr.at[g], grads.partner)
        pair.start()
        pairs.append(pair)
        if g == 1:
            grads.forward(2, part(2))
        if g == 2 and carry_sum:
            for p in range(3):
                early.second(p, half, one, gather, two)
        if g > 0:
            phase(g, core, dq)
        for j in range(8):
            cols = slice((j % 2) * TOK, (j % 2) * TOK + TOK)
            kv_low[g, j, 0:HD, :] = (dkv[j // 2, 0:HD, cols] * (SCALE / EXP_SCALE)).astype(BF16)
            kv_low[g, j, HD:, :] = dkv[j // 2, HD:, cols].astype(BF16)
        for k in range(1, 8):
            to = lax.rem(n + k, 8)
            cp = remote(
                kv_low.at[g, octet_of(to, w)], dkv_part.at[n, pl.ds(TOK * g, TOK)], ks.at[g, k],
                kr.at[g, k], (row, 8 * to + w),
            )
            cp.start()
            flying.append(cp)
        pair.wait_recv()
        out = (dq[...] * SCALE + q_recv[g].astype(F32)).astype(BF16)
        for i in range(4):
            q_y[g, i] = by_chip(out, i)
        for k in range(1, 4):
            to = lax.rem(y + k, 4)
            cp = remote(q_y.at[g, to], dq_part.at[y, pl.ds(192 * g, 192)], ys.at[g, k], yr.at[g, k],
                        grads.chip(k))
            cp.start()
            flying.append(cp)
        dkv_part[n, TOK * g : TOK * g + TOK, :] = kv_low[g, own_k]
        dq_part[y, 192 * g : 192 * g + 192, :] = q_y[g, y]
        if carry_sum:
            for p in range(3):
                if g == 2:
                    early.third(p, gather, two, extra_out)
    grads.finish()
    for cp in pairs:
        cp.wait_send()
    for cp in flying:
        cp.wait()
    if carry_sum:
        for p in range(3):
            early.got(3, p)
        early.finish()
    else:

        @pl.when(core == 1)
        def _():
            move.wait()
            extra_out[...] = extra_in[...]

        @pl.when(core == 0)
        def _():
            extra_out[...] = extra[...]


def attend_back(carry_sum, ins, specs, outs, scratch, limit):
    if carry_sum:
        u = EARLY
        extra_shape = sds(units(u, 3, 4), BF16)
        extra = pltpu.VMEM(units(96 * u), BF16)
        sems = [DMA((5, 3, 4))] * 2
        more = [
            pltpu.VMEM(shape, BF16)
            for shape in (
                units(48 * u), units(4 * u, 3, 3), units(4 * u, 3), units(u, 3, 3),
            )
        ]
    else:
        extra_shape = X_T
        extra = pltpu.VMEM((D, TOK), F32)
        sems = [DMA, DMA]
        more = [pltpu.VMEM((D, TOK), F32)]
    return pl.pallas_call(
        functools.partial(attend_back_kernel, carry_sum, len(ins), len(outs), len(more)),
        name="attend_back_sum" if carry_sum else "attend_back",
        out_shape=tuple(outs + [sds((4, D, TOK), BF16), sds((8, 2 * KV, TOK), BF16), extra_shape]),
        in_specs=specs,
        out_specs=(VM,) * (len(outs) + 3),
        scratch_shapes=[
            pltpu.VMEM((8, D, TOK), BF16),
            pltpu.VMEM((8, 32, TOK), F32),
            pltpu.VMEM((3, 4, 256, HD), BF16),
            pltpu.VMEM((3, 4, 256, HD), BF16),
            pltpu.VMEM((5, 256, 512), F32),
            pltpu.VMEM((2, 1, W3), F32),
            pltpu.VMEM((HD, W3), F32),
            pltpu.VMEM((HD, W3), F32),
            pltpu.VMEM((4, TOK, 256), F32),
            pltpu.VMEM((3, HD, W3), BF16),
            pltpu.VMEM((3, HD, W3), BF16),
            pltpu.VMEM((3, 4, 192, TOK), BF16),
            pltpu.VMEM((3, 8, TOK, TOK), BF16),
            extra,
            DMA((4, 8)), DMA((4, 8)), DMA((3, 8)), DMA((3, 8)),
            DMA((3,)), DMA((3,)), DMA((3, 4)), DMA((3, 4)),
        ]
        + sems
        + more
        + scratch,
        compiler_params=params(5 if carry_sum else 3, limit),
        cost_estimate=cost(40),
    )(*ins)


def both_rows(a, b):
    return jnp.concatenate([a[...], b[...]], axis=0)


def as_units(value):
    return value.astype(BF16).reshape(units(value.shape[0] // 16))


def early_grads(oa, ob, daa, dab, h2a, h2b, dga, dgb, dua, dub, hida, hidb, gma, gmb, g_out):
    ot = jnp.concatenate([oa[...], ob[...]], axis=1)
    h2t = both_rows(h2a, h2b).T
    gmt = both_rows(gma, gmb).T
    for i in range(6):
        cols = slice(256 * i, 256 * i + 256)
        for t, (lhs, a, b) in enumerate(((h2t, dga, dgb), (h2t, dua, dub), (gmt, hida, hidb))):
            rhs = jnp.concatenate([a[:, cols], b[:, cols]], axis=0)
            g_out[36 * (6 * t + i) : 36 * (6 * t + i) + 36] = as_units(dot(lhs, rhs, 1, 0))
    da = both_rows(daa[:, 128:384], dab[:, 128:384])
    g_out[648:672] = as_units(dot(ot[0:384], da, 1, 0))


def late_grads(h1a, h1b, dqa, dqb, oa, ob, daa, dab, g_out):
    h1t = both_rows(h1a, h1b).T
    ot = jnp.concatenate([oa[...], ob[...]], axis=1)
    dat = both_rows(daa, dab).T

    def rows(first, last):
        return jnp.concatenate([dqa[first:last, :], dqb[first:last, :]], axis=1)

    g_out[0:36] = as_units(dot(h1t, rows(0, 256), 1, 1))
    g_out[36:72] = as_units(dot(h1t, rows(256, 512), 1, 1))
    mixed = [dot(h1t, rows(512, 640), 1, 1), dot(ot, dat[0:128], 1, 1)]
    g_out[72:108] = as_units(jnp.concatenate(mixed, axis=1))
    g_out[108:120] = as_units(dot(ot[384:576], dat[128:384], 1, 1))
    low = jnp.concatenate([dat[384:576], jnp.zeros((64, 256), BF16)], axis=0)
    high = jnp.concatenate([jnp.zeros((192, 256), BF16), rows(640, 704)], axis=0)
    g_out[120:156] = as_units(dot(ot, low, 1, 1) + dot(h1t, high, 1, 1))
    g_out[156:192] = as_units(dot(h1t, rows(704, 960), 1, 1))


def spread_kernel(
    early, late, x_in, g_in, gains, ga_out, gm_out, x_out, g_out, gate_out, up_out, down_out, q_out, k_out, v_out, o_out, big, small, kt, vt, sems
):
    def block(ref, first, count=36):
        return ref[first : first + count].reshape(16 * count, 256).astype(F32)

    ga_out[...] = gains[0:1, :]
    gm_out[...] = gains[1:2, :]
    cps = [
        pltpu.make_async_copy(x_in, x_out, sems.at[22]),
        pltpu.make_async_copy(g_in, g_out, sems.at[23]),
    ]
    for cp in cps:
        cp.start()
    for t, ref in enumerate((gate_out, up_out, down_out)):
        for i in range(6):
            rows = pl.ds(96 * i, 96)
            for c in range(6):
                big[t, rows, 256 * c : 256 * c + 256] = block(early, 36 * (6 * t + c) + 6 * i, 6)
            cp = pltpu.make_async_copy(big.at[t, rows], ref.at[rows], sems.at[6 * t + i])
            cp.start()
            cps.append(cp)
    small[0, :, 0:256] = block(late, 0)
    small[0, :, 256:512] = block(late, 36)
    mixed = block(late, 72)
    small[0, :, 512:576] = mixed[:, 0:64]
    small[1, :, 0:128] = mixed[:, 128:256]
    kt[0:64, :] = mixed[:, 0:128].T[64:128]
    small[1, 0:384, 128:384] = block(early, 648, 24)
    small[1, 384:576, 128:384] = block(late, 108, 12)
    mixed = block(late, 120)
    small[1, :, 384:576] = mixed[:, 0:192]
    kt[64:128, :] = mixed[:, 128:256].T[64:128]
    last = block(late, 156).T
    kt[128:192, :] = last[0:64]
    vt[...] = last[64:256]
    for i, (src, dst) in enumerate(
        ((small.at[0], q_out), (small.at[1], o_out), (kt, k_out), (vt, v_out))
    ):
        cp = pltpu.make_async_copy(src, dst, sems.at[18 + i])
        cp.start()
        cps.append(cp)
    for cp in cps:
        cp.wait()


def spread(*ins):
    return pl.pallas_call(
        spread_kernel,
        name="spread",
        out_shape=(
            G_S, G_S, X_T, X_T, sds((D, FF), F32), sds((D, FF), F32), sds((D, FF), F32), sds((D, D), F32),
            sds((KV, D), F32), sds((KV, D), F32), sds((D, D), F32),
        ),
        in_specs=[VM] * 5,
        out_specs=(VM,) * 2 + (ANY,) * 9,
        scratch_shapes=[
            pltpu.VMEM((3, D, FF), F32),
            pltpu.VMEM((2, D, D), F32),
            pltpu.VMEM((KV, D), F32),
            pltpu.VMEM((KV, D), F32),
            DMA((24,)),
        ],
        compiler_params=params(None, 30 << 20),
    )(*ins)


def reduce_kernel(
    mid_ref, dq, dkv, x, dx1, ga, wq, wk, wv, cos, sin, h10, h11, dqkv1, ob0, ob1, da0, da1,
    gga1, ggm0, ggm1, early_out, late_out, gain_out, fin_out,
    late_ref, early_mid, came, half, one, gather, two, three, mid, gain_in, gain_sum, fin_ref, fin_in, dqkv0,
    s_e, r_e, s_l, r_l, gs, gr, fs, fr
):
    row, seq, n, w = place()
    torus = Torus(row, n, w)
    core = torus.core
    bar = pltpu.get_barrier_semaphore()
    pl.semaphore_signal(bar, inc=1, device_id=torus.partner, device_id_type=MESH)
    for axis in range(3):
        for k in range(1, 4):
            pl.semaphore_signal(bar, inc=1, device_id=torus.along(axis, k)[0], device_id_type=MESH)
    mirror = (row, 8 * (7 - n) + w)
    g, gga0 = project_back(
        dq, dkv, x[...], dx1[...], as_row(ga), wq, wk, wv, cos[...], sin[...], dqkv0
    )
    fin_ref[...] = g.T
    late_grads(h10, h11, dqkv0, dqkv1, ob0, ob1, da0, da1, late_ref)
    gain_sum[0] = jnp.concatenate(
        [gga0 + gga1[...], ggm0[...] + ggm1[...], jnp.zeros((6, D), F32)], axis=0
    )

    @pl.when(core == 1)
    def _():
        pl.semaphore_signal(bar, inc=1, device_id=mirror, device_id_type=MESH)
        pl.semaphore_wait(bar, 11)

    @pl.when(core == 0)
    def _():
        pl.semaphore_wait(bar, 10)

    early = Reduce(torus, EARLY, s_e, r_e)
    late = Reduce(torus, LATE, s_l, r_l)
    late.exchange(late_ref, came)

    def early_chunk(chunk):
        for p in range(3):
            if chunk == 0:
                early.got(4, p)
            early.fifth(p, early_mid, early_out, chunk, 4)

    for p in range(3):
        early.fourth(p, mid_ref, early_mid)
    move = remote(fin_ref, fin_in, fs, fr, mirror)

    @pl.when(core == 1)
    def _():
        move.start()

    gains = []

    def gain_round(i, peers, count, at):
        gain_in[i, at] = gain_sum[i]
        for k, peer in enumerate(peers):
            cp = remote(gain_sum.at[i], gain_in.at[i, at], gs.at[i, k], gr.at[i, k], peer)
            cp.start()
            gains.append(cp)

    def gain_total(i, peers, count):
        for cp in gains[-peers:]:
            cp.wait_recv()
        return sum(gain_in[i, j] for j in range(count))

    def axis_peers(axis):
        return [torus.along(axis, k)[0] for k in range(1, 4)]

    gain_round(0, [torus.partner], 2, core)
    for p in range(3):
        late.first(p, late_ref, came, half, one)
    early_chunk(0)
    gain_sum[1] = gain_total(0, 1, 2)
    gain_round(1, axis_peers(0), 4, torus.spot[0])
    for p in range(3):
        late.second(p, half, one, gather, two)
    early_chunk(1)
    gain_sum[2] = gain_total(1, 3, 4)
    gain_round(2, axis_peers(1), 4, torus.spot[1])
    for p in range(3):
        late.third(p, gather, two, three)
    early_chunk(2)
    gain_sum[3] = gain_total(2, 3, 4)
    gain_round(3, axis_peers(2), 4, torus.spot[2])
    for p in range(3):
        late.fourth(p, three, mid)
    early_chunk(3)
    gain_out[...] = gain_total(3, 3, 4)
    for p in range(3):
        late.got(4, p)
        late.fifth(p, mid, late_out)
    for p in range(3):
        early.sixth(p, early_out, 4)
    for p in range(3):
        late.sixth(p, late_out)

    @pl.when(core == 1)
    def _():
        move.wait()
        fin_out[...] = fin_in[...]

    @pl.when(core == 0)
    def _():
        fin_out[...] = fin_ref[...]

    for cp in gains:
        cp.wait_send()
    for p in range(3):
        early.got(6, p)
        late.got(6, p)
    early.finish()
    late.finish()


def reduce_all(*ins):
    u = LATE
    return pl.pallas_call(
        reduce_kernel,
        name="reduce_all",
        out_shape=(
            sds(units(96 * EARLY), BF16), sds(units(96 * LATE), BF16), sds((8, D), F32), X_T
        ),
        in_specs=[VM] * len(ins),
        out_specs=(VM,) * 4,
        scratch_shapes=[
            pltpu.VMEM(shape, BF16)
            for shape in (
                units(96 * u), units(4 * EARLY, 3), units(48 * u), units(48 * u), units(4 * u, 3, 3), units(4 * u, 3), units(u, 3, 3),
                units(u, 3, 4), units(4 * u, 3),
            )
        ]
        + [
            pltpu.VMEM((4, 4, 8, D), F32),
            pltpu.VMEM((4, 8, D), F32),
            pltpu.VMEM((D, TOK), F32),
            pltpu.VMEM((D, TOK), F32),
            pltpu.VMEM((960, TOK), BF16),
        ]
        + [DMA((11, 3, 4))] * 4
        + [DMA((4, 4)), DMA((4, 4)), DMA, DMA],
        compiler_params=params(4, 24 << 20),
        cost_estimate=cost(40),
    )(*ins)


def on_device(
    tokens, cotangent, segment_ids, gain_attn, wq, wk, wv, wo, gain_mlp, wg, wu, wd
):
    ga, gm = gain_attn[None], gain_mlp[None]
    wk, wv, wd = wk.T, wv.T, wd.T
    w_q, w_k, w_v = sds((D, D), BF16), sds((KV, D), BF16), sds((KV, D), BF16)
    table = sds((32, TOK), F32)
    x0, h10, starts, cos, sin, qa0, kva0, part, stat = attend(
        True,
        [tokens[0].T, segment_ids, ga, wq, wk, wv, begin()],
        [HBM, HBM, VM, HBM, HBM, HBM, VM],
        [(o, VM) for o in (X_S, H_S, sds((2, 1, 4 * TOK), jnp.int32), table, table)]
        + [(sds(*a), HBM) for a in GATHERED],
        [
            pltpu.VMEM((D, TOK), F32),
            pltpu.VMEM((64, 1, TOK), jnp.int32),
            pltpu.VMEM((64, 1, TOK), jnp.int32),
        ]
        + [DMA((8,))] * 4
        + [DMA((2,)), DMA]
        + buffers(w_q, w_k, w_v)
        + [DMA((3,))],
        1,
        20 << 20,
    )
    cot, h11, x1, m0, h20, inv0, gate0, up0, hid0, o0, lse0, qa1, kva1, part, stat = attend(
        False,
        [part, stat, x0, cotangent[0].T, ga, wq, wk, wv, wo, gm, wg, wu, wd, cos, sin, starts],
        [VM] * 16,
        [(o, VM) for o in (X_S, H_S, X_S, X_S, H_S, sds((TOK, TOK), F32))]
        + [(F_S, HBM), (F_S, HBM)]
        + [(o, VM) for o in (FB_S, sds((D, TOK), F32), sds((16, TOK), F32))],
        [pltpu.VMEM((TOK, FF), F32), pltpu.VMEM((TOK, FF), F32), DMA((2,)), pltpu.VMEM((D, TOK), F32),
         DMA((2,)), DMA],
        2,
        20 << 20,
    )
    h21, hid1, ob1, gm1, dg1, du1, da1, dx1, ggm1, dq, dkv, output = attend_back(
        False,
        [part, stat, x1, cot, wo, gm, wg, wu, wd, qa1, kva1, starts],
        [VM] * 12,
        [H_S, FB_S, Q_T, H_S, FB_S, FB_S, H_S, X_S, G_S],
        [pltpu.VMEM((D, TOK), F32), pltpu.VMEM((16, TOK), F32)],
        20 << 20,
    )
    dqkv1, gga1, da0, dx0, ggm0, ob0, dq, dkv, mid = attend_back(
        True,
        [dq, dkv, x1, dx1, ga, wq, wk, wv, cos, sin, m0, inv0, gate0, up0, wo, gm, wg, wu, wd, o0,
         lse0, ob1, da1, h20, h21, dg1, du1, hid0, hid1, gm1, qa0, kva0, starts],
        [VM] * 33,
        [sds((960, TOK), BF16), G_S, H_S, X_S, G_S, Q_T],
        [pltpu.VMEM((TOK, D), BF16), pltpu.VMEM((TOK, FF), BF16), pltpu.VMEM((TOK, FF), BF16)],
        28 << 20,
    )
    early, late, gains, grad_tokens = reduce_all(
        mid, dq, dkv, x0, dx0, ga, wq, wk, wv, cos, sin, h10, h11, dqkv1, ob0, ob1, da0, da1, gga1,
        ggm0, ggm1
    )
    gga, ggm, output, grad_tokens, gate, up, down, query, key, value, out = spread(
        early, late, output, grad_tokens, gains
    )
    return (
        output.T[None], grad_tokens.T[None], gga[0], query, key.T, value.T, out, ggm[0], gate, up,
        down.T,
    )


def solution(mesh):
    rows = P("rows", "seq", None)
    in_specs = (rows, rows, P("rows", "seq")) + (P(),) * 9
    out_specs = (rows, rows) + (P(),) * 9
    return jax.shard_map(
        on_device, mesh=mesh, in_specs=in_specs, out_specs=out_specs, check_vma=False
    )
```

```python
import functools
import math

import jax
import jax.numpy as jnp
from jax import lax
from jax.experimental import pallas as pl
from jax.experimental.pallas import tpu as pltpu
from jax.sharding import PartitionSpec as P

F32 = jnp.float32
BF16 = jnp.bfloat16
MESH = pl.DeviceIdType.MESH

D = 576
HEADS = 9
HD = 64
KV = 192
FF = 1536
TOK = 128
DOCS = 16
EPS = 1e-05
SCALE = 0.125
EXP_SCALE = SCALE * 1.4426950408889634
MASKED = -1e30
LOWEST = -1e20
FAR = (4, 3, 5, 2, 6, 1, 7)

VM = pl.BlockSpec(memory_space=pltpu.VMEM)
DMA = pltpu.SemaphoreType.DMA


def dot(a, b, ca, cb):
    return lax.dot_general(a, b, (((ca,), (cb,)), ((), ())), preferred_element_type=F32)


def sds(shape, dtype):
    return jax.ShapeDtypeStruct(shape, dtype)


def params(collective=None, limit=50 << 20):
    if collective is None:
        return pltpu.CompilerParams(vmem_limit_bytes=limit)
    return pltpu.CompilerParams(
        vmem_limit_bytes=limit, collective_id=collective, has_side_effects=True
    )


def cost(us):
    return pl.CostEstimate(flops=us * 1000000000, bytes_accessed=us * 1000000, transcendentals=0)


def place():
    seq = lax.axis_index("seq")
    row = lax.axis_index("rows")
    return row, seq, seq // 8, lax.rem(seq, 8)


def slot_of(w):
    return lax.rem(w, 2) * 4 + w // 2


def octet_of(n, w):
    return jnp.where(lax.rem(w, 2) == 0, n, 7 - n)


def greet(row, n, w):
    bar = pltpu.get_barrier_semaphore()
    for k in range(1, 8):
        pl.semaphore_signal(
            bar, inc=1, device_id=(row, 8 * n + lax.rem(w + k, 8)), device_id_type=MESH
        )
        pl.semaphore_signal(
            bar, inc=1, device_id=(row, 8 * lax.rem(n + k, 8) + w), device_id_type=MESH
        )
    return bar


def remote(src, dst, send, recv, target):
    return pltpu.make_async_remote_copy(
        src_ref=src,
        dst_ref=dst,
        send_sem=send,
        recv_sem=recv,
        device_id=target,
        device_id_type=MESH,
    )


def as_row(ref):
    return ref[...].reshape(1, D)


def norm_in(x, gain):
    inverse = lax.rsqrt(jnp.mean(x * x, axis=-1, keepdims=True) + EPS)
    return (x * inverse * gain).astype(BF16), inverse


def norm_back(x, inverse, gain, grad):
    scaled = grad * gain
    grad_gain = jnp.sum(grad * (x * inverse), axis=0, keepdims=True)
    inner = jnp.mean(scaled * x, axis=-1, keepdims=True)
    return inverse * scaled - x * (inverse * inverse * inverse) * inner, grad_gain


def project(x, gain, wq, wk, wv, h_out):
    h, _ = norm_in(x, gain)
    h_out[...] = h
    return dot(h, wq[...], 1, 0).T, dot(wk[...], h, 1, 1), dot(wv[...], h, 1, 1).astype(BF16)


def rotate(qt, kt, vt, cos, sin, q_out, kv_out):
    scaled_cos, scaled_sin = cos * EXP_SCALE, sin * EXP_SCALE
    for i in range(HEADS):
        a = qt[HD * i : HD * i + 32]
        b = qt[HD * i + 32 : HD * i + 64]
        q_out[HD * i : HD * i + 32, :] = (a * scaled_cos - b * scaled_sin).astype(BF16)
        q_out[HD * i + 32 : HD * i + 64, :] = (b * scaled_cos + a * scaled_sin).astype(BF16)
    for i in range(3):
        a = kt[HD * i : HD * i + 32]
        b = kt[HD * i + 32 : HD * i + 64]
        kv_out[TOK * i : TOK * i + 32, :] = (a * cos - b * sin).astype(BF16)
        kv_out[TOK * i + 32 : TOK * i + 64, :] = (b * cos + a * sin).astype(BF16)
        kv_out[TOK * i + 64 : TOK * i + 128, :] = vt[HD * i : HD * i + 64]


def combine(part, stat, o_out, lse_out):
    for g in range(3):
        tops = [stat[i, 8 * g : 8 * g + 3, :] for i in range(4)]
        top = functools.reduce(jnp.maximum, tops)
        factors = [jnp.exp2(t - top) for t in tops]
        total = sum(f * stat[i, 8 * g + 4 : 8 * g + 7, :] for i, f in enumerate(factors))
        inverse = 1.0 / total
        factors = [f * inverse for f in factors]
        lse_out[3 * g : 3 * g + 3, :] = top + jnp.log2(total)
        for j in range(3):
            rows = slice(192 * g + HD * j, 192 * g + HD * j + HD)
            o_out[rows, :] = sum(
                part[i, rows, :].astype(F32) * factors[i][j : j + 1, :] for i in range(4)
            )


def feed_forward(x, o_t, wo, gain, wg, wu, wd):
    x1 = x + dot(o_t, wo[...], 0, 0)
    h2, inverse = norm_in(x1, gain)
    gate = dot(h2, wg[...], 1, 0)
    up = dot(h2, wu[...], 1, 0)
    hid = (gate * jax.nn.sigmoid(gate) * up).astype(BF16)
    return x1, h2, inverse, gate, up, hid, x1 + dot(hid, wd[...], 1, 1)


def feed_back(g, x1, inverse, gate, up, wo, gain, wg, wu, wd, o_ref, lse,
              do_out, stat_out, gm_out, dgate_out, dup_out, da_out):
    gm = g.astype(BF16)
    gm_out[...] = gm
    dhid = dot(gm, wd[...], 1, 0)
    sg = jax.nn.sigmoid(gate)
    dgate = (dhid * up * sg * (1.0 + gate * (1.0 - sg))).astype(BF16)
    dup = (dhid * gate * sg).astype(BF16)
    dgate_out[...] = dgate
    dup_out[...] = dup
    dh2 = dot(dgate, wg[...], 1, 1) + dot(dup, wu[...], 1, 1)
    dy, grad_gain = norm_back(x1, inverse, gain, dh2)
    dx1 = g + dy
    da = dx1.astype(BF16)
    da_out[...] = da
    do_t = dot(wo[...], da, 1, 1).astype(BF16)
    do_out[...] = do_t
    stat_out[...] = jnp.zeros(stat_out.shape, F32)
    stat_out[0:HEADS, :] = lse
    for h in range(HEADS):
        rows = slice(HD * h, HD * h + HD)
        stat_out[16 + h : 17 + h, :] = jnp.sum(
            do_t[rows].astype(F32) * o_ref[rows, :], axis=0, keepdims=True
        )
    return dx1, grad_gain


def project_back(dq_part, dkv_part, x, dx1, gain, wq, wk, wv, cos, sin, dqkv_out):
    for h in range(HEADS + 3):
        part, base, many = (dq_part, HD * h, 4) if h < HEADS else (dkv_part, TOK * (h - HEADS), 8)
        a = sum(part[i, base : base + 32, :].astype(F32) for i in range(many))
        b = sum(part[i, base + 32 : base + 64, :].astype(F32) for i in range(many))
        dqkv_out[HD * h : HD * h + 32, :] = (a * cos + b * sin).astype(BF16)
        dqkv_out[HD * h + 32 : HD * h + 64, :] = (b * cos - a * sin).astype(BF16)
    for g in range(3):
        base = TOK * g + HD
        dqkv_out[D + KV + HD * g : D + KV + HD * g + HD, :] = sum(
            dkv_part[i, base : base + HD, :].astype(F32) for i in range(8)
        ).astype(BF16)
    dh1 = (
        dot(dqkv_out[0:D, :], wq[...], 0, 1)
        + dot(dqkv_out[D : D + KV, :], wk[...], 0, 0)
        + dot(dqkv_out[D + KV :, :], wv[...], 0, 0)
    )
    inverse = lax.rsqrt(jnp.mean(x * x, axis=-1, keepdims=True) + EPS)
    dy, grad_gain = norm_back(x, inverse, gain, dh1)
    return dx1 + dy, grad_gain


Q_T = sds((D, TOK), BF16)
KV_T = sds((2 * KV, TOK), BF16)
H_S = sds((TOK, D), BF16)
X_S = sds((TOK, D), F32)
X_T = sds((D, TOK), F32)
F_S = sds((TOK, FF), F32)
FB_S = sds((TOK, FF), BF16)
ST_S = sds((32, TOK), F32)
G_S = sds((1, D), F32)


ANY = pl.BlockSpec(memory_space=pl.ANY)
HBM = pl.BlockSpec(memory_space=pltpu.HBM)


class Lazy:
    def __init__(self, src, buf, sem):
        self.copy = pltpu.make_async_copy(src, buf, sem)
        self.copy.start()
        self.buf, self.waited = buf, False

    def ref(self):
        if not self.waited:
            self.copy.wait()
            self.waited = True
        return self.buf

    def __getitem__(self, index):
        return self.ref()[index]


def fetch(srcs, bufs, sems):
    return [Lazy(src, buf, sems.at[i]) for i, (src, buf) in enumerate(zip(srcs, bufs))]


def buffers(*arrays):
    return [pltpu.VMEM(a.shape, a.dtype) for a in arrays] + [DMA((len(arrays),))]


def begin_kernel(out):
    out[...] = jnp.zeros(out.shape, F32)


def begin():
    return pl.pallas_call(
        begin_kernel,
        name="begin",
        out_shape=sds((8, TOK), F32),
        out_specs=VM,
        compiler_params=params(None, 1 << 20),
        cost_estimate=cost(30),
    )()


def mirrored(ctx, src, dst, send, recv):
    move = remote(src, dst, send.at[0], recv, (ctx.row, 8 * (7 - ctx.n) + ctx.w))
    stay = pltpu.make_async_copy(src, dst, send.at[1])

    def both(if_one, if_zero):
        pl.when(ctx.core == 1)(if_one)
        pl.when(ctx.core == 0)(if_zero)

    return lambda: both(move.start, stay.start), lambda: both(move.wait, stay.wait)


def first_part(ctx, ins, outs, scratch):
    tok, ids_ref, ga, wq, wk, wv, _ = ins
    x_out, h_out, starts_ref, cos_ref, sin_ref, q_save, kv_save = outs
    (tok_in, ids_all, starts_all, ysend, yrecv, xsend, xrecv, tsend, trecv,
     bq, bk, bv, bsem, ssem) = scratch
    row, n, w = ctx.row, ctx.n, ctx.w
    seq = 8 * n + w
    get_ids = pltpu.make_async_copy(ids_ref, ids_all.at[seq], ssem.at[0])
    get_ids.start()
    wq, wk, wv = fetch([wq, wk, wv], [bq, bk, bv], bsem)
    get_ids.wait()
    ctx.ready()
    start, wait = mirrored(ctx, tok, tok_in, tsend, trecv)
    start()
    sent = []
    for k in range(1, 8):
        cp = remote(
            ids_all.at[seq], ids_all.at[seq], ysend.at[k], yrecv.at[k],
            (row, 8 * n + lax.rem(w + k, 8)),
        )
        cp.start()
        sent.append(cp)
    for cp in sent:
        cp.wait()
    own = ids_all.at[pl.ds(8 * n, 8)]
    sent = []
    for k in range(1, 8):
        cp = remote(own, own, xsend.at[k], xrecv.at[k], (row, 8 * lax.rem(n + k, 8) + w))
        cp.start()
        sent.append(cp)
    wait()
    x = tok_in[...].T
    x_out[...] = x
    raw = project(x, as_row(ga), wq, wk, wv, h_out)
    for cp in sent:
        cp.wait()

    ids = jnp.concatenate([ids_all[i] for i in range(64)], axis=0)
    total = jnp.zeros((64, TOK), jnp.int32)
    for doc in range(DOCS - 1):
        count = jnp.where(ids == doc, 1.0, 0.0)
        count = jnp.sum(jnp.sum(count, axis=0, keepdims=True), axis=1, keepdims=True)
        total = total + jnp.where(ids > doc, count.astype(jnp.int32), 0)
    starts_all[...] = total[:, None, :]
    for half in range(2):
        octet = n if half == 0 else 7 - n
        for y in range(4):
            starts_ref[half, :, TOK * y : TOK * y + TOK] = starts_all[8 * octet + 2 * y + half]
    mine = 8 * octet_of(n, w) + w
    pos = mine * TOK + lax.broadcasted_iota(jnp.int32, (1, TOK), 1) - starts_all[mine]
    line = lax.broadcasted_iota(jnp.int32, (32, TOK), 0).astype(F32)
    angle = jnp.exp(line * (-2.0 / HD) * math.log(10000.0)) * pos.astype(F32)
    cos_ref[...] = jnp.cos(angle)
    sin_ref[...] = jnp.sin(angle)
    rotate(*raw, cos_ref[...], sin_ref[...], ctx.q_own, ctx.kv_own)

    saves = [
        pltpu.make_async_copy(ctx.q_all, q_save, ssem.at[1]),
        pltpu.make_async_copy(ctx.kv_all, kv_save, ssem.at[2]),
    ]

    def arrived():
        for cp in saves:
            cp.start()

    def end():
        for cp in saves:
            cp.wait()

    return None, arrived, end


def middle_part(ctx, ins, outs, scratch):
    part, stat, x, cot, ga, wq, wk, wv, wo, gm, wg, wu, wd, cos, sin = ins
    g_out, h_out, x_out, x1_out, h2_out, inv_out, gate_out, up_out, hid_out, o_out, lse_out = outs
    gate_s, up_s, ssem, cot_in, csend, crecv = scratch
    start, wait = mirrored(ctx, cot, cot_in, csend, crecv)
    saves = [
        pltpu.make_async_copy(gate_s, gate_out, ssem.at[0]),
        pltpu.make_async_copy(up_s, up_out, ssem.at[1]),
    ]
    combine(part, stat, o_out, lse_out)
    x1, h2, inverse, gate, up, hid, x2 = feed_forward(
        x[...], o_out[...].astype(BF16), wo, as_row(gm), wg, wu, wd
    )
    x_out[...] = x2
    raw = project(x2, as_row(ga), wq, wk, wv, h_out)
    rotate(*raw, cos[...], sin[...], ctx.q_own, ctx.kv_own)
    ctx.ready()

    def late():
        x1_out[...] = x1
        h2_out[...] = h2
        inv_out[...] = jnp.broadcast_to(inverse, inv_out.shape)
        gate_s[...] = gate
        up_s[...] = up
        hid_out[...] = hid
        for cp in saves:
            cp.start()
        start()

    def end():
        for cp in saves:
            cp.wait()
        wait()
        g_out[...] = cot_in[...].T

    return late, None, end


def turn_part(ctx, ins, outs, scratch):
    part, stat, x, g, wo, gm, wg, wu, wd = ins
    h2_out, hid_out, ob_out, gmo, dgate, dup, da, dx1_out, gg_out = outs
    o_s, lse_s = scratch
    combine(part, stat, o_s, lse_s)
    ob = o_s[...].astype(BF16)
    ob_out[...] = ob
    x1, h2, inverse, gate, up, hid, x2 = feed_forward(
        x[...], ob, wo, as_row(gm), wg, wu, wd
    )
    h2_out[...] = h2
    hid_out[...] = hid
    ctx.extra[...] = x2.T
    dx1, gg = feed_back(
        g[...], x1, inverse, gate, up, wo, as_row(gm), wg, wu, wd, o_s,
        lse_s[0:HEADS, :], ctx.do_own, ctx.st_own, gmo, dgate, dup, da
    )
    dx1_out[...] = dx1
    gg_out[...] = gg


def between_part(ctx, ins, outs, scratch):
    (dq, dkv, x, dx1, ga, wq, wk, wv, cos, sin, x1, inv, gate, up, wo, gm, wg, wu, wd, o, lse,
     ob1, da1, h20, h21, dg1, du1, hid0, hid1, gm1) = ins
    dqkv_out, gga_out, da, dx1_out, ggm_out, ob_out = outs
    gmo, dgate, dup = scratch
    g, gga = project_back(
        dq, dkv, x[...], dx1[...], as_row(ga), wq, wk, wv, cos[...], sin[...], dqkv_out
    )
    gga_out[...] = gga
    dx0, ggm = feed_back(
        g, x1[...], inv[:, 0:1], gate[...], up[...], wo, as_row(gm), wg, wu, wd, o,
        lse[0:HEADS, :], ctx.do_own, ctx.st_own, gmo, dgate, dup, da
    )
    dx1_out[...] = dx0
    ggm_out[...] = ggm
    ob_out[...] = o[...].astype(BF16)

    def grads():
        early_grads(
            ob_out, ob1, da, da1, h20, h21, dgate, dg1, dup, du1, hid0, hid1, gmo, gm1, ctx.extra
        )

    return grads


class Torus:
    def __init__(self, row, n, w):
        self.core = lax.rem(w, 2)
        self.spot = (n // 2, w // 2, 2 * row + lax.rem(n, 2))
        self.partner = self.device(self.spot, 1 - self.core)

    def device(self, spot, core):
        x, y, z = spot
        return (z // 2, ((x * 2 + lax.rem(z, 2)) * 4 + y) * 2 + core)

    def along(self, axis, k):
        to = list(self.spot)
        to[axis] = lax.rem(self.spot[axis] + k, 4)
        return self.device(to, self.core), to[axis]


class Reduce:
    def __init__(self, torus, u, send, recv):
        self.torus, self.u, self.send, self.recv = torus, u, send, recv
        self.box = {}

    def go(self, stage, p, k, src, dst, peer):
        cp = remote(src, dst, self.send.at[stage, p, k], self.recv.at[stage, p, k], peer)
        cp.start()
        self.box.setdefault((stage, p), []).append(cp)

    def got(self, stage, p):
        for cp in self.box[stage, p]:
            cp.wait_recv()

    def finish(self):
        for cps in self.box.values():
            for cp in cps:
                cp.wait_send()

    def exchange(self, src, came):
        u, core = self.u, self.torus.core
        for p in range(3):
            self.go(
                0, p, 0, src.at[pl.ds(48 * u * (1 - core) + 16 * u * p, 16 * u)],
                came.at[pl.ds(16 * u * p, 16 * u)], self.torus.partner,
            )

    def first(self, p, src, came, half, one):
        u = self.u
        self.got(0, p)

        def quarter(i, carry):
            at = pl.ds(16 * u * p + 4 * u * i, 4 * u)
            mine = src[pl.ds(48 * u * self.torus.core + 16 * u * p + 4 * u * i, 4 * u)]
            half[at] = (mine.astype(F32) + came[at].astype(F32)).astype(BF16)
            return carry

        lax.fori_loop(0, 4, quarter, 0)
        for k in range(1, 4):
            peer, at = self.torus.along(p, k)
            self.go(1, p, k, half.at[pl.ds(16 * u * p + 4 * u * at, 4 * u)], one.at[p, k - 1], peer)

    def second(self, p, half, one, gather, two):
        u = self.u
        self.got(1, p)
        mine = half[pl.ds(16 * u * p + 4 * u * self.torus.spot[p], 4 * u)]
        gather[p] = (mine.astype(F32) + sum(one[p, k].astype(F32) for k in range(3))).astype(BF16)
        for k in range(1, 4):
            peer, at = self.torus.along((p + 1) % 3, k)
            self.go(2, p, k, gather.at[p, pl.ds(u * at, u)], two.at[p, k - 1], peer)

    def third(self, p, gather, two, three):
        u = self.u
        self.got(2, p)
        c = self.torus.spot[(p + 2) % 3]
        mine = gather[p, pl.ds(u * self.torus.spot[(p + 1) % 3], u)]
        three[p, c] = (mine.astype(F32) + sum(two[p, k].astype(F32) for k in range(3))).astype(BF16)
        for k in range(1, 4):
            self.go(3, p, k, three.at[p, c], three.at[p, c], self.torus.along((p + 2) % 3, k)[0])

    def fourth(self, p, three, mid):
        u = self.u
        if (3, p) in self.box:
            self.got(3, p)
        at = pl.ds(u * self.torus.spot[(p + 1) % 3], u)
        mid[p, at] = sum(three[p, k].astype(F32) for k in range(4)).astype(BF16)
        for k in range(1, 4):
            self.go(4, p, k, mid.at[p, at], mid.at[p, at], self.torus.along((p + 1) % 3, k)[0])

    def fifth(self, p, mid, out, chunk=0, chunks=1):
        u = self.u
        size = 4 * u // chunks
        base = 48 * u * self.torus.core + 16 * u * p + 4 * u * self.torus.spot[p]
        at = pl.ds(base + size * chunk, size)
        out[at] = mid[p, size * chunk : size * chunk + size]
        for k in range(1, 4):
            self.go(7 + chunk, p, k, out.at[at], out.at[at], self.torus.along(p, k)[0])

    def sixth(self, p, out, chunks=1):
        u = self.u
        for chunk in range(chunks):
            self.got(7 + chunk, p)
        at = pl.ds(48 * u * self.torus.core + 16 * u * p, 16 * u)
        self.go(6, p, 0, out.at[at], out.at[at], self.torus.partner)


def units(count, *lead):
    return tuple(lead) + (count, 16, 256)


EARLY, LATE = 7, 2


W3 = 12 * TOK


class Spread:
    def __init__(self, row, n, w, send, recv):
        self.core = lax.rem(w, 2)
        self.y = w // 2
        self.own = self.core * 4 + self.y
        self.row, self.n = row, n
        self.partner = (row, 8 * n + 2 * self.y + 1 - self.core)
        self.send, self.recv = send, recv
        self.first, self.passed = {}, {}

    def chip(self, k):
        return (self.row, 8 * self.n + 2 * lax.rem(self.y + k, 4) + self.core)

    def start(self, part, ref):
        self.first[part], self.passed[part] = {}, []
        for k in (2, 1, 3):
            cp = remote(ref(self.own), ref(self.own), self.send.at[part, k], self.recv.at[part, k],
                        self.chip(k))
            cp.start()
            self.first[part][k] = cp
        self.hand(part, ref, self.own, 4)

    def hand(self, part, ref, slot, k):
        cp = remote(ref(slot), ref(slot), self.send.at[part, k], self.recv.at[part, k], self.partner)
        cp.start()
        self.passed[part].append(cp)

    def forward(self, part, ref):
        for k in (1, 3, 2):
            self.first[part][k].wait_recv()
            self.hand(part, ref, self.core * 4 + lax.rem(self.y + 4 - k, 4), 4 + k)

    def arrive(self, part):
        for cp in self.passed[part]:
            cp.wait_recv()

    def finish(self):
        for part in self.first:
            for cp in list(self.first[part].values()) + self.passed[part]:
                cp.wait_send()


def turns(n):
    return (n + 2) // 2


def fill_masks(bias, starts_ref, n, w):
    turn = turns(n)

    def one(t, carry):
        sel = jnp.where(t >= turn, 1, 0)
        kc = jnp.where(t >= turn, t - turn, t)
        line = lax.broadcasted_iota(jnp.int32, (256, 1), 0)
        key = (2 * kc + line // TOK) * 1024 + w * TOK + lax.rem(line, TOK)
        col = lax.broadcasted_iota(jnp.int32, (1, 512), 1)
        octet = jnp.where(sel == 0, n, 7 - n)
        query = octet * 1024 + (2 * (col // TOK) + sel) * TOK + lax.rem(col, TOK)
        bias[t] = jnp.where((key >= starts_ref[sel]) & (key <= query), 0.0, MASKED)
        return carry

    lax.fori_loop(0, 5, one, 0)


def over_keys(n, sel, step):
    octet = jnp.where(sel == 0, n, 7 - n)
    base = jnp.where(sel == 0, 0, turns(n))
    whole = (octet + 1) // 2

    def chunk(kc, carry):
        step(base + kc, kc, 2 * TOK)
        return carry

    lax.fori_loop(0, whole, chunk, 0)

    @pl.when(lax.rem(octet + 1, 2) == 1)
    def _():
        step(base + whole, whole, TOK)


def three_heads(ref, sel, g):
    return jnp.concatenate(
        [
            ref[4 * sel + y, HD * h : HD * h + HD, :]
            for h in range(3 * g, 3 * g + 3)
            for y in range(4)
        ],
        axis=1,
    )


def key_blocks(ref, kc, first, keys):
    return jnp.concatenate(
        [ref[2 * kc + i, first : first + HD, :] for i in range(keys // TOK)], axis=1
    )


def by_chip(value, y):
    return jnp.concatenate(
        [value[:, 512 * j + TOK * y : 512 * j + TOK * y + TOK] for j in range(3)], axis=0
    )


class Context:
    pass


def attend_kernel(first, n_in, n_out, *refs):
    ins, refs = refs[:n_in], refs[n_in:]
    outs, refs = refs[:n_out], refs[n_out:]
    if first:
        part_ref, stat_ref, q_all, kv_all = refs[:4]
    else:
        q_all, kv_all, part_ref, stat_ref = refs[:4]
    (k_nat, bias, top, total, acc, o_send, o_recv, r_send, r_recv, o_y, s_y,
     qs, qr, ks, kr, ps, pr, ys, yr) = refs[4:23]
    starts_ref = outs[2] if first else ins[-1]
    row, seq, n, w = place()
    bar = greet(row, n, w)
    core, y = lax.rem(w, 2), w // 2
    own_k = octet_of(n, w)
    queries = Spread(row, n, w, qs, qr)
    ctx = Context()
    ctx.row, ctx.n, ctx.w, ctx.core = row, n, w, core
    ctx.q_own, ctx.kv_own = q_all.at[queries.own], kv_all.at[own_k]
    ctx.q_all, ctx.kv_all = q_all, kv_all
    ctx.ready = lambda: pl.semaphore_wait(bar, 14)
    if first:
        late, arrived, end = first_part(ctx, ins, outs, refs[23:])
    else:
        late, arrived, end = middle_part(ctx, ins[:-1], outs, refs[23:])

    def q_part(g):
        return lambda slot: q_all.at[slot, pl.ds(192 * g, 192)]

    keys = {}
    for g in range(3):
        queries.start(g, q_part(g))
        keys[g] = []
        for k in FAR:
            block = kv_all.at[own_k, pl.ds(TOK * g, TOK)]
            cp = remote(
                block, block, ks.at[g, k], kr.at[g, k], (row, 8 * lax.rem(n + k, 8) + w)
            )
            cp.start()
            keys[g].append(cp)
    fill_masks(bias, starts_ref, n, w)
    queries.forward(0, q_part(0))

    def phase(g, sel):
        top[...] = jnp.full(top.shape, LOWEST, F32)
        total[...] = jnp.zeros(total.shape, F32)
        acc[...] = jnp.zeros(acc.shape, F32)

        def step(at, kc, keys):
            scores = dot(k_nat[kc, 0:keys], three_heads(q_all, sel, g), 1, 0)
            mask = bias[at, 0:keys]
            weights, shrinks = [], []
            for j in range(3):
                cols = slice(512 * j, 512 * j + 512)
                s = scores[:, cols] + mask
                old = top[:, cols]
                new = jnp.maximum(old, jnp.max(s, axis=0, keepdims=True))
                p = jnp.exp2(s - new)
                shrink = jnp.exp2(old - new)
                top[:, cols] = new
                total[:, cols] = total[:, cols] * shrink + jnp.sum(p, axis=0, keepdims=True)
                weights.append(p.astype(BF16))
                shrinks.append(shrink)
            values = key_blocks(kv_all, kc, TOK * g + HD, keys)
            acc[...] = acc[...] * jnp.concatenate(shrinks, axis=1) + dot(
                values, jnp.concatenate(weights, axis=1), 1, 0
            )

        over_keys(n, sel, step)

    pairs, flying = [], []
    for g in range(3):
        for cp in keys[g]:
            cp.wait_recv()
        for j in range(8):
            k_nat[j // 2, (j % 2) * TOK : (j % 2) * TOK + TOK, :] = jnp.transpose(
                kv_all[j, TOK * g : TOK * g + HD, :]
            )
        queries.arrive(g)
        if g == 2 and arrived is not None:
            arrived()
        phase(g, 1 - core)
        o_send[g] = acc[...].astype(BF16)
        r_send[g, 0] = top[...]
        r_send[g, 1] = total[...]
        both = [
            remote(o_send.at[g], o_recv.at[g], ps.at[0, g], pr.at[0, g], queries.partner),
            remote(r_send.at[g], r_recv.at[g], ps.at[1, g], pr.at[1, g], queries.partner),
        ]
        for cp in both:
            cp.start()
        pairs += both
        if g < 2:
            queries.forward(g + 1, q_part(g + 1))
        if g == 0 and late is not None:
            late()
        phase(g, core)
        for cp in both:
            cp.wait_recv()
        new = jnp.maximum(top[...], r_recv[g, 0])
        mine = jnp.exp2(top[...] - new)
        theirs = jnp.exp2(r_recv[g, 0] - new)
        length = total[...] * mine + r_recv[g, 1] * theirs
        out = (acc[...] * mine + o_recv[g].astype(F32) * theirs).astype(BF16)
        for i in range(4):
            o_y[g, i] = by_chip(out, i)
            for j in range(3):
                cols = slice(512 * j + TOK * i, 512 * j + TOK * i + TOK)
                s_y[g, i, j : j + 1, :] = new[:, cols]
                s_y[g, i, 4 + j : 5 + j, :] = length[:, cols]
        for k in (2, 1, 3):
            to = lax.rem(y + k, 4)
            peer = queries.chip(k)
            for cp in (
                remote(o_y.at[g, to], part_ref.at[y, pl.ds(192 * g, 192)], ys.at[0, g, k],
                       yr.at[0, g, k], peer),
                remote(s_y.at[g, to], stat_ref.at[y, pl.ds(8 * g, 8)], ys.at[1, g, k],
                       yr.at[1, g, k], peer),
            ):
                cp.start()
                flying.append(cp)
        part_ref[y, 192 * g : 192 * g + 192, :] = o_y[g, y]
        stat_ref[y, 8 * g : 8 * g + 8, :] = s_y[g, y]
    queries.finish()
    for g in range(3):
        for cp in keys[g]:
            cp.wait_send()
    for cp in pairs:
        cp.wait_send()
    for cp in flying:
        cp.wait()
    if end is not None:
        end()


GATHERED = [((8, D, TOK), BF16), ((8, 2 * KV, TOK), BF16)]


def attend(first, ins, specs, outs, scratch, collective, limit):
    count = len(outs)
    here = [] if first else [sds(*a) for a in GATHERED]
    there = [pltpu.VMEM(*a) for a in GATHERED] if first else []
    outs = outs + [(o, VM) for o in here + [sds((4, D, TOK), BF16), sds((4, 24, TOK), F32)]]
    return pl.pallas_call(
        functools.partial(attend_kernel, first, len(ins), count),
        name="attend_first" if first else "attend",
        out_shape=tuple(o for o, _ in outs),
        in_specs=specs,
        out_specs=tuple(spec for _, spec in outs),
        scratch_shapes=there
        + [
            pltpu.VMEM((4, 256, HD), BF16),
            pltpu.VMEM((5, 256, 512), F32),
            pltpu.VMEM((1, W3), F32),
            pltpu.VMEM((1, W3), F32),
            pltpu.VMEM((HD, W3), F32),
            pltpu.VMEM((3, HD, W3), BF16),
            pltpu.VMEM((3, HD, W3), BF16),
            pltpu.VMEM((3, 2, 1, W3), F32),
            pltpu.VMEM((3, 2, 1, W3), F32),
            pltpu.VMEM((3, 4, 192, TOK), BF16),
            pltpu.VMEM((3, 4, 8, TOK), F32),
            DMA((3, 8)), DMA((3, 8)), DMA((3, 8)), DMA((3, 8)),
            DMA((2, 3)), DMA((2, 3)), DMA((2, 3, 4)), DMA((2, 3, 4)),
        ]
        + scratch,
        compiler_params=params(collective, limit),
        cost_estimate=cost(30),
    )(*ins)


def attend_back_kernel(carry_sum, n_in, n_out, n_more, *refs):
    ins, refs = refs[:n_in], refs[n_in:]
    outs, refs = refs[:n_out], refs[n_out:]
    (dq_part, dkv_part, extra_out, do_all, st_all, k_nat, v_nat, bias, rows_s, dq, dq_other, dkv, q_send,
     q_recv, q_y, kv_low, extra, qs, qr, ks, kr, ps, pr, ys, yr, es, er) = refs[:27]
    more, scratch = refs[27 : 27 + n_more], refs[27 + n_more :]
    q_all, kv_all, starts_ref = ins[-3:]
    ctx = Context()
    ctx.q_all, ctx.kv_all = q_all, kv_all
    row, seq, n, w = place()
    bar = greet(row, n, w)
    torus = Torus(row, n, w)
    if carry_sum:
        came, one, gather, two = more
        half = extra.at[pl.ds(48 * EARLY * lax.rem(w, 2), 48 * EARLY)]
        for k in range(1, 4):
            pl.semaphore_signal(bar, inc=1, device_id=torus.along(2, k)[0], device_id_type=MESH)
        early = Reduce(torus, EARLY, es, er)
    else:
        (extra_in,) = more
        move = remote(extra, extra_in, es, er, (row, 8 * (7 - n) + w))
    core, y = lax.rem(w, 2), w // 2
    own_k = octet_of(n, w)
    grads = Spread(row, n, w, qs, qr)
    ctx.do_own, ctx.st_own, ctx.extra = do_all.at[grads.own], st_all.at[grads.own], extra
    make = between_part if carry_sum else turn_part
    grads_of = make(ctx, ins[:-3], outs, scratch)
    pl.semaphore_wait(bar, 17 if carry_sum else 14)

    def part(g):
        return lambda slot: do_all.at[slot, pl.ds(192 * g, 192)]

    def stats(slot):
        return st_all.at[slot]

    grads.start(3, stats)
    for g in range(3):
        grads.start(g, part(g))
    if carry_sum:
        grads_of()
        early.exchange(extra, came)
    fill_masks(bias, starts_ref, n, w)
    for g in range(3):
        for j in range(8):
            at = slice((j % 2) * TOK, (j % 2) * TOK + TOK)
            k_nat[g, j // 2, at, :] = jnp.transpose(kv_all[j, TOK * g : TOK * g + HD, :])
            v_nat[g, j // 2, at, :] = jnp.transpose(kv_all[j, TOK * g + HD : TOK * g + TOK, :])
    grads.forward(3, stats)
    grads.forward(0, part(0))
    if carry_sum:
        for p in range(3):
            early.first(p, extra, came, half, one)
    if not carry_sum:

        @pl.when(core == 1)
        def _():
            move.start()

    def phase(g, sel, dq):
        dq[...] = jnp.zeros(dq.shape, F32)
        for i, first in enumerate((0, 16)):
            for j in range(3):
                for c in range(4):
                    at = 512 * j + TOK * c
                    line = first + 3 * g + j
                    rows_s[i, :, at : at + TOK] = st_all[4 * sel + c, line : line + 1, :]

        def step(at, kc, keys):
            qt = three_heads(q_all, sel, g)
            dt = three_heads(do_all, sel, g)
            scores = dot(k_nat[g, kc, 0:keys], qt, 1, 0)
            dp = dot(v_nat[g, kc, 0:keys], dt, 1, 0)
            mask = bias[at, 0:keys]
            ps_, ds_ = [], []
            for j in range(3):
                cols = slice(512 * j, 512 * j + 512)
                p = jnp.exp2(scores[:, cols] + mask - rows_s[0, :, cols])
                ds_.append((p * (dp[:, cols] - rows_s[1, :, cols])).astype(BF16))
                ps_.append(p.astype(BF16))
            p = jnp.concatenate(ps_, axis=1)
            ds = jnp.concatenate(ds_, axis=1)
            dkv[kc, 0:HD, 0:keys] += dot(ds, qt, 1, 1).T
            dkv[kc, HD:, 0:keys] += dot(p, dt, 1, 1).T
            dq[...] += dot(key_blocks(kv_all, kc, TOK * g, keys), ds, 1, 0)

        over_keys(n, sel, step)

    pairs, flying = [], []
    for g in range(3):
        dkv[...] = jnp.zeros(dkv.shape, F32)
        if g == 0:
            phase(g, core, dq)
            grads.forward(1, part(1))
            grads.arrive(3)
        grads.arrive(g)
        phase(g, 1 - core, dq_other)
        q_send[g] = (dq_other[...] * SCALE).astype(BF16)
        pair = remote(q_send.at[g], q_recv.at[g], ps.at[g], pr.at[g], grads.partner)
        pair.start()
        pairs.append(pair)
        if g == 1:
            grads.forward(2, part(2))
        if g == 2 and carry_sum:
            for p in range(3):
                early.second(p, half, one, gather, two)
        if g > 0:
            phase(g, core, dq)
        for j in range(8):
            cols = slice((j % 2) * TOK, (j % 2) * TOK + TOK)
            kv_low[g, j, 0:HD, :] = (dkv[j // 2, 0:HD, cols] * (SCALE / EXP_SCALE)).astype(BF16)
            kv_low[g, j, HD:, :] = dkv[j // 2, HD:, cols].astype(BF16)
        for k in FAR:
            to = lax.rem(n + k, 8)
            cp = remote(
                kv_low.at[g, octet_of(to, w)], dkv_part.at[n, pl.ds(TOK * g, TOK)], ks.at[g, k],
                kr.at[g, k], (row, 8 * to + w),
            )
            cp.start()
            flying.append(cp)
        pair.wait_recv()
        out = (dq[...] * SCALE + q_recv[g].astype(F32)).astype(BF16)
        for i in range(4):
            q_y[g, i] = by_chip(out, i)
        for k in (2, 1, 3):
            to = lax.rem(y + k, 4)
            cp = remote(q_y.at[g, to], dq_part.at[y, pl.ds(192 * g, 192)], ys.at[g, k], yr.at[g, k],
                        grads.chip(k))
            cp.start()
            flying.append(cp)
        dkv_part[n, TOK * g : TOK * g + TOK, :] = kv_low[g, own_k]
        dq_part[y, 192 * g : 192 * g + 192, :] = q_y[g, y]
        if carry_sum:
            for p in range(3):
                if g == 2:
                    early.third(p, gather, two, extra_out)
    grads.finish()
    for cp in pairs:
        cp.wait_send()
    for cp in flying:
        cp.wait()
    if carry_sum:
        for p in range(3):
            early.got(3, p)
        early.finish()
    else:

        @pl.when(core == 1)
        def _():
            move.wait()
            extra_out[...] = extra_in[...]

        @pl.when(core == 0)
        def _():
            extra_out[...] = extra[...]


def attend_back(carry_sum, ins, specs, outs, scratch, limit):
    if carry_sum:
        u = EARLY
        extra_shape = sds(units(u, 3, 4), BF16)
        extra = pltpu.VMEM(units(96 * u), BF16)
        sems = [DMA((5, 3, 4))] * 2
        more = [
            pltpu.VMEM(shape, BF16)
            for shape in (
                units(48 * u), units(4 * u, 3, 3), units(4 * u, 3), units(u, 3, 3),
            )
        ]
    else:
        extra_shape = X_T
        extra = pltpu.VMEM((D, TOK), F32)
        sems = [DMA, DMA]
        more = [pltpu.VMEM((D, TOK), F32)]
    return pl.pallas_call(
        functools.partial(attend_back_kernel, carry_sum, len(ins), len(outs), len(more)),
        name="attend_back_sum" if carry_sum else "attend_back",
        out_shape=tuple(outs + [sds((4, D, TOK), BF16), sds((8, 2 * KV, TOK), BF16), extra_shape]),
        in_specs=specs,
        out_specs=(VM,) * (len(outs) + 3),
        scratch_shapes=[
            pltpu.VMEM((8, D, TOK), BF16),
            pltpu.VMEM((8, 32, TOK), F32),
            pltpu.VMEM((3, 4, 256, HD), BF16),
            pltpu.VMEM((3, 4, 256, HD), BF16),
            pltpu.VMEM((5, 256, 512), F32),
            pltpu.VMEM((2, 1, W3), F32),
            pltpu.VMEM((HD, W3), F32),
            pltpu.VMEM((HD, W3), F32),
            pltpu.VMEM((4, TOK, 256), F32),
            pltpu.VMEM((3, HD, W3), BF16),
            pltpu.VMEM((3, HD, W3), BF16),
            pltpu.VMEM((3, 4, 192, TOK), BF16),
            pltpu.VMEM((3, 8, TOK, TOK), BF16),
            extra,
            DMA((4, 8)), DMA((4, 8)), DMA((3, 8)), DMA((3, 8)),
            DMA((3,)), DMA((3,)), DMA((3, 4)), DMA((3, 4)),
        ]
        + sems
        + more
        + scratch,
        compiler_params=params(5 if carry_sum else 3, limit),
        cost_estimate=cost(40),
    )(*ins)


def both_rows(a, b):
    return jnp.concatenate([a[...], b[...]], axis=0)


def as_units(value):
    return value.astype(BF16).reshape(units(value.shape[0] // 16))


def early_grads(oa, ob, daa, dab, h2a, h2b, dga, dgb, dua, dub, hida, hidb, gma, gmb, g_out):
    ot = jnp.concatenate([oa[...], ob[...]], axis=1)
    h2t = both_rows(h2a, h2b).T
    gmt = both_rows(gma, gmb).T
    for i in range(6):
        cols = slice(256 * i, 256 * i + 256)
        for t, (lhs, a, b) in enumerate(((h2t, dga, dgb), (h2t, dua, dub), (gmt, hida, hidb))):
            rhs = jnp.concatenate([a[:, cols], b[:, cols]], axis=0)
            g_out[36 * (6 * t + i) : 36 * (6 * t + i) + 36] = as_units(dot(lhs, rhs, 1, 0))
    da = both_rows(daa[:, 128:384], dab[:, 128:384])
    g_out[648:672] = as_units(dot(ot[0:384], da, 1, 0))


def late_grads(h1a, h1b, dqa, dqb, oa, ob, daa, dab, g_out):
    h1t = both_rows(h1a, h1b).T
    ot = jnp.concatenate([oa[...], ob[...]], axis=1)
    dat = both_rows(daa, dab).T

    def rows(first, last):
        return jnp.concatenate([dqa[first:last, :], dqb[first:last, :]], axis=1)

    g_out[0:36] = as_units(dot(h1t, rows(0, 256), 1, 1))
    g_out[36:72] = as_units(dot(h1t, rows(256, 512), 1, 1))
    mixed = [dot(h1t, rows(512, 640), 1, 1), dot(ot, dat[0:128], 1, 1)]
    g_out[72:108] = as_units(jnp.concatenate(mixed, axis=1))
    g_out[108:120] = as_units(dot(ot[384:576], dat[128:384], 1, 1))
    low = jnp.concatenate([dat[384:576], jnp.zeros((64, 256), BF16)], axis=0)
    high = jnp.concatenate([jnp.zeros((192, 256), BF16), rows(640, 704)], axis=0)
    g_out[120:156] = as_units(dot(ot, low, 1, 1) + dot(h1t, high, 1, 1))
    g_out[156:192] = as_units(dot(h1t, rows(704, 960), 1, 1))


def spread_kernel(
    early, late, x_in, g_in, gains, ga_out, gm_out, x_out, g_out, gate_out, up_out, down_out, q_out, k_out, v_out, o_out, big, small, kt, vt, sems
):
    def block(ref, first, count=36):
        return ref[first : first + count].reshape(16 * count, 256).astype(F32)

    ga_out[...] = gains[0:1, :].reshape(D)
    gm_out[...] = gains[1:2, :].reshape(D)
    cps = [
        pltpu.make_async_copy(x_in, x_out, sems.at[22]),
        pltpu.make_async_copy(g_in, g_out, sems.at[23]),
    ]
    for cp in cps:
        cp.start()
    for t, ref in enumerate((gate_out, up_out, down_out)):
        for i in range(6):
            rows = pl.ds(96 * i, 96)
            for c in range(6):
                big[t, rows, 256 * c : 256 * c + 256] = block(early, 36 * (6 * t + c) + 6 * i, 6)
            cp = pltpu.make_async_copy(big.at[t, rows], ref.at[rows], sems.at[6 * t + i])
            cp.start()
            cps.append(cp)
    small[0, :, 0:256] = block(late, 0)
    small[0, :, 256:512] = block(late, 36)
    mixed = block(late, 72)
    small[0, :, 512:576] = mixed[:, 0:64]
    small[1, :, 0:128] = mixed[:, 128:256]
    kt[0:64, :] = mixed[:, 0:128].T[64:128]
    small[1, 0:384, 128:384] = block(early, 648, 24)
    small[1, 384:576, 128:384] = block(late, 108, 12)
    mixed = block(late, 120)
    small[1, :, 384:576] = mixed[:, 0:192]
    kt[64:128, :] = mixed[:, 128:256].T[64:128]
    last = block(late, 156).T
    kt[128:192, :] = last[0:64]
    vt[...] = last[64:256]
    for i, (src, dst) in enumerate(
        ((small.at[0], q_out), (small.at[1], o_out), (kt, k_out), (vt, v_out))
    ):
        cp = pltpu.make_async_copy(src, dst, sems.at[18 + i])
        cp.start()
        cps.append(cp)
    for cp in cps:
        cp.wait()


def spread(*ins):
    return pl.pallas_call(
        spread_kernel,
        name="spread",
        out_shape=(
            sds((D,), F32), sds((D,), F32), X_T, X_T, sds((D, FF), F32), sds((D, FF), F32), sds((D, FF), F32), sds((D, D), F32),
            sds((KV, D), F32), sds((KV, D), F32), sds((D, D), F32),
        ),
        in_specs=[VM] * 5,
        out_specs=(VM,) * 2 + (ANY,) * 9,
        scratch_shapes=[
            pltpu.VMEM((3, D, FF), F32),
            pltpu.VMEM((2, D, D), F32),
            pltpu.VMEM((KV, D), F32),
            pltpu.VMEM((KV, D), F32),
            DMA((24,)),
        ],
        compiler_params=params(None, 30 << 20),
    )(*ins)


def reduce_kernel(
    mid_ref, dq, dkv, x, dx1, ga, wq, wk, wv, cos, sin, h10, h11, dqkv1, ob0, ob1, da0, da1,
    gga1, ggm0, ggm1, early_out, late_out, gain_out, fin_out,
    late_ref, early_mid, came, half, one, gather, two, three, mid, gain_in, gain_sum, fin_ref, fin_in, dqkv0,
    s_e, r_e, s_l, r_l, gs, gr, fs, fr
):
    row, seq, n, w = place()
    torus = Torus(row, n, w)
    core = torus.core
    bar = pltpu.get_barrier_semaphore()
    pl.semaphore_signal(bar, inc=1, device_id=torus.partner, device_id_type=MESH)
    for axis in range(3):
        for k in range(1, 4):
            pl.semaphore_signal(bar, inc=1, device_id=torus.along(axis, k)[0], device_id_type=MESH)
    mirror = (row, 8 * (7 - n) + w)
    g, gga0 = project_back(
        dq, dkv, x[...], dx1[...], as_row(ga), wq, wk, wv, cos[...], sin[...], dqkv0
    )
    fin_ref[...] = g.T
    late_grads(h10, h11, dqkv0, dqkv1, ob0, ob1, da0, da1, late_ref)
    gain_sum[0] = jnp.concatenate(
        [gga0 + gga1[...], ggm0[...] + ggm1[...], jnp.zeros((6, D), F32)], axis=0
    )

    @pl.when(core == 1)
    def _():
        pl.semaphore_signal(bar, inc=1, device_id=mirror, device_id_type=MESH)
        pl.semaphore_wait(bar, 11)

    @pl.when(core == 0)
    def _():
        pl.semaphore_wait(bar, 10)

    early = Reduce(torus, EARLY, s_e, r_e)
    late = Reduce(torus, LATE, s_l, r_l)
    late.exchange(late_ref, came)

    def early_chunk(chunk):
        for p in range(3):
            if chunk == 0:
                early.got(4, p)
            early.fifth(p, early_mid, early_out, chunk, 4)

    for p in range(3):
        early.fourth(p, mid_ref, early_mid)
    move = remote(fin_ref, fin_in, fs, fr, mirror)

    @pl.when(core == 1)
    def _():
        move.start()

    gains = []

    def gain_round(i, peers, count, at):
        gain_in[i, at] = gain_sum[i]
        for k, peer in enumerate(peers):
            cp = remote(gain_sum.at[i], gain_in.at[i, at], gs.at[i, k], gr.at[i, k], peer)
            cp.start()
            gains.append(cp)

    def gain_total(i, peers, count):
        for cp in gains[-peers:]:
            cp.wait_recv()
        return sum(gain_in[i, j] for j in range(count))

    def axis_peers(axis):
        return [torus.along(axis, k)[0] for k in range(1, 4)]

    gain_round(0, [torus.partner], 2, core)
    for p in range(3):
        late.first(p, late_ref, came, half, one)
    early_chunk(0)
    gain_sum[1] = gain_total(0, 1, 2)
    gain_round(1, axis_peers(0), 4, torus.spot[0])
    for p in range(3):
        late.second(p, half, one, gather, two)
    early_chunk(1)
    gain_sum[2] = gain_total(1, 3, 4)
    gain_round(2, axis_peers(1), 4, torus.spot[1])
    for p in range(3):
        late.third(p, gather, two, three)
    early_chunk(2)
    gain_sum[3] = gain_total(2, 3, 4)
    gain_round(3, axis_peers(2), 4, torus.spot[2])
    for p in range(3):
        late.fourth(p, three, mid)
    early_chunk(3)
    gain_out[...] = gain_total(3, 3, 4)
    for p in range(3):
        late.got(4, p)
        late.fifth(p, mid, late_out)
    for p in range(3):
        early.sixth(p, early_out, 4)
    for p in range(3):
        late.sixth(p, late_out)

    @pl.when(core == 1)
    def _():
        move.wait()
        fin_out[...] = fin_in[...]

    @pl.when(core == 0)
    def _():
        fin_out[...] = fin_ref[...]

    for cp in gains:
        cp.wait_send()
    for p in range(3):
        early.got(6, p)
        late.got(6, p)
    early.finish()
    late.finish()


def reduce_all(*ins):
    u = LATE
    return pl.pallas_call(
        reduce_kernel,
        name="reduce_all",
        out_shape=(
            sds(units(96 * EARLY), BF16), sds(units(96 * LATE), BF16), sds((8, D), F32), X_T
        ),
        in_specs=[VM] * len(ins),
        out_specs=(VM,) * 4,
        scratch_shapes=[
            pltpu.VMEM(shape, BF16)
            for shape in (
                units(96 * u), units(4 * EARLY, 3), units(48 * u), units(48 * u), units(4 * u, 3, 3), units(4 * u, 3), units(u, 3, 3),
                units(u, 3, 4), units(4 * u, 3),
            )
        ]
        + [
            pltpu.VMEM((4, 4, 8, D), F32),
            pltpu.VMEM((4, 8, D), F32),
            pltpu.VMEM((D, TOK), F32),
            pltpu.VMEM((D, TOK), F32),
            pltpu.VMEM((960, TOK), BF16),
        ]
        + [DMA((11, 3, 4))] * 4
        + [DMA((4, 4)), DMA((4, 4)), DMA, DMA],
        compiler_params=params(4, 24 << 20),
        cost_estimate=cost(40),
    )(*ins)


def on_device(
    tokens, cotangent, segment_ids, gain_attn, wq, wk, wv, wo, gain_mlp, wg, wu, wd
):
    ga, gm = gain_attn, gain_mlp
    wk, wv, wd = wk.T, wv.T, wd.T
    w_q, w_k, w_v = sds((D, D), BF16), sds((KV, D), BF16), sds((KV, D), BF16)
    table = sds((32, TOK), F32)
    x0, h10, starts, cos, sin, qa0, kva0, part, stat = attend(
        True,
        [tokens[0].T, segment_ids, ga, wq, wk, wv, begin()],
        [HBM, HBM, VM, HBM, HBM, HBM, VM],
        [(o, VM) for o in (X_S, H_S, sds((2, 1, 4 * TOK), jnp.int32), table, table)]
        + [(sds(*a), HBM) for a in GATHERED],
        [
            pltpu.VMEM((D, TOK), F32),
            pltpu.VMEM((64, 1, TOK), jnp.int32),
            pltpu.VMEM((64, 1, TOK), jnp.int32),
        ]
        + [DMA((8,))] * 4
        + [DMA((2,)), DMA]
        + buffers(w_q, w_k, w_v)
        + [DMA((3,))],
        1,
        20 << 20,
    )
    cot, h11, x1, m0, h20, inv0, gate0, up0, hid0, o0, lse0, qa1, kva1, part, stat = attend(
        False,
        [part, stat, x0, cotangent[0].T, ga, wq, wk, wv, wo, gm, wg, wu, wd, cos, sin, starts],
        [VM] * 16,
        [(o, VM) for o in (X_S, H_S, X_S, X_S, H_S, sds((TOK, TOK), F32))]
        + [(F_S, HBM), (F_S, HBM)]
        + [(o, VM) for o in (FB_S, sds((D, TOK), F32), sds((16, TOK), F32))],
        [pltpu.VMEM((TOK, FF), F32), pltpu.VMEM((TOK, FF), F32), DMA((2,)), pltpu.VMEM((D, TOK), F32),
         DMA((2,)), DMA],
        2,
        20 << 20,
    )
    h21, hid1, ob1, gm1, dg1, du1, da1, dx1, ggm1, dq, dkv, output = attend_back(
        False,
        [part, stat, x1, cot, wo, gm, wg, wu, wd, qa1, kva1, starts],
        [VM] * 12,
        [H_S, FB_S, Q_T, H_S, FB_S, FB_S, H_S, X_S, G_S],
        [pltpu.VMEM((D, TOK), F32), pltpu.VMEM((16, TOK), F32)],
        20 << 20,
    )
    dqkv1, gga1, da0, dx0, ggm0, ob0, dq, dkv, mid = attend_back(
        True,
        [dq, dkv, x1, dx1, ga, wq, wk, wv, cos, sin, m0, inv0, gate0, up0, wo, gm, wg, wu, wd, o0,
         lse0, ob1, da1, h20, h21, dg1, du1, hid0, hid1, gm1, qa0, kva0, starts],
        [VM] * 33,
        [sds((960, TOK), BF16), G_S, H_S, X_S, G_S, Q_T],
        [pltpu.VMEM((TOK, D), BF16), pltpu.VMEM((TOK, FF), BF16), pltpu.VMEM((TOK, FF), BF16)],
        28 << 20,
    )
    early, late, gains, grad_tokens = reduce_all(
        mid, dq, dkv, x0, dx0, ga, wq, wk, wv, cos, sin, h10, h11, dqkv1, ob0, ob1, da0, da1, gga1,
        ggm0, ggm1
    )
    gga, ggm, output, grad_tokens, gate, up, down, query, key, value, out = spread(
        early, late, output, grad_tokens, gains
    )
    return (
        output.T[None], grad_tokens.T[None], gga, query, key.T, value.T, out, ggm, gate, up,
        down.T,
    )


def solution(mesh):
    rows = P("rows", "seq", None)
    in_specs = (rows, rows, P("rows", "seq")) + (P(),) * 9
    out_specs = (rows, rows) + (P(),) * 9
    return jax.shard_map(
        on_device, mesh=mesh, in_specs=in_specs, out_specs=out_specs, check_vma=False
    )
```
